128 devices in a mesh: fsdp: 32 (over y, x, z_lo), seq: 4 (over z_hi, core).
Axes of the slice: x: 4, y: 4, z: 4 (z_hi: 2, z_lo: 2; z = z_hi * 2 + z_lo), core: 2. Of those that a mesh axis runs over, the one named last changes fastest.
Arguments:
- tokens: bfloat16 [32768, 1536], P(('fsdp', 'seq')), may hold values from -6 to 6
- segments: int32 [32768], P('fsdp'), may hold values from 0 to 1023, as said below
- routes: int32 [32768, 6], P(('fsdp', 'seq')), may hold values from 0 to 7, all different within a row; in each aligned block of 256 rows (0 to 255, 256 to 511, ...) at most 224 rows name the same one
- shared_mask: int32 [32768], P(('fsdp', 'seq')), may hold values 0 or 1
- norm_gain: bfloat16 [1536], P('fsdp'), may hold values from 0.5 to 1.5
- w_query: bfloat16 [1536, 1536], P('fsdp'), may hold values from -0.21875 to 0.21875
- key_weight: bfloat16 [1536, 512], P('fsdp'), may hold values from -0.15625 to 0.15625
- value_weight: bfloat16 [1536, 512], P('fsdp'), may hold values from -0.15625 to 0.15625
- w_out: bfloat16 [1536, 1536], P('fsdp'), may hold values from -0.625 to 0.625
- ffn_gain: bfloat16 [1536], P('fsdp'), may hold values from 0.5 to 1.5
- w_router: bfloat16 [1536, 8], P('fsdp'), may hold values from -0.078125 to 0.078125
- shared_gate: bfloat16 [1536, 1024], P('fsdp'), may hold values from -0.15625 to 0.15625
- shared_up: bfloat16 [1536, 1024], P('fsdp'), may hold values from -0.15625 to 0.15625
- shared_down: bfloat16 [1536, 1024], P('fsdp'), may hold values from -0.1875 to 0.1875
- expert_gate: bfloat16 [1536, 8, 512], P('fsdp'), may hold values from -0.15625 to 0.15625
- expert_up: bfloat16 [1536, 8, 512], P('fsdp'), may hold values from -0.15625 to 0.15625
- expert_down: bfloat16 [1536, 8, 512], P('fsdp'), may hold values from -0.5 to 0.5
- cotangent: bfloat16 [32768, 1536], P(('fsdp', 'seq')), may hold values from -24 to 24
Outputs:
- output: bfloat16 [32768, 1536], P(('fsdp', 'seq'))
- grad_tokens: bfloat16 [32768, 1536], P(('fsdp', 'seq'))
- grad_norm_gain: float32 [1536], P('fsdp')
- grad_w_query: float32 [1536, 1536], P('fsdp')
- grad_w_key: float32 [1536, 512], P('fsdp')
- grad_w_value: float32 [1536, 512], P('fsdp')
- grad_w_out: float32 [1536, 1536], P('fsdp')
- grad_ffn_gain: float32 [1536], P('fsdp')
- grad_w_router: float32 [1536, 8], P('fsdp')
- grad_shared_gate: float32 [1536, 1024], P('fsdp')
- grad_shared_up: float32 [1536, 1024], P('fsdp')
- grad_shared_down: float32 [1536, 1024], P('fsdp')
- grad_expert_gate: float32 [1536, 8, 512], P('fsdp')
- grad_expert_up: float32 [1536, 8, 512], P('fsdp')
- grad_expert_down: float32 [1536, 8, 512], P('fsdp')
The draws below stay inside these ranges and needn't reach their ends.
Inputs may be any that keep to these rules, and one draw needn't show every extreme that they name: `segments`: in each sequence of 1024 positions a position's id is the position where its document begins: ids never fall, and the last position of every sequence is a document of its own. `routes`: within the 256 rows of one device no expert is named by more than 224 rows; on some device one expert is named by exactly 224.
All inputs are finite; a program needn't handle non-finite values. No bound on the sum of `shared_mask` on one device may be relied on, other than what follows from the above.
Results may differ from the reference program's by a relative error of at most 0.028.
Values may be sent and summed in bfloat16 or wider, within the bound.
A program may use at most 384 MiB of HBM per device.

```python
import math
import jax
import jax.numpy as jnp
import numpy as np
from jax import lax

MODEL_WIDTH = 1536
QUERY_HEADS = 12
KEY_VALUE_HEADS = 4
HEAD_SIZE = 128
FE = 512
FS = 1024
TOPK = 6
E = 8
TOK_DEV = 256
L = 1024
TOKENS = 32768
CAP = 224
N_FSDP = 32


def draw_segments(key, part):
    key = jax.random.fold_in(key, 7)
    start_key, first_key, last_key = jax.random.split(key, 3)
    groups = TOKENS // L
    spread = TOK_DEV // 2
    first = jax.random.randint(first_key, (groups, 1), 1, spread + 1)
    last = L - jax.random.randint(last_key, (groups, 1), 1, spread + 1)
    positions = jnp.arange(L, dtype=jnp.int32)[None, :]
    fresh = jax.random.randint(start_key, (groups, L), 0, 24) == 0
    fresh = fresh & ((positions < first) | (positions > last))
    fresh = fresh | (positions == first) | (positions == last) | (positions == L - 1)
    fresh = fresh & (positions > 0)
    starts_at = jnp.where(fresh, jnp.broadcast_to(positions, (groups, L)), 0).astype(jnp.int32)
    return lax.cummax(starts_at, axis=1).astype(jnp.int32).reshape(groups * L)


def place_ends(array, rng, least, largest):
    longest = array.shape.index(max(array.shape))
    spots = []
    for shift in (0, 1):
        where = [jax.random.randint(jax.random.fold_in(rng, axis), (), 0, length) for axis, length in enumerate(array.shape)]
        where[longest] = (where[longest] + shift) % array.shape[longest]
        spots.append(tuple(where))
    return array.at[spots[0]].set(least).at[spots[1]].set(largest)


def spiked(drawn, rng, source, target, parts, factor):
    def block_of(axis_at):
        return (jnp.arange(drawn.shape[axis_at]) // (drawn.shape[axis_at] // parts)).reshape((-1,) + (1,) * (drawn.ndim - 1 - axis_at))

    one_side = jax.random.permutation(rng, parts)[block_of(target)]
    other_side = (block_of(target) + parts // 2) % parts
    return jnp.where((block_of(source) == one_side) | (block_of(source) == other_side), factor * drawn, drawn)


def block_scale(stream_key, shape, cuts, low, top_value):
    loudness = 1.0
    for position, parts in cuts:
        draws = jax.random.uniform(jax.random.fold_in(jax.random.fold_in(stream_key, 6), position), (parts,), jnp.float32, low / len(cuts), top_value / len(cuts))
        loudness = loudness * jnp.repeat(jnp.exp(draws), shape[position] // parts).reshape((-1,) + (1,) * (len(shape) - 1 - position))
    return loudness


def shared_out(own_key, own, number, rows, amount, top, reach, skew):
    order = jax.random.permutation(own_key, amount)
    crowded, ordinary = load_shares(amount, rows * top, reach, skew, True), load_shares(amount, rows * top, reach, skew, False)
    places = jnp.arange(amount)

    def named(sizes, offset_by):
        used = int((sizes > 0).sum())
        fixed = max(1, used // 4)
        moved = fixed + (places - fixed + offset_by * (used - fixed)) % max(1, amount - fixed)
        return jnp.zeros((amount,), jnp.int32).at[order[jnp.where(places < fixed, places, moved)]].set(jnp.asarray(sizes, jnp.int32))

    sizes = jnp.where(number % 4 == 0, named(crowded, number // 4), named(ordinary, number - number // 4 - 1))
    mixed = jax.random.permutation(jax.random.fold_in(own, 3), amount)
    donor, sink = mixed[0:amount // 2 * 2:2], mixed[1:amount // 2 * 2:2]
    slack = jnp.minimum(sizes[donor] - 1, reach - sizes[sink]) // 2
    slack = jnp.where((donor == order[0]) | (sink == order[0]) | (sizes[sink] == 0), 0, jnp.maximum(slack, 0))
    moved = jax.random.randint(jax.random.fold_in(own, 4), (amount // 2,), 0, 1 << 20) % (slack + 1)
    sizes = sizes.at[donor].add(-moved).at[sink].add(moved)
    items = jnp.searchsorted(jnp.cumsum(sizes), jnp.arange(rows * top), side="right").astype(jnp.int32)
    listing = items.reshape(top, rows).T
    listing = listing[jax.random.permutation(jax.random.fold_in(own, 1), rows)]
    offset_by = jax.random.randint(jax.random.fold_in(own, 2), (rows, 1), 0, top)
    return jnp.take_along_axis(listing, (jnp.arange(top)[None, :] + offset_by) % top, axis=1)


def load_shares(amount, total, limit, lean, full):
    weights = [(1 << 20) // math.isqrt(grade ** lean) + 1 for grade in range(1, amount + 1)]
    largest = limit if full else min(limit, max(-(-total // amount), total * weights[0] // sum(weights)))
    least = 1 if total - largest >= amount - 1 else 0
    holding, surplus = [largest] + [least] * (amount - 1), total - largest - least * (amount - 1)
    while surplus > 0:
        candidates = [i for i in range(1, amount) if holding[i] < largest] or [i for i in range(1, amount) if holding[i] < limit]
        whole, left = sum([weights[i] for i in candidates]), surplus
        for i in candidates:
            more = min(limit - holding[i], max(1, left * weights[i] // whole), surplus)
            holding[i] = holding[i] + more
            surplus = surplus - more
    return np.array(holding)


def gaussian(own_key, shape, width, bound, shards=(), kind=jnp.bfloat16):
    level = block_scale(own_key, shape, shards, -0.22, 0.18) if shards else 1.0
    values = jax.random.normal(own_key, shape, jnp.float32) * width * level
    return jnp.minimum(jnp.maximum(values, -bound), bound).astype(kind)


def noise_with(own_key, dims, scale, reach, cuts, heavy, kind=jnp.bfloat16):
    array = scale * jax.random.normal(own_key, dims, jnp.float32)
    if cuts:
        array = array * block_scale(own_key, dims, cuts, -0.22, 0.18)
    return jnp.clip(spiked(array, jax.random.fold_in(own_key, 3), *heavy), -reach, reach).astype(kind)


def setup_inputs(seed: int = 0) -> dict:
    seeds = jax.random.split(jax.random.key(seed), 19)
    tokens = gaussian(seeds[0], (TOKENS, MODEL_WIDTH), 1.0, 6.0, ((0, 128),))
    segments = draw_segments(jax.random.fold_in(seeds[18], 71), 0)
    routes_keys = jax.random.split(jax.random.fold_in(seeds[2], 1), TOKENS // TOK_DEV)
    routes_turns = jax.random.permutation(jax.random.fold_in(seeds[2], 3), TOKENS // TOK_DEV)
    routes = jax.vmap(lambda own, number: shared_out(jax.random.fold_in(seeds[2], 2), own, number, TOK_DEV, E, TOPK, CAP, 1))(routes_keys, routes_turns).reshape((TOKENS, TOPK))
    shared_mask = place_ends((jax.random.randint(seeds[3], (TOKENS,), 0, 4) < 3).astype(jnp.int32), jax.random.fold_in(seeds[3], 1), 0, 1)
    norm_gain = jnp.clip(1.0 + 0.1 * jax.random.normal(seeds[4], (MODEL_WIDTH,), jnp.float32), 0.5, 1.5).astype(jnp.bfloat16)
    w_query = gaussian(seeds[5], (MODEL_WIDTH, QUERY_HEADS * HEAD_SIZE), (MODEL_WIDTH // 2) ** -0.5, 0.21875, ((0, 32),))
    key_weight = gaussian(seeds[6], (MODEL_WIDTH, KEY_VALUE_HEADS * HEAD_SIZE), MODEL_WIDTH ** -0.5, 0.15625, ((0, 32),))
    value_weight = gaussian(seeds[7], (MODEL_WIDTH, KEY_VALUE_HEADS * HEAD_SIZE), MODEL_WIDTH ** -0.5, 0.15625, ((0, 32),))
    w_out = gaussian(seeds[8], (MODEL_WIDTH, QUERY_HEADS * HEAD_SIZE), (QUERY_HEADS * HEAD_SIZE // 16) ** -0.5, 0.625, ((0, 32),))
    ffn_gain = jnp.clip(1.0 + 0.1 * jax.random.normal(seeds[9], (MODEL_WIDTH,), jnp.float32), 0.5, 1.5).astype(jnp.bfloat16)
    w_router = gaussian(seeds[10], (MODEL_WIDTH, E), (4 * MODEL_WIDTH) ** -0.5, 0.078125, ((0, 32),))
    shared_gate = gaussian(seeds[11], (MODEL_WIDTH, FS), MODEL_WIDTH ** -0.5, 0.15625, ((0, 32),))
    shared_up = gaussian(seeds[12], (MODEL_WIDTH, FS), MODEL_WIDTH ** -0.5, 0.15625, ((0, 32),))
    shared_down = gaussian(seeds[13], (MODEL_WIDTH, FS), FS ** -0.5, 0.1875, ((0, 32),))
    expert_gate = gaussian(seeds[14], (MODEL_WIDTH, E, FE), MODEL_WIDTH ** -0.5, 0.15625, ((0, 32),))
    expert_up = gaussian(seeds[15], (MODEL_WIDTH, E, FE), MODEL_WIDTH ** -0.5, 0.15625, ((0, 32),))
    expert_down = gaussian(seeds[16], (MODEL_WIDTH, E, FE), (FE // 4) ** -0.5, 0.5, ((0, 32),))
    cotangent = noise_with(seeds[17], (TOKENS, MODEL_WIDTH), 1.0, 24.0, ((0, 128),), (0, 1, 128, 5.5))
    return dict(tokens=tokens, segments=segments, routes=routes, shared_mask=shared_mask, norm_gain=norm_gain, w_query=w_query, key_weight=key_weight, value_weight=value_weight, w_out=w_out, ffn_gain=ffn_gain, w_router=w_router, shared_gate=shared_gate, shared_up=shared_up, shared_down=shared_down, expert_gate=expert_gate, expert_up=expert_up, expert_down=expert_down, cotangent=cotangent)


@jax.custom_vjp
def low(v):
    return lax.optimization_barrier(v.astype(jnp.bfloat16)).astype(jnp.float32)

@jax.custom_vjp
def low_back(v):
    return v

def low_keep(v):
    return (low(v), None)

def low_pass(kept, grad):
    return (grad,)

def back_keep(v):
    return (v, None)

def back_low(kept, grad):
    return (low(grad),)
low.defvjp(low_keep, low_pass)
low_back.defvjp(back_keep, back_low)
NORM_EPS = 1e-05
HIGHEST_PRECISION = lax.Precision.HIGHEST

def product(left, right):
    return jnp.dot(left, right, precision=HIGHEST_PRECISION, preferred_element_type=jnp.float32)

def rms_scale(value_rows, gain):
    return value_rows * lax.rsqrt(lax.optimization_barrier(jnp.mean(value_rows * value_rows, axis=-1, keepdims=True)) + NORM_EPS) * gain

def attend_heads(query_rows, key_rows, value_rows, segment_ids):
    length_total = query_rows.shape[0]
    block = min(512, length_total)
    scale = HEAD_SIZE ** (-0.5)
    key_rows_full = jnp.repeat(key_rows, QUERY_HEADS // KEY_VALUE_HEADS, axis=1)
    value_rows_full = jnp.repeat(value_rows, QUERY_HEADS // KEY_VALUE_HEADS, axis=1)
    positions = jnp.arange(length_total, dtype=jnp.int32)

    def block_step(start):
        query_block = lax.dynamic_slice_in_dim(query_rows, start, block, 0)
        seg_block = lax.dynamic_slice_in_dim(segment_ids, start, block, 0)
        row_ids = start + jnp.arange(block, dtype=jnp.int32)
        scores = low_back(jnp.einsum('bhd,khd->hbk', query_block, key_rows_full, precision=HIGHEST_PRECISION) * scale)
        allowed = (row_ids[:, None] >= positions[None, :]) & (seg_block[:, None] == segment_ids[None, :])
        scores = jnp.where(allowed[None], scores, -1e+30)
        top = lax.optimization_barrier(jnp.max(scores, axis=-1, keepdims=True))
        weights = jnp.exp(scores - top)
        probs = weights / lax.optimization_barrier(jnp.sum(weights, axis=-1, keepdims=True))
        return jnp.einsum('hbk,khd->bhd', low(probs), value_rows_full, precision=HIGHEST_PRECISION)
    starts = (jnp.arange(length_total // block) * block).astype(jnp.int32)
    outputs = lax.map(jax.checkpoint(block_step), starts)
    return outputs.reshape(length_total, QUERY_HEADS * HEAD_SIZE)

def layer(tokens_f, segment_ids, route_rows, keep, norm_gain, w_query, key_weight, value_weight, w_out, ffn_gain, w_router, shared_gate, shared_up, shared_down, expert_gate, expert_up, expert_down):
    length_total = tokens_f.shape[0]
    normed = low(rms_scale(tokens_f, norm_gain))
    query_rows = low_back(low(product(normed, w_query)))
    key_rows = low_back(low(product(normed, key_weight)))
    value_rows = low_back(low(product(normed, value_weight)))
    head_count = attend_heads(query_rows.reshape(length_total, QUERY_HEADS, HEAD_SIZE), key_rows.reshape(length_total, KEY_VALUE_HEADS, HEAD_SIZE), value_rows.reshape(length_total, KEY_VALUE_HEADS, HEAD_SIZE), segment_ids)
    head_count = low_back(low(head_count))
    hidden = tokens_f + low_back(product(head_count, w_out.T))
    normed_two = low(rms_scale(hidden, ffn_gain))
    logits = product(normed_two, w_router)
    gates = jax.nn.softmax(jnp.take_along_axis(logits, route_rows, axis=1), axis=1)
    member = (route_rows[:, :, None] == jnp.arange(E, dtype=jnp.int32)[None, None, :]).astype(jnp.float32)
    combine = lax.optimization_barrier(jnp.sum(gates[:, :, None] * member, axis=1))
    shared_pre_gate = low_back(product(normed_two, shared_gate))
    shared_pre_up = low_back(product(normed_two, shared_up))
    shared_hidden = low(jax.nn.silu(shared_pre_gate) * shared_pre_up)
    shared_result = product(shared_hidden, shared_down.T)
    gate_all = low_back(jnp.einsum('td,def->tef', normed_two, expert_gate, precision=HIGHEST_PRECISION))
    up_all = low_back(jnp.einsum('td,def->tef', normed_two, expert_up, precision=HIGHEST_PRECISION))
    expert_hidden = low(jax.nn.silu(gate_all) * up_all)
    expert_result = low_back(jnp.einsum('tef,def->ted', expert_hidden, expert_down, precision=HIGHEST_PRECISION))
    mixture = jnp.einsum('te,ted->td', combine, expert_result, precision=HIGHEST_PRECISION)
    return low(hidden + mixture + keep[:, None] * shared_result)

def reference(tokens, segments, routes, shared_mask, norm_gain, w_query, key_weight, value_weight, w_out, ffn_gain, w_router, shared_gate, shared_up, shared_down, expert_gate, expert_up, expert_down, cotangent):
    params = tuple((w.astype(jnp.float32) for w in (norm_gain, w_query, key_weight, value_weight, w_out, ffn_gain, w_router, shared_gate, shared_up, shared_down, expert_gate, expert_up, expert_down)))
    seg_groups = segments.reshape(N_FSDP, L)
    route_groups = routes.reshape(N_FSDP, L, TOPK)
    keep_groups = shared_mask.astype(jnp.float32).reshape(N_FSDP, L)
    checked = jax.checkpoint(layer)

    def whole(tokens_f, *weights):

        def per_group(items):
            return checked(items[0], items[1], items[2], items[3], *weights)
        outputs = lax.map(per_group, (tokens_f.reshape(N_FSDP, L, MODEL_WIDTH), seg_groups, route_groups, keep_groups))
        return outputs.reshape(TOKENS, MODEL_WIDTH)
    output, pullback = jax.vjp(whole, tokens.astype(jnp.float32), *params)
    grads = pullback(cotangent.astype(jnp.float32))
    return (output.astype(jnp.bfloat16), grads[0].astype(jnp.bfloat16), grads[1], grads[2], grads[3], grads[4], grads[5], grads[6], grads[7], grads[8], grads[9], grads[10], grads[11], grads[12], grads[13])
```

```python
import jax
import jax.numpy as jnp
from jax import lax
from jax.sharding import PartitionSpec as P

HEAD = 128
GROUP = 3
E = 8
NY, NX, NZ = 4, 4, 2
SEQ = 4
MISC = 128
EPS = 1e-05
HIGH = lax.Precision.HIGHEST
BF = jnp.bfloat16
F32 = jnp.float32

SEQ_FAR = [(i, i ^ 2) for i in range(SEQ)]
SEQ_NEAR = [(i, i ^ 1) for i in range(SEQ)]
Z_PAIR = [(i, i ^ 1) for i in range(NY * NX * NZ)]


def shift(dy, dx):
    pairs = []
    for y in range(NY):
        for x in range(NX):
            for z in range(NZ):
                to = (((y + dy) % NY) * NX + (x + dx) % NX) * NZ + z
                pairs.append(((y * NX + x) * NZ + z, to))
    return pairs


AXIS_X = (shift(0, 1), shift(0, -1))
AXIS_Y = (shift(1, 0), shift(-1, 0))


def f32dot(left, right, dims):
    return lax.dot_general(left, right, (dims, ((), ())), preferred_element_type=F32)


def mm(left, right):
    return f32dot(left, right, ((1,), (0,)))


def mm_nt(left, right):
    return f32dot(left, right, ((1,), (1,)))


def mm_tn(left, right):
    return f32dot(left, right, ((0,), (0,)))


def swap(value, pairs, axis):
    return lax.ppermute(value, axis, pairs)


def ring_gather(block, axis):
    plus, minus = axis
    before = swap(block, plus, "fsdp")
    after = swap(block, minus, "fsdp")
    half = block.shape[0] // 2
    far_a = swap(before[:half], plus, "fsdp")
    far_b = swap(after[half:], minus, "fsdp")
    return jnp.stack([block, after, jnp.concatenate([far_a, far_b], axis=0), before])


def ring_scatter(blocks, axis):
    plus, minus = axis
    half = blocks.shape[1] // 2
    a = swap(blocks[2, :half], plus, "fsdp")
    b = swap(blocks[2, half:], minus, "fsdp")
    add = lambda u, v: (u.astype(F32) + v.astype(F32)).astype(BF)
    up = jnp.concatenate([add(blocks[1, :half], a), blocks[1, half:]], axis=0)
    down = jnp.concatenate([blocks[3, :half], add(blocks[3, half:], b)], axis=0)
    c = swap(up, plus, "fsdp")
    d = swap(down, minus, "fsdp")
    return blocks[0].astype(F32) + c.astype(F32) + d.astype(F32)


def unturned(blocks, position):
    out = jnp.zeros_like(blocks)
    for k in range(blocks.shape[0]):
        out = lax.dynamic_update_index_in_dim(out, blocks[k], lax.rem(position + k, blocks.shape[0]), 0)
    return out


def turned(blocks, position):
    n = blocks.shape[0]
    return jnp.stack([lax.dynamic_index_in_dim(blocks, lax.rem(position + k, n), 0, keepdims=False) for k in range(n)])


def gather_weight(block, place, x_first):
    y, x, z = place
    other = swap(block, Z_PAIR, "fsdp")
    pair = jnp.where(z == 0, jnp.stack([block, other]), jnp.stack([other, block]))
    if x_first:
        rows = unturned(ring_gather(pair, AXIS_X), x)
        full = unturned(ring_gather(rows, AXIS_Y), y)
    else:
        rows = unturned(ring_gather(pair, AXIS_Y), y)
        full = jnp.swapaxes(unturned(ring_gather(rows, AXIS_X), x), 0, 1)
    return full.reshape(-1, block.shape[1])


def scatter_grad(grad, place, y_first):
    y, x, z = place
    cols = grad.shape[1]
    blocks = grad.reshape(NY, NX, NZ, -1, cols)
    if y_first:
        part = ring_scatter(turned(blocks, y), AXIS_Y).astype(BF)
        part = ring_scatter(turned(part, x), AXIS_X).astype(BF)
    else:
        part = ring_scatter(turned(jnp.swapaxes(blocks, 0, 1), x), AXIS_X).astype(BF)
        part = ring_scatter(turned(part, y), AXIS_Y).astype(BF)
    mine = lax.dynamic_index_in_dim(part, z, 0, keepdims=False)
    theirs = lax.dynamic_index_in_dim(part, 1 - z, 0, keepdims=False)
    return mine.astype(F32) + swap(theirs, Z_PAIR, "fsdp").astype(F32)


def seq_gather(block, seq):
    z, c = seq
    far = swap(block, SEQ_FAR, "seq")
    pair = jnp.where(z == 0, jnp.stack([block, far]), jnp.stack([far, block]))
    near = swap(pair, SEQ_NEAR, "seq")
    both = jnp.where(c == 0, jnp.stack([pair, near], axis=1), jnp.stack([near, pair], axis=1))
    return both.reshape(SEQ, *block.shape)


def seq_scatter(value, seq):
    z, c = seq
    parts = value.reshape(2, 2, -1, value.shape[1])
    mine = lax.dynamic_index_in_dim(parts, c, 1, keepdims=False)
    theirs = lax.dynamic_index_in_dim(parts, 1 - c, 1, keepdims=False)
    near = swap(theirs, SEQ_NEAR, "seq")
    total = mine.astype(F32) + near.astype(F32)
    away = lax.dynamic_index_in_dim(total, 1 - z, 0, keepdims=False).astype(BF)
    far = swap(away, SEQ_FAR, "seq")
    return lax.dynamic_index_in_dim(total, z, 0, keepdims=False) + far.astype(F32)


def allowed_mask(start, block, segments):
    length = segments.shape[0]
    positions = jnp.arange(length, dtype=jnp.int32)
    rows = start + jnp.arange(block, dtype=jnp.int32)
    own = lax.dynamic_slice_in_dim(segments, start, block, 0)
    return (rows[:, None] >= positions[None, :]) & (own[:, None] == segments[None, :])


def block_scores(query, keys, allowed):
    scores = jnp.einsum("bhd,kd->hbk", query, keys, preferred_element_type=F32) * HEAD ** (-0.5)
    return jnp.where(allowed[None], scores, -1e30)


def attend_forward(queries, keys, values, segments):
    length = queries.shape[0]
    block = 512
    shaped = queries.reshape(length, GROUP, HEAD)

    def step(start):
        query = lax.dynamic_slice_in_dim(shaped, start, block, 0)
        scores = block_scores(query, keys, allowed_mask(start, block, segments))
        top = jnp.max(scores, axis=-1, keepdims=True)
        weights = jnp.exp(scores - top)
        total = jnp.sum(weights, axis=-1, keepdims=True)
        probs = (weights / total).astype(BF)
        result = jnp.einsum("hbk,kd->bhd", probs, values, preferred_element_type=F32)
        return result.astype(BF), (top + jnp.log(total))[..., 0]

    starts = jnp.arange(length // block, dtype=jnp.int32) * block
    results, logs = lax.map(step, starts)
    return results.reshape(length, GROUP * HEAD), logs


def attend_backward(queries, keys, values, segments, logs, grad_heads):
    length = queries.shape[0]
    block = 512
    shaped = queries.reshape(length, GROUP, HEAD)
    grads = grad_heads.reshape(length, GROUP, HEAD)
    scale = HEAD ** (-0.5)

    def step(carry, items):
        grad_keys, grad_values = carry
        start, log_block = items
        query = lax.dynamic_slice_in_dim(shaped, start, block, 0)
        grad = lax.dynamic_slice_in_dim(grads, start, block, 0)
        scores = block_scores(query, keys, allowed_mask(start, block, segments))
        probs = jnp.exp(scores - log_block[..., None])
        grad_values = grad_values + jnp.einsum("hbk,bhd->kd", probs.astype(BF), grad, preferred_element_type=F32)
        grad_probs = jnp.einsum("bhd,kd->hbk", grad, values, preferred_element_type=F32)
        centre = jnp.sum(probs * grad_probs, axis=-1, keepdims=True)
        grad_scores = (probs * (grad_probs - centre)).astype(BF)
        grad_query = jnp.einsum("hbk,kd->bhd", grad_scores, keys, preferred_element_type=F32) * scale
        grad_keys = grad_keys + jnp.einsum("hbk,bhd->kd", grad_scores, query, preferred_element_type=F32) * scale
        return (grad_keys, grad_values), grad_query.astype(BF)

    zeros = jnp.zeros((length, HEAD), F32)
    starts = jnp.arange(length // block, dtype=jnp.int32) * block
    (grad_keys, grad_values), grad_queries = lax.scan(step, (zeros, zeros), (starts, logs))
    return grad_queries.reshape(length, GROUP * HEAD), grad_keys.astype(BF), grad_values.astype(BF)


def norm_backward(grad_normed, unit, inverse, gain):
    scaled = grad_normed * gain
    return inverse * (scaled - unit * jnp.mean(scaled * unit, axis=-1, keepdims=True))


def columns_of(value, at, width):
    return lax.dynamic_slice_in_dim(value, at * width, width, value.ndim - 1)


def half_forward(normed, weight, coef, cot):
    cols = weight.shape[1] // 3
    pre = mm(normed, weight[:, : 2 * cols])
    gate, upper = pre[:, :cols], pre[:, cols:]
    sigma = jax.nn.sigmoid(gate)
    silu = gate * sigma
    hidden = silu * upper
    weighted = (coef * hidden).astype(BF)
    down = weight[:, 2 * cols :]
    out = mm_nt(weighted, down)
    grad_hidden = mm(cot, down)
    grad_gate = jnp.sum((hidden * grad_hidden)[:, :512], axis=1)
    grad_hidden = coef * grad_hidden
    grad_pre = jnp.concatenate(
        [
            (grad_hidden * upper * sigma * (1.0 + gate * (1.0 - sigma))).astype(BF),
            (grad_hidden * silu).astype(BF),
        ],
        axis=1,
    )
    grad_normed = mm_nt(grad_pre, weight[:, : 2 * cols])
    grad_weight = jnp.concatenate([mm_tn(normed, grad_pre).astype(BF), mm_tn(cot, weighted).astype(BF)], axis=1)
    return out, grad_gate, grad_normed, grad_weight


def body(
    tokens,
    segments,
    routes,
    shared_mask,
    norm_gain,
    w_query,
    key_weight,
    value_weight,
    w_out,
    ffn_gain,
    w_router,
    shared_gate,
    shared_up,
    shared_down,
    expert_gate,
    expert_up,
    expert_down,
    cotangent,
):
    f = lax.axis_index("fsdp")
    s = lax.axis_index("seq")
    place = (f // (NX * NZ), (f // NZ) % NX, f % NZ)
    seq = (s // 2, s % 2)
    count, width = tokens.shape
    rows = norm_gain.shape[0]

    member = jnp.sum((routes[:, :, None] == jnp.arange(E, dtype=jnp.int32)).astype(F32), axis=1)
    marks = jnp.concatenate([member, shared_mask.astype(F32)[:, None], jnp.zeros((count, MISC - E - 1), F32)], axis=1)
    all_tokens = seq_gather(jnp.concatenate([tokens, marks.astype(BF)], axis=1), seq).reshape(SEQ * count, -1)

    misc = jnp.concatenate([norm_gain[:, None], ffn_gain[:, None], w_router, jnp.zeros((rows, MISC - 2 - E), BF)], axis=1)
    qkv_block = jnp.concatenate([columns_of(w_query, s, GROUP * HEAD), columns_of(key_weight, s, HEAD), columns_of(value_weight, s, HEAD)], axis=1)
    out_block = jnp.concatenate([columns_of(w_out, s, GROUP * HEAD), misc], axis=1)
    qkv_full = gather_weight(qkv_block, place, True)
    out_full = gather_weight(out_block, place, False)
    out_proj = out_full[:, : GROUP * HEAD]
    gain_one = out_full[:, GROUP * HEAD].astype(F32)
    gain_two = out_full[:, GROUP * HEAD + 1].astype(F32)
    router = out_full[:, GROUP * HEAD + 2 : GROUP * HEAD + 2 + E]

    def ffn_block(k):
        parts = []
        for shared, expert in ((shared_gate, expert_gate), (shared_up, expert_up), (shared_down, expert_down)):
            parts.append(lax.dynamic_index_in_dim(expert, 2 * s + k, 1, keepdims=False))
            parts.append(columns_of(shared, 2 * s + k, shared.shape[1] // 8))
        return jnp.concatenate(parts, axis=1)

    weight_a = gather_weight(ffn_block(0), place, True)
    weight_b = gather_weight(ffn_block(1), place, False)
    all_cot = seq_gather(cotangent, seq).reshape(SEQ * count, width)

    residual = tokens.astype(F32)
    inverse_one = lax.rsqrt(jnp.mean(residual * residual, axis=-1, keepdims=True) + EPS)
    unit_one = residual * inverse_one
    wide = all_tokens[:, :width].astype(F32)
    wide_inverse = lax.rsqrt(jnp.mean(wide * wide, axis=-1, keepdims=True) + EPS)
    normed_one = (wide * wide_inverse * gain_one).astype(BF)
    qkv = mm(normed_one, qkv_full).astype(BF)
    queries, keys, values = qkv[:, : GROUP * HEAD], qkv[:, GROUP * HEAD : (GROUP + 1) * HEAD], qkv[:, (GROUP + 1) * HEAD :]
    heads, logs = attend_forward(queries, keys, values, segments)
    hidden = residual + seq_scatter(mm_nt(heads, out_proj).astype(BF), seq)

    inverse_two = lax.rsqrt(jnp.mean(hidden * hidden, axis=-1, keepdims=True) + EPS)
    unit_two = hidden * inverse_two
    normed_home = (unit_two * gain_two).astype(BF)
    normed_two = seq_gather(normed_home, seq).reshape(SEQ * count, width)
    all_member = all_tokens[:, width : width + E].astype(F32)
    logits = jnp.where(all_member > 0, mm(normed_two, router), -1e30)
    weights = jnp.exp(logits - jnp.max(logits, axis=1, keepdims=True)) * all_member
    gates = weights / jnp.sum(weights, axis=1, keepdims=True)
    keep = all_tokens[:, width + E].astype(F32)[:, None]

    total = 0.0
    grad_normed_two = 0.0
    grad_weights, grad_gates = [], []
    for k, weight in enumerate((weight_a, weight_b)):
        gate = lax.dynamic_slice_in_dim(gates, 2 * s + k, 1, 1)
        coef = jnp.concatenate([jnp.broadcast_to(gate, (SEQ * count, 512)), jnp.broadcast_to(keep, (SEQ * count, 128))], axis=1)
        out, grad_gate, grad_normed, grad_weight = half_forward(normed_two, weight, coef, all_cot)
        total = total + out
        grad_normed_two = grad_normed_two + grad_normed
        grad_weights.append(grad_weight)
        grad_gates.append(grad_gate)
    output = (hidden + seq_scatter(total.astype(BF), seq)).astype(BF)

    slot = jnp.arange(E, dtype=jnp.int32)[None, :]
    grad_gates = jnp.where(slot == 2 * s, grad_gates[0][:, None], 0.0) + jnp.where(slot == 2 * s + 1, grad_gates[1][:, None], 0.0)
    upper_part = grad_gates.astype(BF)
    lower_part = (grad_gates - upper_part.astype(F32)).astype(BF)
    sent = jnp.concatenate(
        [grad_normed_two.astype(BF), upper_part, lower_part, jnp.zeros((SEQ * count, MISC - 2 * E), BF)], axis=1
    )
    arrived = seq_scatter(sent, seq)
    grad_gates = arrived[:, width : width + E] + arrived[:, width + E : width + 2 * E]
    gates_home = lax.dynamic_slice_in_dim(gates, s * count, count, 0)
    grad_logits = gates_home * (grad_gates - jnp.sum(gates_home * grad_gates, axis=1, keepdims=True))
    grad_normed_two = arrived[:, :width] + jnp.dot(grad_logits, router.astype(F32).T, precision=HIGH)
    grad_hidden = cotangent.astype(F32) + norm_backward(grad_normed_two, unit_two, inverse_two, gain_two)
    grad_gain_two = jnp.sum(grad_normed_two * unit_two, axis=0)
    grad_router = jnp.einsum("tc,te->ce", normed_home.astype(F32), grad_logits, precision=HIGH)
    grad_low_home = grad_hidden.astype(BF)
    grad_low = seq_gather(grad_low_home, seq).reshape(SEQ * count, width)

    ffn_a = scatter_grad(grad_weights[0], place, True).astype(BF)
    ffn_b = scatter_grad(grad_weights[1], place, False).astype(BF)

    grad_heads = mm(grad_low, out_proj).astype(BF)
    grad_q, grad_k, grad_v = attend_backward(queries, keys, values, segments, logs, grad_heads)
    grad_qkv = jnp.concatenate([grad_q, grad_k, grad_v], axis=1)
    grad_normed_one = seq_scatter(mm_nt(grad_qkv, qkv_full).astype(BF), seq)
    grad_tokens = (grad_hidden + norm_backward(grad_normed_one, unit_one, inverse_one, gain_one)).astype(BF)
    grad_gain_one = jnp.sum(grad_normed_one * unit_one, axis=0)

    grad_misc = jnp.concatenate(
        [grad_gain_one[:, None], grad_gain_two[:, None], grad_router, jnp.zeros((width, MISC - 2 - E), F32)], axis=1
    )
    qkv_grad = mm_tn(normed_one, grad_qkv).astype(BF)
    out_grad = jnp.concatenate([mm_tn(grad_low, heads).astype(BF), grad_misc.astype(BF)], axis=1)
    qkv_piece = scatter_grad(qkv_grad, place, True).astype(BF)
    out_piece = scatter_grad(out_grad, place, False).astype(BF)

    ffn_all = seq_gather(jnp.concatenate([ffn_a, ffn_b], axis=1), seq).astype(F32)
    attn_all = seq_gather(jnp.concatenate([qkv_piece, out_piece], axis=1), seq).astype(F32)

    def take(value, at, cols):
        return jnp.swapaxes(value[:, :, at : at + cols], 0, 1).reshape(rows, -1)

    q_cols = GROUP * HEAD
    misc_sum = jnp.sum(attn_all[:, :, 2 * q_cols + 2 * HEAD :], axis=0)

    half = ffn_all.shape[2] // 2
    third = half // 3

    def expert(part):
        at = part * third
        both = jnp.stack([ffn_all[:, :, at : at + 512], ffn_all[:, :, half + at : half + at + 512]], axis=1)
        return jnp.moveaxis(both, 2, 0).reshape(rows, E, 512)

    def shared(part):
        at = part * third + 512
        both = jnp.stack([ffn_all[:, :, at : at + 128], ffn_all[:, :, half + at : half + at + 128]], axis=1)
        return jnp.moveaxis(both, 2, 0).reshape(rows, 1024)

    return (
        output,
        grad_tokens,
        misc_sum[:, 0],
        take(attn_all, 0, q_cols),
        take(attn_all, q_cols, HEAD),
        take(attn_all, q_cols + HEAD, HEAD),
        take(attn_all, q_cols + 2 * HEAD, q_cols),
        misc_sum[:, 1],
        misc_sum[:, 2 : 2 + E],
        shared(0),
        shared(1),
        shared(2),
        expert(0),
        expert(1),
        expert(2),
    )


def solution(mesh):
    both = P(("fsdp", "seq"), None)
    one, two, three = P("fsdp"), P("fsdp", None), P("fsdp", None, None)
    return jax.shard_map(
        body,
        mesh=mesh,
        in_specs=(both, one, both, P(("fsdp", "seq")), one, two, two, two, two, one, two, two, two, two, three, three, three, both),
        out_specs=(both, both, one, two, two, two, two, one, two, two, two, two, three, three, three),
        check_vma=False,
    )
```

```python
import jax
import jax.numpy as jnp
from jax import lax
from jax.experimental import pallas as pl
from jax.experimental.pallas import tpu as pltpu
from jax.sharding import PartitionSpec as P

HEAD = 128
GROUP = 3
E = 8
NY, NX, NZ = 4, 4, 2
SEQ = 4
MISC = 128
EPS = 1e-05
BF = jnp.bfloat16
F32 = jnp.float32


def f32dot(left, right, dims):
    return lax.dot_general(left, right, (dims, ((), ())), preferred_element_type=F32)


def mm(left, right):
    return f32dot(left, right, ((1,), (0,)))


def mm_nt(left, right):
    return f32dot(left, right, ((1,), (1,)))


def mm_tn(left, right):
    return f32dot(left, right, ((0,), (0,)))


Q_COLS = GROUP * HEAD
KV = Q_COLS + HEAD
WIDTH = 1536
L = 1024
ROWS = 256
HALF = 640
LANES = 128
LOW = 32
SCALE = HEAD ** (-0.5)
BIG = -1e30
VMEM_ALL = pl.BlockSpec(memory_space=pltpu.VMEM)


def gain_rows(misc):
    eye = (lax.broadcasted_iota(jnp.int32, (LANES, LANES), 0) == lax.broadcasted_iota(jnp.int32, (LANES, LANES), 1)).astype(BF)
    return mm_nt(eye, misc)


def kept(q_at, kv_len, seg_col, seg_row):
    q_pos = q_at + lax.broadcasted_iota(jnp.int32, (ROWS, kv_len), 0)
    k_pos = lax.broadcasted_iota(jnp.int32, (ROWS, kv_len), 1)
    return (q_pos >= k_pos) & (seg_col[q_at : q_at + ROWS, :] == seg_row[:, :kv_len])


def stacked(ref, at):
    return jnp.concatenate([ref[at : at + ROWS, h * HEAD : (h + 1) * HEAD] for h in range(GROUP)], axis=0)


def attend_forward_kernel(tokens, qkv_w, out_w, seg_col, seg_row, normed, qkv, heads, logs, part, gains):
    gains[...] = gain_rows(out_w[:, Q_COLS:])
    gain = gains[0:1, :]
    for b in range(L // ROWS):
        at = slice(b * ROWS, (b + 1) * ROWS)
        x = tokens[at, :WIDTH].astype(F32)
        inverse = lax.rsqrt(jnp.mean(x * x, axis=-1, keepdims=True) + EPS)
        unit = (x * inverse * gain).astype(BF)
        normed[at, :] = unit
        qkv[at, :] = mm(unit, qkv_w[...]).astype(BF)
    for b in range(L // ROWS):
        at, kv_len = b * ROWS, (b + 1) * ROWS
        query = stacked(qkv, at)
        scores = mm_nt(query, qkv[:kv_len, Q_COLS:KV]) * SCALE
        mask = kept(at, kv_len, seg_col, seg_row)
        scores = jnp.where(mask[None], scores.reshape(GROUP, ROWS, kv_len), BIG).reshape(GROUP * ROWS, kv_len)
        top = jnp.max(scores, axis=-1, keepdims=True)
        weights = jnp.exp(scores - top)
        total = jnp.sum(weights, axis=-1, keepdims=True)
        probs = (weights * (1.0 / total)).astype(BF)
        result = mm(probs, qkv[:kv_len, KV:]).astype(BF)
        log = top + jnp.log(total)
        for h in range(GROUP):
            heads[at : at + ROWS, h * HEAD : (h + 1) * HEAD] = result[h * ROWS : (h + 1) * ROWS]
            logs[at : at + ROWS, h : h + 1] = log[h * ROWS : (h + 1) * ROWS]
        part[at : at + ROWS, :] = mm_nt(heads[at : at + ROWS, :], out_w[:, :Q_COLS]).astype(BF)


def attend_backward_kernel(grad_low, normed, qkv, heads, logs, qkv_w, out_w, seg_col, seg_row, part, qkv_grad, out_grad, grad_kv, grad_heads, grad_all):
    for b in range(L // ROWS):
        at = slice(b * ROWS, (b + 1) * ROWS)
        grad_heads[at, :] = mm(grad_low[at, :], out_w[:, :Q_COLS]).astype(BF)
    grad_kv[...] = jnp.zeros_like(grad_kv)
    for b in range(L // ROWS):
        at, kv_len = b * ROWS, (b + 1) * ROWS
        query = stacked(qkv, at)
        grad = stacked(grad_heads, at)
        log = jnp.concatenate([logs[at : at + ROWS, h : h + 1] for h in range(GROUP)], axis=0)
        scores = mm_nt(query, qkv[:kv_len, Q_COLS:KV]) * SCALE
        mask = kept(at, kv_len, seg_col, seg_row)
        scores = jnp.where(mask[None], scores.reshape(GROUP, ROWS, kv_len), BIG).reshape(GROUP * ROWS, kv_len)
        probs = jnp.exp(scores - log)
        grad_probs = mm_nt(grad, qkv[:kv_len, KV:])
        centre = jnp.sum(probs * grad_probs, axis=-1, keepdims=True)
        grad_scores = (probs * (grad_probs - centre)).astype(BF)
        grad_query = (mm(grad_scores, qkv[:kv_len, Q_COLS:KV]) * SCALE).astype(BF)
        for h in range(GROUP):
            grad_all[at : at + ROWS, h * HEAD : (h + 1) * HEAD] = grad_query[h * ROWS : (h + 1) * ROWS]
        grad_kv[:kv_len, :HEAD] += mm_tn(grad_scores, query) * SCALE
        grad_kv[:kv_len, HEAD:] += mm_tn(probs.astype(BF), grad)
    grad_all[:, Q_COLS:] = grad_kv[...].astype(BF)
    for b in range(L // ROWS):
        at = slice(b * ROWS, (b + 1) * ROWS)
        part[at, :] = mm_nt(grad_all[at, :], qkv_w[...]).astype(BF)

    def columns(i, carry):
        at = pl.ds(pl.multiple_of(i * ROWS, ROWS), ROWS)
        qkv_grad[at, :] = mm_tn(normed[:, at], grad_all[...]).astype(BF)
        out_grad[at, :] = mm_tn(grad_low[:, at], heads[...]).astype(BF)
        return carry

    lax.fori_loop(0, WIDTH // ROWS, columns, 0)


def ffn_kernel(seq_ref, normed, tokens_marks, misc, cot, weight_a, weight_b, out, grad, gates_out, grad_a, grad_b, pre_grads, weighted):
    s = seq_ref[0]
    weights = (weight_a, weight_b)
    lane = lax.broadcasted_iota(jnp.int32, (ROWS, LANES), 1)

    def block(b, carry):
        at = pl.ds(pl.multiple_of(b * ROWS, ROWS), ROWS)
        x = normed[at, :]
        c = cot[at, :]
        marks = tokens_marks[at, :].astype(F32)
        member = (marks > 0) & (lane >= 2) & (lane < 2 + E)
        logits = jnp.where(member, mm(x, misc[...]), BIG)
        soft = jnp.where(member, jnp.exp(logits - jnp.max(logits, axis=-1, keepdims=True)), 0.0)
        gates = soft / jnp.sum(soft, axis=-1, keepdims=True)
        gates_out[at, :] = gates
        keep = marks[:, 1:2]
        total = jnp.zeros((ROWS, WIDTH), F32)
        grad_x = jnp.zeros((ROWS, WIDTH), F32)
        grad_marks = jnp.zeros((ROWS, LANES), F32)
        for k, weight in enumerate(weights):
            mine = lane == 2 + 2 * s + k
            gate_e = jnp.sum(jnp.where(mine, gates, 0.0), axis=-1, keepdims=True)
            coef = jnp.concatenate([jnp.broadcast_to(gate_e, (ROWS, 512)), jnp.broadcast_to(keep, (ROWS, HALF - 512))], axis=1)
            pre = mm(x, weight[:, : 2 * HALF])
            gate, upper = pre[:, :HALF], pre[:, HALF:]
            sigma = 1.0 / (1.0 + jnp.exp(-gate))
            silu = gate * sigma
            hidden = silu * upper
            weighted_k = (coef * hidden).astype(BF)
            weighted[at, k * HALF : (k + 1) * HALF] = weighted_k
            total += mm_nt(weighted_k, weight[:, 2 * HALF :])
            grad_hidden = mm(c, weight[:, 2 * HALF :])
            grad_gate = jnp.sum((hidden * grad_hidden)[:, :512], axis=-1, keepdims=True)
            high = grad_gate.astype(BF).astype(F32)
            grad_marks += jnp.where(mine, high, 0.0) + jnp.where(lane == LOW + 2 + 2 * s + k, grad_gate - high, 0.0)
            grad_hidden = coef * grad_hidden
            grad_pre_g = (grad_hidden * upper * (sigma * (1.0 + gate * (1.0 - sigma)))).astype(BF)
            grad_pre_u = (grad_hidden * silu).astype(BF)
            pre_grads[at, 2 * k * HALF : (2 * k + 1) * HALF] = grad_pre_g
            pre_grads[at, (2 * k + 1) * HALF : (2 * k + 2) * HALF] = grad_pre_u
            grad_x += mm_nt(pre_grads[at, 2 * k * HALF : (2 * k + 2) * HALF], weight[:, : 2 * HALF])
        out[at, :] = total.astype(BF)
        grad[at, :WIDTH] = grad_x.astype(BF)
        grad[at, WIDTH:] = grad_marks.astype(BF)
        return carry

    lax.fori_loop(0, L // ROWS, block, 0)

    def columns(i, carry):
        at = pl.ds(pl.multiple_of(i * ROWS, ROWS), ROWS)
        x = normed[:, at]
        c = cot[:, at]
        for k, result in enumerate((grad_a, grad_b)):
            result[at, : 2 * HALF] = mm_tn(x, pre_grads[:, 2 * k * HALF : (2 * k + 2) * HALF]).astype(BF)
            result[at, 2 * HALF :] = mm_tn(c, weighted[:, k * HALF : (k + 1) * HALF]).astype(BF)
        return carry

    lax.fori_loop(0, WIDTH // ROWS, columns, 0)


def shape(rows, cols, dtype=BF):
    return jax.ShapeDtypeStruct((rows, cols), dtype)


def call(kernel, name, outs, ins, scratch=(), scalars=0):
    specs = [pl.BlockSpec(memory_space=pltpu.SMEM)] * scalars + [VMEM_ALL] * (len(ins) - scalars)
    return pl.pallas_call(
        kernel,
        out_shape=outs,
        in_specs=specs,
        out_specs=[VMEM_ALL] * len(outs),
        scratch_shapes=list(scratch),
        compiler_params=pltpu.CompilerParams(vmem_limit_bytes=62 * 1024 * 1024),
        name=name,
    )(*ins)


MESH = pl.DeviceIdType.MESH
ANY = pl.BlockSpec(memory_space=pl.ANY)
DMA = pltpu.SemaphoreType.DMA


def wrap(value):
    return lax.rem(value + 4, 4)


class Here:
    def __init__(self, send_sems):
        f, s = lax.axis_index("fsdp"), lax.axis_index("seq")
        self.y, self.x, self.z = lax.div(f, 8), lax.rem(lax.div(f, 2), 4), lax.rem(f, 2)
        self.s, self.zh, self.core = s, lax.div(s, 2), lax.rem(s, 2)
        y, x, z = self.y, self.x, self.z
        self.axis_x = ({"fsdp": self.number(y, wrap(x + 1), z)}, {"fsdp": self.number(y, wrap(x - 1), z)})
        self.axis_y = ({"fsdp": self.number(wrap(y + 1), x, z)}, {"fsdp": self.number(wrap(y - 1), x, z)})
        self.pair = {"fsdp": self.number(y, x, 1 - z)}
        self.s_far = (1 - self.zh) * 2 + self.core
        self.s_near = self.zh * 2 + 1 - self.core
        self.s_cross = (1 - self.zh) * 2 + 1 - self.core
        self.far = {"seq": self.s_far}
        self.near = {"seq": self.s_near}
        self.sems, self.sent = send_sems, []

    @staticmethod
    def number(y, x, z):
        return (y * 4 + x) * 2 + z

    def greet(self):
        barrier = pltpu.get_barrier_semaphore()
        partners = [*self.axis_x, *self.axis_y, self.pair, self.far, self.near]
        for partner in partners:
            pl.semaphore_signal(barrier, inc=1, device_id=partner, device_id_type=MESH)
        pl.semaphore_wait(barrier, len(partners))

    def send(self, source, target, recv_sem, to):
        copy = pltpu.make_async_remote_copy(
            src_ref=source,
            dst_ref=target,
            send_sem=self.sems.at[len(self.sent)],
            recv_sem=recv_sem,
            device_id=to,
            device_id_type=MESH,
        )
        copy.start()
        self.sent.append(copy)

    def wait(self, target, recv_sem):
        pltpu.make_async_remote_copy(
            src_ref=target,
            dst_ref=target,
            send_sem=self.sems.at[0],
            recv_sem=recv_sem,
            device_id=self.near,
            device_id_type=MESH,
        ).wait_recv()

    def finish(self):
        for copy in self.sent:
            copy.wait_send()


def together(*parts):
    left = list(parts)
    while left:
        for part in list(left):
            if next(part, "end") == "end":
                left.remove(part)


def in_turn(*parts):
    for part in parts:
        yield from part


def gather_weight(here, full, block, recv, own_sem, x_first):
    first, second = (here.axis_x, here.axis_y) if x_first else (here.axis_y, here.axis_x)

    def spot(df, ds, r):
        dy, dx = (ds, df) if x_first else (df, ds)
        return wrap(here.y + dy), wrap(here.x + dx), here.z if r == 0 else 1 - here.z

    def push(df, ds, r, to, source=None):
        at = spot(df, ds, r)
        here.send(full.at[at] if source is None else source, full.at[at], recv.at[at], to)

    def take(df, ds, r):
        at = spot(df, ds, r)
        here.wait(full.at[at], recv.at[at])

    own = pltpu.make_async_copy(block, full.at[spot(0, 0, 0)], own_sem)
    own.start()
    push(0, 0, 0, here.pair, block)
    for to in (*second, *first):
        push(0, 0, 0, to, block)
    yield
    take(0, 0, 1)
    for to in (*first, *second):
        push(0, 0, 1, to)
    for df, r in ((-1, 0), (1, 0), (1, 1), (-1, 1), (2, 0), (2, 1)):
        yield
        take(df, 0, r)
        if (df, r) == (-1, 0):
            push(df, 0, r, first[0])
        if (df, r) == (1, 1):
            push(df, 0, r, first[1])
        for to in second:
            push(df, 0, r, to)
        if (df, r) == (1, 0):
            take(0, -1, 0)
            push(0, -1, 0, second[0])
        if (df, r) == (-1, 1):
            take(0, 1, 1)
            push(0, 1, 1, second[1])
    for df in (-1, 1, 2):
        yield
        take(df, -1, 0)
        push(df, -1, 0, second[0])
        yield
        take(df, 1, 1)
        push(df, 1, 1, second[1])
    yield
    for df in (0, -1, 1, 2):
        take(df, -1, 1)
        take(df, 1, 0)
        take(df, 2, 0)
        take(df, 2, 1)
    own.wait()


def added(*refs):
    total = refs[0].astype(F32)
    for ref in refs[1:]:
        total = total + ref.astype(F32)
    return total


def scatter_buffers(cols):
    units = [(4,), (4,), (4, 2), (4, 2), (1,), (1,), (2,), (2,), (1,)]
    return [pltpu.VMEM((*u, 48, cols), BF) for u in units] + [DMA((31,))]


def scatter_grad(here, grad, buffers, piece, y_first):
    ra, rb, rc, rd, xa, xb, xc, xd, zr, sems = buffers
    second, first = (here.axis_y, here.axis_x) if y_first else (here.axis_x, here.axis_y)

    def own(df, ds, h):
        dy, dx = (ds, df) if y_first else (df, ds)
        return grad.at[wrap(here.y + dy), wrap(here.x + dx), h]

    order = (2, 1, 3, 0)
    for j in order:
        here.send(own(j, 2, 0), ra.at[j], sems.at[j], second[0])
        here.send(own(j, 2, 1), rb.at[j], sems.at[4 + j], second[1])
        here.send(own(j, 1, 1), rc.at[j, 1], sems.at[8 + 2 * j + 1], second[0])
        here.send(own(j, 3, 0), rd.at[j, 0], sems.at[16 + 2 * j], second[1])
    for j in order:
        yield
        here.wait(ra.at[j], sems.at[j])
        ra[j] = added(own(j, 1, 0)[...], ra[j]).astype(BF)
        here.send(ra.at[j], rc.at[j, 0], sems.at[8 + 2 * j], second[0])
        here.wait(rb.at[j], sems.at[4 + j])
        rb[j] = added(own(j, 3, 1)[...], rb[j]).astype(BF)
        here.send(rb.at[j], rd.at[j, 1], sems.at[16 + 2 * j + 1], second[1])
    for j in order:
        yield
        for h in range(2):
            here.wait(rc.at[j, h], sems.at[8 + 2 * j + h])
            here.wait(rd.at[j, h], sems.at[16 + 2 * j + h])
            rc[j, h] = added(own(j, 0, h)[...], rc[j, h], rd[j, h]).astype(BF)
        if j == 2:
            here.send(rc.at[2, 0], xa.at[0], sems.at[24], first[0])
            here.send(rc.at[2, 1], xb.at[0], sems.at[25], first[1])
        if j == 1:
            here.send(rc.at[1, 1], xc.at[1], sems.at[27], first[0])
        if j == 3:
            here.send(rc.at[3, 0], xd.at[0], sems.at[28], first[1])
            here.wait(xa.at[0], sems.at[24])
            xa[0] = added(rc[1, 0], xa[0]).astype(BF)
            here.send(xa.at[0], xc.at[0], sems.at[26], first[0])
            here.wait(xb.at[0], sems.at[25])
            xb[0] = added(rc[3, 1], xb[0]).astype(BF)
            here.send(xb.at[0], xd.at[1], sems.at[29], first[1])
    yield
    for h in range(2):
        here.wait(xc.at[h], sems.at[26 + h])
        here.wait(xd.at[h], sems.at[28 + h])
        xc[h] = added(rc[0, h], xc[h], xd[h]).astype(BF)
    here.send(xc.at[1 - here.z], zr.at[0], sems.at[30], here.pair)
    yield
    here.wait(zr.at[0], sems.at[30])
    piece[...] = added(xc[here.z], zr[0]).astype(piece.dtype)


def seq_gather(here, source, full, sems):
    own = pltpu.make_async_copy(source, full.at[here.s], sems.at[3])
    own.start()
    here.send(source, full.at[here.s], sems.at[0], here.far)
    here.send(source, full.at[here.s], sems.at[1], here.near)
    yield
    here.wait(full.at[here.s_far], sems.at[0])
    here.send(full.at[here.s_far], full.at[here.s_far], sems.at[2], here.near)
    yield
    here.wait(full.at[here.s_near], sems.at[1])
    here.wait(full.at[here.s_cross], sems.at[2])
    own.wait()


def seq_scatter(here, parts, near, far, sems, pause=1):
    n = near.shape[1] // 2
    for k in range(2):
        at = pl.ds(k * n, n)
        here.send(parts.at[here.s_cross, at], near.at[0, at], sems.at[k], here.near)
    here.send(parts.at[here.s_near], near.at[1], sems.at[2], here.near)
    yield
    for k in range(2):
        at = pl.ds(k * n, n)
        here.wait(near.at[0, at], sems.at[k])
        near[0, at] = added(parts[here.s_far, at], near[0, at]).astype(BF)
        here.send(near.at[0, at], far.at[at], sems.at[3 + k], here.far)
    yield
    here.wait(near.at[1], sems.at[2])
    for _ in range(pause):
        yield
    for k in range(2):
        at = pl.ds(k * n, n)
        here.wait(far.at[at], sems.at[3 + k])


def start_kernel(marked, qkv_block, out_block, all_marked, qkv_full, out_full, send_sems, qkv_sems, out_sems, seq_sems, own_sems):
    here = Here(send_sems)
    here.greet()
    together(
        seq_gather(here, marked, all_marked, seq_sems),
        gather_weight(here, qkv_full, qkv_block, qkv_sems, own_sems.at[0], True),
        gather_weight(here, out_full, out_block, out_sems, own_sems.at[1], False),
    )
    here.finish()


def normed_of(x, gain):
    inverse = lax.rsqrt(jnp.mean(x * x, axis=-1, keepdims=True) + EPS)
    unit = x * inverse
    return inverse, unit, (unit * gain).astype(BF)


def middle_kernel(part, tokens, gains, cot, block_a, block_b, normed, all_cot, full_a, full_b, hidden,
                  near, far, normed_home, send_sems, sems_a, sems_b, own_sems, scatter_sems, gather_sems, cot_sems):
    here = Here(send_sems)
    here.greet()

    def rows():
        yield from seq_scatter(here, part, near, far, scatter_sems, 5)
        hidden[...] = added(tokens[...], part[here.s], near[1], far[...])
        normed_home[...] = normed_of(hidden[...], gains[1:2, :])[2]
        together_rows = [seq_gather(here, normed_home, normed, gather_sems), seq_gather(here, cot, all_cot, cot_sems)]
        for _ in range(3):
            for g in together_rows:
                next(g, None)
            yield

    together(
        rows(),
        gather_weight(here, full_a, block_a, sems_a, own_sems.at[0], True),
        gather_weight(here, full_b, block_b, sems_b, own_sems.at[1], False),
    )
    here.finish()


def split_two(value):
    high = value.astype(BF)
    return high, (value - high.astype(F32)).astype(BF)


def one_lane(k):
    return (lax.broadcasted_iota(jnp.int32, (ROWS, LANES), 1) == k).astype(BF)


def turn_kernel(sent, part, hidden, cot, gates, misc, gains, grad_a, grad_b, output, grad_low, grad_hidden, grad_misc, piece_a, piece_b,
                near_g, far_g, near_o, far_o, low_home, send_sems, scatter_sems, out_sems, gather_sems, *buffers):
    here = Here(send_sems)
    here.greet()

    def rows():
        yield from seq_scatter(here, sent, near_g, far_g, scatter_sems, 2)
        marks = added(sent[here.s, :, WIDTH:], near_g[1, :, WIDTH:], far_g[:, WIDTH:])
        grad_gates = marks + pltpu.roll(marks, LANES - LOW, 1)
        own_gates = gates[pl.ds(pl.multiple_of(here.s * ROWS, ROWS), ROWS), :]
        grad_logits = own_gates * (grad_gates - jnp.sum(own_gates * grad_gates, axis=-1, keepdims=True))
        high, low = split_two(grad_logits)
        grad_normed = added(sent[here.s, :, :WIDTH], near_g[1, :, :WIDTH], far_g[:, :WIDTH])
        grad_normed = grad_normed + (mm_nt(high, misc[...]) + mm_nt(low, misc[...]))
        gain = gains[1:2, :]
        inverse, unit, normed = normed_of(hidden[...], gain)
        scaled = grad_normed * gain
        grad = cot[...].astype(F32) + inverse * (scaled - unit * jnp.mean(scaled * unit, axis=-1, keepdims=True))
        grad_hidden[...] = grad
        low_home[...] = grad.astype(BF)
        gather = seq_gather(here, low_home, grad_low, gather_sems)
        next(gather)
        prod_high, prod_low = split_two(grad_normed * unit)
        grad_misc[...] = mm_tn(normed, high) + mm_tn(normed, low) + mm_tn(prod_high, one_lane(1)) + mm_tn(prod_low, one_lane(1))
        scatter = seq_scatter(here, part, near_o, far_o, out_sems)
        next(scatter)
        yield
        next(scatter)
        yield
        next(gather)
        yield
        next(gather, None)
        yield from scatter
        output[...] = added(hidden[...], part[here.s], near_o[1], far_o[...]).astype(BF)

    together(
        rows(),
        scatter_grad(here, grad_a, buffers[:10], piece_a, True),
        scatter_grad(here, grad_b, buffers[10:], piece_b, False),
    )
    here.finish()


def end_kernel(part, tokens, grad_hidden, gains, grad_misc, grad_qkv, grad_out, ffn_a, ffn_b,
               grad_tokens, ffn_a_all, ffn_b_all, qkv_all, out_all, misc_all,
               near, far, misc_grad, qkv_piece, out_piece, misc_piece, send_sems, scatter_sems, gather_sems, *buffers):
    here = Here(send_sems)
    here.greet()

    def rows():
        yield from seq_scatter(here, part, near, far, scatter_sems, 7)
        grad_normed = added(part[here.s], near[1], far[...])
        gain = gains[0:1, :]
        inverse, unit, _ = normed_of(tokens[...].astype(F32), gain)
        high, low = split_two(grad_normed * unit)
        misc = grad_misc[...] + mm_tn(high, one_lane(0)) + mm_tn(low, one_lane(0))
        misc_grad[...] = misc.astype(BF).reshape(misc_grad.shape)
        scatter = scatter_grad(here, misc_grad, buffers[20:], misc_piece, True)
        next(scatter)
        scaled = grad_normed * gain
        grad_tokens[...] = (grad_hidden[...] + inverse * (scaled - unit * jnp.mean(scaled * unit, axis=-1, keepdims=True))).astype(BF)
        yield from scatter
        yield from seq_gather(here, misc_piece, misc_all, gather_sems.at[0])

    def weight(grad, scratch, piece, y_first, full, sems):
        yield from scatter_grad(here, grad, scratch, piece, y_first)
        yield from seq_gather(here, piece, full, sems)

    together(
        rows(),
        weight(grad_qkv, buffers[:10], qkv_piece, True, qkv_all, gather_sems.at[1]),
        weight(grad_out, buffers[10:20], out_piece, False, out_all, gather_sems.at[2]),
        seq_gather(here, ffn_a, ffn_a_all, gather_sems.at[3]),
        seq_gather(here, ffn_b, ffn_b_all, gather_sems.at[4]),
    )
    here.finish()


def remote_call(kernel, name, number, outs, ins, scratch):
    return pl.pallas_call(
        kernel,
        out_shape=[jax.ShapeDtypeStruct(dims, dtype) for dims, dtype, _ in outs],
        in_specs=[VMEM_ALL if fast else ANY for _, fast in ins],
        out_specs=[VMEM_ALL if fast else ANY for _, _, fast in outs],
        scratch_shapes=list(scratch),
        compiler_params=pltpu.CompilerParams(collective_id=number, has_side_effects=True, vmem_limit_bytes=62 * 1024 * 1024),
        name=name,
    )(*[array for array, _ in ins])


def columns_of(value, at, width):
    return lax.dynamic_slice_in_dim(value, at * width, width, value.ndim - 1)


def body(
    tokens,
    segments,
    routes,
    shared_mask,
    norm_gain,
    w_query,
    key_weight,
    value_weight,
    w_out,
    ffn_gain,
    w_router,
    shared_gate,
    shared_up,
    shared_down,
    expert_gate,
    expert_up,
    expert_down,
    cotangent,
):
    s = lax.axis_index("seq")
    count, width = tokens.shape
    rows = norm_gain.shape[0]

    member = jnp.sum((routes[:, :, None] == jnp.arange(E, dtype=jnp.int32)).astype(F32), axis=1)
    zero = jnp.zeros((count, 1), F32)
    marks = jnp.concatenate([zero, shared_mask.astype(F32)[:, None], member, jnp.zeros((count, MISC - E - 2), F32)], axis=1)
    marked = jnp.concatenate([tokens, marks.astype(BF)], axis=1)
    misc = jnp.concatenate([norm_gain[:, None], ffn_gain[:, None], w_router, jnp.zeros((rows, MISC - 2 - E), BF)], axis=1)
    qkv_block = jnp.concatenate([columns_of(w_query, s, Q_COLS), columns_of(key_weight, s, HEAD), columns_of(value_weight, s, HEAD)], axis=1)
    out_block = jnp.concatenate([columns_of(w_out, s, Q_COLS), misc], axis=1)

    def ffn_block(k):
        parts = []
        for shared, expert in ((shared_gate, expert_gate), (shared_up, expert_up), (shared_down, expert_down)):
            parts.append(lax.dynamic_index_in_dim(expert, 2 * s + k, 1, keepdims=False))
            parts.append(columns_of(shared, 2 * s + k, shared.shape[1] // 8))
        return jnp.concatenate(parts, axis=1)

    def blocks(cols):
        return (NY, NX, NZ, rows, cols)

    gather_sems = DMA((NY, NX, NZ))
    ffn_cols, out_cols = 3 * HALF, Q_COLS + MISC
    all_marked, qkv_full, out_full = remote_call(
        start_kernel,
        "gather_first",
        1,
        [((SEQ, count, width + MISC), BF, False), (blocks(HALF), BF, False), (blocks(out_cols), BF, False)],
        [(marked, False), (qkv_block, False), (out_block, False)],
        [DMA((80,)), gather_sems, gather_sems, DMA((4,)), DMA((2,))],
    )
    all_marked = all_marked.reshape(L, width + MISC)
    qkv_full = qkv_full.reshape(width, HALF)
    out_full = out_full.reshape(width, out_cols)

    seg_col, seg_row = segments[:, None], segments[None, :]
    normed_one, qkv, heads, logs, part, gains = call(
        attend_forward_kernel,
        "attend_forward",
        [shape(L, WIDTH), shape(L, HALF), shape(L, Q_COLS), shape(L, 8, F32), shape(L, WIDTH), shape(LANES, WIDTH, F32)],
        [all_marked, qkv_full, out_full, seg_col, seg_row],
    )

    normed_two, all_cot, full_a, full_b, hidden = remote_call(
        middle_kernel,
        "gather_second",
        2,
        [
            ((SEQ, count, width), BF, False),
            ((SEQ, count, width), BF, False),
            (blocks(ffn_cols), BF, False),
            (blocks(ffn_cols), BF, False),
            ((count, width), F32, True),
        ],
        [(part.reshape(SEQ, count, width), True), (tokens, True), (gains, True), (cotangent, False), (ffn_block(0), False), (ffn_block(1), False)],
        [
            pltpu.VMEM((2, count, width), BF),
            pltpu.VMEM((count, width), BF),
            pltpu.VMEM((count, width), BF),
            DMA((96,)),
            gather_sems,
            gather_sems,
            DMA((2,)),
            DMA((5,)),
            DMA((4,)),
            DMA((4,)),
        ],
    )

    out, sent, gates, grad_a, grad_b = call(
        ffn_kernel,
        "experts",
        [shape(L, WIDTH), shape(L, WIDTH + LANES), shape(L, LANES, F32), shape(WIDTH, ffn_cols), shape(WIDTH, ffn_cols)],
        [
            s.astype(jnp.int32)[None],
            normed_two.reshape(L, width),
            all_marked[:, width:],
            out_full[:, Q_COLS:],
            all_cot.reshape(L, width),
            full_a.reshape(width, ffn_cols),
            full_b.reshape(width, ffn_cols),
        ],
        [pltpu.VMEM((L, 4 * HALF), BF), pltpu.VMEM((L, 2 * HALF), BF)],
        scalars=1,
    )

    output, grad_low, grad_hidden, grad_misc, piece_a, piece_b = remote_call(
        turn_kernel,
        "sum_experts",
        3,
        [
            ((count, width), BF, True),
            ((SEQ, count, width), BF, False),
            ((count, width), F32, True),
            ((width, LANES), F32, True),
            ((rows, ffn_cols), BF, True),
            ((rows, ffn_cols), BF, True),
        ],
        [
            (sent.reshape(SEQ, count, width + LANES), True),
            (out.reshape(SEQ, count, width), True),
            (hidden, True),
            (cotangent, True),
            (gates, True),
            (out_full[:, Q_COLS:], True),
            (gains, True),
            (grad_a.reshape(blocks(ffn_cols)), True),
            (grad_b.reshape(blocks(ffn_cols)), True),
        ],
        [
            pltpu.VMEM((2, count, width + LANES), BF),
            pltpu.VMEM((count, width + LANES), BF),
            pltpu.VMEM((2, count, width), BF),
            pltpu.VMEM((count, width), BF),
            pltpu.VMEM((count, width), BF),
            DMA((96,)),
            DMA((5,)),
            DMA((5,)),
            DMA((4,)),
            *scatter_buffers(ffn_cols),
            *scatter_buffers(ffn_cols),
        ],
    )

    part, grad_qkv, grad_out = call(
        attend_backward_kernel,
        "attend_backward",
        [shape(L, WIDTH), shape(WIDTH, HALF), shape(WIDTH, Q_COLS)],
        [grad_low.reshape(L, width), normed_one, qkv, heads, logs, qkv_full, out_full, seg_col, seg_row],
        [pltpu.VMEM((L, 2 * HEAD), F32), pltpu.VMEM((L, Q_COLS), BF), pltpu.VMEM((L, HALF), BF)],
    )

    grad_tokens, ffn_a_all, ffn_b_all, qkv_all, out_all, misc_all = remote_call(
        end_kernel,
        "sum_attention",
        4,
        [
            ((count, width), BF, True),
            ((SEQ, rows, ffn_cols), BF, False),
            ((SEQ, rows, ffn_cols), BF, False),
            ((SEQ, rows, HALF), BF, False),
            ((SEQ, rows, Q_COLS), BF, False),
            ((SEQ, rows, MISC), BF, False),
        ],
        [
            (part.reshape(SEQ, count, width), True),
            (tokens, True),
            (grad_hidden, True),
            (gains, True),
            (grad_misc, True),
            (grad_qkv.reshape(blocks(HALF)), True),
            (grad_out.reshape(blocks(Q_COLS)), True),
            (piece_a, False),
            (piece_b, False),
        ],
        [
            pltpu.VMEM((2, count, width), BF),
            pltpu.VMEM((count, width), BF),
            pltpu.VMEM(blocks(MISC), BF),
            pltpu.VMEM((rows, HALF), BF),
            pltpu.VMEM((rows, Q_COLS), BF),
            pltpu.VMEM((rows, MISC), BF),
            DMA((128,)),
            DMA((5,)),
            DMA((5, 4)),
            *scatter_buffers(HALF),
            *scatter_buffers(Q_COLS),
            *scatter_buffers(MISC),
        ],
    )

    def joined(value):
        return jnp.swapaxes(value.astype(F32), 0, 1).reshape(rows, -1)

    misc_sum = jnp.sum(misc_all.astype(F32), axis=0)

    def expert(part):
        at = part * HALF
        both = jnp.stack([ffn_a_all[:, :, at : at + 512], ffn_b_all[:, :, at : at + 512]], axis=1)
        return jnp.moveaxis(both, 2, 0).reshape(rows, E, 512).astype(F32)

    def shared(part):
        at = part * HALF + 512
        both = jnp.stack([ffn_a_all[:, :, at : at + 128], ffn_b_all[:, :, at : at + 128]], axis=1)
        return jnp.moveaxis(both, 2, 0).reshape(rows, 1024).astype(F32)

    return (
        output,
        grad_tokens,
        misc_sum[:, 0],
        joined(qkv_all[:, :, :Q_COLS]),
        joined(qkv_all[:, :, Q_COLS:KV]),
        joined(qkv_all[:, :, KV:]),
        joined(out_all),
        misc_sum[:, 1],
        misc_sum[:, 2 : 2 + E],
        shared(0),
        shared(1),
        shared(2),
        expert(0),
        expert(1),
        expert(2),
    )


def solution(mesh):
    both = P(("fsdp", "seq"), None)
    one, two, three = P("fsdp"), P("fsdp", None), P("fsdp", None, None)
    return jax.shard_map(
        body,
        mesh=mesh,
        in_specs=(both, one, both, P(("fsdp", "seq")), one, two, two, two, two, one, two, two, two, two, three, three, three, both),
        out_specs=(both, both, one, two, two, two, two, one, two, two, two, two, three, three, three),
        check_vma=False,
    )
```

```python
import jax
import jax.numpy as jnp
from jax import lax
from jax.experimental import pallas as pl
from jax.experimental.pallas import tpu as pltpu
from jax.sharding import PartitionSpec as P

HEAD = 128
GROUP = 3
E = 8
SEQ = 4
EPS = 1e-05
BF = jnp.bfloat16
F32 = jnp.float32
WIDTH = 1536
L = 1024
ROWS = 256
SHARD = 48
Q_COLS = GROUP * HEAD
KV = Q_COLS + HEAD
HALF = 640
FFN = 3 * HALF
LANES = 128
OUT_COLS = Q_COLS + LANES
LOW = 32
CHUNK = 384
SCALE = HEAD ** (-0.5)
BIG = -1e30
MESH = pl.DeviceIdType.MESH
VMEM_ALL = pl.BlockSpec(memory_space=pltpu.VMEM)
ANY = pl.BlockSpec(memory_space=pl.ANY)
DMA = pltpu.SemaphoreType.DMA
LIMIT = 63 * 1024 * 1024


def f32dot(left, right, dims):
    return lax.dot_general(left, right, (dims, ((), ())), preferred_element_type=F32)


def mm(left, right):
    return f32dot(left, right, ((1,), (0,)))


def mm_nt(left, right):
    return f32dot(left, right, ((1,), (1,)))


def mm_tn(left, right):
    return f32dot(left, right, ((0,), (0,)))


def iota(dims, axis):
    return lax.broadcasted_iota(jnp.int32, dims, axis)


def column(row):
    n = row.shape[1]
    same = iota((n, n), 0) == iota((n, n), 1)
    return jnp.sum(jnp.where(same, jnp.broadcast_to(row, (n, n)), 0.0), axis=-1, keepdims=True)


def added(*values):
    total = values[0].astype(F32)
    for value in values[1:]:
        total = total + value.astype(F32)
    return total


def split_two(value):
    high = value.astype(BF)
    return high, (value - high.astype(F32)).astype(BF)


def normed_of(x, gain):
    inverse = lax.rsqrt(jnp.mean(x * x, axis=-1, keepdims=True) + EPS)
    unit = x * inverse
    return inverse, unit, (unit * gain).astype(BF)


def wrap(value):
    return lax.rem(value + 4, 4)


def blocks(cols):
    return (4, 4, 2, SHARD, cols)


class Here:
    def __init__(self, send_sems):
        f, s = lax.axis_index("fsdp"), lax.axis_index("seq")
        self.y, self.x, self.z = lax.div(f, 8), lax.rem(lax.div(f, 2), 4), lax.rem(f, 2)
        self.s, self.zh, self.core = s, lax.div(s, 2), lax.rem(s, 2)
        y, x, z = self.y, self.x, self.z
        self.axis_x = ({"fsdp": self.number(y, wrap(x + 1), z)}, {"fsdp": self.number(y, wrap(x - 1), z)})
        self.axis_y = ({"fsdp": self.number(wrap(y + 1), x, z)}, {"fsdp": self.number(wrap(y - 1), x, z)})
        self.pair = {"fsdp": self.number(y, x, 1 - z)}
        self.s_far = (1 - self.zh) * 2 + self.core
        self.s_near = self.zh * 2 + 1 - self.core
        self.s_cross = (1 - self.zh) * 2 + 1 - self.core
        self.far = {"seq": self.s_far}
        self.near = {"seq": self.s_near}
        self.sems, self.sent = send_sems, []

    @staticmethod
    def number(y, x, z):
        return (y * 4 + x) * 2 + z

    def greet(self):
        barrier = pltpu.get_barrier_semaphore()
        partners = [*self.axis_x, *self.axis_y, self.pair, self.far, self.near]
        for partner in partners:
            pl.semaphore_signal(barrier, inc=1, device_id=partner, device_id_type=MESH)
        pl.semaphore_wait(barrier, len(partners))

    def send(self, source, target, recv_sem, to):
        copy = pltpu.make_async_remote_copy(
            src_ref=source,
            dst_ref=target,
            send_sem=self.sems.at[len(self.sent)],
            recv_sem=recv_sem,
            device_id=to,
            device_id_type=MESH,
        )
        copy.start()
        self.sent.append(copy)

    def wait(self, target, recv_sem):
        pltpu.make_async_remote_copy(
            src_ref=target,
            dst_ref=target,
            send_sem=self.sems.at[0],
            recv_sem=recv_sem,
            device_id=self.near,
            device_id_type=MESH,
        ).wait_recv()

    def finish(self):
        for copy in self.sent:
            copy.wait_send()


class Local:
    def __init__(self, sems):
        self.sems, self.count = sems, 0

    def copy(self, source, target):
        copy = pltpu.make_async_copy(source, target, self.sems.at[self.count])
        copy.start()
        self.count += 1
        return copy


def together(*parts):
    left = list(parts)
    while left:
        for part in list(left):
            if next(part, "end") == "end":
                left.remove(part)


def later(turns, parts):
    for _ in range(turns):
        yield
    for part in parts:
        next(part)


def gather_weight(here, full, block, recv, own_sem, x_first):
    first, second = (here.axis_x, here.axis_y) if x_first else (here.axis_y, here.axis_x)

    def spot(df, ds, r):
        dy, dx = (ds, df) if x_first else (df, ds)
        return wrap(here.y + dy), wrap(here.x + dx), here.z if r == 0 else 1 - here.z

    def push(df, ds, r, to, source=None):
        at = spot(df, ds, r)
        here.send(full.at[at] if source is None else source, full.at[at], recv.at[at], to)

    def take(df, ds, r):
        at = spot(df, ds, r)
        here.wait(full.at[at], recv.at[at])

    own = pltpu.make_async_copy(block, full.at[spot(0, 0, 0)], own_sem)
    own.start()
    push(0, 0, 0, here.pair, block)
    for to in (*second, *first):
        push(0, 0, 0, to, block)
    yield
    take(0, 0, 1)
    for to in (*first, *second):
        push(0, 0, 1, to)
    for df, r in ((-1, 0), (1, 0), (1, 1), (-1, 1), (2, 0), (2, 1)):
        yield
        take(df, 0, r)
        if (df, r) == (-1, 0):
            push(df, 0, r, first[0])
        if (df, r) == (1, 1):
            push(df, 0, r, first[1])
        for to in second:
            push(df, 0, r, to)
        if (df, r) == (1, 0):
            take(0, -1, 0)
            push(0, -1, 0, second[0])
        if (df, r) == (-1, 1):
            take(0, 1, 1)
            push(0, 1, 1, second[1])
    for df in (-1, 1, 2):
        yield
        take(df, -1, 0)
        push(df, -1, 0, second[0])
        yield
        take(df, 1, 1)
        push(df, 1, 1, second[1])
    yield
    for df in (0, -1, 1, 2):
        take(df, -1, 1)
        take(df, 1, 0)
        take(df, 2, 0)
        take(df, 2, 1)
    own.wait()


def scatter_buffers(cols):
    units = [(4,), (4,), (4, 2), (4, 2), (1,), (1,), (2,), (2,), (1,)]
    return [pltpu.VMEM((*u, SHARD, cols), BF) for u in units] + [DMA((31,))]


def scatter_grad(here, grad, own, buffers, piece, y_first):
    ra, rb, rc, rd, xa, xb, xc, xd, zr, sems = buffers
    second, first = (here.axis_y, here.axis_x) if y_first else (here.axis_x, here.axis_y)

    def block(df, ds, h):
        dy, dx = (ds, df) if y_first else (df, ds)
        return grad.at[wrap(here.y + dy), wrap(here.x + dx), h]

    own = own or (lambda df, ds, h: block(df, ds, h)[...])

    def far_send(j):
        here.send(block(j, 2, 0), ra.at[j], sems.at[j], second[0])
        here.send(block(j, 2, 1), rb.at[j], sems.at[4 + j], second[1])

    def near_send(j):
        here.send(block(j, 1, 1), rc.at[j, 1], sems.at[8 + 2 * j + 1], second[0])
        here.send(block(j, 3, 0), rd.at[j, 0], sems.at[16 + 2 * j], second[1])

    def pass_on(j):
        here.wait(ra.at[j], sems.at[j])
        ra[j] = added(own(j, 1, 0), ra[j]).astype(BF)
        here.send(ra.at[j], rc.at[j, 0], sems.at[8 + 2 * j], second[0])
        here.wait(rb.at[j], sems.at[4 + j])
        rb[j] = added(own(j, 3, 1), rb[j]).astype(BF)
        here.send(rb.at[j], rd.at[j, 1], sems.at[16 + 2 * j + 1], second[1])

    def total(j):
        for h in range(2):
            here.wait(rc.at[j, h], sems.at[8 + 2 * j + h])
            here.wait(rd.at[j, h], sems.at[16 + 2 * j + h])
            rc[j, h] = added(own(j, 0, h), rc[j, h], rd[j, h]).astype(BF)

    far_send(2)
    near_send(2)
    far_send(1)
    yield
    pass_on(2)
    near_send(1)
    far_send(3)
    yield
    pass_on(1)
    near_send(3)
    far_send(0)
    yield
    pass_on(3)
    near_send(0)
    yield
    total(2)
    here.send(rc.at[2, 0], xa.at[0], sems.at[24], first[0])
    here.send(rc.at[2, 1], xb.at[0], sems.at[25], first[1])
    yield
    pass_on(0)
    yield
    total(1)
    here.send(rc.at[1, 1], xc.at[1], sems.at[27], first[0])
    here.wait(xa.at[0], sems.at[24])
    xa[0] = added(rc[1, 0], xa[0]).astype(BF)
    here.send(xa.at[0], xc.at[0], sems.at[26], first[0])
    yield
    total(3)
    here.send(rc.at[3, 0], xd.at[0], sems.at[28], first[1])
    here.wait(xb.at[0], sems.at[25])
    xb[0] = added(rc[3, 1], xb[0]).astype(BF)
    here.send(xb.at[0], xd.at[1], sems.at[29], first[1])
    yield
    total(0)
    yield
    for h in range(2):
        here.wait(xc.at[h], sems.at[26 + h])
        here.wait(xd.at[h], sems.at[28 + h])
        xc[h] = added(rc[0, h], xc[h], xd[h]).astype(BF)
    here.send(xc.at[1 - here.z], zr.at[0], sems.at[30], here.pair)
    yield
    here.wait(zr.at[0], sems.at[30])
    piece[...] = added(xc[here.z], zr[0]).astype(piece.dtype)


def seq_gather(here, source, full, sems, pause=1):
    own = pltpu.make_async_copy(source, full.at[here.s], sems.at[3])
    own.start()
    here.send(source, full.at[here.s], sems.at[0], here.far)
    here.send(source, full.at[here.s], sems.at[1], here.near)
    for _ in range(pause):
        yield
    here.wait(full.at[here.s_far], sems.at[0])
    here.send(full.at[here.s_far], full.at[here.s_far], sems.at[2], here.near)
    yield
    here.wait(full.at[here.s_near], sems.at[1])
    here.wait(full.at[here.s_cross], sems.at[2])
    own.wait()


def seq_scatter(here, parts, near, far, sems, make, pause=1):
    make(here.s_cross)
    here.send(parts.at[here.s_cross], near.at[0], sems.at[0], here.near)
    make(here.s_far)
    yield
    here.wait(near.at[0], sems.at[0])
    near[0] = added(parts[here.s_far], near[0]).astype(BF)
    here.send(near.at[0], far, sems.at[2], here.far)
    make(here.s_near)
    here.send(parts.at[here.s_near], near.at[1], sems.at[1], here.near)
    make(here.s)
    yield
    here.wait(near.at[1], sems.at[1])
    for _ in range(pause):
        yield
    here.wait(far, sems.at[2])


def masked(scores, at, kv_len, seg_col, seg_row):
    q_pos = at + iota((ROWS, kv_len), 0)
    k_pos = iota((ROWS, kv_len), 1)
    keep = (q_pos >= k_pos) & (seg_col[at : at + ROWS, :] == seg_row[:, :kv_len])
    return jnp.where(keep, scores, BIG)


def set_segments(seg_row, seg_col):
    for b in range(L // ROWS):
        at = slice(b * ROWS, (b + 1) * ROWS)
        seg_col[at, :] = column(seg_row[:, at].astype(F32))


def lane_sum(pieces, rows):
    lane = iota((rows, LANES), 1)
    total = jnp.zeros((rows, LANES), F32)
    for k, piece in pieces:
        total = total + jnp.where(lane == k, piece, 0.0)
    return total.astype(BF)


def attend_kernel(
    tokens, choice, norm_gain, ffn_gain, w_router, w_query, key_weight, value_weight, w_out,
    shared_gate, shared_up, shared_down, expert_gate, expert_up, expert_down, segments, cot,
    normed_one, qkv, heads, logs, gains, marks, misc, qkv_full, out_full, full_a, full_b, normed_two, all_cot, hidden,
    marked, all_marked, qkv_block, out_block, block_a, block_b, normed, part, near, far, normed_home, seg_col,
    send_sems, token_sems, qkv_sems, out_sems, a_sems, b_sems, local_sems, scatter_sems, gather_sems, cot_sems,
):
    here = Here(send_sems)
    here.greet()
    s = here.s

    def wide(ref, at, width):
        return ref[:, pl.ds(pl.multiple_of(at * width, LANES), width)]

    marked[:, :WIDTH] = tokens[...]
    lane = iota((ROWS, LANES), 1)
    used = lane == choice[:, 1:2] + 2
    for k in range(2, 7):
        used = used | (lane == choice[:, k : k + 1] + 2)
    marked[:, WIDTH:] = (jnp.where(used, 1.0, 0.0) + jnp.where(lane == 1, choice[:, 0:1].astype(F32), 0.0)).astype(BF)
    token_gather = seq_gather(here, marked, all_marked, token_sems, 8)
    next(token_gather)
    qkv_block[:, :Q_COLS] = wide(w_query, s, Q_COLS)
    qkv_block[:, Q_COLS:KV] = wide(key_weight, s, HEAD)
    qkv_block[:, KV:] = wide(value_weight, s, HEAD)
    qkv_gather = gather_weight(here, qkv_full, qkv_block, qkv_sems, local_sems.at[0], True)
    next(qkv_gather)
    out_block[:, :Q_COLS] = wide(w_out, s, Q_COLS)
    singles = [(0, column(norm_gain[...].astype(F32))), (1, column(ffn_gain[...].astype(F32)))]
    singles += [(2 + e, w_router[:, e : e + 1].astype(F32)) for e in range(E)]
    out_block[:, Q_COLS:] = lane_sum(singles, SHARD)
    out_gather = gather_weight(here, out_full, out_block, out_sems, local_sems.at[1], False)
    next(out_gather)
    for k, block in enumerate((block_a, block_b)):
        for i, (shared, expert) in enumerate(((shared_gate, expert_gate), (shared_up, expert_up), (shared_down, expert_down))):
            block[:, i * HALF : i * HALF + 512] = wide(expert, 2 * s + k, 512)
            block[:, i * HALF + 512 : (i + 1) * HALF] = wide(shared, 2 * s + k, HALF - 512)
    set_segments(segments, seg_col)
    weights = [
        gather_weight(here, full_a, block_a, a_sems, local_sems.at[2], True),
        gather_weight(here, full_b, block_b, b_sems, local_sems.at[3], False),
    ]
    together(token_gather, qkv_gather, out_gather, later(10, weights))

    def tick():
        for weight in weights:
            next(weight, None)

    cot_gather = seq_gather(here, cot, all_cot, cot_sems)
    next(cot_gather)
    misc[...] = out_full[:, :, :, :, Q_COLS:].reshape(WIDTH, LANES)
    eye = (iota((LANES, LANES), 0) == iota((LANES, LANES), 1)).astype(BF)
    gains[...] = mm_nt(eye, misc[...])[:8]
    gain = gains[0:1, :]
    seg_row = segments[...].astype(F32)
    for b in range(SEQ):
        at = slice(b * ROWS, (b + 1) * ROWS)
        normed[at, :] = normed_of(all_marked[b, :, :WIDTH].astype(F32), gain)[2]
        qkv[at, :] = mm(normed[at, :], qkv_full[...].reshape(WIDTH, HALF)).astype(BF)
        marks[at, :] = all_marked[b, :, WIDTH:]
        if b % 2 == 1:
            tick()
    save = pltpu.make_async_copy(normed, normed_one, local_sems.at[4])
    save.start()
    for b in range(SEQ):
        at, kv_len = b * ROWS, (b + 1) * ROWS
        for h in range(GROUP):
            cols = slice(h * HEAD, (h + 1) * HEAD)
            scores = mm_nt(qkv[at : at + ROWS, cols], qkv[:kv_len, Q_COLS:KV]) * SCALE
            scores = masked(scores, at, kv_len, seg_col, seg_row)
            top = jnp.max(scores, axis=-1, keepdims=True)
            weight = jnp.exp(scores - top)
            total = jnp.sum(weight, axis=-1, keepdims=True)
            probs = (weight * (1.0 / total)).astype(BF)
            heads[at : at + ROWS, cols] = mm(probs, qkv[:kv_len, KV:]).astype(BF)
            logs[at : at + ROWS, h : h + 1] = top + jnp.log(total)
        tick()

    def project(i):
        rows = heads[pl.ds(pl.multiple_of(i * ROWS, ROWS), ROWS), :]
        part[i] = mm_nt(rows, out_full[:, :, :, :, :Q_COLS].reshape(WIDTH, Q_COLS)).astype(BF)

    def rows():
        yield from seq_scatter(here, part, near, far, scatter_sems, project, 2)
        next(cot_gather)
        hidden[...] = added(tokens[...], part[s], near[1], far[...])
        normed_home[...] = normed_of(hidden[...], gains[1:2, :])[2]
        gather = seq_gather(here, normed_home, normed_two, gather_sems, 3)
        yield from gather
        next(cot_gather, None)

    together(rows(), *weights)
    save.wait()
    here.finish()


def experts_kernel(
    normed, cots, full_a, full_b, marks, misc, gains, hidden,
    grad_a, grad_b, grad_low, grad_hidden, grad_misc, out_far, out_own,
    xs, cs, wa, wb, sent, outs, pre_grads, weighted, near, far, near_out, staged, low_home, own_gates,
    send_sems, local_sems, scatter_sems, out_sems, gather_sems, stage_sems,
):
    here = Here(send_sems)
    local = Local(local_sems)
    s = here.s
    order = (here.s_cross, here.s_far, here.s_near, s)
    loads = [[local.copy(normed.at[order[0]], xs.at[order[0]])]]
    load_a = local.copy(full_a, wa)
    loads[0].append(local.copy(cots.at[order[0]], cs.at[order[0]]))
    load_b = local.copy(full_b, wb)
    for i in order[1:]:
        loads.append([local.copy(normed.at[i], xs.at[i]), local.copy(cots.at[i], cs.at[i])])
    here.greet()
    lane = iota((ROWS, LANES), 1)

    def block(n):
        i = order[n]
        at = pl.ds(pl.multiple_of(i * ROWS, ROWS), ROWS)
        for load in loads[n]:
            load.wait()
        x, c = xs[i], cs[i]
        mark = marks[at, :].astype(F32)
        member = (mark > 0) & (lane >= 2) & (lane < 2 + E)
        logits = jnp.where(member, mm(x, misc[...]), BIG)
        soft = jnp.where(member, jnp.exp(logits - jnp.max(logits, axis=-1, keepdims=True)), 0.0)
        gates = soft / jnp.sum(soft, axis=-1, keepdims=True)
        if n == 3:
            own_gates[...] = gates
        keep = mark[:, 1:2]
        total = jnp.zeros((ROWS, WIDTH), F32)
        grad_x = jnp.zeros((ROWS, WIDTH), F32)
        grad_marks = jnp.zeros((ROWS, LANES), F32)
        for k, weight in enumerate((wa, wb)):
            if n == 0:
                (load_a, load_b)[k].wait()
            mine = lane == 2 + 2 * s + k
            gate_e = jnp.sum(jnp.where(mine, gates, 0.0), axis=-1, keepdims=True)
            coef = jnp.concatenate([jnp.broadcast_to(gate_e, (ROWS, 512)), jnp.broadcast_to(keep, (ROWS, HALF - 512))], axis=1)
            pre = mm(x, weight[:, : 2 * HALF])
            gate, upper = pre[:, :HALF], pre[:, HALF:]
            sigma = 1.0 / (1.0 + jnp.exp(-gate))
            silu = gate * sigma
            units = silu * upper
            weighted_k = (coef * units).astype(BF)
            weighted[at, k * HALF : (k + 1) * HALF] = weighted_k
            total += mm_nt(weighted_k, weight[:, 2 * HALF :])
            grad_units = mm(c, weight[:, 2 * HALF :])
            grad_gate = jnp.sum((units * grad_units)[:, :512], axis=-1, keepdims=True)
            high = grad_gate.astype(BF).astype(F32)
            grad_marks += jnp.where(mine, high, 0.0) + jnp.where(lane == LOW + 2 + 2 * s + k, grad_gate - high, 0.0)
            grad_units = coef * grad_units
            pre_grads[at, 2 * k * HALF : (2 * k + 1) * HALF] = (grad_units * upper * (sigma * (1.0 + gate * (1.0 - sigma)))).astype(BF)
            pre_grads[at, (2 * k + 1) * HALF : (2 * k + 2) * HALF] = (grad_units * silu).astype(BF)
            grad_x += mm_nt(pre_grads[at, 2 * k * HALF : (2 * k + 2) * HALF], weight[:, : 2 * HALF])
        outs[i] = total.astype(BF)
        sent[i, :, :WIDTH] = grad_x.astype(BF)
        sent[i, :, WIDTH:] = grad_marks.astype(BF)

    block(0)
    here.send(sent.at[here.s_cross], near.at[0], scatter_sems.at[0], here.near)
    here.send(outs.at[here.s_cross], near_out.at[0], out_sems.at[0], here.near)
    block(1)
    here.wait(near.at[0], scatter_sems.at[0])
    near[0] = added(sent[here.s_far], near[0]).astype(BF)
    here.send(near.at[0], far, scatter_sems.at[2], here.far)
    here.wait(near_out.at[0], out_sems.at[0])
    out_far[...] = added(outs[here.s_far], near_out[0]).astype(BF)
    block(2)
    here.send(sent.at[here.s_near], near.at[1], scatter_sems.at[1], here.near)
    here.send(outs.at[here.s_near], near_out.at[1], out_sems.at[1], here.near)
    block(3)
    here.wait(near.at[1], scatter_sems.at[1])
    here.wait(near_out.at[1], out_sems.at[1])
    out_own[...] = added(hidden[...], outs[s], near_out[1])
    here.wait(far, scatter_sems.at[2])

    grad_gates = added(sent[s, :, WIDTH:], near[1, :, WIDTH:], far[:, WIDTH:])
    grad_gates = grad_gates + pltpu.roll(grad_gates, LANES - LOW, 1)
    gates = own_gates[...]
    grad_logits = gates * (grad_gates - jnp.sum(gates * grad_gates, axis=-1, keepdims=True))
    high, low = split_two(grad_logits)
    grad_normed = added(sent[s, :, :WIDTH], near[1, :, :WIDTH], far[:, :WIDTH])
    grad_normed = grad_normed + (mm_nt(high, misc[...]) + mm_nt(low, misc[...]))
    gain = gains[1:2, :]
    inverse, unit, normed_home = normed_of(hidden[...], gain)
    scaled = grad_normed * gain
    grad = cs[s].astype(F32) + inverse * (scaled - unit * jnp.mean(scaled * unit, axis=-1, keepdims=True))
    grad_hidden[...] = grad
    low_home[...] = grad.astype(BF)
    gather = seq_gather(here, low_home, grad_low, gather_sems)
    next(gather)
    prod_high, prod_low = split_two(grad_normed * unit)
    one = (lane == 1).astype(BF)
    grad_misc[...] = mm_tn(normed_home, high) + mm_tn(normed_home, low) + mm_tn(prod_high, one) + mm_tn(prod_low, one)

    results = (grad_a, grad_b)

    def stage(k, at):
        return pltpu.make_async_copy(staged.at[k], results[k].at[at], stage_sems.at[k])

    def columns(n, carry):
        at = pl.ds(pl.multiple_of(n * ROWS, ROWS), ROWS)
        for k in range(2):
            @pl.when(n > 0)
            def _():
                stage(k, at).wait()

            for i in range(SEQ):
                rows = slice(i * ROWS, (i + 1) * ROWS)
                x = mm_tn(xs[i, :, at], pre_grads[rows, 2 * k * HALF : (2 * k + 2) * HALF])
                c = mm_tn(cs[i, :, at], weighted[rows, k * HALF : (k + 1) * HALF])
                sum_x = x if i == 0 else sum_x + x
                sum_c = c if i == 0 else sum_c + c
            staged[k, :, : 2 * HALF] = sum_x.astype(BF)
            staged[k, :, 2 * HALF :] = sum_c.astype(BF)
            stage(k, at).start()
        return carry

    lax.fori_loop(0, 5, columns, 0)
    next(gather)
    lax.fori_loop(5, WIDTH // ROWS, columns, 0)
    next(gather, None)
    for k in range(2):
        stage(k, pl.ds(0, ROWS)).wait()
    here.finish()


def finish_kernel(
    grad_low_in, normed_in, qkv_in, heads_in, logs_in, qkv_full_in, out_full_in, out_far, grad_a, grad_b,
    segments, gains, grad_misc, grad_hidden, tokens, out_own,
    output, grad_tokens, ffn_a_all, ffn_b_all, q_all, kv_all, out_all,
    grad_low, normed, qkv, heads, logs, qkv_full, out_full, own_a0, own_a1, own_a3, own_b0, own_b1, own_b3,
    grad_q, grad_kvm, grad_out, grad_heads, grad_all, grad_kv, part, near, far, far_out, gain_sum, seg_col,
    piece_a, piece_b, piece_q, piece_kv, piece_out,
    send_sems, local_sems, scatter_sems, out_sems, gather_sems, *buffers,
):
    here = Here(send_sems)
    local = Local(local_sems)
    s = here.s
    load_low = [local.copy(grad_low_in, grad_low), local.copy(out_full_in, out_full), local.copy(heads_in, heads)]
    load_own = []
    for grad, refs, y_first in ((grad_a, (own_a0, own_a1, own_a3), True), (grad_b, (own_b0, own_b1, own_b3), False)):
        for ref, ds in zip(refs, (0, 1, 3)):
            at = wrap((here.y if y_first else here.x) + ds)
            source = grad.at[at] if y_first else grad.at[:, at]
            load_own.append(local.copy(source if ds == 0 else source.at[:, 0 if ds == 1 else 1], ref))
    load_rest = [local.copy(a, b) for a, b in ((qkv_in, qkv), (logs_in, logs), (normed_in, normed), (qkv_full_in, qkv_full))]
    here.greet()

    def owned(refs, place):
        def own(j, ds, h):
            at = wrap(place + j)
            return refs[0][at, h] if ds == 0 else refs[1 if ds == 1 else 2][at]

        return own

    def summed(grad, own, scratch, piece, y_first, full, sems):
        yield from scatter_grad(here, grad, own, scratch, piece, y_first)
        yield from seq_gather(here, piece, full, sems)

    sums = [
        summed(grad_a, owned((own_a0, own_a1, own_a3), here.x), buffers[:10], piece_a, True, ffn_a_all, gather_sems.at[0]),
        summed(grad_b, owned((own_b0, own_b1, own_b3), here.y), buffers[10:20], piece_b, False, ffn_b_all, gather_sems.at[1]),
    ]

    def tick():
        for part_sum in sums:
            next(part_sum, None)

    tick()
    here.send(out_far, far_out, out_sems.at[0], here.far)
    set_segments(segments, seg_col)
    seg_row = segments[...].astype(F32)
    for load in load_low:
        load.wait()
    for b in range(SEQ):
        at = slice(b * ROWS, (b + 1) * ROWS)
        grad_heads[at, :] = mm(grad_low[at, :], out_full[:, :Q_COLS]).astype(BF)
    for load in load_own:
        load.wait()
    tick()

    def chunk(y):
        return pl.ds(pl.multiple_of(y * CHUNK, CHUNK), CHUNK)

    def out_chunk(y, carry):
        grad_out[y] = mm_tn(grad_low[:, chunk(y)], heads[...]).astype(BF).reshape(4, 2, SHARD, Q_COLS)
        return carry

    lax.fori_loop(0, 4, out_chunk, 0)
    sums.append(summed(grad_out, None, buffers[20:30], piece_out, False, out_all, gather_sems.at[2]))
    tick()
    for load in load_rest:
        load.wait()
    grad_kv[...] = jnp.zeros_like(grad_kv)
    for b in range(SEQ):
        at, kv_len = b * ROWS, (b + 1) * ROWS
        for h in range(GROUP):
            cols = slice(h * HEAD, (h + 1) * HEAD)
            query, grad = qkv[at : at + ROWS, cols], grad_heads[at : at + ROWS, cols]
            scores = mm_nt(query, qkv[:kv_len, Q_COLS:KV]) * SCALE
            probs = jnp.exp(masked(scores, at, kv_len, seg_col, seg_row) - logs[at : at + ROWS, h : h + 1])
            grad_probs = mm_nt(grad, qkv[:kv_len, KV:])
            centre = jnp.sum(probs * grad_probs, axis=-1, keepdims=True)
            grad_scores = (probs * (grad_probs - centre)).astype(BF)
            grad_all[at : at + ROWS, cols] = (mm(grad_scores, qkv[:kv_len, Q_COLS:KV]) * SCALE).astype(BF)
            grad_kv[:kv_len, :HEAD] += mm_tn(grad_scores, query) * SCALE
            grad_kv[:kv_len, HEAD:] += mm_tn(probs.astype(BF), grad)
        if b > 0:
            tick()
    grad_all[:, Q_COLS:] = grad_kv[...].astype(BF)

    def q_chunk(y, carry):
        grad_q[y] = mm_tn(normed[:, chunk(y)], grad_all[:, :Q_COLS]).astype(BF).reshape(4, 2, SHARD, Q_COLS)
        return carry

    lax.fori_loop(0, 4, q_chunk, 0)
    sums.append(summed(grad_q, None, buffers[30:40], piece_q, True, q_all, gather_sems.at[3]))
    next(sums[-1])
    gain_sum[...] = jnp.zeros_like(gain_sum)

    def back(i):
        at = pl.ds(pl.multiple_of(i * ROWS, ROWS), ROWS)
        value = mm_nt(grad_all[at, :], qkv_full[...])
        part[i] = value.astype(BF)
        gain_sum[0:1, :] += jnp.sum(value * normed[at, :].astype(F32), axis=0, keepdims=True)

    row_sum = seq_scatter(here, part, near, far, scatter_sems, back, 5)
    next(row_sum)
    next(row_sum)
    gain = gains[0:1, :]
    high, low = split_two(gain_sum[0:1, :] / gain)
    row = iota((16, WIDTH), 0)
    both = jnp.where(row == 0, high.astype(F32), 0.0) + jnp.where(row == 1, low.astype(F32), 0.0)
    gain_sum[...] = both
    pick = (iota((16, LANES), 1) == 0).astype(BF)

    def kv_chunk(y, carry):
        at = chunk(y)
        pair = mm_tn(normed[:, at], grad_all[:, Q_COLS:])
        single = grad_misc[at, :] + mm_tn(gain_sum[:, at].astype(BF), pick)
        grad_kvm[y] = jnp.concatenate([pair, single], axis=1).astype(BF).reshape(4, 2, SHARD, Q_COLS)
        return carry

    lax.fori_loop(0, 4, kv_chunk, 0)
    sums.append(summed(grad_kvm, None, buffers[40:], piece_kv, False, kv_all, gather_sems.at[4]))

    def rows():
        yield from row_sum
        here.wait(far_out, out_sems.at[0])
        output[...] = added(out_own[...], far_out[...]).astype(BF)
        grad_normed = added(part[s], near[1], far[...])
        inverse, unit, _ = normed_of(tokens[...].astype(F32), gain)
        scaled = grad_normed * gain
        grad_tokens[...] = (grad_hidden[...] + inverse * (scaled - unit * jnp.mean(scaled * unit, axis=-1, keepdims=True))).astype(BF)

    together(*sums, rows())
    here.finish()


def outputs_kernel(
    ffn_a, ffn_b, q, kv, out, wq, wk, wv, wo, misc, shared_gate, shared_up, shared_down, expert_gate, expert_up, expert_down
):
    total = jnp.zeros((SHARD, LANES), F32)
    for s in range(SEQ):
        wq[:, s * Q_COLS : (s + 1) * Q_COLS] = q[s].astype(F32)
        wo[:, s * Q_COLS : (s + 1) * Q_COLS] = out[s].astype(F32)
        wk[:, s * HEAD : (s + 1) * HEAD] = kv[s, :, :HEAD].astype(F32)
        wv[:, s * HEAD : (s + 1) * HEAD] = kv[s, :, HEAD : 2 * HEAD].astype(F32)
        total = total + kv[s, :, 2 * HEAD :].astype(F32)
        for k, ffn in enumerate((ffn_a, ffn_b)):
            n = 2 * s + k
            for i, (shared, expert) in enumerate(((shared_gate, expert_gate), (shared_up, expert_up), (shared_down, expert_down))):
                expert[:, n, :] = ffn[s, :, i * HALF : i * HALF + 512].astype(F32)
                shared[:, n * LANES : (n + 1) * LANES] = ffn[s, :, i * HALF + 512 : (i + 1) * HALF].astype(F32)
    misc[...] = total


def remote_call(kernel, name, number, outs, ins, scratch):
    return pl.pallas_call(
        kernel,
        out_shape=[jax.ShapeDtypeStruct(dims, dtype) for dims, dtype, _ in outs],
        in_specs=[VMEM_ALL if fast else ANY for _, fast in ins],
        out_specs=[VMEM_ALL if fast else ANY for _, _, fast in outs],
        scratch_shapes=list(scratch),
        compiler_params=pltpu.CompilerParams(collective_id=number, has_side_effects=True, vmem_limit_bytes=LIMIT),
        name=name,
    )(*[array for array, _ in ins])


def buf(*dims):
    return pltpu.VMEM(dims, BF)


def buf32(*dims):
    return pltpu.VMEM(dims, F32)


def body(
    tokens,
    segments,
    routes,
    shared_mask,
    norm_gain,
    w_query,
    key_weight,
    value_weight,
    w_out,
    ffn_gain,
    w_router,
    shared_gate,
    shared_up,
    shared_down,
    expert_gate,
    expert_up,
    expert_down,
    cotangent,
):
    choice = jnp.concatenate([shared_mask[:, None], routes], axis=1)
    seg_row = segments[None, :]
    grid = DMA((4, 4, 2))
    rows4 = (SEQ, ROWS, WIDTH)
    flat = [w.reshape(SHARD, -1) for w in (expert_gate, expert_up, expert_down)]
    fast = [tokens, choice, norm_gain[None, :], ffn_gain[None, :], w_router, w_query, key_weight, value_weight, w_out,
            shared_gate, shared_up, shared_down, *flat, seg_row]
    (
        normed_one, qkv, heads, logs, gains, marks, misc, qkv_full, out_full, full_a, full_b, normed_two, all_cot, hidden,
    ) = remote_call(
        attend_kernel,
        "attend",
        1,
        [
            ((L, WIDTH), BF, False),
            ((L, HALF), BF, True),
            ((L, Q_COLS), BF, True),
            ((L, 8), F32, True),
            ((8, WIDTH), F32, True),
            ((L, LANES), BF, True),
            ((WIDTH, LANES), BF, True),
            (blocks(HALF), BF, True),
            (blocks(OUT_COLS), BF, True),
            (blocks(FFN), BF, False),
            (blocks(FFN), BF, False),
            (rows4, BF, False),
            (rows4, BF, False),
            ((ROWS, WIDTH), F32, True),
        ],
        [(a, True) for a in fast] + [(cotangent, False)],
        [
            buf(ROWS, WIDTH + LANES),
            buf(SEQ, ROWS, WIDTH + LANES),
            buf(SHARD, HALF),
            buf(SHARD, OUT_COLS),
            buf(SHARD, FFN),
            buf(SHARD, FFN),
            buf(L, WIDTH),
            buf(*rows4),
            buf(2, ROWS, WIDTH),
            buf(ROWS, WIDTH),
            buf(ROWS, WIDTH),
            buf32(L, 1),
            DMA((160,)),
            DMA((4,)),
            grid,
            grid,
            grid,
            grid,
            DMA((5,)),
            DMA((3,)),
            DMA((4,)),
            DMA((4,)),
        ],
    )

    grad_a, grad_b, grad_low, grad_hidden, grad_misc, out_far, out_own = remote_call(
        experts_kernel,
        "experts",
        2,
        [
            ((WIDTH, FFN), BF, False),
            ((WIDTH, FFN), BF, False),
            (rows4, BF, False),
            ((ROWS, WIDTH), F32, True),
            ((WIDTH, LANES), F32, True),
            ((ROWS, WIDTH), BF, True),
            ((ROWS, WIDTH), F32, True),
        ],
        [
            (normed_two, False),
            (all_cot, False),
            (full_a.reshape(WIDTH, FFN), False),
            (full_b.reshape(WIDTH, FFN), False),
            (marks, True),
            (misc, True),
            (gains, True),
            (hidden, True),
        ],
        [
            buf(*rows4),
            buf(*rows4),
            buf(WIDTH, FFN),
            buf(WIDTH, FFN),
            buf(SEQ, ROWS, WIDTH + LANES),
            buf(*rows4),
            buf(L, 4 * HALF),
            buf(L, 2 * HALF),
            buf(2, ROWS, WIDTH + LANES),
            buf(ROWS, WIDTH + LANES),
            buf(2, ROWS, WIDTH),
            buf(2, ROWS, FFN),
            buf(ROWS, WIDTH),
            buf32(ROWS, LANES),
            DMA((12,)),
            DMA((12,)),
            DMA((3,)),
            DMA((2,)),
            DMA((4,)),
            DMA((2,)),
        ],
    )

    own = [buf(4, 2, SHARD, FFN), buf(4, SHARD, FFN), buf(4, SHARD, FFN)]
    output, grad_tokens, ffn_a_all, ffn_b_all, q_all, kv_all, out_all = remote_call(
        finish_kernel,
        "finish",
        3,
        [
            ((ROWS, WIDTH), BF, True),
            ((ROWS, WIDTH), BF, True),
            ((SEQ, SHARD, FFN), BF, False),
            ((SEQ, SHARD, FFN), BF, False),
            ((SEQ, SHARD, Q_COLS), BF, False),
            ((SEQ, SHARD, Q_COLS), BF, False),
            ((SEQ, SHARD, Q_COLS), BF, False),
        ],
        [
            (grad_low.reshape(L, WIDTH), False),
            (normed_one, False),
            (qkv, False),
            (heads, False),
            (logs, False),
            (qkv_full.reshape(WIDTH, HALF), False),
            (out_full.reshape(WIDTH, OUT_COLS), False),
            (out_far, False),
            (grad_a.reshape(blocks(FFN)), False),
            (grad_b.reshape(blocks(FFN)), False),
            (seg_row, True),
            (gains, True),
            (grad_misc, True),
            (grad_hidden, True),
            (tokens, True),
            (out_own, True),
        ],
        [
            buf(L, WIDTH),
            buf(L, WIDTH),
            buf(L, HALF),
            buf(L, Q_COLS),
            buf32(L, 8),
            buf(WIDTH, HALF),
            buf(WIDTH, OUT_COLS),
            *own,
            *own,
            buf(*blocks(Q_COLS)),
            buf(*blocks(Q_COLS)),
            buf(*blocks(Q_COLS)),
            buf(L, Q_COLS),
            buf(L, HALF),
            buf32(L, 2 * HEAD),
            buf(*rows4),
            buf(2, ROWS, WIDTH),
            buf(ROWS, WIDTH),
            buf(ROWS, WIDTH),
            buf32(16, WIDTH),
            buf32(L, 1),
            buf(SHARD, FFN),
            buf(SHARD, FFN),
            buf(SHARD, Q_COLS),
            buf(SHARD, Q_COLS),
            buf(SHARD, Q_COLS),
            DMA((192,)),
            DMA((16,)),
            DMA((3,)),
            DMA((1,)),
            DMA((5, 4)),
            *scatter_buffers(FFN),
            *scatter_buffers(FFN),
            *scatter_buffers(Q_COLS),
            *scatter_buffers(Q_COLS),
            *scatter_buffers(Q_COLS),
        ],
    )

    dims = [(SHARD, 4 * Q_COLS), (SHARD, 4 * HEAD), (SHARD, 4 * HEAD), (SHARD, 4 * Q_COLS), (SHARD, LANES)]
    dims += [(SHARD, 1024)] * 3 + [(SHARD, E, 512)] * 3
    wq, wk, wv, wo, single, *ffn = pl.pallas_call(
        outputs_kernel,
        out_shape=[jax.ShapeDtypeStruct(d, F32) for d in dims],
        in_specs=[VMEM_ALL] * 5,
        out_specs=[VMEM_ALL] * len(dims),
        compiler_params=pltpu.CompilerParams(vmem_limit_bytes=LIMIT),
        name="outputs",
    )(ffn_a_all, ffn_b_all, q_all, kv_all, out_all)
    return (output, grad_tokens, single[:, 0], wq, wk, wv, wo, single[:, 1], single[:, 2 : 2 + E], *ffn)


def solution(mesh):
    both = P(("fsdp", "seq"), None)
    one, two, three = P("fsdp"), P("fsdp", None), P("fsdp", None, None)
    return jax.shard_map(
        body,
        mesh=mesh,
        in_specs=(both, one, both, P(("fsdp", "seq")), one, two, two, two, two, one, two, two, two, two, three, three, three, both),
        out_specs=(both, both, one, two, two, two, two, one, two, two, two, two, three, three, three),
        check_vma=False,
    )
```

```python
import jax
import jax.numpy as jnp
from jax import lax
from jax.experimental import pallas as pl
from jax.experimental.pallas import tpu as pltpu
from jax.sharding import PartitionSpec as P

HEAD = 128
GROUP = 3
E = 8
SEQ = 4
EPS = 1e-05
BF = jnp.bfloat16
F32 = jnp.float32
WIDTH = 1536
L = 1024
ROWS = 256
SHARD = 48
Q_COLS = GROUP * HEAD
KV = Q_COLS + HEAD
HALF = 640
FFN = 3 * HALF
LANES = 128
OUT_COLS = Q_COLS + LANES
LOW = 32
CHUNK = 384
SCALE = HEAD ** (-0.5)
BIG = -1e30
MESH = pl.DeviceIdType.MESH
VMEM_ALL = pl.BlockSpec(memory_space=pltpu.VMEM)
ANY = pl.BlockSpec(memory_space=pl.ANY)
DMA = pltpu.SemaphoreType.DMA
LIMIT = 63 * 1024 * 1024


def f32dot(left, right, dims):
    return lax.dot_general(left, right, (dims, ((), ())), preferred_element_type=F32)


def mm(left, right):
    return f32dot(left, right, ((1,), (0,)))


def mm_nt(left, right):
    return f32dot(left, right, ((1,), (1,)))


def mm_tn(left, right):
    return f32dot(left, right, ((0,), (0,)))


def iota(dims, axis):
    return lax.broadcasted_iota(jnp.int32, dims, axis)


def column(row):
    n = row.shape[1]
    same = iota((n, n), 0) == iota((n, n), 1)
    return jnp.sum(jnp.where(same, jnp.broadcast_to(row, (n, n)), 0.0), axis=-1, keepdims=True)


def added(*values):
    total = values[0].astype(F32)
    for value in values[1:]:
        total = total + value.astype(F32)
    return total


def split_two(value):
    high = value.astype(BF)
    return high, (value - high.astype(F32)).astype(BF)


def normed_of(x, gain):
    inverse = lax.rsqrt(jnp.mean(x * x, axis=-1, keepdims=True) + EPS)
    unit = x * inverse
    return inverse, unit, (unit * gain).astype(BF)


def wrap(value):
    return lax.rem(value + 4, 4)


def blocks(cols):
    return (4, 4, 2, SHARD, cols)


class Here:
    def __init__(self, send_sems):
        f, s = lax.axis_index("fsdp"), lax.axis_index("seq")
        self.y, self.x, self.z = lax.div(f, 8), lax.rem(lax.div(f, 2), 4), lax.rem(f, 2)
        self.s, self.zh, self.core = s, lax.div(s, 2), lax.rem(s, 2)
        y, x, z = self.y, self.x, self.z
        self.axis_x = ({"fsdp": self.number(y, wrap(x + 1), z)}, {"fsdp": self.number(y, wrap(x - 1), z)})
        self.axis_y = ({"fsdp": self.number(wrap(y + 1), x, z)}, {"fsdp": self.number(wrap(y - 1), x, z)})
        self.pair = {"fsdp": self.number(y, x, 1 - z)}
        self.s_far = (1 - self.zh) * 2 + self.core
        self.s_near = self.zh * 2 + 1 - self.core
        self.s_cross = (1 - self.zh) * 2 + 1 - self.core
        self.far = {"seq": self.s_far}
        self.near = {"seq": self.s_near}
        self.sems, self.sent = send_sems, []

    @staticmethod
    def number(y, x, z):
        return (y * 4 + x) * 2 + z

    def greet(self):
        barrier = pltpu.get_barrier_semaphore()
        partners = [*self.axis_x, *self.axis_y, self.pair, self.far, self.near]
        for partner in partners:
            pl.semaphore_signal(barrier, inc=1, device_id=partner, device_id_type=MESH)
        pl.semaphore_wait(barrier, len(partners))

    def send(self, source, target, recv_sem, to):
        copy = pltpu.make_async_remote_copy(
            src_ref=source,
            dst_ref=target,
            send_sem=self.sems.at[len(self.sent)],
            recv_sem=recv_sem,
            device_id=to,
            device_id_type=MESH,
        )
        copy.start()
        self.sent.append(copy)

    def wait(self, target, recv_sem):
        pltpu.make_async_remote_copy(
            src_ref=target,
            dst_ref=target,
            send_sem=self.sems.at[0],
            recv_sem=recv_sem,
            device_id=self.near,
            device_id_type=MESH,
        ).wait_recv()

    def finish(self):
        for copy in self.sent:
            copy.wait_send()


class Local:
    def __init__(self, sems):
        self.sems, self.count = sems, 0

    def copy(self, source, target):
        copy = pltpu.make_async_copy(source, target, self.sems.at[self.count])
        copy.start()
        self.count += 1
        return copy


def together(*parts):
    left = list(parts)
    while left:
        for part in list(left):
            if next(part, "end") == "end":
                left.remove(part)


def later(turns, parts):
    for _ in range(turns):
        yield
    for part in parts:
        next(part)


def gather_weight(here, full, block, recv, own_sem, x_first):
    first, second = (here.axis_x, here.axis_y) if x_first else (here.axis_y, here.axis_x)

    def spot(df, ds, r):
        dy, dx = (ds, df) if x_first else (df, ds)
        return wrap(here.y + dy), wrap(here.x + dx), here.z if r == 0 else 1 - here.z

    def push(df, ds, r, to, source=None):
        at = spot(df, ds, r)
        here.send(full.at[at] if source is None else source, full.at[at], recv.at[at], to)

    def take(df, ds, r):
        at = spot(df, ds, r)
        here.wait(full.at[at], recv.at[at])

    own = pltpu.make_async_copy(block, full.at[spot(0, 0, 0)], own_sem)
    own.start()
    push(0, 0, 0, here.pair, block)
    yield
    for to in (*second, *first):
        push(0, 0, 0, to, block)
    yield
    take(0, 0, 1)
    for to in (*first, *second):
        push(0, 0, 1, to)
    for df, r in ((-1, 0), (1, 0), (1, 1), (-1, 1), (2, 0), (2, 1)):
        yield
        take(df, 0, r)
        if (df, r) == (-1, 0):
            push(df, 0, r, first[0])
        if (df, r) == (1, 1):
            push(df, 0, r, first[1])
        for to in second:
            push(df, 0, r, to)
        if (df, r) == (1, 0):
            take(0, -1, 0)
            push(0, -1, 0, second[0])
        if (df, r) == (-1, 1):
            take(0, 1, 1)
            push(0, 1, 1, second[1])
    for df in (-1, 1, 2):
        yield
        take(df, -1, 0)
        push(df, -1, 0, second[0])
        yield
        take(df, 1, 1)
        push(df, 1, 1, second[1])
    yield
    for df in (0, -1, 1, 2):
        take(df, -1, 1)
        take(df, 1, 0)
        take(df, 2, 0)
        take(df, 2, 1)
    own.wait()


def scatter_buffers(cols):
    units = [(4,), (4,), (4, 2), (4, 2), (1,), (1,), (2,), (2,), (1,)]
    return [pltpu.VMEM((*u, SHARD, cols), BF) for u in units] + [DMA((31,))]


def scatter_grad(here, block, own, buffers, piece, y_first, small):
    ra, rb, rc, rd, xa, xb, xc, xd, zr, sems = buffers
    second, first = (here.axis_y, here.axis_x) if y_first else (here.axis_x, here.axis_y)
    own = own or (lambda df, ds, h: block(df, ds, h)[...])

    def far_send(j):
        here.send(block(j, 2, 0), ra.at[j], sems.at[j], second[0])
        here.send(block(j, 2, 1), rb.at[j], sems.at[4 + j], second[1])

    def near_plus(j):
        here.send(block(j, 1, 1), rc.at[j, 1], sems.at[8 + 2 * j + 1], second[0])

    def near_minus(j):
        here.send(block(j, 3, 0), rd.at[j, 0], sems.at[16 + 2 * j], second[1])

    def pass_on(j):
        here.wait(ra.at[j], sems.at[j])
        ra[j] = added(own(j, 1, 0), ra[j]).astype(BF)
        here.send(ra.at[j], rc.at[j, 0], sems.at[8 + 2 * j], second[0])
        here.wait(rb.at[j], sems.at[4 + j])
        rb[j] = added(own(j, 3, 1), rb[j]).astype(BF)
        here.send(rb.at[j], rd.at[j, 1], sems.at[16 + 2 * j + 1], second[1])

    def total(j):
        for h in range(2):
            here.wait(rc.at[j, h], sems.at[8 + 2 * j + h])
            here.wait(rd.at[j, h], sems.at[16 + 2 * j + h])
            rc[j, h] = added(own(j, 0, h), rc[j, h], rd[j, h]).astype(BF)

    def turn_two():
        here.send(rc.at[2, 0], xa.at[0], sems.at[24], first[0])
        here.send(rc.at[2, 1], xb.at[0], sems.at[25], first[1])

    def turn_one():
        here.send(rc.at[1, 1], xc.at[1], sems.at[27], first[0])
        here.wait(xa.at[0], sems.at[24])
        xa[0] = added(rc[1, 0], xa[0]).astype(BF)
        here.send(xa.at[0], xc.at[0], sems.at[26], first[0])

    def turn_three():
        here.send(rc.at[3, 0], xd.at[0], sems.at[28], first[1])
        here.wait(xb.at[0], sems.at[25])
        xb[0] = added(rc[3, 1], xb[0]).astype(BF)
        here.send(xb.at[0], xd.at[1], sems.at[29], first[1])

    every = (2, 1, 3, 0)
    if small:
        for j in every:
            far_send(j)
            near_plus(j)
            near_minus(j)
        yield
        for j in every:
            pass_on(j)
        yield
        total(2)
        turn_two()
        total(1)
        total(3)
        turn_one()
        turn_three()
        yield
        total(0)
    else:
        if y_first:
            for send in (far_send, near_plus, near_minus):
                for j in every:
                    send(j)
                yield
        else:
            for j in every:
                far_send(j)
                near_plus(j)
                near_minus(j)
                yield
        if y_first:
            yield
        pass_on(2)
        pass_on(1)
        yield
        pass_on(3)
        pass_on(0)
        yield
        total(2)
        turn_two()
        yield
        total(1)
        turn_one()
        yield
        total(3)
        turn_three()
        yield
        total(0)
        yield
    for h in range(2):
        here.wait(xc.at[h], sems.at[26 + h])
        here.wait(xd.at[h], sems.at[28 + h])
        xc[h] = added(rc[0, h], xc[h], xd[h]).astype(BF)
    here.send(xc.at[1 - here.z], zr.at[0], sems.at[30], here.pair)
    yield
    here.wait(zr.at[0], sems.at[30])
    piece[...] = added(xc[here.z], zr[0]).astype(piece.dtype)


def seq_gather(here, source, full, sems, pause=1):
    own = pltpu.make_async_copy(source, full.at[here.s], sems.at[3])
    own.start()
    here.send(source, full.at[here.s], sems.at[0], here.far)
    here.send(source, full.at[here.s], sems.at[1], here.near)
    for _ in range(pause):
        yield
    here.wait(full.at[here.s_far], sems.at[0])
    here.send(full.at[here.s_far], full.at[here.s_far], sems.at[2], here.near)
    yield
    here.wait(full.at[here.s_near], sems.at[1])
    here.wait(full.at[here.s_cross], sems.at[2])
    own.wait()


def seq_scatter(here, parts, near, far, sems, make, pause=1):
    make(here.s_cross)
    here.send(parts.at[here.s_cross], near.at[0], sems.at[0], here.near)
    make(here.s_far)
    yield
    here.wait(near.at[0], sems.at[0])
    near[0] = added(parts[here.s_far], near[0]).astype(BF)
    here.send(near.at[0], far, sems.at[2], here.far)
    make(here.s_near)
    here.send(parts.at[here.s_near], near.at[1], sems.at[1], here.near)
    make(here.s)
    yield
    here.wait(near.at[1], sems.at[1])
    for _ in range(pause):
        yield
    here.wait(far, sems.at[2])


def masked(scores, at, kv_len, seg_col, seg_row):
    q_pos = at + iota((ROWS, kv_len), 0)
    k_pos = iota((ROWS, kv_len), 1)
    keep = (q_pos >= k_pos) & (seg_col[at : at + ROWS, :] == seg_row[:, :kv_len])
    return jnp.where(keep, scores, BIG)


def set_segments(seg_row, seg_col):
    for b in range(L // ROWS):
        at = slice(b * ROWS, (b + 1) * ROWS)
        seg_col[at, :] = column(seg_row[:, at].astype(F32))


def attend_kernel(
    tokens, routes, shared_mask, norm_gain, ffn_gain, w_router, w_query, key_weight, value_weight, w_out,
    shared_gate, shared_up, shared_down, expert_gate, expert_up, expert_down, segments, cot,
    normed_one, qkv, heads, logs, gains, marks, misc, qkv_full, out_full, full_a, full_b, normed_two, all_cot, hidden,
    marked, all_marked, qkv_block, out_block, block_a, block_b, normed, part, near, far, normed_home, seg_col,
    send_sems, token_sems, qkv_sems, out_sems, a_sems, b_sems, local_sems, scatter_sems, gather_sems, cot_sems,
):
    here = Here(send_sems)
    here.greet()
    s = here.s

    def wide(ref, at, width):
        return ref[:, pl.ds(pl.multiple_of(at * width, LANES), width)]

    marked[:, :WIDTH] = tokens[...]
    line = iota((LANES, ROWS), 0)
    used = line == routes[0:1, :] + 2
    for k in range(1, 6):
        used = used | (line == routes[k : k + 1, :] + 2)
    turned = (jnp.where(used, 1.0, 0.0) + jnp.where(line == 1, shared_mask[...].astype(F32), 0.0)).astype(BF)
    eye = (iota((LANES, LANES), 0) == iota((LANES, LANES), 1)).astype(BF)
    marked[:, WIDTH:] = mm_tn(turned, eye).astype(BF)
    token_gather = seq_gather(here, marked, all_marked, token_sems, 13)
    qkv_block[:, :Q_COLS] = wide(w_query, s, Q_COLS)
    qkv_block[:, Q_COLS:KV] = wide(key_weight, s, HEAD)
    qkv_block[:, KV:] = wide(value_weight, s, HEAD)
    qkv_gather = gather_weight(here, qkv_full, qkv_block, qkv_sems, local_sems.at[0], True)
    next(qkv_gather)
    out_block[:, :Q_COLS] = wide(w_out, s, Q_COLS)
    place = (iota((E, LANES), 1) == iota((E, LANES), 0) + 2).astype(F32)
    single = f32dot(w_router[...].astype(F32), place, ((0,), (0,)))
    lane = iota((SHARD, LANES), 1)
    single = single + jnp.where(lane == 0, column(norm_gain[...].astype(F32)), 0.0)
    out_block[:, Q_COLS:] = (single + jnp.where(lane == 1, column(ffn_gain[...].astype(F32)), 0.0)).astype(BF)
    out_gather = gather_weight(here, out_full, out_block, out_sems, local_sems.at[1], False)
    next(out_gather)
    next(token_gather)
    next(qkv_gather)
    next(out_gather)
    for k, block in enumerate((block_a, block_b)):
        pick = (iota((SHARD, SHARD * E), 1) == iota((SHARD, SHARD * E), 0) * E + 2 * s + k).astype(BF)
        for i, (shared, expert) in enumerate(((shared_gate, expert_gate), (shared_up, expert_up), (shared_down, expert_down))):
            block[:, i * HALF : i * HALF + 512] = mm(pick, expert[...].reshape(SHARD * E, 512)).astype(BF)
            block[:, i * HALF + 512 : (i + 1) * HALF] = wide(shared, 2 * s + k, HALF - 512)
    set_segments(segments, seg_col)
    weights = [
        gather_weight(here, full_a, block_a, a_sems, local_sems.at[2], True),
        gather_weight(here, full_b, block_b, b_sems, local_sems.at[3], False),
    ]
    for weight in weights:
        next(weight)
    together(token_gather, qkv_gather, out_gather, later(9, weights))

    def tick():
        for weight in weights:
            next(weight, None)

    cot_gather = seq_gather(here, cot, all_cot, cot_sems)
    next(cot_gather)
    misc[...] = out_full[:, :, :, :, Q_COLS:].reshape(WIDTH, LANES)
    gains[...] = mm_nt(eye, misc[...])[:8]
    gain = gains[0:1, :]
    seg_row = segments[...].astype(F32)
    for b in range(SEQ):
        at = slice(b * ROWS, (b + 1) * ROWS)
        normed[at, :] = normed_of(all_marked[b, :, :WIDTH].astype(F32), gain)[2]
        qkv[at, :] = mm(normed[at, :], qkv_full[...].reshape(WIDTH, HALF)).astype(BF)
        marks[at, :] = all_marked[b, :, WIDTH:]
        if b % 2 == 1:
            tick()
    save = pltpu.make_async_copy(normed, normed_one, local_sems.at[4])
    save.start()
    for b in range(SEQ):
        at, kv_len = b * ROWS, (b + 1) * ROWS
        for h in range(GROUP):
            cols = slice(h * HEAD, (h + 1) * HEAD)
            scores = mm_nt(qkv[at : at + ROWS, cols], qkv[:kv_len, Q_COLS:KV]) * SCALE
            scores = masked(scores, at, kv_len, seg_col, seg_row)
            top = jnp.max(scores, axis=-1, keepdims=True)
            weight = jnp.exp(scores - top)
            total = jnp.sum(weight, axis=-1, keepdims=True)
            probs = (weight * (1.0 / total)).astype(BF)
            heads[at : at + ROWS, cols] = mm(probs, qkv[:kv_len, KV:]).astype(BF)
            logs[at : at + ROWS, h : h + 1] = top + jnp.log(total)
        tick()

    def project(i):
        rows = heads[pl.ds(pl.multiple_of(i * ROWS, ROWS), ROWS), :]
        part[i] = mm_nt(rows, out_full[:, :, :, :, :Q_COLS].reshape(WIDTH, Q_COLS)).astype(BF)

    def rows():
        yield from seq_scatter(here, part, near, far, scatter_sems, project, 2)
        next(cot_gather)
        hidden[...] = added(tokens[...], part[s], near[1], far[...])
        normed_home[...] = normed_of(hidden[...], gains[1:2, :])[2]
        gather = seq_gather(here, normed_home, normed_two, gather_sems, 3)
        yield from gather
        next(cot_gather, None)

    together(rows(), *weights)
    save.wait()
    here.finish()


def experts_kernel(
    normed, cots, full_a, full_b, marks, misc, gains, hidden,
    pre_a, pre_b, low_home, grad_hidden, grad_misc, out_far, out_own,
    xs, cs, wa, wb, sent, outs, staged, near, far, near_out, own_gates, hidden_out, own_out, far_sum, low_out,
    send_sems, local_sems, scatter_sems, out_sems,
):
    here = Here(send_sems)
    local = Local(local_sems)
    s = here.s
    order = (here.s_cross, here.s_far, here.s_near, s)
    loads = [[local.copy(normed.at[order[0]], xs.at[order[0]])]]
    load_a = local.copy(full_a, wa)
    loads[0].append(local.copy(cots.at[order[0]], cs.at[order[0]]))
    load_b = local.copy(full_b, wb)
    for i in order[1:]:
        loads.append([local.copy(normed.at[i], xs.at[i]), local.copy(cots.at[i], cs.at[i])])
    here.greet()
    lane = iota((ROWS, LANES), 1)
    stored = [[], []]

    def block(n):
        i = order[n]
        at = pl.ds(pl.multiple_of(i * ROWS, ROWS), ROWS)
        for load in loads[n]:
            load.wait()
        x, c = xs[i], cs[i]
        mark = marks[at, :].astype(F32)
        member = (mark > 0) & (lane >= 2) & (lane < 2 + E)
        logits = jnp.where(member, mm(x, misc[...]), BIG)
        soft = jnp.where(member, jnp.exp(logits - jnp.max(logits, axis=-1, keepdims=True)), 0.0)
        gates = soft / jnp.sum(soft, axis=-1, keepdims=True)
        if n == 3:
            own_gates[...] = gates
        keep = mark[:, 1:2]
        total = jnp.zeros((ROWS, WIDTH), F32)
        grad_x = jnp.zeros((ROWS, WIDTH), F32)
        grad_marks = jnp.zeros((ROWS, LANES), F32)
        for k, weight in enumerate((wa, wb)):
            if n == 0:
                (load_a, load_b)[k].wait()
            if n >= 2:
                stored[k][n - 2].wait()
            slot = staged.at[n % 2, k]
            mine = lane == 2 + 2 * s + k
            gate_e = jnp.sum(jnp.where(mine, gates, 0.0), axis=-1, keepdims=True)
            coef = jnp.concatenate([jnp.broadcast_to(gate_e, (ROWS, 512)), jnp.broadcast_to(keep, (ROWS, HALF - 512))], axis=1)
            pre = mm(x, weight[:, : 2 * HALF])
            gate, upper = pre[:, :HALF], pre[:, HALF:]
            sigma = 1.0 / (1.0 + jnp.exp(-gate))
            silu = gate * sigma
            units = silu * upper
            weighted = (coef * units).astype(BF)
            slot[:, 2 * HALF :] = weighted
            total += mm_nt(weighted, weight[:, 2 * HALF :])
            grad_units = mm(c, weight[:, 2 * HALF :])
            grad_gate = jnp.sum((units * grad_units)[:, :512], axis=-1, keepdims=True)
            high = grad_gate.astype(BF).astype(F32)
            grad_marks += jnp.where(mine, high, 0.0) + jnp.where(lane == LOW + 2 + 2 * s + k, grad_gate - high, 0.0)
            grad_units = coef * grad_units
            slot[:, :HALF] = (grad_units * upper * (sigma * (1.0 + gate * (1.0 - sigma)))).astype(BF)
            slot[:, HALF : 2 * HALF] = (grad_units * silu).astype(BF)
            grad_x += mm_nt(slot[:, : 2 * HALF], weight[:, : 2 * HALF])
            stored[k].append(local.copy(slot, (pre_a, pre_b)[k].at[at]))
        outs[i] = total.astype(BF)
        sent[i, :, :WIDTH] = grad_x.astype(BF)
        sent[i, :, WIDTH:] = grad_marks.astype(BF)

    block(0)
    here.send(sent.at[here.s_cross], near.at[0], scatter_sems.at[0], here.near)
    here.send(outs.at[here.s_cross], near_out.at[0], out_sems.at[0], here.near)
    block(1)
    here.wait(near.at[0], scatter_sems.at[0])
    near[0] = added(sent[here.s_far], near[0]).astype(BF)
    here.send(near.at[0], far, scatter_sems.at[2], here.far)
    here.wait(near_out.at[0], out_sems.at[0])
    far_sum[...] = added(outs[here.s_far], near_out[0]).astype(BF)
    saved = [local.copy(far_sum, out_far)]
    block(2)
    here.send(sent.at[here.s_near], near.at[1], scatter_sems.at[1], here.near)
    here.send(outs.at[here.s_near], near_out.at[1], out_sems.at[1], here.near)
    block(3)
    here.wait(near.at[1], scatter_sems.at[1])
    here.wait(near_out.at[1], out_sems.at[1])
    own_out[...] = added(hidden[...], outs[s], near_out[1])
    saved.append(local.copy(own_out, out_own))
    gain = gains[1:2, :]
    inverse, unit, normed_home = normed_of(hidden[...], gain)
    here.wait(far, scatter_sems.at[2])

    grad_gates = added(sent[s, :, WIDTH:], near[1, :, WIDTH:], far[:, WIDTH:])
    grad_gates = grad_gates + pltpu.roll(grad_gates, LANES - LOW, 1)
    gates = own_gates[...]
    grad_logits = gates * (grad_gates - jnp.sum(gates * grad_gates, axis=-1, keepdims=True))
    high, low = split_two(grad_logits)
    grad_normed = added(sent[s, :, :WIDTH], near[1, :, :WIDTH], far[:, :WIDTH])
    grad_normed = grad_normed + (mm_nt(high, misc[...]) + mm_nt(low, misc[...]))
    scaled = grad_normed * gain
    grad = cs[s].astype(F32) + inverse * (scaled - unit * jnp.mean(scaled * unit, axis=-1, keepdims=True))
    low_out[...] = grad.astype(BF)
    saved.append(local.copy(low_out, low_home))
    hidden_out[...] = grad
    saved.append(local.copy(hidden_out, grad_hidden))
    prod_high, prod_low = split_two(grad_normed * unit)
    one = (lane == 1).astype(BF)
    grad_misc[...] = mm_tn(normed_home, high) + mm_tn(normed_home, low) + mm_tn(prod_high, one) + mm_tn(prod_low, one)
    for copy in (*saved, *stored[0][2:], *stored[1][2:]):
        copy.wait()
    here.finish()


def row_of(y, x, z):
    return pl.multiple_of(((y * 4 + x) * 2 + z) * SHARD, SHARD)


def finish_kernel(
    low_home, normed_two_in, cots_in, pre_a_in, pre_b_in,
    normed_in, qkv_in, heads_in, logs_in, qkv_full_in, out_full_in, out_far,
    segments, gains, grad_misc, grad_hidden, tokens,
    far_out, grad_tokens, grad_a, grad_b, ffn_a_all, ffn_b_all, q_all, kv_all, out_all,
    grad_low, normed, part, pre_a, pre_b, staged, qkv, heads, logs, qkv_full, out_full,
    grad_q, grad_kvm, grad_out, grad_heads, grad_all, grad_kv, near, far, gain_sum, seg_col,
    piece_a, piece_b, piece_q, piece_kv, piece_out,
    send_sems, local_sems, scatter_sems, out_sems, gather_sems, low_sems, *buffers,
):
    here = Here(send_sems)
    local = Local(local_sems)
    s = here.s
    load_a = [local.copy(normed_two_in, normed), local.copy(pre_a_in, pre_a), local.copy(cots_in, part)]
    load_b = local.copy(pre_b_in, pre_b)
    load_rest = [
        local.copy(a, b)
        for a, b in ((out_full_in, out_full), (heads_in, heads), (qkv_in, qkv), (logs_in, logs), (qkv_full_in, qkv_full))
    ]
    here.greet()
    low_gather = seq_gather(here, low_home, grad_low, low_sems)
    next(low_gather)

    def summed(sum_of, piece, full, sems):
        yield from sum_of
        yield from seq_gather(here, piece, full, sems)

    def from_hbm(grad, y_first):
        def block(df, ds, h):
            dy, dx = (ds, df) if y_first else (df, ds)
            return grad.at[pl.ds(row_of(wrap(here.y + dy), wrap(here.x + dx), h), SHARD)]

        return block

    def own_unit(place, j, ds, h):
        at = wrap(place + j)
        return at * 2 + h if ds == 0 else (8 if ds == 1 else 12) + at

    def owned(held, place):
        def own(j, ds, h):
            return held[pl.ds(pl.multiple_of(own_unit(place, j, ds, h) * SHARD, SHARD), SHARD), :]

        return own

    sum_a = scatter_grad(here, from_hbm(grad_a, True), owned(pre_a, here.x), buffers[:10], piece_a, True, False)
    sum_b = scatter_grad(here, from_hbm(grad_b, False), owned(pre_b, here.y), buffers[10:20], piece_b, False, False)
    sums = [summed(sum_a, piece_a, ffn_a_all, gather_sems.at[0]), summed(sum_b, piece_b, ffn_b_all, gather_sems.at[1])]

    def chunk(y):
        return pl.ds(pl.multiple_of(y * CHUNK, CHUNK), CHUNK)

    moving = []
    for n, (j, k) in enumerate((j, k) for j in (2, 1, 3, 0) for k in range(2)):
        pre = (pre_a, pre_b)[k]
        if n == 0:
            for load in load_a:
                load.wait()
        if n == 1:
            load_b.wait()
        at = chunk(wrap(here.y + j))
        slot = staged.at[n % 2]
        slot[:, : 2 * HALF] = mm_tn(normed[:, at], pre[:, : 2 * HALF]).astype(BF)
        slot[:, 2 * HALF :] = mm_tn(part[:, :, at].reshape(L, CHUNK), pre[:, 2 * HALF :]).astype(BF)
        moving.append(local.copy(slot, (grad_a, grad_b)[k].at[at]))
        if n > 0:
            moving[n - 1].wait()
            next(sums[(n - 1) % 2])
    moving[-1].wait()
    next(sums[1])
    load_own = []
    for grad, held, y_first in ((grad_a, pre_a, True), (grad_b, pre_b, False)):
        for i in range(4):
            for ds, h in ((0, 0), (0, 1), (1, 0), (3, 1)):
                y, x = (wrap(here.y + ds), i) if y_first else (i, wrap(here.x + ds))
                unit = i * 2 + h if ds == 0 else (8 if ds == 1 else 12) + i
                source = grad.at[pl.ds(row_of(y, x, h), SHARD)]
                load_own.append(local.copy(source, held.at[pl.ds(unit * SHARD, SHARD)]))
    load_rest.append(local.copy(normed_in, normed))
    here.send(out_far, far_out, out_sems.at[0], here.far)
    set_segments(segments, seg_col)
    seg_row = segments[...].astype(F32)
    next(low_gather)
    for load in load_own:
        load.wait()

    def tick():
        for part_sum in sums[:2]:
            next(part_sum)

    tick()
    next(low_gather, None)
    for load in load_rest:
        load.wait()
    for b in range(SEQ):
        at = slice(b * ROWS, (b + 1) * ROWS)
        grad_heads[at, :] = mm(grad_low[b], out_full[:, :Q_COLS]).astype(BF)

    def blocks_of(grad, y_first):
        def block(df, ds, h):
            dy, dx = (ds, df) if y_first else (df, ds)
            return grad.at[wrap(here.y + dy), wrap(here.x + dx), h]

        return block

    def out_chunk(y, carry):
        grad_out[y] = mm_tn(grad_low[:, :, chunk(y)].reshape(L, CHUNK), heads[...]).astype(BF).reshape(4, 2, SHARD, Q_COLS)
        return carry

    lax.fori_loop(0, 4, out_chunk, 0)
    sum_out = scatter_grad(here, blocks_of(grad_out, False), None, buffers[20:30], piece_out, False, True)
    sums.append(summed(sum_out, piece_out, out_all, gather_sems.at[2]))
    next(sums[-1])

    tick()
    grad_kv[...] = jnp.zeros_like(grad_kv)
    for b in range(SEQ):
        at, kv_len = b * ROWS, (b + 1) * ROWS
        for h in range(GROUP):
            cols = slice(h * HEAD, (h + 1) * HEAD)
            query, grad = qkv[at : at + ROWS, cols], grad_heads[at : at + ROWS, cols]
            scores = mm_nt(query, qkv[:kv_len, Q_COLS:KV]) * SCALE
            probs = jnp.exp(masked(scores, at, kv_len, seg_col, seg_row) - logs[at : at + ROWS, h : h + 1])
            grad_probs = mm_nt(grad, qkv[:kv_len, KV:])
            centre = jnp.sum(probs * grad_probs, axis=-1, keepdims=True)
            grad_scores = (probs * (grad_probs - centre)).astype(BF)
            grad_all[at : at + ROWS, cols] = (mm(grad_scores, qkv[:kv_len, Q_COLS:KV]) * SCALE).astype(BF)
            grad_kv[:kv_len, :HEAD] += mm_tn(grad_scores, query) * SCALE
            grad_kv[:kv_len, HEAD:] += mm_tn(probs.astype(BF), grad)
        if b == 1 or b == 2:
            tick()
    grad_all[:, Q_COLS:] = grad_kv[...].astype(BF)

    def q_chunk(y, carry):
        grad_q[y] = mm_tn(normed[:, chunk(y)], grad_all[:, :Q_COLS]).astype(BF).reshape(4, 2, SHARD, Q_COLS)
        return carry

    lax.fori_loop(0, 4, q_chunk, 0)
    sum_q = scatter_grad(here, blocks_of(grad_q, True), None, buffers[30:40], piece_q, True, True)
    sums.append(summed(sum_q, piece_q, q_all, gather_sems.at[3]))
    next(sums[-1])
    tick()
    gain_sum[...] = jnp.zeros_like(gain_sum)

    def back(i):
        at = pl.ds(pl.multiple_of(i * ROWS, ROWS), ROWS)
        value = mm_nt(grad_all[at, :], qkv_full[...])
        part[i] = value.astype(BF)
        gain_sum[0:1, :] += jnp.sum(value * normed[at, :].astype(F32), axis=0, keepdims=True)

    row_sum = seq_scatter(here, part, near, far, scatter_sems, back, 4)
    next(row_sum)
    next(row_sum)
    tick()
    gain = gains[0:1, :]
    high, low = split_two(gain_sum[0:1, :] / gain)
    row = iota((16, WIDTH), 0)
    both = jnp.where(row == 0, high.astype(F32), 0.0) + jnp.where(row == 1, low.astype(F32), 0.0)
    gain_sum[...] = both
    pick = (iota((16, LANES), 1) == 0).astype(BF)

    def kv_chunk(y, carry):
        at = chunk(y)
        pair = mm_tn(normed[:, at], grad_all[:, Q_COLS:])
        single = grad_misc[at, :] + mm_tn(gain_sum[:, at].astype(BF), pick)
        grad_kvm[y] = jnp.concatenate([pair, single], axis=1).astype(BF).reshape(4, 2, SHARD, Q_COLS)
        return carry

    lax.fori_loop(0, 4, kv_chunk, 0)
    sum_kv = scatter_grad(here, blocks_of(grad_kvm, False), None, buffers[40:], piece_kv, False, True)
    sums.append(summed(sum_kv, piece_kv, kv_all, gather_sems.at[4]))

    def rows():
        yield from row_sum
        here.wait(far_out, out_sems.at[0])
        grad_normed = added(part[s], near[1], far[...])
        inverse, unit, _ = normed_of(tokens[...].astype(F32), gain)
        scaled = grad_normed * gain
        grad_tokens[...] = (grad_hidden[...] + inverse * (scaled - unit * jnp.mean(scaled * unit, axis=-1, keepdims=True))).astype(BF)

    next(sums[-1])
    together(*sums[2:], *sums[:2], rows())
    here.finish()


def as_row(col):
    n = col.shape[0]
    return jnp.sum(jnp.where(iota((n, n), 0) == iota((n, n), 1), jnp.broadcast_to(col, (n, n)), 0.0), axis=0, keepdims=True)


def outputs_kernel(
    ffn_a, ffn_b, q, kv, out, out_own, far_out, output, wq, wk, wv, wo, gain_one, gain_two, router, shared_gate, shared_up, shared_down, expert_gate, expert_up, expert_down
):
    output[...] = added(out_own[...], far_out[...]).astype(BF)
    total = jnp.zeros((SHARD, LANES), F32)
    for s in range(SEQ):
        wq[:, s * Q_COLS : (s + 1) * Q_COLS] = q[s].astype(F32)
        wo[:, s * Q_COLS : (s + 1) * Q_COLS] = out[s].astype(F32)
        wk[:, s * HEAD : (s + 1) * HEAD] = kv[s, :, :HEAD].astype(F32)
        wv[:, s * HEAD : (s + 1) * HEAD] = kv[s, :, HEAD : 2 * HEAD].astype(F32)
        total = total + kv[s, :, 2 * HEAD :].astype(F32)
        for k, ffn in enumerate((ffn_a, ffn_b)):
            n = 2 * s + k
            for i, (shared, expert) in enumerate(((shared_gate, expert_gate), (shared_up, expert_up), (shared_down, expert_down))):
                expert[:, n, :] = ffn[s, :, i * HALF : i * HALF + 512].astype(F32)
                shared[:, n * LANES : (n + 1) * LANES] = ffn[s, :, i * HALF + 512 : (i + 1) * HALF].astype(F32)
    gain_one[...] = as_row(total[:, 0:1])
    gain_two[...] = as_row(total[:, 1:2])
    for e in range(E):
        router[e : e + 1, :] = as_row(total[:, 2 + e : 3 + e])


def remote_call(kernel, name, number, outs, ins, scratch):
    return pl.pallas_call(
        kernel,
        out_shape=[jax.ShapeDtypeStruct(dims, dtype) for dims, dtype, _ in outs],
        in_specs=[VMEM_ALL if fast else ANY for _, fast in ins],
        out_specs=[VMEM_ALL if fast else ANY for _, _, fast in outs],
        scratch_shapes=list(scratch),
        compiler_params=pltpu.CompilerParams(collective_id=number, has_side_effects=True, vmem_limit_bytes=LIMIT),
        name=name,
    )(*[array for array, _ in ins])


def buf(*dims):
    return pltpu.VMEM(dims, BF)


def buf32(*dims):
    return pltpu.VMEM(dims, F32)


def body(
    tokens,
    segments,
    routes,
    shared_mask,
    norm_gain,
    w_query,
    key_weight,
    value_weight,
    w_out,
    ffn_gain,
    w_router,
    shared_gate,
    shared_up,
    shared_down,
    expert_gate,
    expert_up,
    expert_down,
    cotangent,
):
    seg_row = segments[None, :]
    grid = DMA((4, 4, 2))
    rows4 = (SEQ, ROWS, WIDTH)
    fast = [tokens, routes.T, shared_mask[None, :], norm_gain[None, :], ffn_gain[None, :], w_router.T, w_query, key_weight,
            value_weight, w_out, shared_gate, shared_up, shared_down, expert_gate, expert_up, expert_down, seg_row]
    (
        normed_one, qkv, heads, logs, gains, marks, misc, qkv_full, out_full, full_a, full_b, normed_two, all_cot, hidden,
    ) = remote_call(
        attend_kernel,
        "attend",
        1,
        [
            ((L, WIDTH), BF, False),
            ((L, HALF), BF, True),
            ((L, Q_COLS), BF, True),
            ((L, 8), F32, True),
            ((8, WIDTH), F32, True),
            ((L, LANES), BF, True),
            ((WIDTH, LANES), BF, True),
            (blocks(HALF), BF, True),
            (blocks(OUT_COLS), BF, True),
            (blocks(FFN), BF, False),
            (blocks(FFN), BF, False),
            (rows4, BF, False),
            (rows4, BF, False),
            ((ROWS, WIDTH), F32, True),
        ],
        [(a, True) for a in fast] + [(cotangent, False)],
        [
            buf(ROWS, WIDTH + LANES),
            buf(SEQ, ROWS, WIDTH + LANES),
            buf(SHARD, HALF),
            buf(SHARD, OUT_COLS),
            buf(SHARD, FFN),
            buf(SHARD, FFN),
            buf(L, WIDTH),
            buf(*rows4),
            buf(2, ROWS, WIDTH),
            buf(ROWS, WIDTH),
            buf(ROWS, WIDTH),
            buf32(L, 1),
            DMA((160,)),
            DMA((4,)),
            grid,
            grid,
            grid,
            grid,
            DMA((5,)),
            DMA((3,)),
            DMA((4,)),
            DMA((4,)),
        ],
    )

    pre_a, pre_b, low_home, grad_hidden, grad_misc, out_far, out_own = remote_call(
        experts_kernel,
        "experts",
        2,
        [
            ((L, FFN), BF, False),
            ((L, FFN), BF, False),
            ((ROWS, WIDTH), BF, False),
            ((ROWS, WIDTH), F32, False),
            ((WIDTH, LANES), F32, True),
            ((ROWS, WIDTH), BF, False),
            ((ROWS, WIDTH), F32, False),
        ],
        [
            (normed_two, False),
            (all_cot, False),
            (full_a.reshape(WIDTH, FFN), False),
            (full_b.reshape(WIDTH, FFN), False),
            (marks, True),
            (misc, True),
            (gains, True),
            (hidden, True),
        ],
        [
            buf(*rows4),
            buf(*rows4),
            buf(WIDTH, FFN),
            buf(WIDTH, FFN),
            buf(SEQ, ROWS, WIDTH + LANES),
            buf(*rows4),
            buf(2, 2, ROWS, FFN),
            buf(2, ROWS, WIDTH + LANES),
            buf(ROWS, WIDTH + LANES),
            buf(2, ROWS, WIDTH),
            buf32(ROWS, LANES),
            buf32(ROWS, WIDTH),
            buf32(ROWS, WIDTH),
            buf(ROWS, WIDTH),
            buf(ROWS, WIDTH),
            DMA((8,)),
            DMA((24,)),
            DMA((3,)),
            DMA((2,)),
        ],
    )

    far_out, grad_tokens, _, _, ffn_a_all, ffn_b_all, q_all, kv_all, out_all = remote_call(
        finish_kernel,
        "finish",
        3,
        [
            ((ROWS, WIDTH), BF, False),
            ((ROWS, WIDTH), BF, True),
            ((WIDTH, FFN), BF, False),
            ((WIDTH, FFN), BF, False),
            ((SEQ, SHARD, FFN), BF, False),
            ((SEQ, SHARD, FFN), BF, False),
            ((SEQ, SHARD, Q_COLS), BF, False),
            ((SEQ, SHARD, Q_COLS), BF, False),
            ((SEQ, SHARD, Q_COLS), BF, False),
        ],
        [
            (low_home, False),
            (normed_two.reshape(L, WIDTH), False),
            (all_cot, False),
            (pre_a, False),
            (pre_b, False),
            (normed_one, False),
            (qkv, False),
            (heads, False),
            (logs, False),
            (qkv_full.reshape(WIDTH, HALF), False),
            (out_full.reshape(WIDTH, OUT_COLS), False),
            (out_far, False),
            (seg_row, True),
            (gains, True),
            (grad_misc, True),
            (grad_hidden, True),
            (tokens, True),
        ],
        [
            buf(*rows4),
            buf(L, WIDTH),
            buf(*rows4),
            buf(L, FFN),
            buf(L, FFN),
            buf(2, CHUNK, FFN),
            buf(L, HALF),
            buf(L, Q_COLS),
            buf32(L, 8),
            buf(WIDTH, HALF),
            buf(WIDTH, OUT_COLS),
            buf(*blocks(Q_COLS)),
            buf(*blocks(Q_COLS)),
            buf(*blocks(Q_COLS)),
            buf(L, Q_COLS),
            buf(L, HALF),
            buf32(L, 2 * HEAD),
            buf(2, ROWS, WIDTH),
            buf(ROWS, WIDTH),
            buf32(16, WIDTH),
            buf32(L, 1),
            buf(SHARD, FFN),
            buf(SHARD, FFN),
            buf(SHARD, Q_COLS),
            buf(SHARD, Q_COLS),
            buf(SHARD, Q_COLS),
            DMA((192,)),
            DMA((56,)),
            DMA((3,)),
            DMA((1,)),
            DMA((5, 4)),
            DMA((4,)),
            *scatter_buffers(FFN),
            *scatter_buffers(FFN),
            *scatter_buffers(Q_COLS),
            *scatter_buffers(Q_COLS),
            *scatter_buffers(Q_COLS),
        ],
    )

    dims = [(ROWS, WIDTH), (SHARD, 4 * Q_COLS), (SHARD, 4 * HEAD), (SHARD, 4 * HEAD), (SHARD, 4 * Q_COLS), (1, SHARD), (1, SHARD), (E, SHARD)]
    dims += [(SHARD, 1024)] * 3 + [(SHARD, E, 512)] * 3
    output, wq, wk, wv, wo, gain_one, gain_two, router, *ffn = pl.pallas_call(
        outputs_kernel,
        out_shape=[jax.ShapeDtypeStruct(d, BF if d[0] == ROWS else F32) for d in dims],
        in_specs=[VMEM_ALL] * 7,
        out_specs=[VMEM_ALL] * len(dims),
        compiler_params=pltpu.CompilerParams(vmem_limit_bytes=LIMIT),
        name="outputs",
    )(ffn_a_all, ffn_b_all, q_all, kv_all, out_all, out_own, far_out)
    return (output, grad_tokens, gain_one[0], wq, wk, wv, wo, gain_two[0], router.T, *ffn)


def solution(mesh):
    both = P(("fsdp", "seq"), None)
    one, two, three = P("fsdp"), P("fsdp", None), P("fsdp", None, None)
    return jax.shard_map(
        body,
        mesh=mesh,
        in_specs=(both, one, both, P(("fsdp", "seq")), one, two, two, two, two, one, two, two, two, two, three, three, three, both),
        out_specs=(both, both, one, two, two, two, two, one, two, two, two, two, three, three, three),
        check_vma=False,
    )
```

```python
import jax
import jax.numpy as jnp
from jax import lax
from jax.experimental import pallas as pl
from jax.experimental.pallas import tpu as pltpu
from jax.sharding import PartitionSpec as P

HEAD = 128
GROUP = 3
E = 8
SEQ = 4
EPS = 1e-05
BF = jnp.bfloat16
F32 = jnp.float32
WIDTH = 1536
L = 1024
ROWS = 256
SHARD = 48
Q_COLS = GROUP * HEAD
KV = Q_COLS + HEAD
HALF = 640
FFN = 3 * HALF
LANES = 128
OUT_COLS = Q_COLS + LANES
LOW = 32
CHUNK = 384
SCALE = HEAD ** (-0.5)
BIG = -1e30
MESH = pl.DeviceIdType.MESH
VMEM_ALL = pl.BlockSpec(memory_space=pltpu.VMEM)
ANY = pl.BlockSpec(memory_space=pl.ANY)
DMA = pltpu.SemaphoreType.DMA
LIMIT = 63 * 1024 * 1024


def f32dot(left, right, dims):
    return lax.dot_general(left, right, (dims, ((), ())), preferred_element_type=F32)


def mm(left, right):
    return f32dot(left, right, ((1,), (0,)))


def mm_nt(left, right):
    return f32dot(left, right, ((1,), (1,)))


def mm_tn(left, right):
    return f32dot(left, right, ((0,), (0,)))


def iota(dims, axis):
    return lax.broadcasted_iota(jnp.int32, dims, axis)


def column(row):
    n = row.shape[1]
    same = iota((n, n), 0) == iota((n, n), 1)
    return jnp.sum(jnp.where(same, jnp.broadcast_to(row, (n, n)), 0.0), axis=-1, keepdims=True)


def added(*values):
    total = values[0].astype(F32)
    for value in values[1:]:
        total = total + value.astype(F32)
    return total


def split_two(value):
    high = value.astype(BF)
    return high, (value - high.astype(F32)).astype(BF)


def normed_of(x, gain):
    inverse = lax.rsqrt(jnp.mean(x * x, axis=-1, keepdims=True) + EPS)
    unit = x * inverse
    return inverse, unit, (unit * gain).astype(BF)


def wrap(value):
    return lax.rem(value + 4, 4)


def blocks(cols):
    return (4, 4, 2, SHARD, cols)


class Here:
    def __init__(self, send_sems):
        f, s = lax.axis_index("fsdp"), lax.axis_index("seq")
        self.y, self.x, self.z = lax.div(f, 8), lax.rem(lax.div(f, 2), 4), lax.rem(f, 2)
        self.s, self.zh, self.core = s, lax.div(s, 2), lax.rem(s, 2)
        y, x, z = self.y, self.x, self.z
        self.axis_x = ({"fsdp": self.number(y, wrap(x + 1), z)}, {"fsdp": self.number(y, wrap(x - 1), z)})
        self.axis_y = ({"fsdp": self.number(wrap(y + 1), x, z)}, {"fsdp": self.number(wrap(y - 1), x, z)})
        self.pair = {"fsdp": self.number(y, x, 1 - z)}
        self.s_far = (1 - self.zh) * 2 + self.core
        self.s_near = self.zh * 2 + 1 - self.core
        self.s_cross = (1 - self.zh) * 2 + 1 - self.core
        self.far = {"seq": self.s_far}
        self.near = {"seq": self.s_near}
        self.sems, self.sent, self.left = send_sems, [], 0

    @staticmethod
    def number(y, x, z):
        return (y * 4 + x) * 2 + z

    def greet(self):
        barrier = pltpu.get_barrier_semaphore()
        partners = [*self.axis_x, *self.axis_y, self.pair, self.far, self.near]
        for partner in partners:
            pl.semaphore_signal(barrier, inc=1, device_id=partner, device_id_type=MESH)
        pl.semaphore_wait(barrier, len(partners))

    def send(self, source, target, recv_sem, to):
        copy = pltpu.make_async_remote_copy(
            src_ref=source,
            dst_ref=target,
            send_sem=self.sems.at[len(self.sent)],
            recv_sem=recv_sem,
            device_id=to,
            device_id_type=MESH,
        )
        copy.start()
        self.sent.append(copy)

    def wait(self, target, recv_sem):
        pltpu.make_async_remote_copy(
            src_ref=target,
            dst_ref=target,
            send_sem=self.sems.at[0],
            recv_sem=recv_sem,
            device_id=self.near,
            device_id_type=MESH,
        ).wait_recv()

    def finish(self):
        for copy in self.sent[self.left :]:
            copy.wait_send()
        self.left = len(self.sent)


class Local:
    def __init__(self, sems):
        self.sems, self.count = sems, 0

    def copy(self, source, target):
        copy = pltpu.make_async_copy(source, target, self.sems.at[self.count])
        copy.start()
        self.count += 1
        return copy


def together(*parts):
    left = list(parts)
    while left:
        for part in list(left):
            if next(part, "end") == "end":
                left.remove(part)


def later(turns, parts):
    for _ in range(turns):
        yield
    for part in parts:
        next(part)


def gather_weight(here, full, block, recv, own_sem, x_first):
    first, second = (here.axis_x, here.axis_y) if x_first else (here.axis_y, here.axis_x)

    def spot(df, ds, r):
        dy, dx = (ds, df) if x_first else (df, ds)
        return wrap(here.y + dy), wrap(here.x + dx), here.z if r == 0 else 1 - here.z

    def push(df, ds, r, to, source=None):
        at = spot(df, ds, r)
        here.send(full.at[at] if source is None else source, full.at[at], recv.at[at], to)

    def take(df, ds, r):
        at = spot(df, ds, r)
        here.wait(full.at[at], recv.at[at])

    own = pltpu.make_async_copy(block, full.at[spot(0, 0, 0)], own_sem)
    own.start()
    push(0, 0, 0, here.pair, block)
    yield
    for to in (*second, *first):
        push(0, 0, 0, to, block)
    yield
    take(0, 0, 1)
    for to in (*first, *second):
        push(0, 0, 1, to)
    for df, r in ((-1, 0), (1, 0), (1, 1), (-1, 1), (2, 0), (2, 1)):
        yield
        take(df, 0, r)
        if (df, r) == (-1, 0):
            push(df, 0, r, first[0])
        if (df, r) == (1, 1):
            push(df, 0, r, first[1])
        for to in second:
            push(df, 0, r, to)
        if (df, r) == (1, 0):
            take(0, -1, 0)
            push(0, -1, 0, second[0])
        if (df, r) == (-1, 1):
            take(0, 1, 1)
            push(0, 1, 1, second[1])
    for df in (-1, 1, 2):
        yield
        take(df, -1, 0)
        push(df, -1, 0, second[0])
        yield
        take(df, 1, 1)
        push(df, 1, 1, second[1])
    yield
    for df in (0, -1, 1, 2):
        take(df, -1, 1)
        take(df, 1, 0)
        take(df, 2, 0)
        take(df, 2, 1)
    own.wait()


def scatter_buffers(cols):
    units = [(4,), (4,), (4, 2), (4, 2), (1,), (1,), (2,), (2,), (1,)]
    return [pltpu.VMEM((*u, SHARD, cols), BF) for u in units] + [DMA((31,))]


def scatter_grad(here, block, own, buffers, piece, y_first, small):
    ra, rb, rc, rd, xa, xb, xc, xd, zr, sems = buffers
    second, first = (here.axis_y, here.axis_x) if y_first else (here.axis_x, here.axis_y)
    own = own or (lambda df, ds, h: block(df, ds, h)[...])

    def far_send(j):
        here.send(block(j, 2, 0), ra.at[j], sems.at[j], second[0])
        here.send(block(j, 2, 1), rb.at[j], sems.at[4 + j], second[1])

    def near_plus(j):
        here.send(block(j, 1, 1), rc.at[j, 1], sems.at[8 + 2 * j + 1], second[0])

    def near_minus(j):
        here.send(block(j, 3, 0), rd.at[j, 0], sems.at[16 + 2 * j], second[1])

    def pass_on(j):
        here.wait(ra.at[j], sems.at[j])
        ra[j] = added(own(j, 1, 0), ra[j]).astype(BF)
        here.send(ra.at[j], rc.at[j, 0], sems.at[8 + 2 * j], second[0])
        here.wait(rb.at[j], sems.at[4 + j])
        rb[j] = added(own(j, 3, 1), rb[j]).astype(BF)
        here.send(rb.at[j], rd.at[j, 1], sems.at[16 + 2 * j + 1], second[1])

    def total(j):
        for h in range(2):
            here.wait(rc.at[j, h], sems.at[8 + 2 * j + h])
            here.wait(rd.at[j, h], sems.at[16 + 2 * j + h])
            rc[j, h] = added(own(j, 0, h), rc[j, h], rd[j, h]).astype(BF)

    def turn_two():
        here.send(rc.at[2, 0], xa.at[0], sems.at[24], first[0])
        here.send(rc.at[2, 1], xb.at[0], sems.at[25], first[1])

    def turn_near():
        here.send(rc.at[1, 1], xc.at[1], sems.at[27], first[0])
        here.send(rc.at[3, 0], xd.at[0], sems.at[28], first[1])

    def turn_on():
        here.wait(xa.at[0], sems.at[24])
        xa[0] = added(rc[1, 0], xa[0]).astype(BF)
        here.send(xa.at[0], xc.at[0], sems.at[26], first[0])
        here.wait(xb.at[0], sems.at[25])
        xb[0] = added(rc[3, 1], xb[0]).astype(BF)
        here.send(xb.at[0], xd.at[1], sems.at[29], first[1])

    every = (2, 1, 3, 0)
    if small:
        for j in every:
            far_send(j)
            near_plus(j)
            near_minus(j)
        yield
        for j in every:
            pass_on(j)
        yield
        total(2)
        turn_two()
        total(1)
        total(3)
        turn_near()
        yield
        turn_on()
        total(0)
        yield
    else:
        if y_first:
            for send in (far_send, near_plus, near_minus):
                for j in every:
                    send(j)
                yield
        else:
            for j in every:
                far_send(j)
                near_plus(j)
                near_minus(j)
                yield
        if y_first:
            yield
        pass_on(2)
        pass_on(1)
        yield
        pass_on(3)
        pass_on(0)
        yield
        total(2)
        turn_two()
        yield
        total(1)
        total(3)
        turn_near()
        yield
        total(0)
        yield
        turn_on()
        yield
    for h in range(2):
        here.wait(xc.at[h], sems.at[26 + h])
        here.wait(xd.at[h], sems.at[28 + h])
        xc[h] = added(rc[0, h], xc[h], xd[h]).astype(BF)
    here.send(xc.at[1 - here.z], zr.at[0], sems.at[30], here.pair)
    yield
    here.wait(zr.at[0], sems.at[30])
    piece[...] = added(xc[here.z], zr[0]).astype(piece.dtype)


def seq_gather(here, source, full, sems, pause=1):
    own = pltpu.make_async_copy(source, full.at[here.s], sems.at[3])
    own.start()
    here.send(source, full.at[here.s], sems.at[0], here.far)
    here.send(source, full.at[here.s], sems.at[1], here.near)
    for _ in range(pause):
        yield
    here.wait(full.at[here.s_far], sems.at[0])
    here.send(full.at[here.s_far], full.at[here.s_far], sems.at[2], here.near)
    yield
    here.wait(full.at[here.s_near], sems.at[1])
    here.wait(full.at[here.s_cross], sems.at[2])
    own.wait()


def seq_scatter(here, parts, near, far, sems, make, pause=1):
    make(here.s_cross)
    here.send(parts.at[here.s_cross], near.at[0], sems.at[0], here.near)
    make(here.s_far)
    yield
    here.wait(near.at[0], sems.at[0])
    near[0] = added(parts[here.s_far], near[0]).astype(BF)
    here.send(near.at[0], far, sems.at[2], here.far)
    make(here.s_near)
    here.send(parts.at[here.s_near], near.at[1], sems.at[1], here.near)
    make(here.s)
    yield
    here.wait(near.at[1], sems.at[1])
    for _ in range(pause):
        yield
    here.wait(far, sems.at[2])


def masked(scores, at, kv_len, seg_col, seg_row):
    q_pos = at + iota((ROWS, kv_len), 0)
    k_pos = iota((ROWS, kv_len), 1)
    keep = (q_pos >= k_pos) & (seg_col[at : at + ROWS, :] == seg_row[:, :kv_len])
    return jnp.where(keep, scores, BIG)


def set_segments(seg_row, seg_col):
    for b in range(L // ROWS):
        at = slice(b * ROWS, (b + 1) * ROWS)
        seg_col[at, :] = column(seg_row[:, at].astype(F32))


def forward_kernel(
    tokens, routes, shared_mask, norm_gain, ffn_gain, w_router, w_query, key_weight, value_weight, w_out,
    shared_gate, shared_up, shared_down, expert_gate, expert_up, expert_down, segments, cot,
    normed_one, qkv_out, heads_out, logs_out, gains, qkv_full_out, out_full_out, normed_two, all_cot,
    pre_a, pre_b, low_home, grad_hidden, grad_misc, out_far, out_own,
    marked, all_marked, qkv_block, out_block, block_a, block_b, qkv_full, out_full, normed, qkv, heads, logs, seg_col,
    marks, misc, part, near, far, normed_home, hidden, xs, cs, full_a, full_b,
    staged, near_g, far_g, near_out, own_gates, own_out,
    send_sems, token_sems, qkv_sems, out_sems, a_sems, b_sems, own_sems, scatter_sems, gather_sems, cot_sems,
    grad_sems, sum_sems, local_sems,
):
    here = Here(send_sems)
    local = Local(local_sems)
    here.greet()
    s = here.s

    def wide(ref, at, width):
        return ref[:, pl.ds(pl.multiple_of(at * width, LANES), width)]

    marked[:, :WIDTH] = tokens[...]
    line = iota((LANES, ROWS), 0)
    used = line == routes[0:1, :] + 2
    for k in range(1, 6):
        used = used | (line == routes[k : k + 1, :] + 2)
    turned = (jnp.where(used, 1.0, 0.0) + jnp.where(line == 1, shared_mask[...].astype(F32), 0.0)).astype(BF)
    eye = (iota((LANES, LANES), 0) == iota((LANES, LANES), 1)).astype(BF)
    marked[:, WIDTH:] = mm_tn(turned, eye).astype(BF)
    token_gather = seq_gather(here, marked, all_marked, token_sems, 13)
    qkv_block[:, :Q_COLS] = wide(w_query, s, Q_COLS)
    qkv_block[:, Q_COLS:KV] = wide(key_weight, s, HEAD)
    qkv_block[:, KV:] = wide(value_weight, s, HEAD)
    qkv_gather = gather_weight(here, qkv_full, qkv_block, qkv_sems, own_sems.at[0], True)
    next(qkv_gather)
    out_block[:, :Q_COLS] = wide(w_out, s, Q_COLS)
    place = (iota((E, LANES), 1) == iota((E, LANES), 0) + 2).astype(F32)
    single = f32dot(w_router[...].astype(F32), place, ((0,), (0,)))
    lane = iota((SHARD, LANES), 1)
    single = single + jnp.where(lane == 0, column(norm_gain[...].astype(F32)), 0.0)
    out_block[:, Q_COLS:] = (single + jnp.where(lane == 1, column(ffn_gain[...].astype(F32)), 0.0)).astype(BF)
    out_gather = gather_weight(here, out_full, out_block, out_sems, own_sems.at[1], False)
    next(out_gather)
    next(token_gather)
    next(qkv_gather)
    next(out_gather)
    for k, block in enumerate((block_a, block_b)):
        pick = (iota((SHARD, SHARD * E), 1) == iota((SHARD, SHARD * E), 0) * E + 2 * s + k).astype(BF)
        for i, (shared, expert) in enumerate(((shared_gate, expert_gate), (shared_up, expert_up), (shared_down, expert_down))):
            block[:, i * HALF : i * HALF + 512] = mm(pick, expert[...].reshape(SHARD * E, 512)).astype(BF)
            block[:, i * HALF + 512 : (i + 1) * HALF] = wide(shared, 2 * s + k, HALF - 512)
    set_segments(segments, seg_col)
    weights = [
        gather_weight(here, full_a, block_a, a_sems, own_sems.at[2], True),
        gather_weight(here, full_b, block_b, b_sems, own_sems.at[3], False),
    ]
    for weight in weights:
        next(weight)
    together(token_gather, qkv_gather, out_gather, later(9, weights))

    def tick():
        for weight in weights:
            next(weight, None)

    cot_gather = seq_gather(here, cot, cs, cot_sems)
    next(cot_gather)
    misc[...] = out_full[:, :, :, :, Q_COLS:].reshape(WIDTH, LANES)
    gains[...] = mm_nt(eye, misc[...])[:8]
    gain = gains[0:1, :]
    seg_row = segments[...].astype(F32)
    for b in range(SEQ):
        at = slice(b * ROWS, (b + 1) * ROWS)
        normed[at, :] = normed_of(all_marked[b, :, :WIDTH].astype(F32), gain)[2]
        qkv[at, :] = mm(normed[at, :], qkv_full[...].reshape(WIDTH, HALF)).astype(BF)
        marks[at, :] = all_marked[b, :, WIDTH:]
        if b % 2 == 1:
            tick()
    saved = [local.copy(normed, normed_one), local.copy(qkv, qkv_out), local.copy(qkv_full, qkv_full_out)]
    saved.append(local.copy(out_full, out_full_out))
    for b in range(SEQ):
        at, kv_len = b * ROWS, (b + 1) * ROWS
        for h in range(GROUP):
            cols = slice(h * HEAD, (h + 1) * HEAD)
            scores = mm_nt(qkv[at : at + ROWS, cols], qkv[:kv_len, Q_COLS:KV]) * SCALE
            scores = masked(scores, at, kv_len, seg_col, seg_row)
            top = jnp.max(scores, axis=-1, keepdims=True)
            weight = jnp.exp(scores - top)
            total = jnp.sum(weight, axis=-1, keepdims=True)
            probs = (weight * (1.0 / total)).astype(BF)
            heads[at : at + ROWS, cols] = mm(probs, qkv[:kv_len, KV:]).astype(BF)
            logs[at : at + ROWS, h : h + 1] = top + jnp.log(total)
        tick()

    saved += [local.copy(heads, heads_out), local.copy(logs, logs_out)]

    def project(i):
        rows = heads[pl.ds(pl.multiple_of(i * ROWS, ROWS), ROWS), :]
        part[i] = mm_nt(rows, out_full[:, :, :, :, :Q_COLS].reshape(WIDTH, Q_COLS)).astype(BF)

    def rows():
        yield from seq_scatter(here, part, near, far, scatter_sems, project, 2)
        next(cot_gather)
        hidden[...] = added(tokens[...], part[s], near[1], far[...])
        normed_home[...] = normed_of(hidden[...], gains[1:2, :])[2]
        yield from seq_gather(here, normed_home, xs, gather_sems, 3)
        next(cot_gather, None)

    together(rows(), *weights)
    for copy in saved:
        copy.wait()
    saved = [local.copy(xs, normed_two), local.copy(cs, all_cot)]
    here.finish()
    order = (here.s_cross, here.s_far, here.s_near, s)
    sent, outs, far_sum, low_out = all_marked, part, far, normed_home
    lane = iota((ROWS, LANES), 1)
    stored = [[], []]

    def block(n):
        i = order[n]
        at = pl.ds(pl.multiple_of(i * ROWS, ROWS), ROWS)
        x, c = xs[i], cs[i]
        mark = marks[at, :].astype(F32)
        member = (mark > 0) & (lane >= 2) & (lane < 2 + E)
        logits = jnp.where(member, mm(x, misc[...]), BIG)
        soft = jnp.where(member, jnp.exp(logits - jnp.max(logits, axis=-1, keepdims=True)), 0.0)
        gates = soft / jnp.sum(soft, axis=-1, keepdims=True)
        if n == 3:
            own_gates[...] = gates
        keep = mark[:, 1:2]
        total = jnp.zeros((ROWS, WIDTH), F32)
        grad_x = jnp.zeros((ROWS, WIDTH), F32)
        grad_marks = jnp.zeros((ROWS, LANES), F32)
        for k, weight in enumerate((full_a, full_b)):
            if n >= 2:
                stored[k][n - 2].wait()
            slot = staged.at[n % 2, k]
            mine = lane == 2 + 2 * s + k
            gate_e = jnp.sum(jnp.where(mine, gates, 0.0), axis=-1, keepdims=True)
            coef = jnp.concatenate([jnp.broadcast_to(gate_e, (ROWS, 512)), jnp.broadcast_to(keep, (ROWS, HALF - 512))], axis=1)
            pre = mm(x, weight[:, :, :, :, : 2 * HALF].reshape(WIDTH, 2 * HALF))
            gate, upper = pre[:, :HALF], pre[:, HALF:]
            sigma = 1.0 / (1.0 + jnp.exp(-gate))
            silu = gate * sigma
            units = silu * upper
            weighted = (coef * units).astype(BF)
            slot[:, 2 * HALF :] = weighted
            total += mm_nt(weighted, weight[:, :, :, :, 2 * HALF :].reshape(WIDTH, HALF))
            grad_units = mm(c, weight[:, :, :, :, 2 * HALF :].reshape(WIDTH, HALF))
            grad_gate = jnp.sum((units * grad_units)[:, :512], axis=-1, keepdims=True)
            high = grad_gate.astype(BF).astype(F32)
            grad_marks += jnp.where(mine, high, 0.0) + jnp.where(lane == LOW + 2 + 2 * s + k, grad_gate - high, 0.0)
            grad_units = coef * grad_units
            slot[:, :HALF] = (grad_units * upper * (sigma * (1.0 + gate * (1.0 - sigma)))).astype(BF)
            slot[:, HALF : 2 * HALF] = (grad_units * silu).astype(BF)
            grad_x += mm_nt(slot[:, : 2 * HALF], weight[:, :, :, :, : 2 * HALF].reshape(WIDTH, 2 * HALF))
            stored[k].append(local.copy(slot, (pre_a, pre_b)[k].at[at]))
        outs[i] = total.astype(BF)
        sent[i, :, :WIDTH] = grad_x.astype(BF)
        sent[i, :, WIDTH:] = grad_marks.astype(BF)

    block(0)
    here.send(sent.at[here.s_cross], near_g.at[0], grad_sems.at[0], here.near)
    here.send(outs.at[here.s_cross], near_out.at[0], sum_sems.at[0], here.near)
    block(1)
    here.wait(near_g.at[0], grad_sems.at[0])
    near_g[0] = added(sent[here.s_far], near_g[0]).astype(BF)
    here.send(near_g.at[0], far_g, grad_sems.at[2], here.far)
    here.wait(near_out.at[0], sum_sems.at[0])
    far_sum[...] = added(outs[here.s_far], near_out[0]).astype(BF)
    saved.append(local.copy(far_sum, out_far))
    block(2)
    here.send(sent.at[here.s_near], near_g.at[1], grad_sems.at[1], here.near)
    here.send(outs.at[here.s_near], near_out.at[1], sum_sems.at[1], here.near)
    block(3)
    here.wait(near_g.at[1], grad_sems.at[1])
    here.wait(near_out.at[1], sum_sems.at[1])
    own_out[...] = added(hidden[...], outs[s], near_out[1])
    saved.append(local.copy(own_out, out_own))
    gain = gains[1:2, :]
    inverse, unit, normed_home = normed_of(hidden[...], gain)
    here.wait(far_g, grad_sems.at[2])

    grad_gates = added(sent[s, :, WIDTH:], near_g[1, :, WIDTH:], far_g[:, WIDTH:])
    grad_gates = grad_gates + pltpu.roll(grad_gates, LANES - LOW, 1)
    gates = own_gates[...]
    grad_logits = gates * (grad_gates - jnp.sum(gates * grad_gates, axis=-1, keepdims=True))
    high, low = split_two(grad_logits)
    grad_normed = added(sent[s, :, :WIDTH], near_g[1, :, :WIDTH], far_g[:, :WIDTH])
    grad_normed = grad_normed + (mm_nt(high, misc[...]) + mm_nt(low, misc[...]))
    scaled = grad_normed * gain
    grad = cs[s].astype(F32) + inverse * (scaled - unit * jnp.mean(scaled * unit, axis=-1, keepdims=True))
    low_out[...] = grad.astype(BF)
    saved.append(local.copy(low_out, low_home))
    hidden[...] = grad
    saved.append(local.copy(hidden, grad_hidden))
    prod_high, prod_low = split_two(grad_normed * unit)
    one = (lane == 1).astype(BF)
    grad_misc[...] = mm_tn(normed_home, high) + mm_tn(normed_home, low) + mm_tn(prod_high, one) + mm_tn(prod_low, one)
    for copy in (*saved, *stored[0][2:], *stored[1][2:]):
        copy.wait()
    here.finish()


def row_of(y, x, z):
    return pl.multiple_of(((y * 4 + x) * 2 + z) * SHARD, SHARD)


def finish_kernel(
    low_home, normed_two_in, cots_in, pre_a_in, pre_b_in,
    normed_in, qkv_in, heads_in, logs_in, qkv_full_in, out_full_in, out_far,
    segments, gains, grad_misc, grad_hidden, tokens,
    far_out, grad_tokens, grad_a, grad_b, ffn_a_all, ffn_b_all, q_all, kv_all, out_all,
    grad_low, normed, part, pre_a, pre_b, staged, qkv, heads, logs, qkv_full, out_full,
    grad_q, grad_kvm, grad_out, grad_heads, grad_all, grad_kv, near, far, gain_sum, seg_col,
    piece_a, piece_b, piece_q, piece_kv, piece_out,
    send_sems, local_sems, scatter_sems, out_sems, gather_sems, low_sems, *buffers,
):
    here = Here(send_sems)
    local = Local(local_sems)
    s = here.s
    load_a = [local.copy(normed_two_in, normed), local.copy(pre_a_in, pre_a), local.copy(cots_in, part)]
    load_b = local.copy(pre_b_in, pre_b)
    load_rest = [
        local.copy(a, b)
        for a, b in ((out_full_in, out_full), (heads_in, heads), (qkv_in, qkv), (logs_in, logs), (qkv_full_in, qkv_full))
    ]
    here.greet()
    low_gather = seq_gather(here, low_home, grad_low, low_sems)
    next(low_gather)

    def summed(sum_of, piece, full, sems, pause=1):
        yield from sum_of
        yield from seq_gather(here, piece, full, sems, pause)

    def from_hbm(grad, y_first):
        def block(df, ds, h):
            dy, dx = (ds, df) if y_first else (df, ds)
            return grad.at[pl.ds(row_of(wrap(here.y + dy), wrap(here.x + dx), h), SHARD)]

        return block

    def own_unit(place, j, ds, h):
        at = wrap(place + j)
        return at * 2 + h if ds == 0 else (8 if ds == 1 else 12) + at

    def owned(held, place):
        def own(j, ds, h):
            return held[pl.ds(pl.multiple_of(own_unit(place, j, ds, h) * SHARD, SHARD), SHARD), :]

        return own

    sum_a = scatter_grad(here, from_hbm(grad_a, True), owned(pre_a, here.x), buffers[:10], piece_a, True, False)
    sum_b = scatter_grad(here, from_hbm(grad_b, False), owned(pre_b, here.y), buffers[10:20], piece_b, False, False)
    sums = [summed(sum_a, piece_a, ffn_a_all, gather_sems.at[0], 4), summed(sum_b, piece_b, ffn_b_all, gather_sems.at[1], 4)]

    def chunk(y):
        return pl.ds(pl.multiple_of(y * CHUNK, CHUNK), CHUNK)

    moving = []
    for n, (j, k) in enumerate((j, k) for j in (2, 1, 3, 0) for k in range(2)):
        pre = (pre_a, pre_b)[k]
        if n == 0:
            for load in load_a:
                load.wait()
        if n == 1:
            load_b.wait()
        at = chunk(wrap(here.y + j))
        slot = staged.at[n % 2]
        slot[:, : 2 * HALF] = mm_tn(normed[:, at], pre[:, : 2 * HALF]).astype(BF)
        slot[:, 2 * HALF :] = mm_tn(part[:, :, at].reshape(L, CHUNK), pre[:, 2 * HALF :]).astype(BF)
        moving.append(local.copy(slot, (grad_a, grad_b)[k].at[at]))
        if n > 0:
            moving[n - 1].wait()
            next(sums[(n - 1) % 2])
    moving[-1].wait()
    next(sums[1])
    load_own = []
    for grad, held, y_first in ((grad_a, pre_a, True), (grad_b, pre_b, False)):
        for i in range(4):
            for ds, h in ((0, 0), (0, 1), (1, 0), (3, 1)):
                y, x = (wrap(here.y + ds), i) if y_first else (i, wrap(here.x + ds))
                unit = i * 2 + h if ds == 0 else (8 if ds == 1 else 12) + i
                source = grad.at[pl.ds(row_of(y, x, h), SHARD)]
                load_own.append(local.copy(source, held.at[pl.ds(unit * SHARD, SHARD)]))
    load_rest.append(local.copy(normed_in, normed))
    here.send(out_far, far_out, out_sems.at[0], here.far)
    set_segments(segments, seg_col)
    seg_row = segments[...].astype(F32)
    next(low_gather)
    for load in load_own:
        load.wait()

    def tick():
        for part_sum in sums[:2]:
            next(part_sum)

    tick()
    next(low_gather, None)
    for load in load_rest:
        load.wait()
    for b in range(SEQ):
        at = slice(b * ROWS, (b + 1) * ROWS)
        grad_heads[at, :] = mm(grad_low[b], out_full[:, :Q_COLS]).astype(BF)

    def blocks_of(grad, y_first):
        def block(df, ds, h):
            dy, dx = (ds, df) if y_first else (df, ds)
            return grad.at[wrap(here.y + dy), wrap(here.x + dx), h]

        return block

    def out_chunk(y, carry):
        grad_out[y] = mm_tn(grad_low[:, :, chunk(y)].reshape(L, CHUNK), heads[...]).astype(BF).reshape(4, 2, SHARD, Q_COLS)
        return carry

    lax.fori_loop(0, 4, out_chunk, 0)
    sum_out = scatter_grad(here, blocks_of(grad_out, False), None, buffers[20:30], piece_out, False, True)
    sums.append(summed(sum_out, piece_out, out_all, gather_sems.at[2]))
    next(sums[-1])

    tick()
    grad_kv[...] = jnp.zeros_like(grad_kv)
    for b in range(SEQ):
        at, kv_len = b * ROWS, (b + 1) * ROWS
        for h in range(GROUP):
            cols = slice(h * HEAD, (h + 1) * HEAD)
            query, grad = qkv[at : at + ROWS, cols], grad_heads[at : at + ROWS, cols]
            scores = mm_nt(query, qkv[:kv_len, Q_COLS:KV]) * SCALE
            probs = jnp.exp(masked(scores, at, kv_len, seg_col, seg_row) - logs[at : at + ROWS, h : h + 1])
            grad_probs = mm_nt(grad, qkv[:kv_len, KV:])
            centre = jnp.sum(probs * grad_probs, axis=-1, keepdims=True)
            grad_scores = (probs * (grad_probs - centre)).astype(BF)
            grad_all[at : at + ROWS, cols] = (mm(grad_scores, qkv[:kv_len, Q_COLS:KV]) * SCALE).astype(BF)
            grad_kv[:kv_len, :HEAD] += mm_tn(grad_scores, query) * SCALE
            grad_kv[:kv_len, HEAD:] += mm_tn(probs.astype(BF), grad)
    tick()
    grad_all[:, Q_COLS:] = grad_kv[...].astype(BF)

    def q_chunk(y, carry):
        grad_q[y] = mm_tn(normed[:, chunk(y)], grad_all[:, :Q_COLS]).astype(BF).reshape(4, 2, SHARD, Q_COLS)
        return carry

    gain_sum[...] = jnp.zeros_like(gain_sum)

    def back(i):
        at = pl.ds(pl.multiple_of(i * ROWS, ROWS), ROWS)
        value = mm_nt(grad_all[at, :], qkv_full[...])
        part[i] = value.astype(BF)
        gain_sum[0:1, :] += jnp.sum(value * normed[at, :].astype(F32), axis=0, keepdims=True)

    row_sum = seq_scatter(here, part, near, far, scatter_sems, back, 4)
    next(row_sum)
    next(row_sum)
    tick()
    lax.fori_loop(0, 4, q_chunk, 0)
    sum_q = scatter_grad(here, blocks_of(grad_q, True), None, buffers[30:40], piece_q, True, True)
    sums.append(summed(sum_q, piece_q, q_all, gather_sems.at[3]))
    next(sums[-1])
    tick()
    gain = gains[0:1, :]
    high, low = split_two(gain_sum[0:1, :] / gain)
    row = iota((16, WIDTH), 0)
    both = jnp.where(row == 0, high.astype(F32), 0.0) + jnp.where(row == 1, low.astype(F32), 0.0)
    gain_sum[...] = both
    pick = (iota((16, LANES), 1) == 0).astype(BF)

    def kv_chunk(y, carry):
        at = chunk(y)
        pair = mm_tn(normed[:, at], grad_all[:, Q_COLS:])
        single = grad_misc[at, :] + mm_tn(gain_sum[:, at].astype(BF), pick)
        grad_kvm[y] = jnp.concatenate([pair, single], axis=1).astype(BF).reshape(4, 2, SHARD, Q_COLS)
        return carry

    lax.fori_loop(0, 4, kv_chunk, 0)
    sum_kv = scatter_grad(here, blocks_of(grad_kvm, False), None, buffers[40:], piece_kv, False, True)
    sums.append(summed(sum_kv, piece_kv, kv_all, gather_sems.at[4]))

    def rows():
        yield from row_sum
        here.wait(far_out, out_sems.at[0])
        grad_normed = added(part[s], near[1], far[...])
        inverse, unit, _ = normed_of(tokens[...].astype(F32), gain)
        scaled = grad_normed * gain
        grad_tokens[...] = (grad_hidden[...] + inverse * (scaled - unit * jnp.mean(scaled * unit, axis=-1, keepdims=True))).astype(BF)

    next(sums[-1])
    together(*sums[:2], *sums[2:], rows())
    here.finish()


def as_row(col):
    n = col.shape[0]
    return jnp.sum(jnp.where(iota((n, n), 0) == iota((n, n), 1), jnp.broadcast_to(col, (n, n)), 0.0), axis=0, keepdims=True)


def outputs_kernel(
    ffn_a, ffn_b, q, kv, out, out_own, far_out, output, wq, wk, wv, wo, gain_one, gain_two, router, shared_gate, shared_up, shared_down, expert_gate, expert_up, expert_down
):
    output[...] = added(out_own[...], far_out[...]).astype(BF)
    total = jnp.zeros((SHARD, LANES), F32)
    for s in range(SEQ):
        wq[:, s * Q_COLS : (s + 1) * Q_COLS] = q[s].astype(F32)
        wo[:, s * Q_COLS : (s + 1) * Q_COLS] = out[s].astype(F32)
        wk[:, s * HEAD : (s + 1) * HEAD] = kv[s, :, :HEAD].astype(F32)
        wv[:, s * HEAD : (s + 1) * HEAD] = kv[s, :, HEAD : 2 * HEAD].astype(F32)
        total = total + kv[s, :, 2 * HEAD :].astype(F32)
        for k, ffn in enumerate((ffn_a, ffn_b)):
            n = 2 * s + k
            for i, (shared, expert) in enumerate(((shared_gate, expert_gate), (shared_up, expert_up), (shared_down, expert_down))):
                expert[:, n, :] = ffn[s, :, i * HALF : i * HALF + 512].astype(F32)
                shared[:, n * LANES : (n + 1) * LANES] = ffn[s, :, i * HALF + 512 : (i + 1) * HALF].astype(F32)
    gain_one[...] = as_row(total[:, 0:1])
    gain_two[...] = as_row(total[:, 1:2])
    for e in range(E):
        router[e : e + 1, :] = as_row(total[:, 2 + e : 3 + e])


def remote_call(kernel, name, number, outs, ins, scratch):
    return pl.pallas_call(
        kernel,
        out_shape=[jax.ShapeDtypeStruct(dims, dtype) for dims, dtype, _ in outs],
        in_specs=[VMEM_ALL if fast else ANY for _, fast in ins],
        out_specs=[VMEM_ALL if fast else ANY for _, _, fast in outs],
        scratch_shapes=list(scratch),
        compiler_params=pltpu.CompilerParams(collective_id=number, has_side_effects=True, vmem_limit_bytes=LIMIT),
        name=name,
    )(*[array for array, _ in ins])


def buf(*dims):
    return pltpu.VMEM(dims, BF)


def buf32(*dims):
    return pltpu.VMEM(dims, F32)


def body(
    tokens,
    segments,
    routes,
    shared_mask,
    norm_gain,
    w_query,
    key_weight,
    value_weight,
    w_out,
    ffn_gain,
    w_router,
    shared_gate,
    shared_up,
    shared_down,
    expert_gate,
    expert_up,
    expert_down,
    cotangent,
):
    seg_row = segments[None, :]
    grid = DMA((4, 4, 2))
    rows4 = (SEQ, ROWS, WIDTH)
    fast = [tokens, routes.T, shared_mask[None, :], norm_gain[None, :], ffn_gain[None, :], w_router.T, w_query, key_weight,
            value_weight, w_out, shared_gate, shared_up, shared_down, expert_gate, expert_up, expert_down, seg_row]
    (
        normed_one, qkv, heads, logs, gains, qkv_full, out_full, normed_two, all_cot,
        pre_a, pre_b, low_home, grad_hidden, grad_misc, out_far, out_own,
    ) = remote_call(
        forward_kernel,
        "forward",
        1,
        [
            ((L, WIDTH), BF, False),
            ((L, HALF), BF, False),
            ((L, Q_COLS), BF, False),
            ((L, 8), F32, False),
            ((8, WIDTH), F32, True),
            (blocks(HALF), BF, False),
            (blocks(OUT_COLS), BF, False),
            (rows4, BF, False),
            (rows4, BF, False),
            ((L, FFN), BF, False),
            ((L, FFN), BF, False),
            ((ROWS, WIDTH), BF, False),
            ((ROWS, WIDTH), F32, False),
            ((WIDTH, LANES), F32, True),
            ((ROWS, WIDTH), BF, False),
            ((ROWS, WIDTH), F32, False),
        ],
        [(a, True) for a in fast] + [(cotangent, False)],
        [
            buf(ROWS, WIDTH + LANES),
            buf(SEQ, ROWS, WIDTH + LANES),
            buf(SHARD, HALF),
            buf(SHARD, OUT_COLS),
            buf(SHARD, FFN),
            buf(SHARD, FFN),
            buf(*blocks(HALF)),
            buf(*blocks(OUT_COLS)),
            buf(L, WIDTH),
            buf(L, HALF),
            buf(L, Q_COLS),
            buf32(L, 8),
            buf32(L, 1),
            buf(L, LANES),
            buf(WIDTH, LANES),
            buf(*rows4),
            buf(2, ROWS, WIDTH),
            buf(ROWS, WIDTH),
            buf(ROWS, WIDTH),
            buf32(ROWS, WIDTH),
            buf(*rows4),
            buf(*rows4),
            buf(*blocks(FFN)),
            buf(*blocks(FFN)),
            buf(2, 2, ROWS, FFN),
            buf(2, ROWS, WIDTH + LANES),
            buf(ROWS, WIDTH + LANES),
            buf(2, ROWS, WIDTH),
            buf32(ROWS, LANES),
            buf32(ROWS, WIDTH),
            DMA((160,)),
            DMA((4,)),
            grid,
            grid,
            grid,
            grid,
            DMA((4,)),
            DMA((3,)),
            DMA((4,)),
            DMA((4,)),
            DMA((3,)),
            DMA((2,)),
            DMA((24,)),
        ],
    )

    far_out, grad_tokens, _, _, ffn_a_all, ffn_b_all, q_all, kv_all, out_all = remote_call(
        finish_kernel,
        "finish",
        2,
        [
            ((ROWS, WIDTH), BF, False),
            ((ROWS, WIDTH), BF, True),
            ((WIDTH, FFN), BF, False),
            ((WIDTH, FFN), BF, False),
            ((SEQ, SHARD, FFN), BF, False),
            ((SEQ, SHARD, FFN), BF, False),
            ((SEQ, SHARD, Q_COLS), BF, False),
            ((SEQ, SHARD, Q_COLS), BF, False),
            ((SEQ, SHARD, Q_COLS), BF, False),
        ],
        [
            (low_home, False),
            (normed_two.reshape(L, WIDTH), False),
            (all_cot, False),
            (pre_a, False),
            (pre_b, False),
            (normed_one, False),
            (qkv, False),
            (heads, False),
            (logs, False),
            (qkv_full.reshape(WIDTH, HALF), False),
            (out_full.reshape(WIDTH, OUT_COLS), False),
            (out_far, False),
            (seg_row, True),
            (gains, True),
            (grad_misc, True),
            (grad_hidden, True),
            (tokens, True),
        ],
        [
            buf(*rows4),
            buf(L, WIDTH),
            buf(*rows4),
            buf(L, FFN),
            buf(L, FFN),
            buf(2, CHUNK, FFN),
            buf(L, HALF),
            buf(L, Q_COLS),
            buf32(L, 8),
            buf(WIDTH, HALF),
            buf(WIDTH, OUT_COLS),
            buf(*blocks(Q_COLS)),
            buf(*blocks(Q_COLS)),
            buf(*blocks(Q_COLS)),
            buf(L, Q_COLS),
            buf(L, HALF),
            buf32(L, 2 * HEAD),
            buf(2, ROWS, WIDTH),
            buf(ROWS, WIDTH),
            buf32(16, WIDTH),
            buf32(L, 1),
            buf(SHARD, FFN),
            buf(SHARD, FFN),
            buf(SHARD, Q_COLS),
            buf(SHARD, Q_COLS),
            buf(SHARD, Q_COLS),
            DMA((192,)),
            DMA((56,)),
            DMA((3,)),
            DMA((1,)),
            DMA((5, 4)),
            DMA((4,)),
            *scatter_buffers(FFN),
            *scatter_buffers(FFN),
            *scatter_buffers(Q_COLS),
            *scatter_buffers(Q_COLS),
            *scatter_buffers(Q_COLS),
        ],
    )

    dims = [(ROWS, WIDTH), (SHARD, 4 * Q_COLS), (SHARD, 4 * HEAD), (SHARD, 4 * HEAD), (SHARD, 4 * Q_COLS), (1, SHARD), (1, SHARD), (E, SHARD)]
    dims += [(SHARD, 1024)] * 3 + [(SHARD, E, 512)] * 3
    output, wq, wk, wv, wo, gain_one, gain_two, router, *ffn = pl.pallas_call(
        outputs_kernel,
        out_shape=[jax.ShapeDtypeStruct(d, BF if d[0] == ROWS else F32) for d in dims],
        in_specs=[VMEM_ALL] * 7,
        out_specs=[VMEM_ALL] * len(dims),
        compiler_params=pltpu.CompilerParams(vmem_limit_bytes=LIMIT),
        name="outputs",
    )(ffn_a_all, ffn_b_all, q_all, kv_all, out_all, out_own, far_out)
    return (output, grad_tokens, gain_one[0], wq, wk, wv, wo, gain_two[0], router.T, *ffn)


def solution(mesh):
    both = P(("fsdp", "seq"), None)
    one, two, three = P("fsdp"), P("fsdp", None), P("fsdp", None, None)
    return jax.shard_map(
        body,
        mesh=mesh,
        in_specs=(both, one, both, P(("fsdp", "seq")), one, two, two, two, two, one, two, two, two, two, three, three, three, both),
        out_specs=(both, both, one, two, two, two, two, one, two, two, two, two, three, three, three),
        check_vma=False,
    )
```

```python
import jax
import jax.numpy as jnp
from jax import lax
from jax.experimental import pallas as pl
from jax.experimental.pallas import tpu as pltpu
from jax.sharding import PartitionSpec as P

HEAD = 128
GROUP = 3
E = 8
SEQ = 4
EPS = 1e-05
BF = jnp.bfloat16
F32 = jnp.float32
WIDTH = 1536
L = 1024
ROWS = 256
SHARD = 48
Q_COLS = GROUP * HEAD
KV = Q_COLS + HEAD
HALF = 640
FFN = 3 * HALF
LANES = 128
OUT_COLS = Q_COLS + LANES
LOW = 32
CHUNK = 384
SCALE = HEAD ** (-0.5)
BIG = -1e30
MESH = pl.DeviceIdType.MESH
VMEM_ALL = pl.BlockSpec(memory_space=pltpu.VMEM)
ANY = pl.BlockSpec(memory_space=pl.ANY)
DMA = pltpu.SemaphoreType.DMA
LIMIT = 63 * 1024 * 1024


def f32dot(left, right, dims):
    return lax.dot_general(left, right, (dims, ((), ())), preferred_element_type=F32)


def mm(left, right):
    return f32dot(left, right, ((1,), (0,)))


def mm_nt(left, right):
    return f32dot(left, right, ((1,), (1,)))


def mm_tn(left, right):
    return f32dot(left, right, ((0,), (0,)))


def iota(dims, axis):
    return lax.broadcasted_iota(jnp.int32, dims, axis)


def column(row):
    n = row.shape[1]
    same = iota((n, n), 0) == iota((n, n), 1)
    return jnp.sum(jnp.where(same, jnp.broadcast_to(row, (n, n)), 0.0), axis=-1, keepdims=True)


def added(*values):
    total = values[0].astype(F32)
    for value in values[1:]:
        total = total + value.astype(F32)
    return total


def split_two(value):
    high = value.astype(BF)
    return high, (value - high.astype(F32)).astype(BF)


def normed_of(x, gain):
    inverse = lax.rsqrt(jnp.mean(x * x, axis=-1, keepdims=True) + EPS)
    unit = x * inverse
    return inverse, unit, (unit * gain).astype(BF)


def wrap(value):
    return lax.rem(value + 4, 4)


def blocks(cols):
    return (4, 4, 2, SHARD, cols)


class Here:
    def __init__(self, send_sems):
        f, s = lax.axis_index("fsdp"), lax.axis_index("seq")
        self.y, self.x, self.z = lax.div(f, 8), lax.rem(lax.div(f, 2), 4), lax.rem(f, 2)
        self.s, self.zh, self.core = s, lax.div(s, 2), lax.rem(s, 2)
        y, x, z = self.y, self.x, self.z
        self.axis_x = ({"fsdp": self.number(y, wrap(x + 1), z)}, {"fsdp": self.number(y, wrap(x - 1), z)})
        self.axis_y = ({"fsdp": self.number(wrap(y + 1), x, z)}, {"fsdp": self.number(wrap(y - 1), x, z)})
        self.pair = {"fsdp": self.number(y, x, 1 - z)}
        self.s_far = (1 - self.zh) * 2 + self.core
        self.s_near = self.zh * 2 + 1 - self.core
        self.s_cross = (1 - self.zh) * 2 + 1 - self.core
        self.far = {"seq": self.s_far}
        self.near = {"seq": self.s_near}
        self.sems, self.sent, self.left = send_sems, [], 0

    @staticmethod
    def number(y, x, z):
        return (y * 4 + x) * 2 + z

    def greet(self):
        partners = [*self.axis_x, *self.axis_y, self.pair, self.far, self.near]
        for partner in partners:
            pl.semaphore_signal(pltpu.get_barrier_semaphore(), inc=1, device_id=partner, device_id_type=MESH)

    def meet(self):
        pl.semaphore_wait(pltpu.get_barrier_semaphore(), 7)

    def send(self, source, target, recv_sem, to):
        copy = pltpu.make_async_remote_copy(
            src_ref=source,
            dst_ref=target,
            send_sem=self.sems.at[len(self.sent)],
            recv_sem=recv_sem,
            device_id=to,
            device_id_type=MESH,
        )
        copy.start()
        self.sent.append(copy)

    def wait(self, target, recv_sem):
        pltpu.make_async_remote_copy(
            src_ref=target,
            dst_ref=target,
            send_sem=self.sems.at[0],
            recv_sem=recv_sem,
            device_id=self.near,
            device_id_type=MESH,
        ).wait_recv()

    def finish(self):
        for copy in self.sent[self.left :]:
            copy.wait_send()
        self.left = len(self.sent)


class Local:
    def __init__(self, sems):
        self.sems, self.count = sems, 0

    def copy(self, source, target):
        copy = pltpu.make_async_copy(source, target, self.sems.at[self.count])
        copy.start()
        self.count += 1
        return copy


def together(*parts):
    left = list(parts)
    while left:
        for part in list(left):
            if next(part, "end") == "end":
                left.remove(part)


def later(turns, parts):
    for _ in range(turns):
        yield
    for part in parts:
        next(part)


def gather_weight(here, full, block, recv, own_sem, x_first):
    first, second = (here.axis_x, here.axis_y) if x_first else (here.axis_y, here.axis_x)

    def spot(df, ds, r):
        dy, dx = (ds, df) if x_first else (df, ds)
        return wrap(here.y + dy), wrap(here.x + dx), here.z if r == 0 else 1 - here.z

    def push(df, ds, r, to, source=None):
        at = spot(df, ds, r)
        here.send(full.at[at] if source is None else source, full.at[at], recv.at[at], to)

    def take(df, ds, r):
        at = spot(df, ds, r)
        here.wait(full.at[at], recv.at[at])

    own = pltpu.make_async_copy(block, full.at[spot(0, 0, 0)], own_sem)
    own.start()
    push(0, 0, 0, here.pair, block)
    yield
    for to in (*second, *first):
        push(0, 0, 0, to, block)
    yield
    take(0, 0, 1)
    for to in (*first, *second):
        push(0, 0, 1, to)
    for df, r in ((-1, 0), (1, 0), (1, 1), (-1, 1), (2, 0), (2, 1)):
        yield
        take(df, 0, r)
        if (df, r) == (-1, 0):
            push(df, 0, r, first[0])
        if (df, r) == (1, 1):
            push(df, 0, r, first[1])
        for to in second:
            push(df, 0, r, to)
        if (df, r) == (1, 0):
            take(0, -1, 0)
            push(0, -1, 0, second[0])
        if (df, r) == (-1, 1):
            take(0, 1, 1)
            push(0, 1, 1, second[1])
    for df in (-1, 1, 2):
        yield
        take(df, -1, 0)
        push(df, -1, 0, second[0])
        yield
        take(df, 1, 1)
        push(df, 1, 1, second[1])
    yield
    for df in (0, -1, 1, 2):
        take(df, -1, 1)
        take(df, 1, 0)
        take(df, 2, 0)
        take(df, 2, 1)
    own.wait()


def scatter_buffers(cols):
    units = [(4,), (4,), (4, 2), (4, 2), (1,), (1,), (2,), (2,), (1,)]
    return [pltpu.VMEM((*u, SHARD, cols), BF) for u in units] + [DMA((31,))]


def scatter_grad(here, block, own, buffers, piece, y_first, small):
    ra, rb, rc, rd, xa, xb, xc, xd, zr, sems = buffers
    second, first = (here.axis_y, here.axis_x) if y_first else (here.axis_x, here.axis_y)
    own = own or (lambda df, ds, h: block(df, ds, h)[...])

    def far_send(j):
        here.send(block(j, 2, 0), ra.at[j], sems.at[j], second[0])
        here.send(block(j, 2, 1), rb.at[j], sems.at[4 + j], second[1])

    def near_plus(j):
        here.send(block(j, 1, 1), rc.at[j, 1], sems.at[8 + 2 * j + 1], second[0])

    def near_minus(j):
        here.send(block(j, 3, 0), rd.at[j, 0], sems.at[16 + 2 * j], second[1])

    def pass_on(j):
        here.wait(ra.at[j], sems.at[j])
        ra[j] = added(own(j, 1, 0), ra[j]).astype(BF)
        here.send(ra.at[j], rc.at[j, 0], sems.at[8 + 2 * j], second[0])
        here.wait(rb.at[j], sems.at[4 + j])
        rb[j] = added(own(j, 3, 1), rb[j]).astype(BF)
        here.send(rb.at[j], rd.at[j, 1], sems.at[16 + 2 * j + 1], second[1])

    def total(j):
        for h in range(2):
            here.wait(rc.at[j, h], sems.at[8 + 2 * j + h])
            here.wait(rd.at[j, h], sems.at[16 + 2 * j + h])
            rc[j, h] = added(own(j, 0, h), rc[j, h], rd[j, h]).astype(BF)

    def turn_two():
        here.send(rc.at[2, 0], xa.at[0], sems.at[24], first[0])
        here.send(rc.at[2, 1], xb.at[0], sems.at[25], first[1])

    def turn_near():
        here.send(rc.at[1, 1], xc.at[1], sems.at[27], first[0])
        here.send(rc.at[3, 0], xd.at[0], sems.at[28], first[1])

    def turn_on():
        here.wait(xa.at[0], sems.at[24])
        xa[0] = added(rc[1, 0], xa[0]).astype(BF)
        here.send(xa.at[0], xc.at[0], sems.at[26], first[0])
        here.wait(xb.at[0], sems.at[25])
        xb[0] = added(rc[3, 1], xb[0]).astype(BF)
        here.send(xb.at[0], xd.at[1], sems.at[29], first[1])

    every = (2, 1, 3, 0)
    if small:
        for j in every:
            far_send(j)
            near_plus(j)
            near_minus(j)
        yield
        for j in every:
            pass_on(j)
        yield
        total(2)
        turn_two()
        total(1)
        total(3)
        turn_near()
        yield
        turn_on()
        total(0)
        yield
    else:
        if y_first:
            for send in (far_send, near_plus, near_minus):
                for j in every:
                    send(j)
                yield
        else:
            for j in every:
                far_send(j)
                near_plus(j)
                near_minus(j)
                yield
        if y_first:
            yield
        pass_on(2)
        pass_on(1)
        yield
        pass_on(3)
        pass_on(0)
        yield
        total(2)
        turn_two()
        yield
        total(1)
        total(3)
        turn_near()
        yield
        total(0)
        yield
        turn_on()
        yield
    for h in range(2):
        here.wait(xc.at[h], sems.at[26 + h])
        here.wait(xd.at[h], sems.at[28 + h])
        xc[h] = added(rc[0, h], xc[h], xd[h]).astype(BF)
    here.send(xc.at[1 - here.z], zr.at[0], sems.at[30], here.pair)
    yield
    here.wait(zr.at[0], sems.at[30])
    piece[...] = added(xc[here.z], zr[0]).astype(piece.dtype)


def seq_gather(here, source, full, sems, pause=1):
    own = pltpu.make_async_copy(source, full.at[here.s], sems.at[3])
    own.start()
    here.send(source, full.at[here.s], sems.at[0], here.far)
    here.send(source, full.at[here.s], sems.at[1], here.near)
    for _ in range(pause):
        yield
    here.wait(full.at[here.s_far], sems.at[0])
    here.send(full.at[here.s_far], full.at[here.s_far], sems.at[2], here.near)
    yield
    here.wait(full.at[here.s_near], sems.at[1])
    here.wait(full.at[here.s_cross], sems.at[2])
    own.wait()


def seq_scatter(here, parts, near, far, sems, make, pause=1):
    make(here.s_cross)
    here.send(parts.at[here.s_cross], near.at[0], sems.at[0], here.near)
    make(here.s_far)
    yield
    here.wait(near.at[0], sems.at[0])
    near[0] = added(parts[here.s_far], near[0]).astype(BF)
    here.send(near.at[0], far, sems.at[2], here.far)
    make(here.s_near)
    here.send(parts.at[here.s_near], near.at[1], sems.at[1], here.near)
    make(here.s)
    yield
    here.wait(near.at[1], sems.at[1])
    for _ in range(pause):
        yield
    here.wait(far, sems.at[2])


def masked(scores, at, kv_len, seg_col, seg_row):
    q_pos = at + iota((ROWS, kv_len), 0)
    k_pos = iota((ROWS, kv_len), 1)
    keep = (q_pos >= k_pos) & (seg_col[at : at + ROWS, :] == seg_row[:, :kv_len])
    return jnp.where(keep, scores, BIG)


def set_segments(seg_row, seg_col):
    for b in range(L // ROWS):
        at = slice(b * ROWS, (b + 1) * ROWS)
        seg_col[at, :] = column(seg_row[:, at].astype(F32))


def forward_kernel(
    tokens, routes, shared_mask, norm_gain, ffn_gain, w_router, w_query, key_weight, value_weight, w_out,
    shared_gate, shared_up, shared_down, expert_gate, expert_up, expert_down, segments, cot,
    normed_one, qkv_out, heads_out, logs_out, gains, qkv_full_out, out_full_out, normed_two, all_cot,
    pre_a, pre_b, low_home, grad_hidden, grad_misc, out_far, out_own,
    marked, all_marked, qkv_block, out_block, block_a, block_b, qkv_full, out_full, normed, qkv, heads, logs, seg_col,
    marks, misc, part, near, far, normed_home, hidden, xs, cs, full_a, full_b,
    staged, near_g, far_g, near_out, own_gates, own_out,
    send_sems, token_sems, qkv_sems, out_sems, a_sems, b_sems, own_sems, scatter_sems, gather_sems, cot_sems,
    grad_sems, sum_sems, local_sems,
):
    here = Here(send_sems)
    local = Local(local_sems)
    here.greet()
    s = here.s

    def wide(ref, at, width):
        return ref[:, pl.ds(pl.multiple_of(at * width, LANES), width)]

    marked[:, :WIDTH] = tokens[...]
    line = iota((LANES, ROWS), 0)
    used = line == routes[0:1, :] + 2
    for k in range(1, 6):
        used = used | (line == routes[k : k + 1, :] + 2)
    turned = (jnp.where(used, 1.0, 0.0) + jnp.where(line == 1, shared_mask[...].astype(F32), 0.0)).astype(BF)
    eye = (iota((LANES, LANES), 0) == iota((LANES, LANES), 1)).astype(BF)
    marked[:, WIDTH:] = mm_tn(turned, eye).astype(BF)
    token_gather = seq_gather(here, marked, all_marked, token_sems, 13)
    qkv_block[:, :Q_COLS] = wide(w_query, s, Q_COLS)
    qkv_block[:, Q_COLS:KV] = wide(key_weight, s, HEAD)
    qkv_block[:, KV:] = wide(value_weight, s, HEAD)
    here.meet()
    qkv_gather = gather_weight(here, qkv_full, qkv_block, qkv_sems, own_sems.at[0], True)
    next(qkv_gather)
    out_block[:, :Q_COLS] = wide(w_out, s, Q_COLS)
    place = (iota((E, LANES), 1) == iota((E, LANES), 0) + 2).astype(F32)
    single = f32dot(w_router[...].astype(F32), place, ((0,), (0,)))
    lane = iota((SHARD, LANES), 1)
    single = single + jnp.where(lane == 0, column(norm_gain[...].astype(F32)), 0.0)
    out_block[:, Q_COLS:] = (single + jnp.where(lane == 1, column(ffn_gain[...].astype(F32)), 0.0)).astype(BF)
    out_gather = gather_weight(here, out_full, out_block, out_sems, own_sems.at[1], False)
    next(out_gather)
    next(token_gather)
    next(qkv_gather)
    next(out_gather)
    for k, block in enumerate((block_a, block_b)):
        pick = (iota((SHARD, SHARD * E), 1) == iota((SHARD, SHARD * E), 0) * E + 2 * s + k).astype(BF)
        for i, (shared, expert) in enumerate(((shared_gate, expert_gate), (shared_up, expert_up), (shared_down, expert_down))):
            block[:, i * HALF : i * HALF + 512] = mm(pick, expert[...].reshape(SHARD * E, 512)).astype(BF)
            block[:, i * HALF + 512 : (i + 1) * HALF] = wide(shared, 2 * s + k, HALF - 512)
    set_segments(segments, seg_col)
    weights = [
        gather_weight(here, full_a, block_a, a_sems, own_sems.at[2], True),
        gather_weight(here, full_b, block_b, b_sems, own_sems.at[3], False),
    ]
    for weight in weights:
        next(weight)
    together(token_gather, qkv_gather, out_gather, later(9, weights))

    def tick():
        for weight in weights:
            next(weight, None)

    cot_gather = seq_gather(here, cot, cs, cot_sems)
    next(cot_gather)
    misc[...] = out_full[:, :, :, :, Q_COLS:].reshape(WIDTH, LANES)
    gains[...] = mm_nt(eye, misc[...])[:8]
    gain = gains[0:1, :]
    seg_row = segments[...].astype(F32)
    for b in range(SEQ):
        at = slice(b * ROWS, (b + 1) * ROWS)
        normed[at, :] = normed_of(all_marked[b, :, :WIDTH].astype(F32), gain)[2]
        qkv[at, :] = mm(normed[at, :], qkv_full[...].reshape(WIDTH, HALF)).astype(BF)
        marks[at, :] = all_marked[b, :, WIDTH:]
        if b == 3:
            tick()
    saved = [local.copy(normed, normed_one), local.copy(qkv, qkv_out), local.copy(qkv_full, qkv_full_out)]
    saved.append(local.copy(out_full, out_full_out))
    for b in range(SEQ):
        at, kv_len = b * ROWS, (b + 1) * ROWS
        for h in range(GROUP):
            cols = slice(h * HEAD, (h + 1) * HEAD)
            scores = mm_nt(qkv[at : at + ROWS, cols], qkv[:kv_len, Q_COLS:KV]) * SCALE
            scores = masked(scores, at, kv_len, seg_col, seg_row)
            top = jnp.max(scores, axis=-1, keepdims=True)
            weight = jnp.exp(scores - top)
            total = jnp.sum(weight, axis=-1, keepdims=True)
            probs = (weight * (1.0 / total)).astype(BF)
            heads[at : at + ROWS, cols] = mm(probs, qkv[:kv_len, KV:]).astype(BF)
            logs[at : at + ROWS, h : h + 1] = top + jnp.log(total)
        tick()

    saved += [local.copy(heads, heads_out), local.copy(logs, logs_out)]

    def project(i):
        rows = heads[pl.ds(pl.multiple_of(i * ROWS, ROWS), ROWS), :]
        part[i] = mm_nt(rows, out_full[:, :, :, :, :Q_COLS].reshape(WIDTH, Q_COLS)).astype(BF)

    def rows():
        yield from seq_scatter(here, part, near, far, scatter_sems, project, 2)
        next(cot_gather)
        hidden[...] = added(tokens[...], part[s], near[1], far[...])
        normed_home[...] = normed_of(hidden[...], gains[1:2, :])[2]
        yield from seq_gather(here, normed_home, xs, gather_sems, 3)
        next(cot_gather, None)

    together(rows(), *weights)
    for copy in saved:
        copy.wait()
    saved = [local.copy(xs, normed_two), local.copy(cs, all_cot)]
    here.finish()
    order = (here.s_cross, here.s_far, here.s_near, s)
    sent, outs, far_sum, low_out = all_marked, part, far, normed_home
    lane = iota((ROWS, LANES), 1)
    stored = [[], []]

    def block(n):
        i = order[n]
        at = pl.ds(pl.multiple_of(i * ROWS, ROWS), ROWS)
        x, c = xs[i], cs[i]
        mark = marks[at, :].astype(F32)
        member = (mark > 0) & (lane >= 2) & (lane < 2 + E)
        logits = jnp.where(member, mm(x, misc[...]), BIG)
        soft = jnp.where(member, jnp.exp(logits - jnp.max(logits, axis=-1, keepdims=True)), 0.0)
        gates = soft / jnp.sum(soft, axis=-1, keepdims=True)
        if n == 3:
            own_gates[...] = gates
        keep = mark[:, 1:2]
        total = jnp.zeros((ROWS, WIDTH), F32)
        grad_x = jnp.zeros((ROWS, WIDTH), F32)
        grad_marks = jnp.zeros((ROWS, LANES), F32)
        for k, weight in enumerate((full_a, full_b)):
            if n >= 2:
                stored[k][n - 2].wait()
            slot = staged.at[n % 2, k]
            mine = lane == 2 + 2 * s + k
            gate_e = jnp.sum(jnp.where(mine, gates, 0.0), axis=-1, keepdims=True)
            coef = jnp.concatenate([jnp.broadcast_to(gate_e, (ROWS, 512)), jnp.broadcast_to(keep, (ROWS, HALF - 512))], axis=1)
            pre = mm(x, weight[:, :, :, :, : 2 * HALF].reshape(WIDTH, 2 * HALF))
            gate, upper = pre[:, :HALF], pre[:, HALF:]
            sigma = 1.0 / (1.0 + jnp.exp(-gate))
            silu = gate * sigma
            units = silu * upper
            weighted = (coef * units).astype(BF)
            slot[:, 2 * HALF :] = weighted
            total += mm_nt(weighted, weight[:, :, :, :, 2 * HALF :].reshape(WIDTH, HALF))
            grad_units = mm(c, weight[:, :, :, :, 2 * HALF :].reshape(WIDTH, HALF))
            grad_gate = jnp.sum((units * grad_units)[:, :512], axis=-1, keepdims=True)
            high = grad_gate.astype(BF).astype(F32)
            grad_marks += jnp.where(mine, high, 0.0) + jnp.where(lane == LOW + 2 + 2 * s + k, grad_gate - high, 0.0)
            grad_units = coef * grad_units
            slot[:, :HALF] = (grad_units * upper * (sigma * (1.0 + gate * (1.0 - sigma)))).astype(BF)
            slot[:, HALF : 2 * HALF] = (grad_units * silu).astype(BF)
            grad_x += mm_nt(slot[:, : 2 * HALF], weight[:, :, :, :, : 2 * HALF].reshape(WIDTH, 2 * HALF))
            stored[k].append(local.copy(slot, (pre_a, pre_b)[k].at[at]))
        outs[i] = total.astype(BF)
        sent[i, :, :WIDTH] = grad_x.astype(BF)
        sent[i, :, WIDTH:] = grad_marks.astype(BF)

    block(0)
    here.send(sent.at[here.s_cross], near_g.at[0], grad_sems.at[0], here.near)
    here.send(outs.at[here.s_cross], near_out.at[0], sum_sems.at[0], here.near)
    block(1)
    here.wait(near_g.at[0], grad_sems.at[0])
    near_g[0] = added(sent[here.s_far], near_g[0]).astype(BF)
    here.send(near_g.at[0], far_g, grad_sems.at[2], here.far)
    here.wait(near_out.at[0], sum_sems.at[0])
    far_sum[...] = added(outs[here.s_far], near_out[0]).astype(BF)
    saved.append(local.copy(far_sum, out_far))
    block(2)
    here.send(sent.at[here.s_near], near_g.at[1], grad_sems.at[1], here.near)
    here.send(outs.at[here.s_near], near_out.at[1], sum_sems.at[1], here.near)
    block(3)
    here.wait(near_g.at[1], grad_sems.at[1])
    here.wait(near_out.at[1], sum_sems.at[1])
    own_out[...] = added(hidden[...], outs[s], near_out[1])
    saved.append(local.copy(own_out, out_own))
    gain = gains[1:2, :]
    inverse, unit, normed_home = normed_of(hidden[...], gain)
    here.wait(far_g, grad_sems.at[2])

    grad_gates = added(sent[s, :, WIDTH:], near_g[1, :, WIDTH:], far_g[:, WIDTH:])
    grad_gates = grad_gates + pltpu.roll(grad_gates, LANES - LOW, 1)
    gates = own_gates[...]
    grad_logits = gates * (grad_gates - jnp.sum(gates * grad_gates, axis=-1, keepdims=True))
    high, low = split_two(grad_logits)
    grad_normed = added(sent[s, :, :WIDTH], near_g[1, :, :WIDTH], far_g[:, :WIDTH])
    grad_normed = grad_normed + (mm_nt(high, misc[...]) + mm_nt(low, misc[...]))
    scaled = grad_normed * gain
    grad = cs[s].astype(F32) + inverse * (scaled - unit * jnp.mean(scaled * unit, axis=-1, keepdims=True))
    low_out[...] = grad.astype(BF)
    saved.append(local.copy(low_out, low_home))
    hidden[...] = grad
    saved.append(local.copy(hidden, grad_hidden))
    prod_high, prod_low = split_two(grad_normed * unit)
    one = (lane == 1).astype(BF)
    grad_misc[...] = mm_tn(normed_home, high) + mm_tn(normed_home, low) + mm_tn(prod_high, one) + mm_tn(prod_low, one)
    for copy in (*saved, *stored[0][2:], *stored[1][2:]):
        copy.wait()
    here.finish()


def row_of(y, x, z):
    return pl.multiple_of(((y * 4 + x) * 2 + z) * SHARD, SHARD)


def finish_kernel(
    low_home, normed_two_in, cots_in, pre_a_in, pre_b_in,
    normed_in, qkv_in, heads_in, logs_in, qkv_full_in, out_full_in, out_far,
    segments, gains, grad_misc, grad_hidden, tokens,
    far_out, grad_tokens, grad_a, grad_b, ffn_a_all, ffn_b_all, q_all, kv_all, out_all,
    grad_low, normed, part, pre_a, pre_b, staged, qkv, heads, logs, qkv_full, out_full,
    grad_q, grad_pair, grad_out, grad_heads, grad_all, grad_kv, near, far, gain_sum, seg_col,
    piece_a, piece_b, piece_q, piece_kv, piece_out,
    send_sems, local_sems, scatter_sems, out_sems, gather_sems, low_sems, *buffers,
):
    here = Here(send_sems)
    local = Local(local_sems)
    s = here.s
    load_a = [local.copy(normed_two_in, normed), local.copy(pre_a_in, pre_a), local.copy(cots_in, part)]
    load_b = local.copy(pre_b_in, pre_b)
    load_rest = [
        local.copy(a, b)
        for a, b in ((out_full_in, out_full), (heads_in, heads), (qkv_in, qkv), (logs_in, logs), (qkv_full_in, qkv_full))
    ]
    here.greet()
    here.meet()
    low_gather = seq_gather(here, low_home, grad_low, low_sems)
    next(low_gather)

    def summed(sum_of, piece, full, sems, pause=1):
        yield from sum_of
        yield from seq_gather(here, piece, full, sems, pause)

    def from_hbm(grad, y_first):
        def block(df, ds, h):
            dy, dx = (ds, df) if y_first else (df, ds)
            return grad.at[pl.ds(row_of(wrap(here.y + dy), wrap(here.x + dx), h), SHARD)]

        return block

    def own_unit(place, j, ds, h):
        at = wrap(place + j)
        return at * 2 + h if ds == 0 else (8 if ds == 1 else 12) + at

    def owned(held, place):
        def own(j, ds, h):
            return held[pl.ds(pl.multiple_of(own_unit(place, j, ds, h) * SHARD, SHARD), SHARD), :]

        return own

    sum_a = scatter_grad(here, from_hbm(grad_a, True), owned(pre_a, here.x), buffers[:10], piece_a, True, False)
    sum_b = scatter_grad(here, from_hbm(grad_b, False), owned(pre_b, here.y), buffers[10:20], piece_b, False, False)
    sums = [summed(sum_a, piece_a, ffn_a_all, gather_sems.at[0], 4), summed(sum_b, piece_b, ffn_b_all, gather_sems.at[1], 4)]

    def chunk(y):
        return pl.ds(pl.multiple_of(y * CHUNK, CHUNK), CHUNK)

    moving = []
    for n, (j, k) in enumerate((j, k) for j in (2, 1, 3, 0) for k in range(2)):
        pre = (pre_a, pre_b)[k]
        if n == 0:
            for load in load_a:
                load.wait()
        if n == 1:
            load_b.wait()
        at = chunk(wrap(here.y + j))
        slot = staged.at[n % 2]
        slot[:, : 2 * HALF] = mm_tn(normed[:, at], pre[:, : 2 * HALF]).astype(BF)
        slot[:, 2 * HALF :] = mm_tn(part[:, :, at].reshape(L, CHUNK), pre[:, 2 * HALF :]).astype(BF)
        moving.append(local.copy(slot, (grad_a, grad_b)[k].at[at]))
        if n > 0:
            moving[n - 1].wait()
            next(sums[(n - 1) % 2])
    moving[-1].wait()
    next(sums[1])
    load_own = []
    for grad, held, y_first in ((grad_a, pre_a, True), (grad_b, pre_b, False)):
        for i in range(4):
            for ds, h in ((0, 0), (0, 1), (1, 0), (3, 1)):
                y, x = (wrap(here.y + ds), i) if y_first else (i, wrap(here.x + ds))
                unit = i * 2 + h if ds == 0 else (8 if ds == 1 else 12) + i
                source = grad.at[pl.ds(row_of(y, x, h), SHARD)]
                load_own.append(local.copy(source, held.at[pl.ds(unit * SHARD, SHARD)]))
    load_rest.append(local.copy(normed_in, normed))
    here.send(out_far, far_out, out_sems.at[0], here.far)
    set_segments(segments, seg_col)
    seg_row = segments[...].astype(F32)
    next(low_gather)
    for load in load_own:
        load.wait()

    def tick():
        for part_sum in sums[:2]:
            next(part_sum)

    tick()
    next(low_gather, None)
    for load in load_rest:
        load.wait()
    for b in range(SEQ):
        at = slice(b * ROWS, (b + 1) * ROWS)
        grad_heads[at, :] = mm(grad_low[b], out_full[:, :Q_COLS]).astype(BF)

    def blocks_of(grad, y_first):
        def block(df, ds, h):
            dy, dx = (ds, df) if y_first else (df, ds)
            return grad.at[wrap(here.y + dy), wrap(here.x + dx), h]

        return block

    def out_chunk(y, carry):
        value = mm_tn(grad_low[:, :, chunk(y)].reshape(L, CHUNK), heads[...])
        grad_out[y, :, :, :, :Q_COLS] = value.astype(BF).reshape(4, 2, SHARD, Q_COLS)
        return carry

    lax.fori_loop(0, 4, out_chunk, 0)
    tick()
    grad_kv[...] = jnp.zeros_like(grad_kv)
    for b in range(SEQ):
        at, kv_len = b * ROWS, (b + 1) * ROWS
        for h in range(GROUP):
            cols = slice(h * HEAD, (h + 1) * HEAD)
            query, grad = qkv[at : at + ROWS, cols], grad_heads[at : at + ROWS, cols]
            scores = mm_nt(query, qkv[:kv_len, Q_COLS:KV]) * SCALE
            probs = jnp.exp(masked(scores, at, kv_len, seg_col, seg_row) - logs[at : at + ROWS, h : h + 1])
            grad_probs = mm_nt(grad, qkv[:kv_len, KV:])
            centre = jnp.sum(probs * grad_probs, axis=-1, keepdims=True)
            grad_scores = (probs * (grad_probs - centre)).astype(BF)
            grad_all[at : at + ROWS, cols] = (mm(grad_scores, qkv[:kv_len, Q_COLS:KV]) * SCALE).astype(BF)
            grad_kv[:kv_len, :HEAD] += mm_tn(grad_scores, query) * SCALE
            grad_kv[:kv_len, HEAD:] += mm_tn(probs.astype(BF), grad)
    tick()
    grad_all[:, Q_COLS:] = grad_kv[...].astype(BF)

    def q_chunk(y, carry):
        grad_q[y] = mm_tn(normed[:, chunk(y)], grad_all[:, :Q_COLS]).astype(BF).reshape(4, 2, SHARD, Q_COLS)
        return carry

    def weight_chunk(y, carry):
        at = chunk(y)
        value = mm_tn(normed[:, at], grad_all[...]).astype(BF)
        grad_q[y] = value[:, :Q_COLS].reshape(4, 2, SHARD, Q_COLS)
        grad_pair[y] = value[:, Q_COLS:].reshape(4, 2, SHARD, 2 * HEAD)
        return carry

    lax.fori_loop(0, 4, weight_chunk, 0)
    sum_q = scatter_grad(here, blocks_of(grad_q, True), None, buffers[20:30], piece_q, True, True)
    sums.append(summed(sum_q, piece_q, q_all, gather_sems.at[2]))
    sum_kv = scatter_grad(here, blocks_of(grad_pair, False), None, buffers[30:40], piece_kv, False, True)
    sums.append(summed(sum_kv, piece_kv, kv_all, gather_sems.at[3]))
    tick()
    gain_sum[...] = jnp.zeros_like(gain_sum)

    def back(i):
        at = pl.ds(pl.multiple_of(i * ROWS, ROWS), ROWS)
        value = mm_nt(grad_all[at, :], qkv_full[...])
        part[i] = value.astype(BF)
        gain_sum[0:1, :] += jnp.sum(value * normed[at, :].astype(F32), axis=0, keepdims=True)

    row_sum = seq_scatter(here, part, near, far, scatter_sems, back, 4)
    next(row_sum)
    next(row_sum)
    tick()
    gain = gains[0:1, :]
    high, low = split_two(gain_sum[0:1, :] / gain)
    row = iota((16, WIDTH), 0)
    both = jnp.where(row == 0, high.astype(F32), 0.0) + jnp.where(row == 1, low.astype(F32), 0.0)
    pick = (iota((16, LANES), 1) == 0).astype(BF)
    single = (grad_misc[...] + mm_tn(both.astype(BF), pick)).astype(BF)
    grad_out[:, :, :, :, Q_COLS:] = single.reshape(4, 4, 2, SHARD, LANES)
    sum_out = scatter_grad(here, blocks_of(grad_out, False), None, buffers[40:], piece_out, False, True)
    sums.append(summed(sum_out, piece_out, out_all, gather_sems.at[4]))

    def rows():
        yield from row_sum
        here.wait(far_out, out_sems.at[0])
        grad_normed = added(part[s], near[1], far[...])
        inverse, unit, _ = normed_of(tokens[...].astype(F32), gain)
        scaled = grad_normed * gain
        grad_tokens[...] = (grad_hidden[...] + inverse * (scaled - unit * jnp.mean(scaled * unit, axis=-1, keepdims=True))).astype(BF)

    together(*sums, rows())
    here.finish()


def as_row(col):
    n = col.shape[0]
    return jnp.sum(jnp.where(iota((n, n), 0) == iota((n, n), 1), jnp.broadcast_to(col, (n, n)), 0.0), axis=0, keepdims=True)


def outputs_kernel(
    ffn_a, ffn_b, q, kv, out, out_own, far_out, output, wq, wk, wv, wo, gain_one, gain_two, router, shared_gate, shared_up, shared_down, expert_gate, expert_up, expert_down
):
    output[...] = added(out_own[...], far_out[...]).astype(BF)
    total = jnp.zeros((SHARD, LANES), F32)
    for s in range(SEQ):
        wq[:, s * Q_COLS : (s + 1) * Q_COLS] = q[s].astype(F32)
        wo[:, s * Q_COLS : (s + 1) * Q_COLS] = out[s, :, :Q_COLS].astype(F32)
        wk[:, s * HEAD : (s + 1) * HEAD] = kv[s, :, :HEAD].astype(F32)
        wv[:, s * HEAD : (s + 1) * HEAD] = kv[s, :, HEAD:].astype(F32)
        total = total + out[s, :, Q_COLS:].astype(F32)
        for k, ffn in enumerate((ffn_a, ffn_b)):
            n = 2 * s + k
            for i, (shared, expert) in enumerate(((shared_gate, expert_gate), (shared_up, expert_up), (shared_down, expert_down))):
                expert[:, n, :] = ffn[s, :, i * HALF : i * HALF + 512].astype(F32)
                shared[:, n * LANES : (n + 1) * LANES] = ffn[s, :, i * HALF + 512 : (i + 1) * HALF].astype(F32)
    gain_one[...] = as_row(total[:, 0:1])
    gain_two[...] = as_row(total[:, 1:2])
    for e in range(E):
        router[e : e + 1, :] = as_row(total[:, 2 + e : 3 + e])


def remote_call(kernel, name, number, outs, ins, scratch):
    return pl.pallas_call(
        kernel,
        out_shape=[jax.ShapeDtypeStruct(dims, dtype) for dims, dtype, _ in outs],
        in_specs=[VMEM_ALL if fast else ANY for _, fast in ins],
        out_specs=[VMEM_ALL if fast else ANY for _, _, fast in outs],
        scratch_shapes=list(scratch),
        compiler_params=pltpu.CompilerParams(collective_id=number, has_side_effects=True, vmem_limit_bytes=LIMIT),
        name=name,
    )(*[array for array, _ in ins])


def buf(*dims):
    return pltpu.VMEM(dims, BF)


def buf32(*dims):
    return pltpu.VMEM(dims, F32)


def body(
    tokens,
    segments,
    routes,
    shared_mask,
    norm_gain,
    w_query,
    key_weight,
    value_weight,
    w_out,
    ffn_gain,
    w_router,
    shared_gate,
    shared_up,
    shared_down,
    expert_gate,
    expert_up,
    expert_down,
    cotangent,
):
    seg_row = segments[None, :]
    grid = DMA((4, 4, 2))
    rows4 = (SEQ, ROWS, WIDTH)
    fast = [tokens, routes.T, shared_mask[None, :], norm_gain[None, :], ffn_gain[None, :], w_router.T, w_query, key_weight,
            value_weight, w_out, shared_gate, shared_up, shared_down, expert_gate, expert_up, expert_down, seg_row]
    (
        normed_one, qkv, heads, logs, gains, qkv_full, out_full, normed_two, all_cot,
        pre_a, pre_b, low_home, grad_hidden, grad_misc, out_far, out_own,
    ) = remote_call(
        forward_kernel,
        "forward",
        1,
        [
            ((L, WIDTH), BF, False),
            ((L, HALF), BF, False),
            ((L, Q_COLS), BF, False),
            ((L, 8), F32, False),
            ((8, WIDTH), F32, True),
            (blocks(HALF), BF, False),
            (blocks(OUT_COLS), BF, False),
            (rows4, BF, False),
            (rows4, BF, False),
            ((L, FFN), BF, False),
            ((L, FFN), BF, False),
            ((ROWS, WIDTH), BF, False),
            ((ROWS, WIDTH), F32, False),
            ((WIDTH, LANES), F32, True),
            ((ROWS, WIDTH), BF, False),
            ((ROWS, WIDTH), F32, False),
        ],
        [(a, True) for a in fast] + [(cotangent, False)],
        [
            buf(ROWS, WIDTH + LANES),
            buf(SEQ, ROWS, WIDTH + LANES),
            buf(SHARD, HALF),
            buf(SHARD, OUT_COLS),
            buf(SHARD, FFN),
            buf(SHARD, FFN),
            buf(*blocks(HALF)),
            buf(*blocks(OUT_COLS)),
            buf(L, WIDTH),
            buf(L, HALF),
            buf(L, Q_COLS),
            buf32(L, 8),
            buf32(L, 1),
            buf(L, LANES),
            buf(WIDTH, LANES),
            buf(*rows4),
            buf(2, ROWS, WIDTH),
            buf(ROWS, WIDTH),
            buf(ROWS, WIDTH),
            buf32(ROWS, WIDTH),
            buf(*rows4),
            buf(*rows4),
            buf(*blocks(FFN)),
            buf(*blocks(FFN)),
            buf(2, 2, ROWS, FFN),
            buf(2, ROWS, WIDTH + LANES),
            buf(ROWS, WIDTH + LANES),
            buf(2, ROWS, WIDTH),
            buf32(ROWS, LANES),
            buf32(ROWS, WIDTH),
            DMA((160,)),
            DMA((4,)),
            grid,
            grid,
            grid,
            grid,
            DMA((4,)),
            DMA((3,)),
            DMA((4,)),
            DMA((4,)),
            DMA((3,)),
            DMA((2,)),
            DMA((24,)),
        ],
    )

    far_out, grad_tokens, _, _, ffn_a_all, ffn_b_all, q_all, kv_all, out_all = remote_call(
        finish_kernel,
        "finish",
        2,
        [
            ((ROWS, WIDTH), BF, False),
            ((ROWS, WIDTH), BF, True),
            ((WIDTH, FFN), BF, False),
            ((WIDTH, FFN), BF, False),
            ((SEQ, SHARD, FFN), BF, False),
            ((SEQ, SHARD, FFN), BF, False),
            ((SEQ, SHARD, Q_COLS), BF, False),
            ((SEQ, SHARD, 2 * HEAD), BF, False),
            ((SEQ, SHARD, OUT_COLS), BF, False),
        ],
        [
            (low_home, False),
            (normed_two.reshape(L, WIDTH), False),
            (all_cot, False),
            (pre_a, False),
            (pre_b, False),
            (normed_one, False),
            (qkv, False),
            (heads, False),
            (logs, False),
            (qkv_full.reshape(WIDTH, HALF), False),
            (out_full.reshape(WIDTH, OUT_COLS), False),
            (out_far, False),
            (seg_row, True),
            (gains, True),
            (grad_misc, True),
            (grad_hidden, True),
            (tokens, True),
        ],
        [
            buf(*rows4),
            buf(L, WIDTH),
            buf(*rows4),
            buf(L, FFN),
            buf(L, FFN),
            buf(2, CHUNK, FFN),
            buf(L, HALF),
            buf(L, Q_COLS),
            buf32(L, 8),
            buf(WIDTH, HALF),
            buf(WIDTH, OUT_COLS),
            buf(*blocks(Q_COLS)),
            buf(*blocks(2 * HEAD)),
            buf(*blocks(OUT_COLS)),
            buf(L, Q_COLS),
            buf(L, HALF),
            buf32(L, 2 * HEAD),
            buf(2, ROWS, WIDTH),
            buf(ROWS, WIDTH),
            buf32(16, WIDTH),
            buf32(L, 1),
            buf(SHARD, FFN),
            buf(SHARD, FFN),
            buf(SHARD, Q_COLS),
            buf(SHARD, 2 * HEAD),
            buf(SHARD, OUT_COLS),
            DMA((192,)),
            DMA((56,)),
            DMA((3,)),
            DMA((1,)),
            DMA((5, 4)),
            DMA((4,)),
            *scatter_buffers(FFN),
            *scatter_buffers(FFN),
            *scatter_buffers(Q_COLS),
            *scatter_buffers(2 * HEAD),
            *scatter_buffers(OUT_COLS),
        ],
    )

    dims = [(ROWS, WIDTH), (SHARD, 4 * Q_COLS), (SHARD, 4 * HEAD), (SHARD, 4 * HEAD), (SHARD, 4 * Q_COLS), (1, SHARD), (1, SHARD), (E, SHARD)]
    dims += [(SHARD, 1024)] * 3 + [(SHARD, E, 512)] * 3
    output, wq, wk, wv, wo, gain_one, gain_two, router, *ffn = pl.pallas_call(
        outputs_kernel,
        out_shape=[jax.ShapeDtypeStruct(d, BF if d[0] == ROWS else F32) for d in dims],
        in_specs=[VMEM_ALL] * 7,
        out_specs=[VMEM_ALL] * len(dims),
        compiler_params=pltpu.CompilerParams(vmem_limit_bytes=LIMIT),
        name="outputs",
    )(ffn_a_all, ffn_b_all, q_all, kv_all, out_all, out_own, far_out)
    return (output, grad_tokens, gain_one[0], wq, wk, wv, wo, gain_two[0], router.T, *ffn)


def solution(mesh):
    both = P(("fsdp", "seq"), None)
    one, two, three = P("fsdp"), P("fsdp", None), P("fsdp", None, None)
    return jax.shard_map(
        body,
        mesh=mesh,
        in_specs=(both, one, both, P(("fsdp", "seq")), one, two, two, two, two, one, two, two, two, two, three, three, three, both),
        out_specs=(both, both, one, two, two, two, two, one, two, two, two, two, three, three, three),
        check_vma=False,
    )
```

```python
import jax
import jax.numpy as jnp
from jax import lax
from jax.experimental import pallas as pl
from jax.experimental.pallas import tpu as pltpu
from jax.sharding import PartitionSpec as P

HEAD = 128
GROUP = 3
E = 8
SEQ = 4
EPS = 1e-05
BF = jnp.bfloat16
F32 = jnp.float32
WIDTH = 1536
L = 1024
ROWS = 256
SHARD = 48
Q_COLS = GROUP * HEAD
KV = Q_COLS + HEAD
HALF = 640
FFN = 3 * HALF
LANES = 128
OUT_COLS = Q_COLS + LANES
LOW = 32
CHUNK = 384
SCALE = HEAD ** (-0.5)
BIG = -1e30
MESH = pl.DeviceIdType.MESH
VMEM_ALL = pl.BlockSpec(memory_space=pltpu.VMEM)
ANY = pl.BlockSpec(memory_space=pl.ANY)
DMA = pltpu.SemaphoreType.DMA
LIMIT = 63 * 1024 * 1024


def f32dot(left, right, dims):
    return lax.dot_general(left, right, (dims, ((), ())), preferred_element_type=F32)


def mm(left, right):
    return f32dot(left, right, ((1,), (0,)))


def mm_nt(left, right):
    return f32dot(left, right, ((1,), (1,)))


def mm_tn(left, right):
    return f32dot(left, right, ((0,), (0,)))


def iota(dims, axis):
    return lax.broadcasted_iota(jnp.int32, dims, axis)


def column(row):
    n = row.shape[1]
    same = iota((n, n), 0) == iota((n, n), 1)
    return jnp.sum(jnp.where(same, jnp.broadcast_to(row, (n, n)), 0.0), axis=-1, keepdims=True)


def added(*values):
    total = values[0].astype(F32)
    for value in values[1:]:
        total = total + value.astype(F32)
    return total


def split_two(value):
    high = value.astype(BF)
    return high, (value - high.astype(F32)).astype(BF)


def normed_of(x, gain):
    inverse = lax.rsqrt(jnp.mean(x * x, axis=-1, keepdims=True) + EPS)
    unit = x * inverse
    return inverse, unit, (unit * gain).astype(BF)


def wrap(value):
    return lax.rem(value + 4, 4)


def blocks(cols):
    return (4, 4, 2, SHARD, cols)


class Here:
    def __init__(self, send_sems):
        f, s = lax.axis_index("fsdp"), lax.axis_index("seq")
        self.y, self.x, self.z = lax.div(f, 8), lax.rem(lax.div(f, 2), 4), lax.rem(f, 2)
        self.s, self.zh, self.core = s, lax.div(s, 2), lax.rem(s, 2)
        y, x, z = self.y, self.x, self.z
        self.axis_x = ({"fsdp": self.number(y, wrap(x + 1), z)}, {"fsdp": self.number(y, wrap(x - 1), z)})
        self.axis_y = ({"fsdp": self.number(wrap(y + 1), x, z)}, {"fsdp": self.number(wrap(y - 1), x, z)})
        self.pair = {"fsdp": self.number(y, x, 1 - z)}
        self.s_far = (1 - self.zh) * 2 + self.core
        self.s_near = self.zh * 2 + 1 - self.core
        self.s_cross = (1 - self.zh) * 2 + 1 - self.core
        self.far = {"seq": self.s_far}
        self.near = {"seq": self.s_near}
        self.sems, self.count, self.sent, self.row_sent = send_sems, 0, [], []

    @staticmethod
    def number(y, x, z):
        return (y * 4 + x) * 2 + z

    def greet(self):
        partners = [*self.axis_x, *self.axis_y, self.pair, self.far, self.near]
        for partner in partners:
            pl.semaphore_signal(pltpu.get_barrier_semaphore(), inc=1, device_id=partner, device_id_type=MESH)

    def meet(self):
        pl.semaphore_wait(pltpu.get_barrier_semaphore(), 7)

    def send(self, source, target, recv_sem, to, rows=False):
        copy = pltpu.make_async_remote_copy(
            src_ref=source,
            dst_ref=target,
            send_sem=self.sems.at[self.count],
            recv_sem=recv_sem,
            device_id=to,
            device_id_type=MESH,
        )
        copy.start()
        self.count += 1
        (self.row_sent if rows else self.sent).append(copy)

    def wait(self, target, recv_sem):
        pltpu.make_async_remote_copy(
            src_ref=target,
            dst_ref=target,
            send_sem=self.sems.at[0],
            recv_sem=recv_sem,
            device_id=self.near,
            device_id_type=MESH,
        ).wait_recv()

    def finish(self, most=None):
        for copy in self.sent[:most]:
            copy.wait_send()
        self.sent = [] if most is None else self.sent[most:]

    def finish_rows(self):
        for copy in self.row_sent:
            copy.wait_send()
        self.row_sent = []


class Local:
    def __init__(self, sems):
        self.sems, self.count = sems, 0

    def copy(self, source, target):
        copy = pltpu.make_async_copy(source, target, self.sems.at[self.count])
        copy.start()
        self.count += 1
        return copy


def together(*parts):
    left = list(parts)
    while left:
        for part in list(left):
            if next(part, "end") == "end":
                left.remove(part)


def later(turns, parts):
    for _ in range(turns):
        yield
    for part in parts:
        next(part)


def gather_weight(here, full, block, recv, own_sem, x_first):
    first, second = (here.axis_x, here.axis_y) if x_first else (here.axis_y, here.axis_x)

    def spot(df, ds, r):
        dy, dx = (ds, df) if x_first else (df, ds)
        return wrap(here.y + dy), wrap(here.x + dx), here.z if r == 0 else 1 - here.z

    def push(df, ds, r, to, source=None):
        at = spot(df, ds, r)
        here.send(full.at[at] if source is None else source, full.at[at], recv.at[at], to)

    def take(df, ds, r):
        at = spot(df, ds, r)
        here.wait(full.at[at], recv.at[at])

    own = pltpu.make_async_copy(block, full.at[spot(0, 0, 0)], own_sem)
    own.start()
    push(0, 0, 0, here.pair, block)
    yield
    for to in (*second, *first):
        push(0, 0, 0, to, block)
    yield
    take(0, 0, 1)
    for to in (*first, *second):
        push(0, 0, 1, to)
    for df, r in ((-1, 0), (1, 0), (1, 1), (-1, 1), (2, 0), (2, 1)):
        yield
        take(df, 0, r)
        if (df, r) == (-1, 0):
            push(df, 0, r, first[0])
        if (df, r) == (1, 1):
            push(df, 0, r, first[1])
        for to in second:
            push(df, 0, r, to)
        if (df, r) == (1, 0):
            take(0, -1, 0)
            push(0, -1, 0, second[0])
        if (df, r) == (-1, 1):
            take(0, 1, 1)
            push(0, 1, 1, second[1])
    for df in (-1, 1, 2):
        yield
        take(df, -1, 0)
        push(df, -1, 0, second[0])
        yield
        take(df, 1, 1)
        push(df, 1, 1, second[1])
    yield
    for df in (0, -1, 1, 2):
        take(df, -1, 1)
        take(df, 1, 0)
        take(df, 2, 0)
        take(df, 2, 1)
    own.wait()


def scatter_buffers(cols):
    units = [(4,), (4,), (4, 2), (4, 2), (1,), (1,), (2,), (2,), (1,)]
    return [pltpu.VMEM((*u, SHARD, cols), BF) for u in units] + [DMA((31,))]


def scatter_grad(here, block, own, buffers, piece, y_first, small):
    ra, rb, rc, rd, xa, xb, xc, xd, zr, sems = buffers
    second, first = (here.axis_y, here.axis_x) if y_first else (here.axis_x, here.axis_y)
    own = own or (lambda df, ds, h: block(df, ds, h)[...])

    def far_send(j):
        here.send(block(j, 2, 0), ra.at[j], sems.at[j], second[0])
        here.send(block(j, 2, 1), rb.at[j], sems.at[4 + j], second[1])

    def near_plus(j):
        here.send(block(j, 1, 1), rc.at[j, 1], sems.at[8 + 2 * j + 1], second[0])

    def near_minus(j):
        here.send(block(j, 3, 0), rd.at[j, 0], sems.at[16 + 2 * j], second[1])

    def pass_on(j):
        here.wait(ra.at[j], sems.at[j])
        ra[j] = added(own(j, 1, 0), ra[j]).astype(BF)
        here.send(ra.at[j], rc.at[j, 0], sems.at[8 + 2 * j], second[0])
        here.wait(rb.at[j], sems.at[4 + j])
        rb[j] = added(own(j, 3, 1), rb[j]).astype(BF)
        here.send(rb.at[j], rd.at[j, 1], sems.at[16 + 2 * j + 1], second[1])

    def total(j):
        for h in range(2):
            here.wait(rc.at[j, h], sems.at[8 + 2 * j + h])
            here.wait(rd.at[j, h], sems.at[16 + 2 * j + h])
            rc[j, h] = added(own(j, 0, h), rc[j, h], rd[j, h]).astype(BF)

    def turn_two():
        here.send(rc.at[2, 0], xa.at[0], sems.at[24], first[0])
        here.send(rc.at[2, 1], xb.at[0], sems.at[25], first[1])

    def turn_near():
        here.send(rc.at[1, 1], xc.at[1], sems.at[27], first[0])
        here.send(rc.at[3, 0], xd.at[0], sems.at[28], first[1])

    def turn_on():
        here.wait(xa.at[0], sems.at[24])
        xa[0] = added(rc[1, 0], xa[0]).astype(BF)
        here.send(xa.at[0], xc.at[0], sems.at[26], first[0])
        here.wait(xb.at[0], sems.at[25])
        xb[0] = added(rc[3, 1], xb[0]).astype(BF)
        here.send(xb.at[0], xd.at[1], sems.at[29], first[1])

    every = (2, 1, 3, 0)
    if small:
        for j in every:
            far_send(j)
            near_plus(j)
            near_minus(j)
        yield
        for j in every:
            pass_on(j)
        yield
        total(2)
        turn_two()
        total(1)
        total(3)
        turn_near()
        yield
        turn_on()
        total(0)
        yield
    else:
        if y_first:
            for send in (far_send, near_plus, near_minus):
                for j in every:
                    send(j)
                yield
        else:
            for j in every:
                far_send(j)
                near_plus(j)
                near_minus(j)
                yield
        if y_first:
            yield
        pass_on(2)
        pass_on(1)
        yield
        pass_on(3)
        pass_on(0)
        yield
        total(2)
        turn_two()
        yield
        total(1)
        total(3)
        turn_near()
        yield
        total(0)
        yield
        turn_on()
        yield
    for h in range(2):
        here.wait(xc.at[h], sems.at[26 + h])
        here.wait(xd.at[h], sems.at[28 + h])
        xc[h] = added(rc[0, h], xc[h], xd[h]).astype(BF)
    here.send(xc.at[1 - here.z], zr.at[0], sems.at[30], here.pair)
    yield
    here.wait(zr.at[0], sems.at[30])
    piece[...] = added(xc[here.z], zr[0]).astype(piece.dtype)


def seq_gather(here, source, full, sems, pause=1):
    own = pltpu.make_async_copy(source, full.at[here.s], sems.at[3])
    own.start()
    here.send(source, full.at[here.s], sems.at[0], here.far, True)
    here.send(source, full.at[here.s], sems.at[1], here.near, True)
    for _ in range(pause):
        yield
    here.wait(full.at[here.s_far], sems.at[0])
    here.send(full.at[here.s_far], full.at[here.s_far], sems.at[2], here.near, True)
    yield
    here.wait(full.at[here.s_near], sems.at[1])
    here.wait(full.at[here.s_cross], sems.at[2])
    own.wait()


def seq_scatter(here, parts, near, far, sems, make, pause=1):
    make(here.s_cross)
    here.send(parts.at[here.s_cross], near.at[0], sems.at[0], here.near, True)
    make(here.s_far)
    yield
    here.wait(near.at[0], sems.at[0])
    near[0] = added(parts[here.s_far], near[0]).astype(BF)
    here.send(near.at[0], far, sems.at[2], here.far, True)
    make(here.s_near)
    here.send(parts.at[here.s_near], near.at[1], sems.at[1], here.near, True)
    make(here.s)
    yield
    here.wait(near.at[1], sems.at[1])
    for _ in range(pause):
        yield
    here.wait(far, sems.at[2])


def masked(scores, at, kv_len, seg_col, seg_row):
    q_pos = at + iota((ROWS, kv_len), 0)
    k_pos = iota((ROWS, kv_len), 1)
    keep = (q_pos >= k_pos) & (seg_col[at : at + ROWS, :] == seg_row[:, :kv_len])
    return jnp.where(keep, scores, BIG)


def set_segments(seg_row, seg_col):
    for b in range(L // ROWS):
        at = slice(b * ROWS, (b + 1) * ROWS)
        seg_col[at, :] = column(seg_row[:, at].astype(F32))


def forward_kernel(
    tokens, routes, shared_mask, norm_gain, ffn_gain, w_router, w_query, key_weight, value_weight, w_out,
    shared_gate, shared_up, shared_down, expert_gate, expert_up, expert_down, segments, cot,
    normed_one, qkv_out, heads_out, logs_out, gains, qkv_full_out, out_full_out, normed_two, all_cot,
    pre_a, pre_b, low_home, grad_hidden, grad_misc, out_far, out_own,
    marked, all_marked, qkv_block, out_block, block_a, block_b, qkv_full, out_full, normed, qkv, heads, logs, seg_col,
    marks, misc, part, near, far, normed_home, hidden, xs, cs, full_a, full_b,
    staged, near_g, far_g, near_out, own_gates, own_out,
    send_sems, token_sems, qkv_sems, out_sems, a_sems, b_sems, own_sems, scatter_sems, gather_sems, cot_sems,
    grad_sems, sum_sems, local_sems,
):
    here = Here(send_sems)
    local = Local(local_sems)
    here.greet()
    s = here.s

    def wide(ref, at, width):
        return ref[:, pl.ds(pl.multiple_of(at * width, LANES), width)]

    marked[:, :WIDTH] = tokens[...]
    line = iota((LANES, ROWS), 0)
    used = line == routes[0:1, :] + 2
    for k in range(1, 6):
        used = used | (line == routes[k : k + 1, :] + 2)
    turned = (jnp.where(used, 1.0, 0.0) + jnp.where(line == 1, shared_mask[...].astype(F32), 0.0)).astype(BF)
    eye = (iota((LANES, LANES), 0) == iota((LANES, LANES), 1)).astype(BF)
    marked[:, WIDTH:] = mm_tn(turned, eye).astype(BF)
    token_gather = seq_gather(here, marked, all_marked, token_sems, 13)
    qkv_block[:, :Q_COLS] = wide(w_query, s, Q_COLS)
    qkv_block[:, Q_COLS:KV] = wide(key_weight, s, HEAD)
    qkv_block[:, KV:] = wide(value_weight, s, HEAD)
    here.meet()
    qkv_gather = gather_weight(here, qkv_full, qkv_block, qkv_sems, own_sems.at[0], True)
    next(qkv_gather)
    out_block[:, :Q_COLS] = wide(w_out, s, Q_COLS)
    place = (iota((E, LANES), 1) == iota((E, LANES), 0) + 2).astype(F32)
    single = f32dot(w_router[...].astype(F32), place, ((0,), (0,)))
    lane = iota((SHARD, LANES), 1)
    single = single + jnp.where(lane == 0, column(norm_gain[...].astype(F32)), 0.0)
    out_block[:, Q_COLS:] = (single + jnp.where(lane == 1, column(ffn_gain[...].astype(F32)), 0.0)).astype(BF)
    out_gather = gather_weight(here, out_full, out_block, out_sems, own_sems.at[1], False)
    next(out_gather)
    next(token_gather)
    next(qkv_gather)
    next(out_gather)
    for k, block in enumerate((block_a, block_b)):
        pick = (iota((SHARD, SHARD * E), 1) == iota((SHARD, SHARD * E), 0) * E + 2 * s + k).astype(BF)
        for i, (shared, expert) in enumerate(((shared_gate, expert_gate), (shared_up, expert_up), (shared_down, expert_down))):
            block[:, i * HALF : i * HALF + 512] = mm(pick, expert[...].reshape(SHARD * E, 512)).astype(BF)
            block[:, i * HALF + 512 : (i + 1) * HALF] = wide(shared, 2 * s + k, HALF - 512)
    set_segments(segments, seg_col)
    weights = [
        gather_weight(here, full_a, block_a, a_sems, own_sems.at[2], True),
        gather_weight(here, full_b, block_b, b_sems, own_sems.at[3], False),
    ]
    for weight in weights:
        next(weight)
    together(token_gather, qkv_gather, out_gather, later(9, weights))

    def tick():
        for weight in weights:
            next(weight, None)

    cot_gather = seq_gather(here, cot, cs, cot_sems)
    next(cot_gather)
    misc[...] = out_full[:, :, :, :, Q_COLS:].reshape(WIDTH, LANES)
    gains[...] = mm_nt(eye, misc[...])[:8]
    gain = gains[0:1, :]
    seg_row = segments[...].astype(F32)
    for b in range(SEQ):
        at = slice(b * ROWS, (b + 1) * ROWS)
        normed[at, :] = normed_of(all_marked[b, :, :WIDTH].astype(F32), gain)[2]
        qkv[at, :] = mm(normed[at, :], qkv_full[...].reshape(WIDTH, HALF)).astype(BF)
        marks[at, :] = all_marked[b, :, WIDTH:]
        if b == 3:
            tick()
    saved = [local.copy(normed, normed_one), local.copy(qkv, qkv_out), local.copy(qkv_full, qkv_full_out)]
    saved.append(local.copy(out_full, out_full_out))
    for b in range(SEQ):
        at, kv_len = b * ROWS, (b + 1) * ROWS
        for h in range(GROUP):
            cols = slice(h * HEAD, (h + 1) * HEAD)
            scores = mm_nt(qkv[at : at + ROWS, cols], qkv[:kv_len, Q_COLS:KV]) * SCALE
            scores = masked(scores, at, kv_len, seg_col, seg_row)
            top = jnp.max(scores, axis=-1, keepdims=True)
            weight = jnp.exp(scores - top)
            total = jnp.sum(weight, axis=-1, keepdims=True)
            probs = (weight * (1.0 / total)).astype(BF)
            heads[at : at + ROWS, cols] = mm(probs, qkv[:kv_len, KV:]).astype(BF)
            logs[at : at + ROWS, h : h + 1] = top + jnp.log(total)
        tick()

    saved += [local.copy(heads, heads_out), local.copy(logs, logs_out)]

    def project(i):
        rows = heads[pl.ds(pl.multiple_of(i * ROWS, ROWS), ROWS), :]
        part[i] = mm_nt(rows, out_full[:, :, :, :, :Q_COLS].reshape(WIDTH, Q_COLS)).astype(BF)

    def rows():
        yield from seq_scatter(here, part, near, far, scatter_sems, project, 2)
        next(cot_gather)
        hidden[...] = added(tokens[...], part[s], near[1], far[...])
        normed_home[...] = normed_of(hidden[...], gains[1:2, :])[2]
        yield from seq_gather(here, normed_home, xs, gather_sems, 3)
        next(cot_gather, None)

    together(rows(), *weights)
    for copy in saved:
        copy.wait()
    saved = [local.copy(xs, normed_two), local.copy(cs, all_cot)]
    here.finish_rows()
    order = (here.s_cross, here.s_far, here.s_near, s)
    sent, outs, far_sum, low_out = all_marked, part, far, normed_home
    lane = iota((ROWS, LANES), 1)
    stored = [[], []]

    def block(n):
        i = order[n]
        at = pl.ds(pl.multiple_of(i * ROWS, ROWS), ROWS)
        x, c = xs[i], cs[i]
        mark = marks[at, :].astype(F32)
        member = (mark > 0) & (lane >= 2) & (lane < 2 + E)
        logits = jnp.where(member, mm(x, misc[...]), BIG)
        soft = jnp.where(member, jnp.exp(logits - jnp.max(logits, axis=-1, keepdims=True)), 0.0)
        gates = soft / jnp.sum(soft, axis=-1, keepdims=True)
        if n == 3:
            own_gates[...] = gates
        keep = mark[:, 1:2]
        total = jnp.zeros((ROWS, WIDTH), F32)
        grad_x = jnp.zeros((ROWS, WIDTH), F32)
        grad_marks = jnp.zeros((ROWS, LANES), F32)
        for k, weight in enumerate((full_a, full_b)):
            if n >= 2:
                stored[k][n - 2].wait()
            slot = staged.at[n % 2, k]
            mine = lane == 2 + 2 * s + k
            gate_e = jnp.sum(jnp.where(mine, gates, 0.0), axis=-1, keepdims=True)
            coef = jnp.concatenate([jnp.broadcast_to(gate_e, (ROWS, 512)), jnp.broadcast_to(keep, (ROWS, HALF - 512))], axis=1)
            pre = mm(x, weight[:, :, :, :, : 2 * HALF].reshape(WIDTH, 2 * HALF))
            gate, upper = pre[:, :HALF], pre[:, HALF:]
            sigma = 1.0 / (1.0 + jnp.exp(-gate))
            silu = gate * sigma
            units = silu * upper
            weighted = (coef * units).astype(BF)
            slot[:, 2 * HALF :] = weighted
            total += mm_nt(weighted, weight[:, :, :, :, 2 * HALF :].reshape(WIDTH, HALF))
            grad_units = mm(c, weight[:, :, :, :, 2 * HALF :].reshape(WIDTH, HALF))
            grad_gate = jnp.sum((units * grad_units)[:, :512], axis=-1, keepdims=True)
            high = grad_gate.astype(BF).astype(F32)
            grad_marks += jnp.where(mine, high, 0.0) + jnp.where(lane == LOW + 2 + 2 * s + k, grad_gate - high, 0.0)
            grad_units = coef * grad_units
            slot[:, :HALF] = (grad_units * upper * (sigma * (1.0 + gate * (1.0 - sigma)))).astype(BF)
            slot[:, HALF : 2 * HALF] = (grad_units * silu).astype(BF)
            grad_x += mm_nt(slot[:, : 2 * HALF], weight[:, :, :, :, : 2 * HALF].reshape(WIDTH, 2 * HALF))
            stored[k].append(local.copy(slot, (pre_a, pre_b)[k].at[at]))
        outs[i] = total.astype(BF)
        sent[i, :, :WIDTH] = grad_x.astype(BF)
        sent[i, :, WIDTH:] = grad_marks.astype(BF)

    block(0)
    here.send(sent.at[here.s_cross], near_g.at[0], grad_sems.at[0], here.near, True)
    here.send(outs.at[here.s_cross], near_out.at[0], sum_sems.at[0], here.near, True)
    block(1)
    here.wait(near_g.at[0], grad_sems.at[0])
    near_g[0] = added(sent[here.s_far], near_g[0]).astype(BF)
    here.send(near_g.at[0], far_g, grad_sems.at[2], here.far, True)
    here.wait(near_out.at[0], sum_sems.at[0])
    far_sum[...] = added(outs[here.s_far], near_out[0]).astype(BF)
    saved.append(local.copy(far_sum, out_far))
    block(2)
    here.send(sent.at[here.s_near], near_g.at[1], grad_sems.at[1], here.near, True)
    here.send(outs.at[here.s_near], near_out.at[1], sum_sems.at[1], here.near, True)
    block(3)
    here.wait(near_g.at[1], grad_sems.at[1])
    here.wait(near_out.at[1], sum_sems.at[1])
    own_out[...] = added(hidden[...], outs[s], near_out[1])
    saved.append(local.copy(own_out, out_own))
    gain = gains[1:2, :]
    inverse, unit, normed_home = normed_of(hidden[...], gain)
    here.finish()
    here.wait(far_g, grad_sems.at[2])

    grad_gates = added(sent[s, :, WIDTH:], near_g[1, :, WIDTH:], far_g[:, WIDTH:])
    grad_gates = grad_gates + pltpu.roll(grad_gates, LANES - LOW, 1)
    gates = own_gates[...]
    grad_logits = gates * (grad_gates - jnp.sum(gates * grad_gates, axis=-1, keepdims=True))
    high, low = split_two(grad_logits)
    grad_normed = added(sent[s, :, :WIDTH], near_g[1, :, :WIDTH], far_g[:, :WIDTH])
    grad_normed = grad_normed + (mm_nt(high, misc[...]) + mm_nt(low, misc[...]))
    scaled = grad_normed * gain
    grad = cs[s].astype(F32) + inverse * (scaled - unit * jnp.mean(scaled * unit, axis=-1, keepdims=True))
    low_out[...] = grad.astype(BF)
    saved.append(local.copy(low_out, low_home))
    hidden[...] = grad
    saved.append(local.copy(hidden, grad_hidden))
    prod_high, prod_low = split_two(grad_normed * unit)
    one = (lane == 1).astype(BF)
    grad_misc[...] = mm_tn(normed_home, high) + mm_tn(normed_home, low) + mm_tn(prod_high, one) + mm_tn(prod_low, one)
    for copy in (*saved, *stored[0][2:], *stored[1][2:]):
        copy.wait()
    here.finish_rows()


def row_of(y, x, z):
    return pl.multiple_of(((y * 4 + x) * 2 + z) * SHARD, SHARD)


def finish_kernel(
    low_home, normed_two_in, cots_in, pre_a_in, pre_b_in,
    normed_in, qkv_in, heads_in, logs_in, qkv_full_in, out_full_in, out_far,
    segments, gains, grad_misc, grad_hidden, tokens,
    far_out, grad_tokens, grad_a, grad_b, ffn_a_all, ffn_b_all, q_all, kv_all, out_all,
    grad_low, normed, part, pre_a, pre_b, staged, qkv, heads, logs, qkv_full, out_full,
    grad_q, grad_pair, grad_out, grad_heads, grad_all, grad_kv, near, far, gain_sum, seg_col,
    piece_a, piece_b, piece_q, piece_kv, piece_out,
    send_sems, local_sems, scatter_sems, out_sems, gather_sems, low_sems, *buffers,
):
    here = Here(send_sems)
    local = Local(local_sems)
    s = here.s
    load_a = [local.copy(normed_two_in, normed), local.copy(pre_a_in, pre_a), local.copy(cots_in, part)]
    load_b = local.copy(pre_b_in, pre_b)
    load_rest = [
        local.copy(a, b)
        for a, b in ((out_full_in, out_full), (heads_in, heads), (qkv_in, qkv), (logs_in, logs), (qkv_full_in, qkv_full))
    ]
    here.greet()
    here.meet()
    low_gather = seq_gather(here, low_home, grad_low, low_sems)
    next(low_gather)

    def summed(sum_of, piece, full, sems, pause=1):
        yield from sum_of
        yield from seq_gather(here, piece, full, sems, pause)

    def from_hbm(grad, y_first):
        def block(df, ds, h):
            dy, dx = (ds, df) if y_first else (df, ds)
            return grad.at[pl.ds(row_of(wrap(here.y + dy), wrap(here.x + dx), h), SHARD)]

        return block

    def own_unit(place, j, ds, h):
        at = wrap(place + j)
        return at * 2 + h if ds == 0 else (8 if ds == 1 else 12) + at

    def owned(held, place):
        def own(j, ds, h):
            return held[pl.ds(pl.multiple_of(own_unit(place, j, ds, h) * SHARD, SHARD), SHARD), :]

        return own

    sum_a = scatter_grad(here, from_hbm(grad_a, True), owned(pre_a, here.x), buffers[:10], piece_a, True, False)
    sum_b = scatter_grad(here, from_hbm(grad_b, False), owned(pre_b, here.y), buffers[10:20], piece_b, False, False)
    sums = [summed(sum_a, piece_a, ffn_a_all, gather_sems.at[0], 4), summed(sum_b, piece_b, ffn_b_all, gather_sems.at[1], 4)]

    def chunk(y):
        return pl.ds(pl.multiple_of(y * CHUNK, CHUNK), CHUNK)

    moving = []
    for n, (j, k) in enumerate((j, k) for j in (2, 1, 3, 0) for k in range(2)):
        pre = (pre_a, pre_b)[k]
        if n == 0:
            load_a[0].wait()
            load_a[1].wait()
        if n == 1:
            load_b.wait()
        at = chunk(wrap(here.y + j))
        slot = staged.at[n % 2]
        slot[:, : 2 * HALF] = mm_tn(normed[:, at], pre[:, : 2 * HALF]).astype(BF)
        if n == 0:
            load_a[2].wait()
        if n > 1:
            moving[n - 1].wait()
            next(sums[(n - 1) % 2])
        slot[:, 2 * HALF :] = mm_tn(part[:, :, at].reshape(L, CHUNK), pre[:, 2 * HALF :]).astype(BF)
        moving.append(local.copy(slot, (grad_a, grad_b)[k].at[at]))
        if n == 0:
            moving[0].wait()
            next(sums[0])
    moving[-1].wait()
    next(sums[1])
    load_own = []
    for grad, held, y_first in ((grad_a, pre_a, True), (grad_b, pre_b, False)):
        for i in range(4):
            for ds, h in ((0, 0), (0, 1), (1, 0), (3, 1)):
                y, x = (wrap(here.y + ds), i) if y_first else (i, wrap(here.x + ds))
                unit = i * 2 + h if ds == 0 else (8 if ds == 1 else 12) + i
                source = grad.at[pl.ds(row_of(y, x, h), SHARD)]
                load_own.append(local.copy(source, held.at[pl.ds(unit * SHARD, SHARD)]))
    load_rest.append(local.copy(normed_in, normed))
    here.send(out_far, far_out, out_sems.at[0], here.far, True)
    set_segments(segments, seg_col)
    seg_row = segments[...].astype(F32)
    next(low_gather)
    for load in load_own:
        load.wait()

    def tick():
        for part_sum in sums[:2]:
            next(part_sum)

    tick()
    next(low_gather, None)
    for load in load_rest:
        load.wait()
    for b in range(SEQ):
        at = slice(b * ROWS, (b + 1) * ROWS)
        grad_heads[at, :] = mm(grad_low[b], out_full[:, :Q_COLS]).astype(BF)

    def blocks_of(grad, y_first):
        def block(df, ds, h):
            dy, dx = (ds, df) if y_first else (df, ds)
            return grad.at[wrap(here.y + dy), wrap(here.x + dx), h]

        return block

    def out_chunk(y, carry):
        value = mm_tn(grad_low[:, :, chunk(y)].reshape(L, CHUNK), heads[...])
        grad_out[y, :, :, :, :Q_COLS] = value.astype(BF).reshape(4, 2, SHARD, Q_COLS)
        return carry

    lax.fori_loop(0, 4, out_chunk, 0)
    tick()
    grad_kv[...] = jnp.zeros_like(grad_kv)
    for b in range(SEQ):
        at, kv_len = b * ROWS, (b + 1) * ROWS
        for h in range(GROUP):
            cols = slice(h * HEAD, (h + 1) * HEAD)
            query, grad = qkv[at : at + ROWS, cols], grad_heads[at : at + ROWS, cols]
            scores = mm_nt(query, qkv[:kv_len, Q_COLS:KV]) * SCALE
            probs = jnp.exp(masked(scores, at, kv_len, seg_col, seg_row) - logs[at : at + ROWS, h : h + 1])
            grad_probs = mm_nt(grad, qkv[:kv_len, KV:])
            centre = jnp.sum(probs * grad_probs, axis=-1, keepdims=True)
            grad_scores = (probs * (grad_probs - centre)).astype(BF)
            grad_all[at : at + ROWS, cols] = (mm(grad_scores, qkv[:kv_len, Q_COLS:KV]) * SCALE).astype(BF)
            grad_kv[:kv_len, :HEAD] += mm_tn(grad_scores, query) * SCALE
            grad_kv[:kv_len, HEAD:] += mm_tn(probs.astype(BF), grad)
    tick()
    grad_all[:, Q_COLS:] = grad_kv[...].astype(BF)

    def q_chunk(y, carry):
        grad_q[y] = mm_tn(normed[:, chunk(y)], grad_all[:, :Q_COLS]).astype(BF).reshape(4, 2, SHARD, Q_COLS)
        return carry

    def weight_chunk(y, carry):
        at = chunk(y)
        value = mm_tn(normed[:, at], grad_all[...]).astype(BF)
        grad_q[y] = value[:, :Q_COLS].reshape(4, 2, SHARD, Q_COLS)
        grad_pair[y] = value[:, Q_COLS:].reshape(4, 2, SHARD, 2 * HEAD)
        return carry

    lax.fori_loop(0, 4, weight_chunk, 0)
    sum_q = scatter_grad(here, blocks_of(grad_q, True), None, buffers[20:30], piece_q, True, True)
    sums.append(summed(sum_q, piece_q, q_all, gather_sems.at[2]))
    sum_kv = scatter_grad(here, blocks_of(grad_pair, False), None, buffers[30:40], piece_kv, False, True)
    sums.append(summed(sum_kv, piece_kv, kv_all, gather_sems.at[3]))
    tick()
    gain_sum[...] = jnp.zeros_like(gain_sum)

    def back(i):
        at = pl.ds(pl.multiple_of(i * ROWS, ROWS), ROWS)
        value = mm_nt(grad_all[at, :], qkv_full[...])
        part[i] = value.astype(BF)
        gain_sum[0:1, :] += jnp.sum(value * normed[at, :].astype(F32), axis=0, keepdims=True)

    row_sum = seq_scatter(here, part, near, far, scatter_sems, back, 4)
    next(row_sum)
    next(row_sum)
    tick()
    gain = gains[0:1, :]
    high, low = split_two(gain_sum[0:1, :] / gain)
    row = iota((16, WIDTH), 0)
    both = jnp.where(row == 0, high.astype(F32), 0.0) + jnp.where(row == 1, low.astype(F32), 0.0)
    pick = (iota((16, LANES), 1) == 0).astype(BF)
    single = (grad_misc[...] + mm_tn(both.astype(BF), pick)).astype(BF)
    grad_out[:, :, :, :, Q_COLS:] = single.reshape(4, 4, 2, SHARD, LANES)
    sum_out = scatter_grad(here, blocks_of(grad_out, False), None, buffers[40:], piece_out, False, True)
    sums.append(summed(sum_out, piece_out, out_all, gather_sems.at[4]))

    def rows():
        yield from row_sum
        here.wait(far_out, out_sems.at[0])
        grad_normed = added(part[s], near[1], far[...])
        inverse, unit, _ = normed_of(tokens[...].astype(F32), gain)
        scaled = grad_normed * gain
        grad_tokens[...] = (grad_hidden[...] + inverse * (scaled - unit * jnp.mean(scaled * unit, axis=-1, keepdims=True))).astype(BF)

    here.finish(64)
    together(*sums, rows())
    here.finish()
    here.finish_rows()


def as_row(col):
    n = col.shape[0]
    return jnp.sum(jnp.where(iota((n, n), 0) == iota((n, n), 1), jnp.broadcast_to(col, (n, n)), 0.0), axis=0, keepdims=True)


def outputs_kernel(
    ffn_a, ffn_b, q, kv, out, out_own, far_out, output, wq, wk, wv, wo, gain_one, gain_two, router, shared_gate, shared_up, shared_down, expert_gate, expert_up, expert_down
):
    output[...] = added(out_own[...], far_out[...]).astype(BF)
    total = jnp.zeros((SHARD, LANES), F32)
    for s in range(SEQ):
        wq[:, s * Q_COLS : (s + 1) * Q_COLS] = q[s].astype(F32)
        wo[:, s * Q_COLS : (s + 1) * Q_COLS] = out[s, :, :Q_COLS].astype(F32)
        wk[:, s * HEAD : (s + 1) * HEAD] = kv[s, :, :HEAD].astype(F32)
        wv[:, s * HEAD : (s + 1) * HEAD] = kv[s, :, HEAD:].astype(F32)
        total = total + out[s, :, Q_COLS:].astype(F32)
        for k, ffn in enumerate((ffn_a, ffn_b)):
            n = 2 * s + k
            for i, (shared, expert) in enumerate(((shared_gate, expert_gate), (shared_up, expert_up), (shared_down, expert_down))):
                expert[:, n, :] = ffn[s, :, i * HALF : i * HALF + 512].astype(F32)
                shared[:, n * LANES : (n + 1) * LANES] = ffn[s, :, i * HALF + 512 : (i + 1) * HALF].astype(F32)
    gain_one[...] = as_row(total[:, 0:1])
    gain_two[...] = as_row(total[:, 1:2])
    for e in range(E):
        router[e : e + 1, :] = as_row(total[:, 2 + e : 3 + e])


def remote_call(kernel, name, number, outs, ins, scratch):
    return pl.pallas_call(
        kernel,
        out_shape=[jax.ShapeDtypeStruct(dims, dtype) for dims, dtype, _ in outs],
        in_specs=[VMEM_ALL if fast else ANY for _, fast in ins],
        out_specs=[VMEM_ALL if fast else ANY for _, _, fast in outs],
        scratch_shapes=list(scratch),
        compiler_params=pltpu.CompilerParams(collective_id=number, has_side_effects=True, vmem_limit_bytes=LIMIT),
        name=name,
    )(*[array for array, _ in ins])


def buf(*dims):
    return pltpu.VMEM(dims, BF)


def buf32(*dims):
    return pltpu.VMEM(dims, F32)


def body(
    tokens,
    segments,
    routes,
    shared_mask,
    norm_gain,
    w_query,
    key_weight,
    value_weight,
    w_out,
    ffn_gain,
    w_router,
    shared_gate,
    shared_up,
    shared_down,
    expert_gate,
    expert_up,
    expert_down,
    cotangent,
):
    seg_row = segments[None, :]
    grid = DMA((4, 4, 2))
    rows4 = (SEQ, ROWS, WIDTH)
    fast = [tokens, routes.T, shared_mask[None, :], norm_gain[None, :], ffn_gain[None, :], w_router.T, w_query, key_weight,
            value_weight, w_out, shared_gate, shared_up, shared_down, expert_gate, expert_up, expert_down, seg_row]
    (
        normed_one, qkv, heads, logs, gains, qkv_full, out_full, normed_two, all_cot,
        pre_a, pre_b, low_home, grad_hidden, grad_misc, out_far, out_own,
    ) = remote_call(
        forward_kernel,
        "forward",
        1,
        [
            ((L, WIDTH), BF, False),
            ((L, HALF), BF, False),
            ((L, Q_COLS), BF, False),
            ((L, 8), F32, False),
            ((8, WIDTH), F32, True),
            (blocks(HALF), BF, False),
            (blocks(OUT_COLS), BF, False),
            (rows4, BF, False),
            (rows4, BF, False),
            ((L, FFN), BF, False),
            ((L, FFN), BF, False),
            ((ROWS, WIDTH), BF, False),
            ((ROWS, WIDTH), F32, False),
            ((WIDTH, LANES), F32, True),
            ((ROWS, WIDTH), BF, False),
            ((ROWS, WIDTH), F32, False),
        ],
        [(a, True) for a in fast] + [(cotangent, False)],
        [
            buf(ROWS, WIDTH + LANES),
            buf(SEQ, ROWS, WIDTH + LANES),
            buf(SHARD, HALF),
            buf(SHARD, OUT_COLS),
            buf(SHARD, FFN),
            buf(SHARD, FFN),
            buf(*blocks(HALF)),
            buf(*blocks(OUT_COLS)),
            buf(L, WIDTH),
            buf(L, HALF),
            buf(L, Q_COLS),
            buf32(L, 8),
            buf32(L, 1),
            buf(L, LANES),
            buf(WIDTH, LANES),
            buf(*rows4),
            buf(2, ROWS, WIDTH),
            buf(ROWS, WIDTH),
            buf(ROWS, WIDTH),
            buf32(ROWS, WIDTH),
            buf(*rows4),
            buf(*rows4),
            buf(*blocks(FFN)),
            buf(*blocks(FFN)),
            buf(2, 2, ROWS, FFN),
            buf(2, ROWS, WIDTH + LANES),
            buf(ROWS, WIDTH + LANES),
            buf(2, ROWS, WIDTH),
            buf32(ROWS, LANES),
            buf32(ROWS, WIDTH),
            DMA((160,)),
            DMA((4,)),
            grid,
            grid,
            grid,
            grid,
            DMA((4,)),
            DMA((3,)),
            DMA((4,)),
            DMA((4,)),
            DMA((3,)),
            DMA((2,)),
            DMA((24,)),
        ],
    )

    far_out, grad_tokens, _, _, ffn_a_all, ffn_b_all, q_all, kv_all, out_all = remote_call(
        finish_kernel,
        "finish",
        2,
        [
            ((ROWS, WIDTH), BF, False),
            ((ROWS, WIDTH), BF, True),
            ((WIDTH, FFN), BF, False),
            ((WIDTH, FFN), BF, False),
            ((SEQ, SHARD, FFN), BF, False),
            ((SEQ, SHARD, FFN), BF, False),
            ((SEQ, SHARD, Q_COLS), BF, False),
            ((SEQ, SHARD, 2 * HEAD), BF, False),
            ((SEQ, SHARD, OUT_COLS), BF, False),
        ],
        [
            (low_home, False),
            (normed_two.reshape(L, WIDTH), False),
            (all_cot, False),
            (pre_a, False),
            (pre_b, False),
            (normed_one, False),
            (qkv, False),
            (heads, False),
            (logs, False),
            (qkv_full.reshape(WIDTH, HALF), False),
            (out_full.reshape(WIDTH, OUT_COLS), False),
            (out_far, False),
            (seg_row, True),
            (gains, True),
            (grad_misc, True),
            (grad_hidden, True),
            (tokens, True),
        ],
        [
            buf(*rows4),
            buf(L, WIDTH),
            buf(*rows4),
            buf(L, FFN),
            buf(L, FFN),
            buf(2, CHUNK, FFN),
            buf(L, HALF),
            buf(L, Q_COLS),
            buf32(L, 8),
            buf(WIDTH, HALF),
            buf(WIDTH, OUT_COLS),
            buf(*blocks(Q_COLS)),
            buf(*blocks(2 * HEAD)),
            buf(*blocks(OUT_COLS)),
            buf(L, Q_COLS),
            buf(L, HALF),
            buf32(L, 2 * HEAD),
            buf(2, ROWS, WIDTH),
            buf(ROWS, WIDTH),
            buf32(16, WIDTH),
            buf32(L, 1),
            buf(SHARD, FFN),
            buf(SHARD, FFN),
            buf(SHARD, Q_COLS),
            buf(SHARD, 2 * HEAD),
            buf(SHARD, OUT_COLS),
            DMA((192,)),
            DMA((56,)),
            DMA((3,)),
            DMA((1,)),
            DMA((5, 4)),
            DMA((4,)),
            *scatter_buffers(FFN),
            *scatter_buffers(FFN),
            *scatter_buffers(Q_COLS),
            *scatter_buffers(2 * HEAD),
            *scatter_buffers(OUT_COLS),
        ],
    )

    dims = [(ROWS, WIDTH), (SHARD, 4 * Q_COLS), (SHARD, 4 * HEAD), (SHARD, 4 * HEAD), (SHARD, 4 * Q_COLS), (1, SHARD), (1, SHARD), (E, SHARD)]
    dims += [(SHARD, 1024)] * 3 + [(SHARD, E, 512)] * 3
    output, wq, wk, wv, wo, gain_one, gain_two, router, *ffn = pl.pallas_call(
        outputs_kernel,
        out_shape=[jax.ShapeDtypeStruct(d, BF if d[0] == ROWS else F32) for d in dims],
        in_specs=[VMEM_ALL] * 7,
        out_specs=[VMEM_ALL] * len(dims),
        compiler_params=pltpu.CompilerParams(vmem_limit_bytes=LIMIT),
        name="outputs",
    )(ffn_a_all, ffn_b_all, q_all, kv_all, out_all, out_own, far_out)
    return (output, grad_tokens, gain_one[0], wq, wk, wv, wo, gain_two[0], router.T, *ffn)


def solution(mesh):
    both = P(("fsdp", "seq"), None)
    one, two, three = P("fsdp"), P("fsdp", None), P("fsdp", None, None)
    return jax.shard_map(
        body,
        mesh=mesh,
        in_specs=(both, one, both, P(("fsdp", "seq")), one, two, two, two, two, one, two, two, two, two, three, three, three, both),
        out_specs=(both, both, one, two, two, two, two, one, two, two, two, two, three, three, three),
        check_vma=False,
    )
```

```python
import jax
import jax.numpy as jnp
from jax import lax
from jax.experimental import pallas as pl
from jax.experimental.pallas import tpu as pltpu
from jax.sharding import PartitionSpec as P

HEAD = 128
GROUP = 3
E = 8
SEQ = 4
EPS = 1e-05
BF = jnp.bfloat16
F32 = jnp.float32
WIDTH = 1536
L = 1024
ROWS = 256
SHARD = 48
Q_COLS = GROUP * HEAD
KV = Q_COLS + HEAD
HALF = 640
FFN = 3 * HALF
LANES = 128
OUT_COLS = Q_COLS + LANES
LOW = 32
CHUNK = 384
SCALE = HEAD ** (-0.5)
BIG = -1e30
MESH = pl.DeviceIdType.MESH
VMEM_ALL = pl.BlockSpec(memory_space=pltpu.VMEM)
ANY = pl.BlockSpec(memory_space=pl.ANY)
DMA = pltpu.SemaphoreType.DMA
LIMIT = 63 * 1024 * 1024


def f32dot(left, right, dims):
    return lax.dot_general(left, right, (dims, ((), ())), preferred_element_type=F32)


def mm(left, right):
    return f32dot(left, right, ((1,), (0,)))


def mm_nt(left, right):
    return f32dot(left, right, ((1,), (1,)))


def mm_tn(left, right):
    return f32dot(left, right, ((0,), (0,)))


def iota(dims, axis):
    return lax.broadcasted_iota(jnp.int32, dims, axis)


def column(row):
    n = row.shape[1]
    same = iota((n, n), 0) == iota((n, n), 1)
    return jnp.sum(jnp.where(same, jnp.broadcast_to(row, (n, n)), 0.0), axis=-1, keepdims=True)


def added(*values):
    total = values[0].astype(F32)
    for value in values[1:]:
        total = total + value.astype(F32)
    return total


def split_two(value):
    high = value.astype(BF)
    return high, (value - high.astype(F32)).astype(BF)


def normed_of(x, gain):
    inverse = lax.rsqrt(jnp.mean(x * x, axis=-1, keepdims=True) + EPS)
    unit = x * inverse
    return inverse, unit, (unit * gain).astype(BF)


def wrap(value):
    return lax.rem(value + 4, 4)


def blocks(cols):
    return (4, 4, 2, SHARD, cols)


class Here:
    def __init__(self, send_sems):
        f, s = lax.axis_index("fsdp"), lax.axis_index("seq")
        self.y, self.x, self.z = lax.div(f, 8), lax.rem(lax.div(f, 2), 4), lax.rem(f, 2)
        self.s, self.zh, self.core = s, lax.div(s, 2), lax.rem(s, 2)
        y, x, z = self.y, self.x, self.z
        self.axis_x = ({"fsdp": self.number(y, wrap(x + 1), z)}, {"fsdp": self.number(y, wrap(x - 1), z)})
        self.axis_y = ({"fsdp": self.number(wrap(y + 1), x, z)}, {"fsdp": self.number(wrap(y - 1), x, z)})
        self.pair = {"fsdp": self.number(y, x, 1 - z)}
        self.s_far = (1 - self.zh) * 2 + self.core
        self.s_near = self.zh * 2 + 1 - self.core
        self.s_cross = (1 - self.zh) * 2 + 1 - self.core
        self.far = {"seq": self.s_far}
        self.near = {"seq": self.s_near}
        self.sems, self.count, self.sent, self.row_sent = send_sems, 0, [], []

    @staticmethod
    def number(y, x, z):
        return (y * 4 + x) * 2 + z

    def greet(self):
        partners = [*self.axis_x, *self.axis_y, self.pair, self.far, self.near]
        for partner in partners:
            pl.semaphore_signal(pltpu.get_barrier_semaphore(), inc=1, device_id=partner, device_id_type=MESH)

    def meet(self):
        pl.semaphore_wait(pltpu.get_barrier_semaphore(), 7)

    def send(self, source, target, recv_sem, to, rows=False):
        copy = pltpu.make_async_remote_copy(
            src_ref=source,
            dst_ref=target,
            send_sem=self.sems.at[self.count],
            recv_sem=recv_sem,
            device_id=to,
            device_id_type=MESH,
        )
        copy.start()
        self.count += 1
        (self.row_sent if rows else self.sent).append(copy)

    def wait(self, target, recv_sem):
        pltpu.make_async_remote_copy(
            src_ref=target,
            dst_ref=target,
            send_sem=self.sems.at[0],
            recv_sem=recv_sem,
            device_id=self.near,
            device_id_type=MESH,
        ).wait_recv()

    def finish(self, most=None):
        for copy in self.sent[:most]:
            copy.wait_send()
        self.sent = [] if most is None else self.sent[most:]

    def finish_rows(self):
        for copy in self.row_sent:
            copy.wait_send()
        self.row_sent = []


class Local:
    def __init__(self, sems):
        self.sems, self.count = sems, 0

    def copy(self, source, target):
        copy = pltpu.make_async_copy(source, target, self.sems.at[self.count])
        copy.start()
        self.count += 1
        return copy


def together(*parts):
    left = list(parts)
    while left:
        for part in list(left):
            if next(part, "end") == "end":
                left.remove(part)


def later(turns, parts):
    for _ in range(turns):
        yield
    for part in parts:
        next(part)


def gather_weight(here, full, block, recv, own_sem, x_first):
    first, second = (here.axis_x, here.axis_y) if x_first else (here.axis_y, here.axis_x)

    def spot(df, ds, r):
        dy, dx = (ds, df) if x_first else (df, ds)
        return wrap(here.y + dy), wrap(here.x + dx), here.z if r == 0 else 1 - here.z

    def push(df, ds, r, to, source=None):
        at = spot(df, ds, r)
        here.send(full.at[at] if source is None else source, full.at[at], recv.at[at], to)

    def take(df, ds, r):
        at = spot(df, ds, r)
        here.wait(full.at[at], recv.at[at])

    own = pltpu.make_async_copy(block, full.at[spot(0, 0, 0)], own_sem)
    own.start()
    push(0, 0, 0, here.pair, block)
    yield
    for to in (*second, *first):
        push(0, 0, 0, to, block)
    yield
    take(0, 0, 1)
    for to in (*first, *second):
        push(0, 0, 1, to)
    for df, r in ((-1, 0), (1, 0), (1, 1), (-1, 1), (2, 0), (2, 1)):
        yield
        take(df, 0, r)
        if (df, r) == (-1, 0):
            push(df, 0, r, first[0])
        if (df, r) == (1, 1):
            push(df, 0, r, first[1])
        for to in second:
            push(df, 0, r, to)
        if (df, r) == (1, 0):
            take(0, -1, 0)
            push(0, -1, 0, second[0])
        if (df, r) == (-1, 1):
            take(0, 1, 1)
            push(0, 1, 1, second[1])
    for df in (-1, 1, 2):
        yield
        take(df, -1, 0)
        push(df, -1, 0, second[0])
        yield
        take(df, 1, 1)
        push(df, 1, 1, second[1])
    yield
    for df in (0, -1, 1, 2):
        take(df, -1, 1)
        take(df, 1, 0)
        take(df, 2, 0)
        take(df, 2, 1)
    own.wait()


def scatter_buffers(cols):
    units = [(4,), (4,), (4, 2), (4, 2), (1,), (1,), (2,), (2,), (1,)]
    return [pltpu.VMEM((*u, SHARD, cols), BF) for u in units] + [DMA((31,))]


def scatter_grad(here, block, own, buffers, piece, y_first, small):
    ra, rb, rc, rd, xa, xb, xc, xd, zr, sems = buffers
    second, first = (here.axis_y, here.axis_x) if y_first else (here.axis_x, here.axis_y)
    own = own or (lambda df, ds, h: block(df, ds, h)[...])

    def far_send(j):
        here.send(block(j, 2, 0), ra.at[j], sems.at[j], second[0])
        here.send(block(j, 2, 1), rb.at[j], sems.at[4 + j], second[1])

    def near_plus(j):
        here.send(block(j, 1, 1), rc.at[j, 1], sems.at[8 + 2 * j + 1], second[0])

    def near_minus(j):
        here.send(block(j, 3, 0), rd.at[j, 0], sems.at[16 + 2 * j], second[1])

    def pass_on(j):
        here.wait(ra.at[j], sems.at[j])
        ra[j] = own(j, 1, 0) + ra[j]
        here.send(ra.at[j], rc.at[j, 0], sems.at[8 + 2 * j], second[0])
        here.wait(rb.at[j], sems.at[4 + j])
        rb[j] = own(j, 3, 1) + rb[j]
        here.send(rb.at[j], rd.at[j, 1], sems.at[16 + 2 * j + 1], second[1])

    def total(j):
        for h in range(2):
            here.wait(rc.at[j, h], sems.at[8 + 2 * j + h])
            here.wait(rd.at[j, h], sems.at[16 + 2 * j + h])
            rc[j, h] = own(j, 0, h) + (rc[j, h] + rd[j, h])

    def turn_two():
        here.send(rc.at[2, 0], xa.at[0], sems.at[24], first[0])
        here.send(rc.at[2, 1], xb.at[0], sems.at[25], first[1])

    def turn_near():
        here.send(rc.at[1, 1], xc.at[1], sems.at[27], first[0])
        here.send(rc.at[3, 0], xd.at[0], sems.at[28], first[1])

    def turn_on():
        here.wait(xa.at[0], sems.at[24])
        xa[0] = rc[1, 0] + xa[0]
        here.send(xa.at[0], xc.at[0], sems.at[26], first[0])
        here.wait(xb.at[0], sems.at[25])
        xb[0] = rc[3, 1] + xb[0]
        here.send(xb.at[0], xd.at[1], sems.at[29], first[1])

    every = (2, 1, 3, 0)
    if small:
        for j in every:
            far_send(j)
            near_plus(j)
            near_minus(j)
        yield
        for j in every:
            pass_on(j)
        yield
        total(2)
        turn_two()
        total(1)
        total(3)
        turn_near()
        yield
        turn_on()
        total(0)
        yield
    else:
        if y_first:
            for send in (far_send, near_plus, near_minus):
                for j in every:
                    send(j)
                yield
        else:
            for j in every:
                far_send(j)
                near_plus(j)
                near_minus(j)
                yield
        if y_first:
            yield
        pass_on(2)
        pass_on(1)
        yield
        pass_on(3)
        pass_on(0)
        yield
        total(2)
        turn_two()
        yield
        total(1)
        total(3)
        turn_near()
        yield
        total(0)
        yield
        turn_on()
        yield
    for h in range(2):
        here.wait(xc.at[h], sems.at[26 + h])
        here.wait(xd.at[h], sems.at[28 + h])
        xc[h] = rc[0, h] + (xc[h] + xd[h])
    here.send(xc.at[1 - here.z], zr.at[0], sems.at[30], here.pair)
    yield
    here.wait(zr.at[0], sems.at[30])
    piece[...] = added(xc[here.z], zr[0]).astype(piece.dtype)


def seq_gather(here, source, full, sems, pause=1):
    own = pltpu.make_async_copy(source, full.at[here.s], sems.at[3])
    own.start()
    here.send(source, full.at[here.s], sems.at[0], here.far, True)
    here.send(source, full.at[here.s], sems.at[1], here.near, True)
    for _ in range(pause):
        yield
    here.wait(full.at[here.s_far], sems.at[0])
    here.send(full.at[here.s_far], full.at[here.s_far], sems.at[2], here.near, True)
    yield
    here.wait(full.at[here.s_near], sems.at[1])
    here.wait(full.at[here.s_cross], sems.at[2])
    own.wait()


def seq_scatter(here, parts, near, far, sems, make, pause=1):
    make(here.s_cross)
    here.send(parts.at[here.s_cross], near.at[0], sems.at[0], here.near, True)
    make(here.s_far)
    yield
    here.wait(near.at[0], sems.at[0])
    near[0] = parts[here.s_far] + near[0]
    here.send(near.at[0], far, sems.at[2], here.far, True)
    make(here.s_near)
    here.send(parts.at[here.s_near], near.at[1], sems.at[1], here.near, True)
    make(here.s)
    yield
    here.wait(near.at[1], sems.at[1])
    for _ in range(pause):
        yield
    here.wait(far, sems.at[2])


def masked(scores, at, kv_len, seg_col, seg_row):
    q_pos = at + iota((ROWS, kv_len), 0)
    k_pos = iota((ROWS, kv_len), 1)
    keep = (q_pos >= k_pos) & (seg_col[at : at + ROWS, :] == seg_row[:, :kv_len])
    return jnp.where(keep, scores, BIG)


def set_segments(seg_row, seg_col):
    for b in range(L // ROWS):
        at = slice(b * ROWS, (b + 1) * ROWS)
        seg_col[at, :] = column(seg_row[:, at].astype(F32))


def forward_kernel(
    tokens, routes, shared_mask, norm_gain, ffn_gain, w_router, w_query, key_weight, value_weight, w_out,
    shared_gate, shared_up, shared_down, expert_gate, expert_up, expert_down, segments, cot,
    normed_one, qkv_out, heads_out, logs_out, gains, qkv_full_out, out_full_out, normed_two, all_cot,
    pre_a, pre_b, low_home, grad_hidden, grad_misc, out_far, out_own,
    marked, all_marked, qkv_block, out_block, block_a, block_b, qkv_full, out_full, normed, qkv, heads, logs, seg_col,
    marks, misc, part, near, far, normed_home, hidden, xs, cs, full_a, full_b,
    staged, near_g, far_g, near_out, own_gates, own_out,
    send_sems, token_sems, qkv_sems, out_sems, a_sems, b_sems, own_sems, scatter_sems, gather_sems, cot_sems,
    grad_sems, sum_sems, local_sems,
):
    here = Here(send_sems)
    local = Local(local_sems)
    here.greet()
    s = here.s

    def wide(ref, at, width):
        return ref[:, pl.ds(pl.multiple_of(at * width, LANES), width)]

    marked[:, :WIDTH] = tokens[...]
    line = iota((LANES, ROWS), 0)
    used = line == routes[0:1, :] + 2
    for k in range(1, 6):
        used = used | (line == routes[k : k + 1, :] + 2)
    turned = (jnp.where(used, 1.0, 0.0) + jnp.where(line == 1, shared_mask[...].astype(F32), 0.0)).astype(BF)
    eye = (iota((LANES, LANES), 0) == iota((LANES, LANES), 1)).astype(BF)
    marked[:, WIDTH:] = mm_tn(turned, eye).astype(BF)
    token_gather = seq_gather(here, marked, all_marked, token_sems, 13)
    qkv_block[:, :Q_COLS] = wide(w_query, s, Q_COLS)
    qkv_block[:, Q_COLS:KV] = wide(key_weight, s, HEAD)
    qkv_block[:, KV:] = wide(value_weight, s, HEAD)
    here.meet()
    qkv_gather = gather_weight(here, qkv_full, qkv_block, qkv_sems, own_sems.at[0], True)
    next(qkv_gather)
    out_block[:, :Q_COLS] = wide(w_out, s, Q_COLS)
    place = (iota((E, LANES), 1) == iota((E, LANES), 0) + 2).astype(F32)
    single = f32dot(w_router[...].astype(F32), place, ((0,), (0,)))
    lane = iota((SHARD, LANES), 1)
    single = single + jnp.where(lane == 0, column(norm_gain[...].astype(F32)), 0.0)
    out_block[:, Q_COLS:] = (single + jnp.where(lane == 1, column(ffn_gain[...].astype(F32)), 0.0)).astype(BF)
    out_gather = gather_weight(here, out_full, out_block, out_sems, own_sems.at[1], False)
    next(out_gather)
    next(token_gather)
    next(qkv_gather)
    next(out_gather)
    for k, block in enumerate((block_a, block_b)):
        pick = (iota((SHARD, SHARD * E), 1) == iota((SHARD, SHARD * E), 0) * E + 2 * s + k).astype(BF)
        for i, (shared, expert) in enumerate(((shared_gate, expert_gate), (shared_up, expert_up), (shared_down, expert_down))):
            block[:, i * HALF : i * HALF + 512] = mm(pick, expert[...].reshape(SHARD * E, 512)).astype(BF)
            block[:, i * HALF + 512 : (i + 1) * HALF] = wide(shared, 2 * s + k, HALF - 512)
    set_segments(segments, seg_col)
    weights = [
        gather_weight(here, full_a, block_a, a_sems, own_sems.at[2], True),
        gather_weight(here, full_b, block_b, b_sems, own_sems.at[3], False),
    ]
    for weight in weights:
        next(weight)
    together(token_gather, qkv_gather, out_gather, later(9, weights))

    def tick():
        for weight in weights:
            next(weight, None)

    cot_gather = seq_gather(here, cot, cs, cot_sems)
    next(cot_gather)
    misc[...] = out_full[:, :, :, :, Q_COLS:].reshape(WIDTH, LANES)
    gains[...] = mm_nt(eye, misc[...])[:8]
    gain = gains[0:1, :]
    seg_row = segments[...].astype(F32)
    for b in range(SEQ):
        at = slice(b * ROWS, (b + 1) * ROWS)
        normed[at, :] = normed_of(all_marked[b, :, :WIDTH].astype(F32), gain)[2]
        qkv[at, :] = mm(normed[at, :], qkv_full[...].reshape(WIDTH, HALF)).astype(BF)
        marks[at, :] = all_marked[b, :, WIDTH:]
        if b == 3:
            tick()
    saved = [local.copy(normed, normed_one), local.copy(qkv, qkv_out), local.copy(qkv_full, qkv_full_out)]
    saved.append(local.copy(out_full, out_full_out))
    for b in range(SEQ):
        at, kv_len = b * ROWS, (b + 1) * ROWS
        for h in range(GROUP):
            cols = slice(h * HEAD, (h + 1) * HEAD)
            scores = mm_nt(qkv[at : at + ROWS, cols], qkv[:kv_len, Q_COLS:KV]) * SCALE
            scores = masked(scores, at, kv_len, seg_col, seg_row)
            top = jnp.max(scores, axis=-1, keepdims=True)
            weight = jnp.exp(scores - top)
            total = jnp.sum(weight, axis=-1, keepdims=True)
            probs = (weight * (1.0 / total)).astype(BF)
            heads[at : at + ROWS, cols] = mm(probs, qkv[:kv_len, KV:]).astype(BF)
            logs[at : at + ROWS, h : h + 1] = top + jnp.log(total)
        tick()

    saved += [local.copy(heads, heads_out), local.copy(logs, logs_out)]

    def project(i):
        rows = heads[pl.ds(pl.multiple_of(i * ROWS, ROWS), ROWS), :]
        part[i] = mm_nt(rows, out_full[:, :, :, :, :Q_COLS].reshape(WIDTH, Q_COLS)).astype(BF)

    def rows():
        yield from seq_scatter(here, part, near, far, scatter_sems, project, 2)
        next(cot_gather)
        hidden[...] = added(tokens[...], part[s], near[1], far[...])
        normed_home[...] = normed_of(hidden[...], gains[1:2, :])[2]
        yield from seq_gather(here, normed_home, xs, gather_sems, 3)
        next(cot_gather, None)

    together(rows(), *weights)
    for copy in saved:
        copy.wait()
    saved = [local.copy(xs, normed_two), local.copy(cs, all_cot)]
    here.finish_rows()
    order = (here.s_cross, here.s_far, here.s_near, s)
    sent, outs, far_sum, low_out = all_marked, part, far, normed_home
    lane = iota((ROWS, LANES), 1)
    stored = [[], []]

    def block(n):
        i = order[n]
        at = pl.ds(pl.multiple_of(i * ROWS, ROWS), ROWS)
        x, c = xs[i], cs[i]
        mark = marks[at, :].astype(F32)
        member = (mark > 0) & (lane >= 2) & (lane < 2 + E)
        logits = jnp.where(member, mm(x, misc[...]), BIG)
        soft = jnp.where(member, jnp.exp(logits - jnp.max(logits, axis=-1, keepdims=True)), 0.0)
        gates = soft / jnp.sum(soft, axis=-1, keepdims=True)
        if n == 3:
            own_gates[...] = gates
        keep = mark[:, 1:2]
        total = jnp.zeros((ROWS, WIDTH), F32)
        grad_x = jnp.zeros((ROWS, WIDTH), F32)
        grad_marks = jnp.zeros((ROWS, LANES), F32)
        for k, weight in enumerate((full_a, full_b)):
            if n >= 2:
                stored[k][n - 2].wait()
            slot = staged.at[n % 2, k]
            mine = lane == 2 + 2 * s + k
            gate_e = jnp.sum(jnp.where(mine, gates, 0.0), axis=-1, keepdims=True)
            coef = jnp.concatenate([jnp.broadcast_to(gate_e, (ROWS, 512)), jnp.broadcast_to(keep, (ROWS, HALF - 512))], axis=1)
            pre = mm(x, weight[:, :, :, :, : 2 * HALF].reshape(WIDTH, 2 * HALF))
            gate, upper = pre[:, :HALF], pre[:, HALF:]
            sigma = 1.0 / (1.0 + jnp.exp(-gate))
            silu = gate * sigma
            units = silu * upper
            weighted = (coef * units).astype(BF)
            slot[:, 2 * HALF :] = weighted
            total += mm_nt(weighted, weight[:, :, :, :, 2 * HALF :].reshape(WIDTH, HALF))
            grad_units = mm(c, weight[:, :, :, :, 2 * HALF :].reshape(WIDTH, HALF))
            grad_gate = jnp.sum((units * grad_units)[:, :512], axis=-1, keepdims=True)
            high = grad_gate.astype(BF).astype(F32)
            grad_marks += jnp.where(mine, high, 0.0) + jnp.where(lane == LOW + 2 + 2 * s + k, grad_gate - high, 0.0)
            grad_units = coef * grad_units
            slot[:, :HALF] = (grad_units * upper * (sigma * (1.0 + gate * (1.0 - sigma)))).astype(BF)
            slot[:, HALF : 2 * HALF] = (grad_units * silu).astype(BF)
            grad_x += mm_nt(slot[:, : 2 * HALF], weight[:, :, :, :, : 2 * HALF].reshape(WIDTH, 2 * HALF))
            stored[k].append(local.copy(slot, (pre_a, pre_b)[k].at[at]))
        outs[i] = total.astype(BF)
        sent[i, :, :WIDTH] = grad_x.astype(BF)
        sent[i, :, WIDTH:] = grad_marks.astype(BF)

    block(0)
    here.send(sent.at[here.s_cross], near_g.at[0], grad_sems.at[0], here.near, True)
    here.send(outs.at[here.s_cross], near_out.at[0], sum_sems.at[0], here.near, True)
    block(1)
    here.wait(near_g.at[0], grad_sems.at[0])
    near_g[0] = sent[here.s_far] + near_g[0]
    here.send(near_g.at[0], far_g, grad_sems.at[2], here.far, True)
    here.wait(near_out.at[0], sum_sems.at[0])
    far_sum[...] = outs[here.s_far] + near_out[0]
    saved.append(local.copy(far_sum, out_far))
    block(2)
    here.send(sent.at[here.s_near], near_g.at[1], grad_sems.at[1], here.near, True)
    here.send(outs.at[here.s_near], near_out.at[1], sum_sems.at[1], here.near, True)
    block(3)
    here.wait(near_g.at[1], grad_sems.at[1])
    here.wait(near_out.at[1], sum_sems.at[1])
    own_out[...] = added(hidden[...], outs[s], near_out[1])
    saved.append(local.copy(own_out, out_own))
    gain = gains[1:2, :]
    inverse, unit, normed_home = normed_of(hidden[...], gain)
    here.finish()
    here.wait(far_g, grad_sems.at[2])

    grad_gates = added(sent[s, :, WIDTH:], near_g[1, :, WIDTH:], far_g[:, WIDTH:])
    grad_gates = grad_gates + pltpu.roll(grad_gates, LANES - LOW, 1)
    gates = own_gates[...]
    grad_logits = gates * (grad_gates - jnp.sum(gates * grad_gates, axis=-1, keepdims=True))
    high, low = split_two(grad_logits)
    grad_normed = added(sent[s, :, :WIDTH], near_g[1, :, :WIDTH], far_g[:, :WIDTH])
    grad_normed = grad_normed + (mm_nt(high, misc[...]) + mm_nt(low, misc[...]))
    scaled = grad_normed * gain
    grad = cs[s].astype(F32) + inverse * (scaled - unit * jnp.mean(scaled * unit, axis=-1, keepdims=True))
    low_out[...] = grad.astype(BF)
    saved.append(local.copy(low_out, low_home))
    hidden[...] = grad
    saved.append(local.copy(hidden, grad_hidden))
    prod_high, prod_low = split_two(grad_normed * unit)
    one = (lane == 1).astype(BF)
    grad_misc[...] = mm_tn(normed_home, high) + mm_tn(normed_home, low) + mm_tn(prod_high, one) + mm_tn(prod_low, one)
    for copy in (*saved, *stored[0][2:], *stored[1][2:]):
        copy.wait()
    here.finish_rows()


def row_of(y, x, z):
    return pl.multiple_of(((y * 4 + x) * 2 + z) * SHARD, SHARD)


def finish_kernel(
    low_home, normed_two_in, cots_in, pre_a_in, pre_b_in,
    normed_in, qkv_in, heads_in, logs_in, qkv_full_in, out_full_in, out_far,
    segments, gains, grad_misc, grad_hidden, tokens,
    far_out, grad_tokens, grad_a, grad_b, ffn_a_all, ffn_b_all, one_all, two_all,
    grad_low, normed, part, pre_a, pre_b, staged, qkv, heads, logs, qkv_full, out_full,
    grad_one, grad_two, grad_heads, grad_all, grad_kv, near, far, gain_sum, seg_col,
    piece_a, piece_b, piece_one, piece_two,
    send_sems, local_sems, scatter_sems, out_sems, gather_sems, low_sems, *buffers,
):
    here = Here(send_sems)
    local = Local(local_sems)
    s = here.s
    load_a = [local.copy(normed_two_in, normed), local.copy(pre_a_in, pre_a), local.copy(cots_in, part)]
    load_b = local.copy(pre_b_in, pre_b)
    load_rest = [
        local.copy(a, b)
        for a, b in ((out_full_in, out_full), (heads_in, heads), (qkv_in, qkv), (logs_in, logs), (qkv_full_in, qkv_full))
    ]
    here.greet()
    here.meet()
    low_gather = seq_gather(here, low_home, grad_low, low_sems)
    next(low_gather)

    def summed(sum_of, piece, full, sems, pause=1):
        yield from sum_of
        yield from seq_gather(here, piece, full, sems, pause)

    def from_hbm(grad, y_first):
        def block(df, ds, h):
            dy, dx = (ds, df) if y_first else (df, ds)
            return grad.at[pl.ds(row_of(wrap(here.y + dy), wrap(here.x + dx), h), SHARD)]

        return block

    def own_unit(place, j, ds, h):
        at = wrap(place + j)
        return at * 2 + h if ds == 0 else (8 if ds == 1 else 12) + at

    def owned(held, place):
        def own(j, ds, h):
            return held[pl.ds(pl.multiple_of(own_unit(place, j, ds, h) * SHARD, SHARD), SHARD), :]

        return own

    sum_a = scatter_grad(here, from_hbm(grad_a, True), owned(pre_a, here.x), buffers[:10], piece_a, True, False)
    sum_b = scatter_grad(here, from_hbm(grad_b, False), owned(pre_b, here.y), buffers[10:20], piece_b, False, False)
    sums = [summed(sum_a, piece_a, ffn_a_all, gather_sems.at[0], 4), summed(sum_b, piece_b, ffn_b_all, gather_sems.at[1], 4)]

    def chunk(y):
        return pl.ds(pl.multiple_of(y * CHUNK, CHUNK), CHUNK)

    moving = []
    for n, (j, k) in enumerate((j, k) for j in (2, 1, 3, 0) for k in range(2)):
        pre = (pre_a, pre_b)[k]
        if n == 0:
            load_a[0].wait()
            load_a[1].wait()
        if n == 1:
            load_b.wait()
        at = chunk(wrap(here.y + j))
        slot = staged.at[n % 2]
        slot[:, : 2 * HALF] = mm_tn(normed[:, at], pre[:, : 2 * HALF]).astype(BF)
        if n == 0:
            load_a[2].wait()
        if n > 1:
            moving[n - 1].wait()
            next(sums[(n - 1) % 2])
        slot[:, 2 * HALF :] = mm_tn(part[:, :, at].reshape(L, CHUNK), pre[:, 2 * HALF :]).astype(BF)
        moving.append(local.copy(slot, (grad_a, grad_b)[k].at[at]))
        if n == 0:
            moving[0].wait()
            next(sums[0])
    moving[-1].wait()
    next(sums[1])
    load_own = []
    for grad, held, y_first in ((grad_a, pre_a, True), (grad_b, pre_b, False)):
        for i in range(4):
            for ds, h in ((0, 0), (0, 1), (1, 0), (3, 1)):
                y, x = (wrap(here.y + ds), i) if y_first else (i, wrap(here.x + ds))
                unit = i * 2 + h if ds == 0 else (8 if ds == 1 else 12) + i
                source = grad.at[pl.ds(row_of(y, x, h), SHARD)]
                load_own.append(local.copy(source, held.at[pl.ds(unit * SHARD, SHARD)]))
    load_rest.append(local.copy(normed_in, normed))
    here.send(out_far, far_out, out_sems.at[0], here.far, True)
    set_segments(segments, seg_col)
    seg_row = segments[...].astype(F32)
    next(low_gather)
    for load in load_own:
        load.wait()

    def tick():
        for part_sum in sums[:2]:
            next(part_sum)

    tick()
    next(low_gather, None)
    for load in load_rest:
        load.wait()
    for b in range(SEQ):
        at = slice(b * ROWS, (b + 1) * ROWS)
        grad_heads[at, :] = mm(grad_low[b], out_full[:, :Q_COLS]).astype(BF)

    def blocks_of(grad, y_first):
        def block(df, ds, h):
            dy, dx = (ds, df) if y_first else (df, ds)
            return grad.at[wrap(here.y + dy), wrap(here.x + dx), h]

        return block

    def out_chunk(y, carry):
        value = mm_tn(grad_low[:, :, chunk(y)].reshape(L, CHUNK), heads[...])
        grad_two[y, :, :, :, HEAD:KV] = value.astype(BF).reshape(4, 2, SHARD, Q_COLS)
        return carry

    lax.fori_loop(0, 4, out_chunk, 0)
    tick()
    grad_kv[...] = jnp.zeros_like(grad_kv)
    for b in range(SEQ):
        at, kv_len = b * ROWS, (b + 1) * ROWS
        for h in range(GROUP):
            cols = slice(h * HEAD, (h + 1) * HEAD)
            query, grad = qkv[at : at + ROWS, cols], grad_heads[at : at + ROWS, cols]
            scores = mm_nt(query, qkv[:kv_len, Q_COLS:KV]) * SCALE
            probs = jnp.exp(masked(scores, at, kv_len, seg_col, seg_row) - logs[at : at + ROWS, h : h + 1])
            grad_probs = mm_nt(grad, qkv[:kv_len, KV:])
            centre = jnp.sum(probs * grad_probs, axis=-1, keepdims=True)
            grad_scores = (probs * (grad_probs - centre)).astype(BF)
            grad_all[at : at + ROWS, cols] = (mm(grad_scores, qkv[:kv_len, Q_COLS:KV]) * SCALE).astype(BF)
            grad_kv[:kv_len, :HEAD] += mm_tn(grad_scores, query) * SCALE
            grad_kv[:kv_len, HEAD:] += mm_tn(probs.astype(BF), grad)
    tick()
    grad_all[:, Q_COLS:] = grad_kv[...].astype(BF)

    def weight_chunk(y, carry):
        at = chunk(y)
        value = mm_tn(normed[:, at], grad_all[...]).astype(BF)
        grad_one[y] = value[:, :KV].reshape(4, 2, SHARD, KV)
        grad_two[y, :, :, :, :HEAD] = value[:, KV:].reshape(4, 2, SHARD, HEAD)
        return carry

    lax.fori_loop(0, 4, weight_chunk, 0)
    sum_one = scatter_grad(here, blocks_of(grad_one, True), None, buffers[20:30], piece_one, True, True)
    sums.append(summed(sum_one, piece_one, one_all, gather_sems.at[2]))
    tick()
    gain_sum[...] = jnp.zeros_like(gain_sum)

    def back(i):
        at = pl.ds(pl.multiple_of(i * ROWS, ROWS), ROWS)
        value = mm_nt(grad_all[at, :], qkv_full[...])
        part[i] = value.astype(BF)
        gain_sum[0:1, :] += jnp.sum(value * normed[at, :].astype(F32), axis=0, keepdims=True)

    row_sum = seq_scatter(here, part, near, far, scatter_sems, back, 4)
    next(row_sum)
    next(row_sum)
    tick()
    gain = gains[0:1, :]
    high, low = split_two(gain_sum[0:1, :] / gain)
    row = iota((16, WIDTH), 0)
    both = jnp.where(row == 0, high.astype(F32), 0.0) + jnp.where(row == 1, low.astype(F32), 0.0)
    pick = (iota((16, LANES), 1) == 0).astype(BF)
    single = (grad_misc[...] + mm_tn(both.astype(BF), pick)).astype(BF)
    grad_two[:, :, :, :, KV:] = single.reshape(4, 4, 2, SHARD, LANES)
    sum_two = scatter_grad(here, blocks_of(grad_two, False), None, buffers[30:], piece_two, False, True)
    sums.append(summed(sum_two, piece_two, two_all, gather_sems.at[3]))

    def rows():
        yield from row_sum
        here.wait(far_out, out_sems.at[0])
        grad_normed = added(part[s], near[1], far[...])
        inverse, unit, _ = normed_of(tokens[...].astype(F32), gain)
        scaled = grad_normed * gain
        grad_tokens[...] = (grad_hidden[...] + inverse * (scaled - unit * jnp.mean(scaled * unit, axis=-1, keepdims=True))).astype(BF)

    here.finish(64)
    together(*sums, rows())
    here.finish()
    here.finish_rows()


def as_row(col):
    n = col.shape[0]
    return jnp.sum(jnp.where(iota((n, n), 0) == iota((n, n), 1), jnp.broadcast_to(col, (n, n)), 0.0), axis=0, keepdims=True)


def outputs_kernel(
    ffn_a, ffn_b, one, two, out_own, far_out, output, wq, wk, wv, wo, gain_one, gain_two, router, shared_gate, shared_up, shared_down, expert_gate, expert_up, expert_down
):
    output[...] = added(out_own[...], far_out[...]).astype(BF)
    total = jnp.zeros((SHARD, LANES), F32)
    for s in range(SEQ):
        wq[:, s * Q_COLS : (s + 1) * Q_COLS] = one[s, :, :Q_COLS].astype(F32)
        wo[:, s * Q_COLS : (s + 1) * Q_COLS] = two[s, :, HEAD:KV].astype(F32)
        wk[:, s * HEAD : (s + 1) * HEAD] = one[s, :, Q_COLS:].astype(F32)
        wv[:, s * HEAD : (s + 1) * HEAD] = two[s, :, :HEAD].astype(F32)
        total = total + two[s, :, KV:].astype(F32)
        for k, ffn in enumerate((ffn_a, ffn_b)):
            n = 2 * s + k
            for i, (shared, expert) in enumerate(((shared_gate, expert_gate), (shared_up, expert_up), (shared_down, expert_down))):
                expert[:, n, :] = ffn[s, :, i * HALF : i * HALF + 512].astype(F32)
                shared[:, n * LANES : (n + 1) * LANES] = ffn[s, :, i * HALF + 512 : (i + 1) * HALF].astype(F32)
    gain_one[...] = as_row(total[:, 0:1])
    gain_two[...] = as_row(total[:, 1:2])
    for e in range(E):
        router[e : e + 1, :] = as_row(total[:, 2 + e : 3 + e])


def remote_call(kernel, name, number, outs, ins, scratch):
    return pl.pallas_call(
        kernel,
        out_shape=[jax.ShapeDtypeStruct(dims, dtype) for dims, dtype, _ in outs],
        in_specs=[VMEM_ALL if fast else ANY for _, fast in ins],
        out_specs=[VMEM_ALL if fast else ANY for _, _, fast in outs],
        scratch_shapes=list(scratch),
        compiler_params=pltpu.CompilerParams(collective_id=number, has_side_effects=True, vmem_limit_bytes=LIMIT),
        name=name,
    )(*[array for array, _ in ins])


def buf(*dims):
    return pltpu.VMEM(dims, BF)


def buf32(*dims):
    return pltpu.VMEM(dims, F32)


def body(
    tokens,
    segments,
    routes,
    shared_mask,
    norm_gain,
    w_query,
    key_weight,
    value_weight,
    w_out,
    ffn_gain,
    w_router,
    shared_gate,
    shared_up,
    shared_down,
    expert_gate,
    expert_up,
    expert_down,
    cotangent,
):
    seg_row = segments[None, :]
    grid = DMA((4, 4, 2))
    rows4 = (SEQ, ROWS, WIDTH)
    fast = [tokens, routes.T, shared_mask[None, :], norm_gain[None, :], ffn_gain[None, :], w_router.T, w_query, key_weight,
            value_weight, w_out, shared_gate, shared_up, shared_down, expert_gate, expert_up, expert_down, seg_row]
    (
        normed_one, qkv, heads, logs, gains, qkv_full, out_full, normed_two, all_cot,
        pre_a, pre_b, low_home, grad_hidden, grad_misc, out_far, out_own,
    ) = remote_call(
        forward_kernel,
        "forward",
        1,
        [
            ((L, WIDTH), BF, False),
            ((L, HALF), BF, False),
            ((L, Q_COLS), BF, False),
            ((L, 8), F32, False),
            ((8, WIDTH), F32, True),
            (blocks(HALF), BF, False),
            (blocks(OUT_COLS), BF, False),
            (rows4, BF, False),
            (rows4, BF, False),
            ((L, FFN), BF, False),
            ((L, FFN), BF, False),
            ((ROWS, WIDTH), BF, False),
            ((ROWS, WIDTH), F32, False),
            ((WIDTH, LANES), F32, True),
            ((ROWS, WIDTH), BF, False),
            ((ROWS, WIDTH), F32, False),
        ],
        [(a, True) for a in fast] + [(cotangent, False)],
        [
            buf(ROWS, WIDTH + LANES),
            buf(SEQ, ROWS, WIDTH + LANES),
            buf(SHARD, HALF),
            buf(SHARD, OUT_COLS),
            buf(SHARD, FFN),
            buf(SHARD, FFN),
            buf(*blocks(HALF)),
            buf(*blocks(OUT_COLS)),
            buf(L, WIDTH),
            buf(L, HALF),
            buf(L, Q_COLS),
            buf32(L, 8),
            buf32(L, 1),
            buf(L, LANES),
            buf(WIDTH, LANES),
            buf(*rows4),
            buf(2, ROWS, WIDTH),
            buf(ROWS, WIDTH),
            buf(ROWS, WIDTH),
            buf32(ROWS, WIDTH),
            buf(*rows4),
            buf(*rows4),
            buf(*blocks(FFN)),
            buf(*blocks(FFN)),
            buf(2, 2, ROWS, FFN),
            buf(2, ROWS, WIDTH + LANES),
            buf(ROWS, WIDTH + LANES),
            buf(2, ROWS, WIDTH),
            buf32(ROWS, LANES),
            buf32(ROWS, WIDTH),
            DMA((160,)),
            DMA((4,)),
            grid,
            grid,
            grid,
            grid,
            DMA((4,)),
            DMA((3,)),
            DMA((4,)),
            DMA((4,)),
            DMA((3,)),
            DMA((2,)),
            DMA((24,)),
        ],
    )

    far_out, grad_tokens, _, _, ffn_a_all, ffn_b_all, one_all, two_all = remote_call(
        finish_kernel,
        "finish",
        2,
        [
            ((ROWS, WIDTH), BF, False),
            ((ROWS, WIDTH), BF, True),
            ((WIDTH, FFN), BF, False),
            ((WIDTH, FFN), BF, False),
            ((SEQ, SHARD, FFN), BF, False),
            ((SEQ, SHARD, FFN), BF, False),
            ((SEQ, SHARD, KV), BF, False),
            ((SEQ, SHARD, HALF), BF, False),
        ],
        [
            (low_home, False),
            (normed_two.reshape(L, WIDTH), False),
            (all_cot, False),
            (pre_a, False),
            (pre_b, False),
            (normed_one, False),
            (qkv, False),
            (heads, False),
            (logs, False),
            (qkv_full.reshape(WIDTH, HALF), False),
            (out_full.reshape(WIDTH, OUT_COLS), False),
            (out_far, False),
            (seg_row, True),
            (gains, True),
            (grad_misc, True),
            (grad_hidden, True),
            (tokens, True),
        ],
        [
            buf(*rows4),
            buf(L, WIDTH),
            buf(*rows4),
            buf(L, FFN),
            buf(L, FFN),
            buf(2, CHUNK, FFN),
            buf(L, HALF),
            buf(L, Q_COLS),
            buf32(L, 8),
            buf(WIDTH, HALF),
            buf(WIDTH, OUT_COLS),
            buf(*blocks(KV)),
            buf(*blocks(HALF)),
            buf(L, Q_COLS),
            buf(L, HALF),
            buf32(L, 2 * HEAD),
            buf(2, ROWS, WIDTH),
            buf(ROWS, WIDTH),
            buf32(16, WIDTH),
            buf32(L, 1),
            buf(SHARD, FFN),
            buf(SHARD, FFN),
            buf(SHARD, KV),
            buf(SHARD, HALF),
            DMA((192,)),
            DMA((56,)),
            DMA((3,)),
            DMA((1,)),
            DMA((4, 4)),
            DMA((4,)),
            *scatter_buffers(FFN),
            *scatter_buffers(FFN),
            *scatter_buffers(KV),
            *scatter_buffers(HALF),
        ],
    )

    dims = [(ROWS, WIDTH), (SHARD, 4 * Q_COLS), (SHARD, 4 * HEAD), (SHARD, 4 * HEAD), (SHARD, 4 * Q_COLS), (1, SHARD), (1, SHARD), (E, SHARD)]
    dims += [(SHARD, 1024)] * 3 + [(SHARD, E, 512)] * 3
    output, wq, wk, wv, wo, gain_one, gain_two, router, *ffn = pl.pallas_call(
        outputs_kernel,
        out_shape=[jax.ShapeDtypeStruct(d, BF if d[0] == ROWS else F32) for d in dims],
        in_specs=[VMEM_ALL] * 6,
        out_specs=[VMEM_ALL] * len(dims),
        compiler_params=pltpu.CompilerParams(vmem_limit_bytes=LIMIT),
        name="outputs",
    )(ffn_a_all, ffn_b_all, one_all, two_all, out_own, far_out)
    return (output, grad_tokens, gain_one[0], wq, wk, wv, wo, gain_two[0], router.T, *ffn)


def solution(mesh):
    both = P(("fsdp", "seq"), None)
    one, two, three = P("fsdp"), P("fsdp", None), P("fsdp", None, None)
    return jax.shard_map(
        body,
        mesh=mesh,
        in_specs=(both, one, both, P(("fsdp", "seq")), one, two, two, two, two, one, two, two, two, two, three, three, three, both),
        out_specs=(both, both, one, two, two, two, two, one, two, two, two, two, three, three, three),
        check_vma=False,
    )
```

```python
import jax
import jax.numpy as jnp
from jax import lax
from jax.experimental import pallas as pl
from jax.experimental.pallas import tpu as pltpu
from jax.sharding import PartitionSpec as P

HEAD = 128
GROUP = 3
E = 8
SEQ = 4
EPS = 1e-05
BF = jnp.bfloat16
F32 = jnp.float32
WIDTH = 1536
L = 1024
ROWS = 256
SHARD = 48
Q_COLS = GROUP * HEAD
KV = Q_COLS + HEAD
HALF = 640
FFN = 3 * HALF
LANES = 128
OUT_COLS = Q_COLS + LANES
LOW = 32
CHUNK = 384
SCALE = HEAD ** (-0.5)
BIG = -1e30
MESH = pl.DeviceIdType.MESH
VMEM_ALL = pl.BlockSpec(memory_space=pltpu.VMEM)
ANY = pl.BlockSpec(memory_space=pl.ANY)
DMA = pltpu.SemaphoreType.DMA
LIMIT = 63 * 1024 * 1024


def f32dot(left, right, dims):
    return lax.dot_general(left, right, (dims, ((), ())), preferred_element_type=F32)


def mm(left, right):
    return f32dot(left, right, ((1,), (0,)))


def mm_nt(left, right):
    return f32dot(left, right, ((1,), (1,)))


def mm_tn(left, right):
    return f32dot(left, right, ((0,), (0,)))


def iota(dims, axis):
    return lax.broadcasted_iota(jnp.int32, dims, axis)


def column(row):
    n = row.shape[1]
    same = iota((n, n), 0) == iota((n, n), 1)
    return jnp.sum(jnp.where(same, jnp.broadcast_to(row, (n, n)), 0.0), axis=-1, keepdims=True)


def added(*values):
    total = values[0].astype(F32)
    for value in values[1:]:
        total = total + value.astype(F32)
    return total


def split_two(value):
    high = value.astype(BF)
    return high, (value - high.astype(F32)).astype(BF)


def normed_of(x, gain):
    inverse = lax.rsqrt(jnp.mean(x * x, axis=-1, keepdims=True) + EPS)
    unit = x * inverse
    return inverse, unit, (unit * gain).astype(BF)


def wrap(value):
    return lax.rem(value + 4, 4)


def blocks(cols):
    return (4, 4, 2, SHARD, cols)


class Here:
    def __init__(self, send_sems):
        f, s = lax.axis_index("fsdp"), lax.axis_index("seq")
        self.y, self.x, self.z = lax.div(f, 8), lax.rem(lax.div(f, 2), 4), lax.rem(f, 2)
        self.s, self.zh, self.core = s, lax.div(s, 2), lax.rem(s, 2)
        y, x, z = self.y, self.x, self.z
        self.axis_x = ({"fsdp": self.number(y, wrap(x + 1), z)}, {"fsdp": self.number(y, wrap(x - 1), z)})
        self.axis_y = ({"fsdp": self.number(wrap(y + 1), x, z)}, {"fsdp": self.number(wrap(y - 1), x, z)})
        self.pair = {"fsdp": self.number(y, x, 1 - z)}
        self.s_far = (1 - self.zh) * 2 + self.core
        self.s_near = self.zh * 2 + 1 - self.core
        self.s_cross = (1 - self.zh) * 2 + 1 - self.core
        self.far = {"seq": self.s_far}
        self.near = {"seq": self.s_near}
        self.sems, self.count, self.sent, self.row_sent = send_sems, 0, [], []

    @staticmethod
    def number(y, x, z):
        return (y * 4 + x) * 2 + z

    def greet(self):
        partners = [*self.axis_x, *self.axis_y, self.pair, self.far, self.near]
        for partner in partners:
            pl.semaphore_signal(pltpu.get_barrier_semaphore(), inc=1, device_id=partner, device_id_type=MESH)

    def meet(self):
        pl.semaphore_wait(pltpu.get_barrier_semaphore(), 7)

    def send(self, source, target, recv_sem, to, rows=False):
        copy = pltpu.make_async_remote_copy(
            src_ref=source,
            dst_ref=target,
            send_sem=self.sems.at[self.count],
            recv_sem=recv_sem,
            device_id=to,
            device_id_type=MESH,
        )
        copy.start()
        self.count += 1
        (self.row_sent if rows else self.sent).append(copy)

    def wait(self, target, recv_sem):
        pltpu.make_async_remote_copy(
            src_ref=target,
            dst_ref=target,
            send_sem=self.sems.at[0],
            recv_sem=recv_sem,
            device_id=self.near,
            device_id_type=MESH,
        ).wait_recv()

    def finish(self, most=None):
        for copy in self.sent[:most]:
            copy.wait_send()
        self.sent = [] if most is None else self.sent[most:]

    def finish_rows(self):
        for copy in self.row_sent:
            copy.wait_send()
        self.row_sent = []


class Local:
    def __init__(self, sems):
        self.sems, self.count = sems, 0

    def copy(self, source, target):
        copy = pltpu.make_async_copy(source, target, self.sems.at[self.count])
        copy.start()
        self.count += 1
        return copy


def together(*parts):
    left = list(parts)
    while left:
        for part in list(left):
            if next(part, "end") == "end":
                left.remove(part)


def later(turns, parts):
    for _ in range(turns):
        yield
    for part in parts:
        next(part)


def gather_weight(here, full, block, recv, own_sem, x_first):
    first, second = (here.axis_x, here.axis_y) if x_first else (here.axis_y, here.axis_x)

    def spot(df, ds, r):
        dy, dx = (ds, df) if x_first else (df, ds)
        return wrap(here.y + dy), wrap(here.x + dx), here.z if r == 0 else 1 - here.z

    def push(df, ds, r, to, source=None):
        at = spot(df, ds, r)
        here.send(full.at[at] if source is None else source, full.at[at], recv.at[at], to)

    def take(df, ds, r):
        at = spot(df, ds, r)
        here.wait(full.at[at], recv.at[at])

    own = pltpu.make_async_copy(block, full.at[spot(0, 0, 0)], own_sem)
    own.start()
    push(0, 0, 0, here.pair, block)
    yield
    for to in (*second, *first):
        push(0, 0, 0, to, block)
    yield
    take(0, 0, 1)
    for to in (*first, *second):
        push(0, 0, 1, to)
    for df, r in ((-1, 0), (1, 0), (1, 1), (-1, 1), (2, 0), (2, 1)):
        yield
        take(df, 0, r)
        if (df, r) == (-1, 0):
            push(df, 0, r, first[0])
        if (df, r) == (1, 1):
            push(df, 0, r, first[1])
        for to in second:
            push(df, 0, r, to)
        if (df, r) == (1, 0):
            take(0, -1, 0)
            push(0, -1, 0, second[0])
        if (df, r) == (-1, 1):
            take(0, 1, 1)
            push(0, 1, 1, second[1])
    for df in (-1, 1, 2):
        yield
        take(df, -1, 0)
        push(df, -1, 0, second[0])
        yield
        take(df, 1, 1)
        push(df, 1, 1, second[1])
    yield
    for df in (0, -1, 1, 2):
        take(df, -1, 1)
        take(df, 1, 0)
        take(df, 2, 0)
        take(df, 2, 1)
    own.wait()


def scatter_buffers(cols):
    units = [(4,), (4,), (4, 2), (4, 2), (1,), (1,), (2,), (2,), (1,)]
    return [pltpu.VMEM((*u, SHARD, cols), BF) for u in units] + [DMA((31,))]


def scatter_grad(here, block, own, buffers, piece, y_first, small):
    ra, rb, rc, rd, xa, xb, xc, xd, zr, sems = buffers
    second, first = (here.axis_y, here.axis_x) if y_first else (here.axis_x, here.axis_y)
    own = own or (lambda df, ds, h: block(df, ds, h)[...])

    def far_send(j):
        here.send(block(j, 2, 0), ra.at[j], sems.at[j], second[0])
        here.send(block(j, 2, 1), rb.at[j], sems.at[4 + j], second[1])

    def near_plus(j):
        here.send(block(j, 1, 1), rc.at[j, 1], sems.at[8 + 2 * j + 1], second[0])

    def near_minus(j):
        here.send(block(j, 3, 0), rd.at[j, 0], sems.at[16 + 2 * j], second[1])

    def pass_on(j):
        here.wait(ra.at[j], sems.at[j])
        ra[j] = own(j, 1, 0) + ra[j]
        here.send(ra.at[j], rc.at[j, 0], sems.at[8 + 2 * j], second[0])
        here.wait(rb.at[j], sems.at[4 + j])
        rb[j] = own(j, 3, 1) + rb[j]
        here.send(rb.at[j], rd.at[j, 1], sems.at[16 + 2 * j + 1], second[1])

    def total(j):
        for h in range(2):
            here.wait(rc.at[j, h], sems.at[8 + 2 * j + h])
            here.wait(rd.at[j, h], sems.at[16 + 2 * j + h])
            rc[j, h] = own(j, 0, h) + (rc[j, h] + rd[j, h])

    def turn_two():
        here.send(rc.at[2, 0], xa.at[0], sems.at[24], first[0])
        here.send(rc.at[2, 1], xb.at[0], sems.at[25], first[1])

    def turn_near():
        here.send(rc.at[1, 1], xc.at[1], sems.at[27], first[0])
        here.send(rc.at[3, 0], xd.at[0], sems.at[28], first[1])

    def turn_on():
        here.wait(xa.at[0], sems.at[24])
        xa[0] = rc[1, 0] + xa[0]
        here.send(xa.at[0], xc.at[0], sems.at[26], first[0])
        here.wait(xb.at[0], sems.at[25])
        xb[0] = rc[3, 1] + xb[0]
        here.send(xb.at[0], xd.at[1], sems.at[29], first[1])

    every = (2, 1, 3, 0)
    if small:
        for j in every:
            far_send(j)
            near_plus(j)
            near_minus(j)
        yield
        for j in every:
            pass_on(j)
        yield
        total(2)
        turn_two()
        total(1)
        total(3)
        turn_near()
        yield
        turn_on()
        total(0)
        yield
    else:
        if y_first:
            for send in (far_send, near_plus, near_minus):
                for j in every:
                    send(j)
                yield
        else:
            for j in every:
                far_send(j)
                near_plus(j)
                near_minus(j)
                yield
        if y_first:
            yield
        pass_on(2)
        pass_on(1)
        yield
        pass_on(3)
        pass_on(0)
        yield
        total(2)
        turn_two()
        yield
        total(1)
        total(3)
        turn_near()
        yield
        total(0)
        yield
        turn_on()
        yield
    for h in range(2):
        here.wait(xc.at[h], sems.at[26 + h])
        here.wait(xd.at[h], sems.at[28 + h])
        xc[h] = rc[0, h] + (xc[h] + xd[h])
    here.send(xc.at[1 - here.z], zr.at[0], sems.at[30], here.pair)
    yield
    here.wait(zr.at[0], sems.at[30])
    piece[...] = added(xc[here.z], zr[0]).astype(piece.dtype)


def seq_gather(here, source, full, sems, pause=1):
    own = pltpu.make_async_copy(source, full.at[here.s], sems.at[3])
    own.start()
    here.send(source, full.at[here.s], sems.at[0], here.far, True)
    here.send(source, full.at[here.s], sems.at[1], here.near, True)
    for _ in range(pause):
        yield
    here.wait(full.at[here.s_far], sems.at[0])
    here.send(full.at[here.s_far], full.at[here.s_far], sems.at[2], here.near, True)
    yield
    here.wait(full.at[here.s_near], sems.at[1])
    here.wait(full.at[here.s_cross], sems.at[2])
    own.wait()


def seq_scatter(here, parts, near, far, sems, make, pause=1):
    make(here.s_cross)
    here.send(parts.at[here.s_cross], near.at[0], sems.at[0], here.near, True)
    make(here.s_far)
    yield
    here.wait(near.at[0], sems.at[0])
    near[0] = parts[here.s_far] + near[0]
    here.send(near.at[0], far, sems.at[2], here.far, True)
    make(here.s_near)
    here.send(parts.at[here.s_near], near.at[1], sems.at[1], here.near, True)
    make(here.s)
    yield
    here.wait(near.at[1], sems.at[1])
    for _ in range(pause):
        yield
    here.wait(far, sems.at[2])


def mask_bias(at, kv_len, seg_col, seg_row):
    q_pos = at + iota((ROWS, kv_len), 0)
    k_pos = iota((ROWS, kv_len), 1)
    keep = (q_pos >= k_pos) & (seg_col[at : at + ROWS, :] == seg_row[:, :kv_len])
    return jnp.where(keep, 0.0, BIG)


def set_segments(seg_row, seg_col):
    for b in range(L // ROWS):
        at = slice(b * ROWS, (b + 1) * ROWS)
        seg_col[at, :] = column(seg_row[:, at].astype(F32))


def forward_kernel(
    tokens, routes, shared_mask, norm_gain, ffn_gain, w_router, w_query, key_weight, value_weight, w_out,
    shared_gate, shared_up, shared_down, expert_gate, expert_up, expert_down, segments, cot,
    normed_one, qkv_out, heads_out, logs_out, gains, qkv_full_out, out_full_out, normed_two, all_cot,
    pre_a, pre_b, low_home, grad_hidden, grad_misc, out_far, out_own,
    marked, all_marked, qkv_block, out_block, block_a, block_b, qkv_full, out_full, normed, qkv, heads, logs, seg_col,
    marks, misc, part, near, far, normed_home, hidden, xs, cs, full_a, full_b,
    staged, near_g, far_g, near_out, own_gates, own_out,
    send_sems, token_sems, qkv_sems, out_sems, a_sems, b_sems, own_sems, scatter_sems, gather_sems, cot_sems,
    grad_sems, sum_sems, local_sems,
):
    here = Here(send_sems)
    local = Local(local_sems)
    here.greet()
    s = here.s

    def wide(ref, at, width):
        return ref[:, pl.ds(pl.multiple_of(at * width, LANES), width)]

    marked[:, :WIDTH] = tokens[...]
    line = iota((LANES, ROWS), 0)
    used = line == routes[0:1, :] + 2
    for k in range(1, 6):
        used = used | (line == routes[k : k + 1, :] + 2)
    turned = (jnp.where(used, 1.0, 0.0) + jnp.where(line == 1, shared_mask[...].astype(F32), 0.0)).astype(BF)
    eye = (iota((LANES, LANES), 0) == iota((LANES, LANES), 1)).astype(BF)
    marked[:, WIDTH:] = mm_tn(turned, eye).astype(BF)
    token_gather = seq_gather(here, marked, all_marked, token_sems, 13)
    qkv_block[:, :Q_COLS] = wide(w_query, s, Q_COLS)
    qkv_block[:, Q_COLS:KV] = wide(key_weight, s, HEAD)
    qkv_block[:, KV:] = wide(value_weight, s, HEAD)
    here.meet()
    qkv_gather = gather_weight(here, qkv_full, qkv_block, qkv_sems, own_sems.at[0], True)
    next(qkv_gather)
    out_block[:, :Q_COLS] = wide(w_out, s, Q_COLS)
    place = (iota((E, LANES), 1) == iota((E, LANES), 0) + 2).astype(F32)
    single = f32dot(w_router[...].astype(F32), place, ((0,), (0,)))
    lane = iota((SHARD, LANES), 1)
    single = single + jnp.where(lane == 0, column(norm_gain[...].astype(F32)), 0.0)
    out_block[:, Q_COLS:] = (single + jnp.where(lane == 1, column(ffn_gain[...].astype(F32)), 0.0)).astype(BF)
    out_gather = gather_weight(here, out_full, out_block, out_sems, own_sems.at[1], False)
    next(out_gather)
    next(token_gather)
    next(qkv_gather)
    next(out_gather)
    for k, block in enumerate((block_a, block_b)):
        pick = (iota((SHARD, SHARD * E), 1) == iota((SHARD, SHARD * E), 0) * E + 2 * s + k).astype(BF)
        for i, (shared, expert) in enumerate(((shared_gate, expert_gate), (shared_up, expert_up), (shared_down, expert_down))):
            block[:, i * HALF : i * HALF + 512] = mm(pick, expert[...].reshape(SHARD * E, 512)).astype(BF)
            block[:, i * HALF + 512 : (i + 1) * HALF] = wide(shared, 2 * s + k, HALF - 512)
    set_segments(segments, seg_col)
    weights = [
        gather_weight(here, full_a, block_a, a_sems, own_sems.at[2], True),
        gather_weight(here, full_b, block_b, b_sems, own_sems.at[3], False),
    ]
    for weight in weights:
        next(weight)
    together(token_gather, qkv_gather, out_gather, later(9, weights))

    def tick():
        for weight in weights:
            next(weight, None)

    cot_gather = seq_gather(here, cot, cs, cot_sems)
    next(cot_gather)
    misc[...] = out_full[:, :, :, :, Q_COLS:].reshape(WIDTH, LANES)
    gains[...] = mm_nt(eye, misc[...])[:8]
    gain = gains[0:1, :]
    seg_row = segments[...].astype(F32)
    for b in range(SEQ):
        at = slice(b * ROWS, (b + 1) * ROWS)
        normed[at, :] = normed_of(all_marked[b, :, :WIDTH].astype(F32), gain)[2]
        qkv[at, :] = mm(normed[at, :], qkv_full[...].reshape(WIDTH, HALF)).astype(BF)
        marks[at, :] = all_marked[b, :, WIDTH:]
        if b == 3:
            tick()
    saved = [local.copy(normed, normed_one), local.copy(qkv, qkv_out), local.copy(qkv_full, qkv_full_out)]
    saved.append(local.copy(out_full, out_full_out))
    for b in range(SEQ):
        at, kv_len = b * ROWS, (b + 1) * ROWS
        bias = mask_bias(at, kv_len, seg_col, seg_row)
        for h in range(GROUP):
            cols = slice(h * HEAD, (h + 1) * HEAD)
            scores = mm_nt(qkv[at : at + ROWS, cols], qkv[:kv_len, Q_COLS:KV]) * SCALE + bias
            top = jnp.max(scores, axis=-1, keepdims=True)
            weight = jnp.exp(scores - top)
            total = jnp.sum(weight, axis=-1, keepdims=True)
            probs = (weight * (1.0 / total)).astype(BF)
            heads[at : at + ROWS, cols] = mm(probs, qkv[:kv_len, KV:]).astype(BF)
            logs[at : at + ROWS, h : h + 1] = top + jnp.log(total)
        tick()

    saved += [local.copy(heads, heads_out), local.copy(logs, logs_out)]

    def project(i):
        rows = heads[pl.ds(pl.multiple_of(i * ROWS, ROWS), ROWS), :]
        part[i] = mm_nt(rows, out_full[:, :, :, :, :Q_COLS].reshape(WIDTH, Q_COLS)).astype(BF)

    def rows():
        yield from seq_scatter(here, part, near, far, scatter_sems, project, 2)
        next(cot_gather)
        hidden[...] = added(tokens[...], part[s], near[1], far[...])
        normed_home[...] = normed_of(hidden[...], gains[1:2, :])[2]
        yield from seq_gather(here, normed_home, xs, gather_sems, 3)
        next(cot_gather, None)

    together(rows(), *weights)
    for copy in saved:
        copy.wait()
    saved = [local.copy(xs, normed_two), local.copy(cs, all_cot)]
    here.finish_rows()
    order = (here.s_cross, here.s_far, here.s_near, s)
    sent, outs, far_sum, low_out = all_marked, part, far, normed_home
    lane = iota((ROWS, LANES), 1)
    stored = [[], []]

    def block(n):
        i = order[n]
        at = pl.ds(pl.multiple_of(i * ROWS, ROWS), ROWS)
        x, c = xs[i], cs[i]
        mark = marks[at, :].astype(F32)
        member = (mark > 0) & (lane >= 2) & (lane < 2 + E)
        logits = jnp.where(member, mm(x, misc[...]), BIG)
        soft = jnp.where(member, jnp.exp(logits - jnp.max(logits, axis=-1, keepdims=True)), 0.0)
        gates = soft / jnp.sum(soft, axis=-1, keepdims=True)
        if n == 3:
            own_gates[...] = gates
        keep = mark[:, 1:2]
        total = jnp.zeros((ROWS, WIDTH), F32)
        grad_x = jnp.zeros((ROWS, WIDTH), F32)
        grad_marks = jnp.zeros((ROWS, LANES), F32)
        for k, weight in enumerate((full_a, full_b)):
            if n >= 2:
                stored[k][n - 2].wait()
            slot = staged.at[n % 2, k]
            mine = lane == 2 + 2 * s + k
            gate_e = jnp.sum(jnp.where(mine, gates, 0.0), axis=-1, keepdims=True)
            coef = jnp.concatenate([jnp.broadcast_to(gate_e, (ROWS, 512)), jnp.broadcast_to(keep, (ROWS, HALF - 512))], axis=1)
            pre = mm(x, weight[:, :, :, :, : 2 * HALF].reshape(WIDTH, 2 * HALF))
            gate, upper = pre[:, :HALF], pre[:, HALF:]
            sigma = 1.0 / (1.0 + jnp.exp(-gate))
            silu = gate * sigma
            units = silu * upper
            weighted = (coef * units).astype(BF)
            slot[:, 2 * HALF :] = weighted
            total += mm_nt(weighted, weight[:, :, :, :, 2 * HALF :].reshape(WIDTH, HALF))
            grad_units = mm(c, weight[:, :, :, :, 2 * HALF :].reshape(WIDTH, HALF))
            grad_gate = jnp.sum((units * grad_units)[:, :512], axis=-1, keepdims=True)
            high = grad_gate.astype(BF).astype(F32)
            grad_marks += jnp.where(mine, high, 0.0) + jnp.where(lane == LOW + 2 + 2 * s + k, grad_gate - high, 0.0)
            grad_units = coef * grad_units
            slot[:, :HALF] = (grad_units * upper * (sigma * (1.0 + gate * (1.0 - sigma)))).astype(BF)
            slot[:, HALF : 2 * HALF] = (grad_units * silu).astype(BF)
            grad_x += mm_nt(slot[:, : 2 * HALF], weight[:, :, :, :, : 2 * HALF].reshape(WIDTH, 2 * HALF))
            stored[k].append(local.copy(slot, (pre_a, pre_b)[k].at[at]))
        outs[i] = total.astype(BF)
        sent[i, :, :WIDTH] = grad_x.astype(BF)
        sent[i, :, WIDTH:] = grad_marks.astype(BF)

    block(0)
    here.send(sent.at[here.s_cross], near_g.at[0], grad_sems.at[0], here.near, True)
    here.send(outs.at[here.s_cross], near_out.at[0], sum_sems.at[0], here.near, True)
    block(1)
    here.wait(near_g.at[0], grad_sems.at[0])
    near_g[0] = sent[here.s_far] + near_g[0]
    here.send(near_g.at[0], far_g, grad_sems.at[2], here.far, True)
    here.wait(near_out.at[0], sum_sems.at[0])
    far_sum[...] = outs[here.s_far] + near_out[0]
    saved.append(local.copy(far_sum, out_far))
    block(2)
    here.send(sent.at[here.s_near], near_g.at[1], grad_sems.at[1], here.near, True)
    here.send(outs.at[here.s_near], near_out.at[1], sum_sems.at[1], here.near, True)
    block(3)
    here.wait(near_g.at[1], grad_sems.at[1])
    here.wait(near_out.at[1], sum_sems.at[1])
    own_out[...] = added(hidden[...], outs[s], near_out[1])
    saved.append(local.copy(own_out, out_own))
    gain = gains[1:2, :]
    inverse, unit, normed_home = normed_of(hidden[...], gain)
    here.finish()
    here.wait(far_g, grad_sems.at[2])

    grad_gates = added(sent[s, :, WIDTH:], near_g[1, :, WIDTH:], far_g[:, WIDTH:])
    grad_gates = grad_gates + pltpu.roll(grad_gates, LANES - LOW, 1)
    gates = own_gates[...]
    grad_logits = gates * (grad_gates - jnp.sum(gates * grad_gates, axis=-1, keepdims=True))
    high, low = split_two(grad_logits)
    grad_normed = added(sent[s, :, :WIDTH], near_g[1, :, :WIDTH], far_g[:, :WIDTH])
    grad_normed = grad_normed + (mm_nt(high, misc[...]) + mm_nt(low, misc[...]))
    scaled = grad_normed * gain
    grad = cs[s].astype(F32) + inverse * (scaled - unit * jnp.mean(scaled * unit, axis=-1, keepdims=True))
    low_out[...] = grad.astype(BF)
    saved.append(local.copy(low_out, low_home))
    hidden[...] = grad
    saved.append(local.copy(hidden, grad_hidden))
    prod_high, prod_low = split_two(grad_normed * unit)
    one = (lane == 1).astype(BF)
    grad_misc[...] = mm_tn(normed_home, high) + mm_tn(normed_home, low) + mm_tn(prod_high, one) + mm_tn(prod_low, one)
    for copy in (*saved, *stored[0][2:], *stored[1][2:]):
        copy.wait()
    here.finish_rows()


def row_of(y, x, z):
    return pl.multiple_of(((y * 4 + x) * 2 + z) * SHARD, SHARD)


def finish_kernel(
    low_home, normed_two_in, cots_in, pre_a_in, pre_b_in,
    normed_in, qkv_in, heads_in, logs_in, qkv_full_in, out_full_in, out_far,
    segments, gains, grad_misc, grad_hidden, tokens,
    far_out, grad_tokens, grad_a, grad_b, ffn_a_all, ffn_b_all, one_all, two_all,
    grad_low, normed, part, pre_a, pre_b, staged, qkv, heads, logs, qkv_full, out_full,
    grad_one, grad_two, grad_heads, grad_all, grad_kv, near, far, gain_sum, seg_col,
    piece_a, piece_b, piece_one, piece_two,
    send_sems, local_sems, scatter_sems, out_sems, gather_sems, low_sems, *buffers,
):
    here = Here(send_sems)
    local = Local(local_sems)
    s = here.s
    load_a = [local.copy(normed_two_in, normed), local.copy(pre_a_in, pre_a), local.copy(cots_in, part)]
    load_b = local.copy(pre_b_in, pre_b)
    load_rest = [
        local.copy(a, b)
        for a, b in ((out_full_in, out_full), (heads_in, heads), (qkv_in, qkv), (logs_in, logs), (qkv_full_in, qkv_full))
    ]
    here.greet()
    here.meet()
    low_gather = seq_gather(here, low_home, grad_low, low_sems)
    next(low_gather)
    set_segments(segments, seg_col)
    seg_row = segments[...].astype(F32)

    def summed(sum_of, piece, full, sems, pause=1):
        yield from sum_of
        yield from seq_gather(here, piece, full, sems, pause)

    def from_hbm(grad, y_first):
        def block(df, ds, h):
            dy, dx = (ds, df) if y_first else (df, ds)
            return grad.at[pl.ds(row_of(wrap(here.y + dy), wrap(here.x + dx), h), SHARD)]

        return block

    def own_unit(place, j, ds, h):
        at = wrap(place + j)
        return at * 2 + h if ds == 0 else (8 if ds == 1 else 12) + at

    def owned(held, place):
        def own(j, ds, h):
            return held[pl.ds(pl.multiple_of(own_unit(place, j, ds, h) * SHARD, SHARD), SHARD), :]

        return own

    sum_a = scatter_grad(here, from_hbm(grad_a, True), owned(pre_a, here.x), buffers[:10], piece_a, True, False)
    sum_b = scatter_grad(here, from_hbm(grad_b, False), owned(pre_b, here.y), buffers[10:20], piece_b, False, False)
    sums = [summed(sum_a, piece_a, ffn_a_all, gather_sems.at[0], 4), summed(sum_b, piece_b, ffn_b_all, gather_sems.at[1], 4)]

    def chunk(y):
        return pl.ds(pl.multiple_of(y * CHUNK, CHUNK), CHUNK)

    moving = []
    for n, (j, k) in enumerate((j, k) for j in (2, 1, 3, 0) for k in range(2)):
        pre = (pre_a, pre_b)[k]
        if n == 0:
            load_a[0].wait()
            load_a[1].wait()
        if n == 1:
            load_b.wait()
        at = chunk(wrap(here.y + j))
        slot = staged.at[n % 2]
        slot[:, : 2 * HALF] = mm_tn(normed[:, at], pre[:, : 2 * HALF]).astype(BF)
        if n == 0:
            load_a[2].wait()
        if n > 1:
            moving[n - 1].wait()
            next(sums[(n - 1) % 2])
        slot[:, 2 * HALF :] = mm_tn(part[:, :, at].reshape(L, CHUNK), pre[:, 2 * HALF :]).astype(BF)
        moving.append(local.copy(slot, (grad_a, grad_b)[k].at[at]))
        if n == 0:
            moving[0].wait()
            next(sums[0])
    moving[-1].wait()
    next(sums[1])
    load_own = []
    for grad, held, y_first in ((grad_a, pre_a, True), (grad_b, pre_b, False)):
        for i in range(4):
            for ds, h in ((0, 0), (0, 1), (1, 0), (3, 1)):
                y, x = (wrap(here.y + ds), i) if y_first else (i, wrap(here.x + ds))
                unit = i * 2 + h if ds == 0 else (8 if ds == 1 else 12) + i
                source = grad.at[pl.ds(row_of(y, x, h), SHARD)]
                load_own.append(local.copy(source, held.at[pl.ds(unit * SHARD, SHARD)]))
    load_rest.append(local.copy(normed_in, normed))
    here.send(out_far, far_out, out_sems.at[0], here.far, True)
    next(low_gather)
    for load in load_own:
        load.wait()

    def tick():
        for part_sum in sums[:2]:
            next(part_sum)

    tick()
    next(low_gather, None)
    for load in load_rest:
        load.wait()
    for b in range(SEQ):
        at = slice(b * ROWS, (b + 1) * ROWS)
        grad_heads[at, :] = mm(grad_low[b], out_full[:, :Q_COLS]).astype(BF)

    def blocks_of(grad, y_first):
        def block(df, ds, h):
            dy, dx = (ds, df) if y_first else (df, ds)
            return grad.at[wrap(here.y + dy), wrap(here.x + dx), h]

        return block

    def out_chunk(y, carry):
        value = mm_tn(grad_low[:, :, chunk(y)].reshape(L, CHUNK), heads[...])
        grad_two[y, :, :, :, HEAD:KV] = value.astype(BF).reshape(4, 2, SHARD, Q_COLS)
        return carry

    lax.fori_loop(0, 4, out_chunk, 0)
    tick()
    grad_kv[...] = jnp.zeros_like(grad_kv)
    for b in range(SEQ):
        at, kv_len = b * ROWS, (b + 1) * ROWS
        bias = mask_bias(at, kv_len, seg_col, seg_row)
        for h in range(GROUP):
            cols = slice(h * HEAD, (h + 1) * HEAD)
            query, grad = qkv[at : at + ROWS, cols], grad_heads[at : at + ROWS, cols]
            scores = mm_nt(query, qkv[:kv_len, Q_COLS:KV]) * SCALE
            probs = jnp.exp((scores + bias) - logs[at : at + ROWS, h : h + 1])
            grad_probs = mm_nt(grad, qkv[:kv_len, KV:])
            centre = jnp.sum(probs * grad_probs, axis=-1, keepdims=True)
            grad_scores = (probs * (grad_probs - centre)).astype(BF)
            grad_all[at : at + ROWS, cols] = (mm(grad_scores, qkv[:kv_len, Q_COLS:KV]) * SCALE).astype(BF)
            grad_kv[:kv_len, :HEAD] += mm_tn(grad_scores, query) * SCALE
            grad_kv[:kv_len, HEAD:] += mm_tn(probs.astype(BF), grad)
    tick()
    grad_all[:, Q_COLS:] = grad_kv[...].astype(BF)

    def weight_chunk(y, carry):
        at = chunk(y)
        value = mm_tn(normed[:, at], grad_all[...]).astype(BF)
        grad_one[y] = value[:, :KV].reshape(4, 2, SHARD, KV)
        grad_two[y, :, :, :, :HEAD] = value[:, KV:].reshape(4, 2, SHARD, HEAD)
        return carry

    lax.fori_loop(0, 4, weight_chunk, 0)
    sum_one = scatter_grad(here, blocks_of(grad_one, True), None, buffers[20:30], piece_one, True, True)
    sums.append(summed(sum_one, piece_one, one_all, gather_sems.at[2]))
    tick()
    gain_sum[...] = jnp.zeros_like(gain_sum)

    def back(i):
        at = pl.ds(pl.multiple_of(i * ROWS, ROWS), ROWS)
        value = mm_nt(grad_all[at, :], qkv_full[...])
        part[i] = value.astype(BF)
        gain_sum[0:1, :] += jnp.sum(value * normed[at, :].astype(F32), axis=0, keepdims=True)

    row_sum = seq_scatter(here, part, near, far, scatter_sems, back, 4)
    next(row_sum)
    next(row_sum)
    tick()
    gain = gains[0:1, :]
    high, low = split_two(gain_sum[0:1, :] / gain)
    row = iota((16, WIDTH), 0)
    both = jnp.where(row == 0, high.astype(F32), 0.0) + jnp.where(row == 1, low.astype(F32), 0.0)
    pick = (iota((16, LANES), 1) == 0).astype(BF)
    single = (grad_misc[...] + mm_tn(both.astype(BF), pick)).astype(BF)
    grad_two[:, :, :, :, KV:] = single.reshape(4, 4, 2, SHARD, LANES)
    sum_two = scatter_grad(here, blocks_of(grad_two, False), None, buffers[30:], piece_two, False, True)
    sums.append(summed(sum_two, piece_two, two_all, gather_sems.at[3]))

    def rows():
        yield from row_sum
        here.wait(far_out, out_sems.at[0])
        grad_normed = added(part[s], near[1], far[...])
        inverse, unit, _ = normed_of(tokens[...].astype(F32), gain)
        scaled = grad_normed * gain
        grad_tokens[...] = (grad_hidden[...] + inverse * (scaled - unit * jnp.mean(scaled * unit, axis=-1, keepdims=True))).astype(BF)

    here.finish(64)
    together(*sums, rows())
    here.finish()
    here.finish_rows()


def as_row(col):
    n = col.shape[0]
    return jnp.sum(jnp.where(iota((n, n), 0) == iota((n, n), 1), jnp.broadcast_to(col, (n, n)), 0.0), axis=0, keepdims=True)


def outputs_kernel(
    ffn_a, ffn_b, one, two, out_own, far_out, output, wq, wk, wv, wo, gain_one, gain_two, router, shared_gate, shared_up, shared_down, expert_gate, expert_up, expert_down
):
    output[...] = added(out_own[...], far_out[...]).astype(BF)
    total = jnp.zeros((SHARD, LANES), F32)
    for s in range(SEQ):
        wq[:, s * Q_COLS : (s + 1) * Q_COLS] = one[s, :, :Q_COLS].astype(F32)
        wo[:, s * Q_COLS : (s + 1) * Q_COLS] = two[s, :, HEAD:KV].astype(F32)
        wk[:, s * HEAD : (s + 1) * HEAD] = one[s, :, Q_COLS:].astype(F32)
        wv[:, s * HEAD : (s + 1) * HEAD] = two[s, :, :HEAD].astype(F32)
        total = total + two[s, :, KV:].astype(F32)
        for k, ffn in enumerate((ffn_a, ffn_b)):
            n = 2 * s + k
            for i, (shared, expert) in enumerate(((shared_gate, expert_gate), (shared_up, expert_up), (shared_down, expert_down))):
                expert[:, n, :] = ffn[s, :, i * HALF : i * HALF + 512].astype(F32)
                shared[:, n * LANES : (n + 1) * LANES] = ffn[s, :, i * HALF + 512 : (i + 1) * HALF].astype(F32)
    gain_one[...] = as_row(total[:, 0:1])
    gain_two[...] = as_row(total[:, 1:2])
    for e in range(E):
        router[e : e + 1, :] = as_row(total[:, 2 + e : 3 + e])


def remote_call(kernel, name, number, outs, ins, scratch):
    return pl.pallas_call(
        kernel,
        out_shape=[jax.ShapeDtypeStruct(dims, dtype) for dims, dtype, _ in outs],
        in_specs=[VMEM_ALL if fast else ANY for _, fast in ins],
        out_specs=[VMEM_ALL if fast else ANY for _, _, fast in outs],
        scratch_shapes=list(scratch),
        compiler_params=pltpu.CompilerParams(collective_id=number, has_side_effects=True, vmem_limit_bytes=LIMIT),
        name=name,
    )(*[array for array, _ in ins])


def buf(*dims):
    return pltpu.VMEM(dims, BF)


def buf32(*dims):
    return pltpu.VMEM(dims, F32)


def body(
    tokens,
    segments,
    routes,
    shared_mask,
    norm_gain,
    w_query,
    key_weight,
    value_weight,
    w_out,
    ffn_gain,
    w_router,
    shared_gate,
    shared_up,
    shared_down,
    expert_gate,
    expert_up,
    expert_down,
    cotangent,
):
    seg_row = segments[None, :]
    grid = DMA((4, 4, 2))
    rows4 = (SEQ, ROWS, WIDTH)
    fast = [tokens, routes.T, shared_mask[None, :], norm_gain[None, :], ffn_gain[None, :], w_router.T, w_query, key_weight,
            value_weight, w_out, shared_gate, shared_up, shared_down, expert_gate, expert_up, expert_down, seg_row]
    (
        normed_one, qkv, heads, logs, gains, qkv_full, out_full, normed_two, all_cot,
        pre_a, pre_b, low_home, grad_hidden, grad_misc, out_far, out_own,
    ) = remote_call(
        forward_kernel,
        "forward",
        1,
        [
            ((L, WIDTH), BF, False),
            ((L, HALF), BF, False),
            ((L, Q_COLS), BF, False),
            ((L, 8), F32, False),
            ((8, WIDTH), F32, True),
            (blocks(HALF), BF, False),
            (blocks(OUT_COLS), BF, False),
            (rows4, BF, False),
            (rows4, BF, False),
            ((L, FFN), BF, False),
            ((L, FFN), BF, False),
            ((ROWS, WIDTH), BF, False),
            ((ROWS, WIDTH), F32, False),
            ((WIDTH, LANES), F32, True),
            ((ROWS, WIDTH), BF, False),
            ((ROWS, WIDTH), F32, False),
        ],
        [(a, True) for a in fast] + [(cotangent, False)],
        [
            buf(ROWS, WIDTH + LANES),
            buf(SEQ, ROWS, WIDTH + LANES),
            buf(SHARD, HALF),
            buf(SHARD, OUT_COLS),
            buf(SHARD, FFN),
            buf(SHARD, FFN),
            buf(*blocks(HALF)),
            buf(*blocks(OUT_COLS)),
            buf(L, WIDTH),
            buf(L, HALF),
            buf(L, Q_COLS),
            buf32(L, 8),
            buf32(L, 1),
            buf(L, LANES),
            buf(WIDTH, LANES),
            buf(*rows4),
            buf(2, ROWS, WIDTH),
            buf(ROWS, WIDTH),
            buf(ROWS, WIDTH),
            buf32(ROWS, WIDTH),
            buf(*rows4),
            buf(*rows4),
            buf(*blocks(FFN)),
            buf(*blocks(FFN)),
            buf(2, 2, ROWS, FFN),
            buf(2, ROWS, WIDTH + LANES),
            buf(ROWS, WIDTH + LANES),
            buf(2, ROWS, WIDTH),
            buf32(ROWS, LANES),
            buf32(ROWS, WIDTH),
            DMA((160,)),
            DMA((4,)),
            grid,
            grid,
            grid,
            grid,
            DMA((4,)),
            DMA((3,)),
            DMA((4,)),
            DMA((4,)),
            DMA((3,)),
            DMA((2,)),
            DMA((24,)),
        ],
    )

    far_out, grad_tokens, _, _, ffn_a_all, ffn_b_all, one_all, two_all = remote_call(
        finish_kernel,
        "finish",
        2,
        [
            ((ROWS, WIDTH), BF, False),
            ((ROWS, WIDTH), BF, True),
            ((WIDTH, FFN), BF, False),
            ((WIDTH, FFN), BF, False),
            ((SEQ, SHARD, FFN), BF, False),
            ((SEQ, SHARD, FFN), BF, False),
            ((SEQ, SHARD, KV), BF, False),
            ((SEQ, SHARD, HALF), BF, False),
        ],
        [
            (low_home, False),
            (normed_two.reshape(L, WIDTH), False),
            (all_cot, False),
            (pre_a, False),
            (pre_b, False),
            (normed_one, False),
            (qkv, False),
            (heads, False),
            (logs, False),
            (qkv_full.reshape(WIDTH, HALF), False),
            (out_full.reshape(WIDTH, OUT_COLS), False),
            (out_far, False),
            (seg_row, True),
            (gains, True),
            (grad_misc, True),
            (grad_hidden, True),
            (tokens, True),
        ],
        [
            buf(*rows4),
            buf(L, WIDTH),
            buf(*rows4),
            buf(L, FFN),
            buf(L, FFN),
            buf(2, CHUNK, FFN),
            buf(L, HALF),
            buf(L, Q_COLS),
            buf32(L, 8),
            buf(WIDTH, HALF),
            buf(WIDTH, OUT_COLS),
            buf(*blocks(KV)),
            buf(*blocks(HALF)),
            buf(L, Q_COLS),
            buf(L, HALF),
            buf32(L, 2 * HEAD),
            buf(2, ROWS, WIDTH),
            buf(ROWS, WIDTH),
            buf32(16, WIDTH),
            buf32(L, 1),
            buf(SHARD, FFN),
            buf(SHARD, FFN),
            buf(SHARD, KV),
            buf(SHARD, HALF),
            DMA((192,)),
            DMA((56,)),
            DMA((3,)),
            DMA((1,)),
            DMA((4, 4)),
            DMA((4,)),
            *scatter_buffers(FFN),
            *scatter_buffers(FFN),
            *scatter_buffers(KV),
            *scatter_buffers(HALF),
        ],
    )

    dims = [(ROWS, WIDTH), (SHARD, 4 * Q_COLS), (SHARD, 4 * HEAD), (SHARD, 4 * HEAD), (SHARD, 4 * Q_COLS), (1, SHARD), (1, SHARD), (E, SHARD)]
    dims += [(SHARD, 1024)] * 3 + [(SHARD, E, 512)] * 3
    output, wq, wk, wv, wo, gain_one, gain_two, router, *ffn = pl.pallas_call(
        outputs_kernel,
        out_shape=[jax.ShapeDtypeStruct(d, BF if d[0] == ROWS else F32) for d in dims],
        in_specs=[VMEM_ALL] * 6,
        out_specs=[VMEM_ALL] * len(dims),
        compiler_params=pltpu.CompilerParams(vmem_limit_bytes=LIMIT),
        name="outputs",
    )(ffn_a_all, ffn_b_all, one_all, two_all, out_own, far_out)
    return (output, grad_tokens, gain_one[0], wq, wk, wv, wo, gain_two[0], router.T, *ffn)


def solution(mesh):
    both = P(("fsdp", "seq"), None)
    one, two, three = P("fsdp"), P("fsdp", None), P("fsdp", None, None)
    return jax.shard_map(
        body,
        mesh=mesh,
        in_specs=(both, one, both, P(("fsdp", "seq")), one, two, two, two, two, one, two, two, two, two, three, three, three, both),
        out_specs=(both, both, one, two, two, two, two, one, two, two, two, two, three, three, three),
        check_vma=False,
    )
```

```python
import jax
import jax.numpy as jnp
from jax import lax
from jax.experimental import pallas as pl
from jax.experimental.pallas import tpu as pltpu
from jax.sharding import PartitionSpec as P

HEAD = 128
GROUP = 3
E = 8
SEQ = 4
EPS = 1e-05
BF = jnp.bfloat16
F32 = jnp.float32
WIDTH = 1536
L = 1024
ROWS = 256
SHARD = 48
Q_COLS = GROUP * HEAD
KV = Q_COLS + HEAD
HALF = 640
FFN = 3 * HALF
LANES = 128
OUT_COLS = Q_COLS + LANES
LOW = 32
CHUNK = 384
SCALE = HEAD ** (-0.5)
BIG = -1e30
MESH = pl.DeviceIdType.MESH
VMEM_ALL = pl.BlockSpec(memory_space=pltpu.VMEM)
ANY = pl.BlockSpec(memory_space=pl.ANY)
DMA = pltpu.SemaphoreType.DMA
LIMIT = 63 * 1024 * 1024


def f32dot(left, right, dims):
    return lax.dot_general(left, right, (dims, ((), ())), preferred_element_type=F32)


def mm(left, right):
    return f32dot(left, right, ((1,), (0,)))


def mm_nt(left, right):
    return f32dot(left, right, ((1,), (1,)))


def mm_tn(left, right):
    return f32dot(left, right, ((0,), (0,)))


def iota(dims, axis):
    return lax.broadcasted_iota(jnp.int32, dims, axis)


def column(row):
    n = row.shape[1]
    same = iota((n, n), 0) == iota((n, n), 1)
    return jnp.sum(jnp.where(same, jnp.broadcast_to(row, (n, n)), 0.0), axis=-1, keepdims=True)


def added(*values):
    total = values[0].astype(F32)
    for value in values[1:]:
        total = total + value.astype(F32)
    return total


def split_two(value):
    high = value.astype(BF)
    return high, (value - high.astype(F32)).astype(BF)


def normed_of(x, gain):
    inverse = lax.rsqrt(jnp.mean(x * x, axis=-1, keepdims=True) + EPS)
    unit = x * inverse
    return inverse, unit, (unit * gain).astype(BF)


def wrap(value):
    return lax.rem(value + 4, 4)


def blocks(cols):
    return (4, 4, 2, SHARD, cols)


class Here:
    def __init__(self, send_sems):
        f, s = lax.axis_index("fsdp"), lax.axis_index("seq")
        self.y, self.x, self.z = lax.div(f, 8), lax.rem(lax.div(f, 2), 4), lax.rem(f, 2)
        self.s, self.zh, self.core = s, lax.div(s, 2), lax.rem(s, 2)
        y, x, z = self.y, self.x, self.z
        self.axis_x = ({"fsdp": self.number(y, wrap(x + 1), z)}, {"fsdp": self.number(y, wrap(x - 1), z)})
        self.axis_y = ({"fsdp": self.number(wrap(y + 1), x, z)}, {"fsdp": self.number(wrap(y - 1), x, z)})
        self.pair = {"fsdp": self.number(y, x, 1 - z)}
        self.s_far = (1 - self.zh) * 2 + self.core
        self.s_near = self.zh * 2 + 1 - self.core
        self.s_cross = (1 - self.zh) * 2 + 1 - self.core
        self.far = {"seq": self.s_far}
        self.near = {"seq": self.s_near}
        self.sems, self.count, self.sent, self.row_sent = send_sems, 0, [], []

    @staticmethod
    def number(y, x, z):
        return (y * 4 + x) * 2 + z

    def greet(self):
        partners = [*self.axis_x, *self.axis_y, self.pair, self.far, self.near]
        for partner in partners:
            pl.semaphore_signal(pltpu.get_barrier_semaphore(), inc=1, device_id=partner, device_id_type=MESH)

    def meet(self):
        pl.semaphore_wait(pltpu.get_barrier_semaphore(), 7)

    def send(self, source, target, recv_sem, to, rows=False):
        copy = pltpu.make_async_remote_copy(
            src_ref=source,
            dst_ref=target,
            send_sem=self.sems.at[self.count],
            recv_sem=recv_sem,
            device_id=to,
            device_id_type=MESH,
        )
        copy.start()
        self.count += 1
        (self.row_sent if rows else self.sent).append(copy)

    def wait(self, target, recv_sem):
        pltpu.make_async_remote_copy(
            src_ref=target,
            dst_ref=target,
            send_sem=self.sems.at[0],
            recv_sem=recv_sem,
            device_id=self.near,
            device_id_type=MESH,
        ).wait_recv()

    def finish(self, most=None):
        for copy in self.sent[:most]:
            copy.wait_send()
        self.sent = [] if most is None else self.sent[most:]

    def finish_rows(self):
        for copy in self.row_sent:
            copy.wait_send()
        self.row_sent = []


class Local:
    def __init__(self, sems):
        self.sems, self.count = sems, 0

    def copy(self, source, target):
        copy = pltpu.make_async_copy(source, target, self.sems.at[self.count])
        copy.start()
        self.count += 1
        return copy


def together(*parts):
    left = list(parts)
    while left:
        for part in list(left):
            if next(part, "end") == "end":
                left.remove(part)


def later(turns, parts):
    for _ in range(turns):
        yield
    for part in parts:
        next(part)


def gather_weight(here, full, block, recv, own_sem, x_first):
    first, second = (here.axis_x, here.axis_y) if x_first else (here.axis_y, here.axis_x)

    def spot(df, ds, r):
        dy, dx = (ds, df) if x_first else (df, ds)
        return wrap(here.y + dy), wrap(here.x + dx), here.z if r == 0 else 1 - here.z

    def push(df, ds, r, to, source=None):
        at = spot(df, ds, r)
        here.send(full.at[at] if source is None else source, full.at[at], recv.at[at], to)

    def take(df, ds, r):
        at = spot(df, ds, r)
        here.wait(full.at[at], recv.at[at])

    own = pltpu.make_async_copy(block, full.at[spot(0, 0, 0)], own_sem)
    own.start()
    push(0, 0, 0, here.pair, block)
    yield
    for to in (*second, *first):
        push(0, 0, 0, to, block)
    yield
    take(0, 0, 1)
    for to in (*first, *second):
        push(0, 0, 1, to)
    for df, r in ((-1, 0), (1, 0), (1, 1), (-1, 1), (2, 0), (2, 1)):
        yield
        take(df, 0, r)
        if (df, r) == (-1, 0):
            push(df, 0, r, first[0])
        if (df, r) == (1, 1):
            push(df, 0, r, first[1])
        for to in second:
            push(df, 0, r, to)
        if (df, r) == (1, 0):
            take(0, -1, 0)
            push(0, -1, 0, second[0])
        if (df, r) == (-1, 1):
            take(0, 1, 1)
            push(0, 1, 1, second[1])
    for df in (-1, 1, 2):
        yield
        take(df, -1, 0)
        push(df, -1, 0, second[0])
        yield
        take(df, 1, 1)
        push(df, 1, 1, second[1])
    yield
    for df in (0, -1, 1, 2):
        take(df, -1, 1)
        take(df, 1, 0)
        take(df, 2, 0)
        take(df, 2, 1)
    own.wait()


def scatter_buffers(cols):
    units = [(4,), (4,), (4, 2), (4, 2), (1,), (1,), (2,), (2,), (1,)]
    return [pltpu.VMEM((*u, SHARD, cols), BF) for u in units] + [DMA((31,))]


def scatter_grad(here, block, own, buffers, piece, y_first, small):
    ra, rb, rc, rd, xa, xb, xc, xd, zr, sems = buffers
    second, first = (here.axis_y, here.axis_x) if y_first else (here.axis_x, here.axis_y)
    own = own or (lambda df, ds, h: block(df, ds, h)[...])

    def far_send(j):
        here.send(block(j, 2, 0), ra.at[j], sems.at[j], second[0])
        here.send(block(j, 2, 1), rb.at[j], sems.at[4 + j], second[1])

    def near_plus(j):
        here.send(block(j, 1, 1), rc.at[j, 1], sems.at[8 + 2 * j + 1], second[0])

    def near_minus(j):
        here.send(block(j, 3, 0), rd.at[j, 0], sems.at[16 + 2 * j], second[1])

    def pass_on(j):
        here.wait(ra.at[j], sems.at[j])
        ra[j] = own(j, 1, 0) + ra[j]
        here.send(ra.at[j], rc.at[j, 0], sems.at[8 + 2 * j], second[0])
        here.wait(rb.at[j], sems.at[4 + j])
        rb[j] = own(j, 3, 1) + rb[j]
        here.send(rb.at[j], rd.at[j, 1], sems.at[16 + 2 * j + 1], second[1])

    def total(j):
        for h in range(2):
            here.wait(rc.at[j, h], sems.at[8 + 2 * j + h])
            here.wait(rd.at[j, h], sems.at[16 + 2 * j + h])
            rc[j, h] = own(j, 0, h) + (rc[j, h] + rd[j, h])

    def turn_two():
        here.send(rc.at[2, 0], xa.at[0], sems.at[24], first[0])
        here.send(rc.at[2, 1], xb.at[0], sems.at[25], first[1])

    def turn_near():
        here.send(rc.at[1, 1], xc.at[1], sems.at[27], first[0])
        here.send(rc.at[3, 0], xd.at[0], sems.at[28], first[1])

    def turn_on():
        here.wait(xa.at[0], sems.at[24])
        xa[0] = rc[1, 0] + xa[0]
        here.send(xa.at[0], xc.at[0], sems.at[26], first[0])
        here.wait(xb.at[0], sems.at[25])
        xb[0] = rc[3, 1] + xb[0]
        here.send(xb.at[0], xd.at[1], sems.at[29], first[1])

    every = (2, 1, 3, 0)
    if small:
        for j in every:
            far_send(j)
            near_plus(j)
            near_minus(j)
        yield
        for j in every:
            pass_on(j)
        yield
        total(2)
        turn_two()
        total(1)
        total(3)
        turn_near()
        yield
        turn_on()
        total(0)
        yield
    else:
        if y_first:
            for send in (far_send, near_plus, near_minus):
                for j in every:
                    send(j)
                yield
        else:
            for j in every:
                far_send(j)
                near_plus(j)
                near_minus(j)
                yield
        if y_first:
            yield
        pass_on(2)
        pass_on(1)
        yield
        pass_on(3)
        pass_on(0)
        yield
        total(2)
        turn_two()
        yield
        total(1)
        total(3)
        turn_near()
        yield
        total(0)
        yield
        turn_on()
        yield
    for h in range(2):
        here.wait(xc.at[h], sems.at[26 + h])
        here.wait(xd.at[h], sems.at[28 + h])
        xc[h] = rc[0, h] + (xc[h] + xd[h])
    here.send(xc.at[1 - here.z], zr.at[0], sems.at[30], here.pair)
    yield
    here.wait(zr.at[0], sems.at[30])
    piece[...] = added(xc[here.z], zr[0]).astype(piece.dtype)


def row_parts(count):
    return [pl.ds(0, count // 2), pl.ds(count // 2, count // 2)] if count == ROWS else [pl.ds(0, count)]


def seq_gather(here, source, full, sems, pause=1):
    parts = row_parts(source.shape[0])
    own = pltpu.make_async_copy(source, full.at[here.s], sems.at[5])
    own.start()
    for k, rows in enumerate(parts):
        here.send(source.at[rows], full.at[here.s, rows], sems.at[k], here.far, True)
    here.send(source, full.at[here.s], sems.at[4], here.near, True)
    for _ in range(pause):
        yield
    for k, rows in enumerate(parts):
        here.wait(full.at[here.s_far, rows], sems.at[k])
        here.send(full.at[here.s_far, rows], full.at[here.s_far, rows], sems.at[2 + k], here.near, True)
    yield
    here.wait(full.at[here.s_near], sems.at[4])
    for k, rows in enumerate(parts):
        here.wait(full.at[here.s_cross, rows], sems.at[2 + k])
    own.wait()


def seq_scatter(here, parts, near, far, sems, make, pause=1):
    make(here.s_cross)
    for k, rows in enumerate(row_parts(ROWS)):
        here.send(parts.at[here.s_cross, rows], near.at[0, rows], sems.at[k], here.near, True)
    make(here.s_far)
    yield
    for k, rows in enumerate(row_parts(ROWS)):
        here.wait(near.at[0, rows], sems.at[k])
        near[0, rows] = parts[here.s_far, rows] + near[0, rows]
        here.send(near.at[0, rows], far.at[rows], sems.at[3 + k], here.far, True)
    make(here.s_near)
    here.send(parts.at[here.s_near], near.at[1], sems.at[2], here.near, True)
    make(here.s)
    yield
    here.wait(near.at[1], sems.at[2])
    for _ in range(pause):
        yield
    for k, rows in enumerate(row_parts(ROWS)):
        here.wait(far.at[rows], sems.at[3 + k])


def mask_bias(at, kv_len, seg_col, seg_row):
    q_pos = at + iota((ROWS, kv_len), 0)
    k_pos = iota((ROWS, kv_len), 1)
    keep = (q_pos >= k_pos) & (seg_col[at : at + ROWS, :] == seg_row[:, :kv_len])
    return jnp.where(keep, 0.0, BIG)


def set_segments(seg_row, seg_col):
    for b in range(L // ROWS):
        at = slice(b * ROWS, (b + 1) * ROWS)
        seg_col[at, :] = column(seg_row[:, at].astype(F32))


def forward_kernel(
    tokens, routes, shared_mask, norm_gain, ffn_gain, w_router, w_query, key_weight, value_weight, w_out,
    shared_gate, shared_up, shared_down, expert_gate, expert_up, expert_down, segments, cot,
    normed_one, qkv_out, heads_out, logs_out, gains, qkv_full_out, out_full_out, normed_two, all_cot,
    pre_a, pre_b, low_home, grad_hidden, grad_misc, out_far, out_own,
    marked, all_marked, qkv_block, out_block, block_a, block_b, qkv_full, out_full, normed, qkv, heads, logs, seg_col,
    marks, misc, part, near, far, normed_home, hidden, xs, cs, full_a, full_b,
    staged, near_g, far_g, near_out, own_gates, own_out,
    send_sems, token_sems, qkv_sems, out_sems, a_sems, b_sems, own_sems, scatter_sems, gather_sems, cot_sems,
    grad_sems, sum_sems, local_sems,
):
    here = Here(send_sems)
    local = Local(local_sems)
    here.greet()
    s = here.s

    def wide(ref, at, width):
        return ref[:, pl.ds(pl.multiple_of(at * width, LANES), width)]

    marked[:, :WIDTH] = tokens[...]
    line = iota((LANES, ROWS), 0)
    used = line == routes[0:1, :] + 2
    for k in range(1, 6):
        used = used | (line == routes[k : k + 1, :] + 2)
    turned = (jnp.where(used, 1.0, 0.0) + jnp.where(line == 1, shared_mask[...].astype(F32), 0.0)).astype(BF)
    eye = (iota((LANES, LANES), 0) == iota((LANES, LANES), 1)).astype(BF)
    marked[:, WIDTH:] = mm_tn(turned, eye).astype(BF)
    token_gather = seq_gather(here, marked, all_marked, token_sems, 13)
    qkv_block[:, :Q_COLS] = wide(w_query, s, Q_COLS)
    qkv_block[:, Q_COLS:KV] = wide(key_weight, s, HEAD)
    qkv_block[:, KV:] = wide(value_weight, s, HEAD)
    here.meet()
    qkv_gather = gather_weight(here, qkv_full, qkv_block, qkv_sems, own_sems.at[0], True)
    next(qkv_gather)
    out_block[:, :Q_COLS] = wide(w_out, s, Q_COLS)
    place = (iota((E, LANES), 1) == iota((E, LANES), 0) + 2).astype(F32)
    single = f32dot(w_router[...].astype(F32), place, ((0,), (0,)))
    lane = iota((SHARD, LANES), 1)
    single = single + jnp.where(lane == 0, column(norm_gain[...].astype(F32)), 0.0)
    out_block[:, Q_COLS:] = (single + jnp.where(lane == 1, column(ffn_gain[...].astype(F32)), 0.0)).astype(BF)
    out_gather = gather_weight(here, out_full, out_block, out_sems, own_sems.at[1], False)
    next(out_gather)
    next(token_gather)
    next(qkv_gather)
    next(out_gather)
    for k, block in enumerate((block_a, block_b)):
        pick = (iota((SHARD, SHARD * E), 1) == iota((SHARD, SHARD * E), 0) * E + 2 * s + k).astype(BF)
        for i, (shared, expert) in enumerate(((shared_gate, expert_gate), (shared_up, expert_up), (shared_down, expert_down))):
            block[:, i * HALF : i * HALF + 512] = mm(pick, expert[...].reshape(SHARD * E, 512)).astype(BF)
            block[:, i * HALF + 512 : (i + 1) * HALF] = wide(shared, 2 * s + k, HALF - 512)
    set_segments(segments, seg_col)
    weights = [
        gather_weight(here, full_a, block_a, a_sems, own_sems.at[2], True),
        gather_weight(here, full_b, block_b, b_sems, own_sems.at[3], False),
    ]
    for weight in weights:
        next(weight)
    together(token_gather, qkv_gather, out_gather, later(9, weights))

    def tick():
        for weight in weights:
            next(weight, None)

    cot_gather = seq_gather(here, cot, cs, cot_sems)
    next(cot_gather)
    misc[...] = out_full[:, :, :, :, Q_COLS:].reshape(WIDTH, LANES)
    gains[...] = mm_nt(eye, misc[...])[:8]
    gain = gains[0:1, :]
    seg_row = segments[...].astype(F32)
    for b in range(SEQ):
        at = slice(b * ROWS, (b + 1) * ROWS)
        normed[at, :] = normed_of(all_marked[b, :, :WIDTH].astype(F32), gain)[2]
        qkv[at, :] = mm(normed[at, :], qkv_full[...].reshape(WIDTH, HALF)).astype(BF)
        marks[at, :] = all_marked[b, :, WIDTH:]
        if b == 3:
            tick()
    saved = [local.copy(normed, normed_one), local.copy(qkv, qkv_out), local.copy(qkv_full, qkv_full_out)]
    saved.append(local.copy(out_full, out_full_out))
    for b in range(SEQ):
        at, kv_len = b * ROWS, (b + 1) * ROWS
        bias = mask_bias(at, kv_len, seg_col, seg_row)
        for h in range(GROUP):
            cols = slice(h * HEAD, (h + 1) * HEAD)
            scores = mm_nt(qkv[at : at + ROWS, cols], qkv[:kv_len, Q_COLS:KV]) * SCALE + bias
            top = jnp.max(scores, axis=-1, keepdims=True)
            weight = jnp.exp(scores - top)
            total = jnp.sum(weight, axis=-1, keepdims=True)
            probs = (weight * (1.0 / total)).astype(BF)
            heads[at : at + ROWS, cols] = mm(probs, qkv[:kv_len, KV:]).astype(BF)
            logs[at : at + ROWS, h : h + 1] = top + jnp.log(total)
        tick()

    saved += [local.copy(heads, heads_out), local.copy(logs, logs_out)]

    def project(i):
        rows = heads[pl.ds(pl.multiple_of(i * ROWS, ROWS), ROWS), :]
        part[i] = mm_nt(rows, out_full[:, :, :, :, :Q_COLS].reshape(WIDTH, Q_COLS)).astype(BF)

    def rows():
        yield from seq_scatter(here, part, near, far, scatter_sems, project, 2)
        next(cot_gather)
        hidden[...] = added(tokens[...], part[s], near[1], far[...])
        normed_home[...] = normed_of(hidden[...], gains[1:2, :])[2]
        yield from seq_gather(here, normed_home, xs, gather_sems, 3)
        next(cot_gather, None)

    together(rows(), *weights)
    for copy in saved:
        copy.wait()
    saved = [local.copy(xs, normed_two), local.copy(cs, all_cot)]
    here.finish_rows()
    order = (here.s_cross, here.s_far, here.s_near, s)
    sent, outs, far_sum, low_out = all_marked, part, far, normed_home
    lane = iota((ROWS, LANES), 1)
    stored = [[], []]

    def block(n):
        i = order[n]
        at = pl.ds(pl.multiple_of(i * ROWS, ROWS), ROWS)
        x, c = xs[i], cs[i]
        mark = marks[at, :].astype(F32)
        member = (mark > 0) & (lane >= 2) & (lane < 2 + E)
        logits = jnp.where(member, mm(x, misc[...]), BIG)
        soft = jnp.where(member, jnp.exp(logits - jnp.max(logits, axis=-1, keepdims=True)), 0.0)
        gates = soft / jnp.sum(soft, axis=-1, keepdims=True)
        if n == 3:
            own_gates[...] = gates
        keep = mark[:, 1:2]
        total = jnp.zeros((ROWS, WIDTH), F32)
        grad_x = jnp.zeros((ROWS, WIDTH), F32)
        grad_marks = jnp.zeros((ROWS, LANES), F32)
        for k, weight in enumerate((full_a, full_b)):
            if n >= 2:
                stored[k][n - 2].wait()
            slot = staged.at[n % 2, k]
            mine = lane == 2 + 2 * s + k
            gate_e = jnp.sum(jnp.where(mine, gates, 0.0), axis=-1, keepdims=True)
            coef = jnp.concatenate([jnp.broadcast_to(gate_e, (ROWS, 512)), jnp.broadcast_to(keep, (ROWS, HALF - 512))], axis=1)
            pre = mm(x, weight[:, :, :, :, : 2 * HALF].reshape(WIDTH, 2 * HALF))
            gate, upper = pre[:, :HALF], pre[:, HALF:]
            sigma = 1.0 / (1.0 + jnp.exp(-gate))
            silu = gate * sigma
            units = silu * upper
            weighted = (coef * units).astype(BF)
            slot[:, 2 * HALF :] = weighted
            total += mm_nt(weighted, weight[:, :, :, :, 2 * HALF :].reshape(WIDTH, HALF))
            grad_units = mm(c, weight[:, :, :, :, 2 * HALF :].reshape(WIDTH, HALF))
            grad_gate = jnp.sum((units * grad_units)[:, :512], axis=-1, keepdims=True)
            high = grad_gate.astype(BF).astype(F32)
            grad_marks += jnp.where(mine, high, 0.0) + jnp.where(lane == LOW + 2 + 2 * s + k, grad_gate - high, 0.0)
            grad_units = coef * grad_units
            slot[:, :HALF] = (grad_units * upper * (sigma * (1.0 + gate * (1.0 - sigma)))).astype(BF)
            slot[:, HALF : 2 * HALF] = (grad_units * silu).astype(BF)
            grad_x += mm_nt(slot[:, : 2 * HALF], weight[:, :, :, :, : 2 * HALF].reshape(WIDTH, 2 * HALF))
            stored[k].append(local.copy(slot, (pre_a, pre_b)[k].at[at]))
        outs[i] = total.astype(BF)
        sent[i, :, :WIDTH] = grad_x.astype(BF)
        sent[i, :, WIDTH:] = grad_marks.astype(BF)

    block(0)
    here.send(sent.at[here.s_cross], near_g.at[0], grad_sems.at[0], here.near, True)
    here.send(outs.at[here.s_cross], near_out.at[0], sum_sems.at[0], here.near, True)
    block(1)
    here.wait(near_g.at[0], grad_sems.at[0])
    near_g[0] = sent[here.s_far] + near_g[0]
    here.send(near_g.at[0], far_g, grad_sems.at[2], here.far, True)
    here.wait(near_out.at[0], sum_sems.at[0])
    far_sum[...] = outs[here.s_far] + near_out[0]
    saved.append(local.copy(far_sum, out_far))
    block(2)
    here.send(sent.at[here.s_near], near_g.at[1], grad_sems.at[1], here.near, True)
    here.send(outs.at[here.s_near], near_out.at[1], sum_sems.at[1], here.near, True)
    block(3)
    here.wait(near_g.at[1], grad_sems.at[1])
    here.wait(near_out.at[1], sum_sems.at[1])
    own_out[...] = added(hidden[...], outs[s], near_out[1])
    saved.append(local.copy(own_out, out_own))
    gain = gains[1:2, :]
    inverse, unit, normed_home = normed_of(hidden[...], gain)
    here.finish()
    here.wait(far_g, grad_sems.at[2])

    grad_gates = added(sent[s, :, WIDTH:], near_g[1, :, WIDTH:], far_g[:, WIDTH:])
    grad_gates = grad_gates + pltpu.roll(grad_gates, LANES - LOW, 1)
    gates = own_gates[...]
    grad_logits = gates * (grad_gates - jnp.sum(gates * grad_gates, axis=-1, keepdims=True))
    high, low = split_two(grad_logits)
    grad_normed = added(sent[s, :, :WIDTH], near_g[1, :, :WIDTH], far_g[:, :WIDTH])
    grad_normed = grad_normed + (mm_nt(high, misc[...]) + mm_nt(low, misc[...]))
    scaled = grad_normed * gain
    grad = cs[s].astype(F32) + inverse * (scaled - unit * jnp.mean(scaled * unit, axis=-1, keepdims=True))
    low_out[...] = grad.astype(BF)
    saved.append(local.copy(low_out, low_home))
    hidden[...] = grad
    saved.append(local.copy(hidden, grad_hidden))
    prod_high, prod_low = split_two(grad_normed * unit)
    one = (lane == 1).astype(BF)
    grad_misc[...] = mm_tn(normed_home, high) + mm_tn(normed_home, low) + mm_tn(prod_high, one) + mm_tn(prod_low, one)
    for copy in (*saved, *stored[0][2:], *stored[1][2:]):
        copy.wait()
    here.finish_rows()


def row_of(y, x, z):
    return pl.multiple_of(((y * 4 + x) * 2 + z) * SHARD, SHARD)


def finish_kernel(
    low_home, normed_two_in, cots_in, pre_a_in, pre_b_in,
    normed_in, qkv_in, heads_in, logs_in, qkv_full_in, out_full_in, out_far,
    segments, gains, grad_misc, grad_hidden, tokens,
    far_out, grad_tokens, grad_a, grad_b, ffn_a_all, ffn_b_all, one_all, two_all,
    grad_low, normed, part, pre_a, pre_b, staged, qkv, heads, logs, qkv_full, out_full,
    grad_one, grad_two, grad_heads, grad_all, grad_kv, near, far, gain_sum, seg_col,
    piece_a, piece_b, piece_one, piece_two,
    send_sems, local_sems, scatter_sems, out_sems, gather_sems, low_sems, *buffers,
):
    here = Here(send_sems)
    local = Local(local_sems)
    s = here.s
    load_a = [local.copy(normed_two_in, normed), local.copy(pre_a_in, pre_a), local.copy(cots_in, part)]
    load_b = local.copy(pre_b_in, pre_b)
    load_rest = [
        local.copy(a, b)
        for a, b in ((out_full_in, out_full), (heads_in, heads), (qkv_in, qkv), (logs_in, logs), (qkv_full_in, qkv_full))
    ]
    here.greet()
    here.meet()
    low_gather = seq_gather(here, low_home, grad_low, low_sems)
    next(low_gather)
    set_segments(segments, seg_col)
    seg_row = segments[...].astype(F32)

    def summed(sum_of, piece, full, sems, pause=1):
        yield from sum_of
        yield from seq_gather(here, piece, full, sems, pause)

    def from_hbm(grad, y_first):
        def block(df, ds, h):
            dy, dx = (ds, df) if y_first else (df, ds)
            return grad.at[pl.ds(row_of(wrap(here.y + dy), wrap(here.x + dx), h), SHARD)]

        return block

    def own_unit(place, j, ds, h):
        at = wrap(place + j)
        return at * 2 + h if ds == 0 else (8 if ds == 1 else 12) + at

    def owned(held, place):
        def own(j, ds, h):
            return held[pl.ds(pl.multiple_of(own_unit(place, j, ds, h) * SHARD, SHARD), SHARD), :]

        return own

    sum_a = scatter_grad(here, from_hbm(grad_a, True), owned(pre_a, here.x), buffers[:10], piece_a, True, False)
    sum_b = scatter_grad(here, from_hbm(grad_b, False), owned(pre_b, here.y), buffers[10:20], piece_b, False, False)
    sums = [summed(sum_a, piece_a, ffn_a_all, gather_sems.at[0], 4), summed(sum_b, piece_b, ffn_b_all, gather_sems.at[1], 4)]

    def chunk(y):
        return pl.ds(pl.multiple_of(y * CHUNK, CHUNK), CHUNK)

    moving = []
    for n, (j, k) in enumerate((j, k) for j in (2, 1, 3, 0) for k in range(2)):
        pre = (pre_a, pre_b)[k]
        if n == 0:
            load_a[0].wait()
            load_a[1].wait()
        if n == 1:
            load_b.wait()
        at = chunk(wrap(here.y + j))
        slot = staged.at[n % 2]
        slot[:, : 2 * HALF] = mm_tn(normed[:, at], pre[:, : 2 * HALF]).astype(BF)
        if n == 0:
            load_a[2].wait()
        if n > 1:
            moving[n - 1].wait()
            next(sums[(n - 1) % 2])
        slot[:, 2 * HALF :] = mm_tn(part[:, :, at].reshape(L, CHUNK), pre[:, 2 * HALF :]).astype(BF)
        moving.append(local.copy(slot, (grad_a, grad_b)[k].at[at]))
        if n == 0:
            moving[0].wait()
            next(sums[0])
    moving[-1].wait()
    next(sums[1])
    load_own = []
    for grad, held, y_first in ((grad_a, pre_a, True), (grad_b, pre_b, False)):
        for i in range(4):
            for ds, h in ((0, 0), (0, 1), (1, 0), (3, 1)):
                y, x = (wrap(here.y + ds), i) if y_first else (i, wrap(here.x + ds))
                unit = i * 2 + h if ds == 0 else (8 if ds == 1 else 12) + i
                source = grad.at[pl.ds(row_of(y, x, h), SHARD)]
                load_own.append(local.copy(source, held.at[pl.ds(unit * SHARD, SHARD)]))
    load_rest.append(local.copy(normed_in, normed))
    here.send(out_far, far_out, out_sems.at[0], here.far, True)
    next(low_gather)
    for load in load_own:
        load.wait()

    def tick():
        for part_sum in sums[:2]:
            next(part_sum)

    tick()
    next(low_gather, None)
    for load in load_rest:
        load.wait()
    for b in range(SEQ):
        at = slice(b * ROWS, (b + 1) * ROWS)
        grad_heads[at, :] = mm(grad_low[b], out_full[:, :Q_COLS]).astype(BF)

    def blocks_of(grad, y_first):
        def block(df, ds, h):
            dy, dx = (ds, df) if y_first else (df, ds)
            return grad.at[wrap(here.y + dy), wrap(here.x + dx), h]

        return block

    def out_chunk(y, carry):
        value = mm_tn(grad_low[:, :, chunk(y)].reshape(L, CHUNK), heads[...])
        grad_two[y, :, :, :, HEAD:KV] = value.astype(BF).reshape(4, 2, SHARD, Q_COLS)
        return carry

    lax.fori_loop(0, 4, out_chunk, 0)
    tick()
    grad_kv[...] = jnp.zeros_like(grad_kv)
    for b in range(SEQ):
        at, kv_len = b * ROWS, (b + 1) * ROWS
        bias = mask_bias(at, kv_len, seg_col, seg_row)
        for h in range(GROUP):
            cols = slice(h * HEAD, (h + 1) * HEAD)
            query, grad = qkv[at : at + ROWS, cols], grad_heads[at : at + ROWS, cols]
            scores = mm_nt(query, qkv[:kv_len, Q_COLS:KV]) * SCALE
            probs = jnp.exp((scores + bias) - logs[at : at + ROWS, h : h + 1])
            grad_probs = mm_nt(grad, qkv[:kv_len, KV:])
            centre = jnp.sum(probs * grad_probs, axis=-1, keepdims=True)
            grad_scores = (probs * (grad_probs - centre)).astype(BF)
            grad_all[at : at + ROWS, cols] = (mm(grad_scores, qkv[:kv_len, Q_COLS:KV]) * SCALE).astype(BF)
            grad_kv[:kv_len, :HEAD] += mm_tn(grad_scores, query) * SCALE
            grad_kv[:kv_len, HEAD:] += mm_tn(probs.astype(BF), grad)
    tick()
    grad_all[:, Q_COLS:] = grad_kv[...].astype(BF)

    def weight_chunk(y, carry):
        at = chunk(y)
        value = mm_tn(normed[:, at], grad_all[...]).astype(BF)
        grad_one[y] = value[:, :KV].reshape(4, 2, SHARD, KV)
        grad_two[y, :, :, :, :HEAD] = value[:, KV:].reshape(4, 2, SHARD, HEAD)
        return carry

    lax.fori_loop(0, 4, weight_chunk, 0)
    sum_one = scatter_grad(here, blocks_of(grad_one, True), None, buffers[20:30], piece_one, True, True)
    sums.append(summed(sum_one, piece_one, one_all, gather_sems.at[2]))
    tick()
    gain_sum[...] = jnp.zeros_like(gain_sum)

    def back(i):
        at = pl.ds(pl.multiple_of(i * ROWS, ROWS), ROWS)
        value = mm_nt(grad_all[at, :], qkv_full[...])
        part[i] = value.astype(BF)
        gain_sum[0:1, :] += jnp.sum(value * normed[at, :].astype(F32), axis=0, keepdims=True)

    row_sum = seq_scatter(here, part, near, far, scatter_sems, back, 4)
    next(row_sum)
    next(row_sum)
    tick()
    gain = gains[0:1, :]
    high, low = split_two(gain_sum[0:1, :] / gain)
    row = iota((16, WIDTH), 0)
    both = jnp.where(row == 0, high.astype(F32), 0.0) + jnp.where(row == 1, low.astype(F32), 0.0)
    pick = (iota((16, LANES), 1) == 0).astype(BF)
    single = (grad_misc[...] + mm_tn(both.astype(BF), pick)).astype(BF)
    grad_two[:, :, :, :, KV:] = single.reshape(4, 4, 2, SHARD, LANES)
    sum_two = scatter_grad(here, blocks_of(grad_two, False), None, buffers[30:], piece_two, False, True)
    sums.append(summed(sum_two, piece_two, two_all, gather_sems.at[3]))

    def rows():
        yield from row_sum
        here.wait(far_out, out_sems.at[0])
        grad_normed = added(part[s], near[1], far[...])
        inverse, unit, _ = normed_of(tokens[...].astype(F32), gain)
        scaled = grad_normed * gain
        grad_tokens[...] = (grad_hidden[...] + inverse * (scaled - unit * jnp.mean(scaled * unit, axis=-1, keepdims=True))).astype(BF)

    here.finish(64)
    together(*sums, rows())
    here.finish()
    here.finish_rows()


def as_row(col):
    n = col.shape[0]
    return jnp.sum(jnp.where(iota((n, n), 0) == iota((n, n), 1), jnp.broadcast_to(col, (n, n)), 0.0), axis=0, keepdims=True)


def outputs_kernel(
    ffn_a, ffn_b, one, two, out_own, far_out, output, wq, wk, wv, wo, gain_one, gain_two, router, shared_gate, shared_up, shared_down, expert_gate, expert_up, expert_down
):
    output[...] = added(out_own[...], far_out[...]).astype(BF)
    total = jnp.zeros((SHARD, LANES), F32)
    for s in range(SEQ):
        wq[:, s * Q_COLS : (s + 1) * Q_COLS] = one[s, :, :Q_COLS].astype(F32)
        wo[:, s * Q_COLS : (s + 1) * Q_COLS] = two[s, :, HEAD:KV].astype(F32)
        wk[:, s * HEAD : (s + 1) * HEAD] = one[s, :, Q_COLS:].astype(F32)
        wv[:, s * HEAD : (s + 1) * HEAD] = two[s, :, :HEAD].astype(F32)
        total = total + two[s, :, KV:].astype(F32)
        for k, ffn in enumerate((ffn_a, ffn_b)):
            n = 2 * s + k
            for i, (shared, expert) in enumerate(((shared_gate, expert_gate), (shared_up, expert_up), (shared_down, expert_down))):
                expert[:, n, :] = ffn[s, :, i * HALF : i * HALF + 512].astype(F32)
                shared[:, n * LANES : (n + 1) * LANES] = ffn[s, :, i * HALF + 512 : (i + 1) * HALF].astype(F32)
    gain_one[...] = as_row(total[:, 0:1])
    gain_two[...] = as_row(total[:, 1:2])
    for e in range(E):
        router[e : e + 1, :] = as_row(total[:, 2 + e : 3 + e])


def remote_call(kernel, name, number, outs, ins, scratch):
    return pl.pallas_call(
        kernel,
        out_shape=[jax.ShapeDtypeStruct(dims, dtype) for dims, dtype, _ in outs],
        in_specs=[VMEM_ALL if fast else ANY for _, fast in ins],
        out_specs=[VMEM_ALL if fast else ANY for _, _, fast in outs],
        scratch_shapes=list(scratch),
        compiler_params=pltpu.CompilerParams(collective_id=number, has_side_effects=True, vmem_limit_bytes=LIMIT),
        name=name,
    )(*[array for array, _ in ins])


def buf(*dims):
    return pltpu.VMEM(dims, BF)


def buf32(*dims):
    return pltpu.VMEM(dims, F32)


def body(
    tokens,
    segments,
    routes,
    shared_mask,
    norm_gain,
    w_query,
    key_weight,
    value_weight,
    w_out,
    ffn_gain,
    w_router,
    shared_gate,
    shared_up,
    shared_down,
    expert_gate,
    expert_up,
    expert_down,
    cotangent,
):
    seg_row = segments[None, :]
    grid = DMA((4, 4, 2))
    rows4 = (SEQ, ROWS, WIDTH)
    fast = [tokens, routes.T, shared_mask[None, :], norm_gain[None, :], ffn_gain[None, :], w_router.T, w_query, key_weight,
            value_weight, w_out, shared_gate, shared_up, shared_down, expert_gate, expert_up, expert_down, seg_row]
    (
        normed_one, qkv, heads, logs, gains, qkv_full, out_full, normed_two, all_cot,
        pre_a, pre_b, low_home, grad_hidden, grad_misc, out_far, out_own,
    ) = remote_call(
        forward_kernel,
        "forward",
        1,
        [
            ((L, WIDTH), BF, False),
            ((L, HALF), BF, False),
            ((L, Q_COLS), BF, False),
            ((L, 8), F32, False),
            ((8, WIDTH), F32, True),
            (blocks(HALF), BF, False),
            (blocks(OUT_COLS), BF, False),
            (rows4, BF, False),
            (rows4, BF, False),
            ((L, FFN), BF, False),
            ((L, FFN), BF, False),
            ((ROWS, WIDTH), BF, False),
            ((ROWS, WIDTH), F32, False),
            ((WIDTH, LANES), F32, True),
            ((ROWS, WIDTH), BF, False),
            ((ROWS, WIDTH), F32, False),
        ],
        [(a, True) for a in fast] + [(cotangent, False)],
        [
            buf(ROWS, WIDTH + LANES),
            buf(SEQ, ROWS, WIDTH + LANES),
            buf(SHARD, HALF),
            buf(SHARD, OUT_COLS),
            buf(SHARD, FFN),
            buf(SHARD, FFN),
            buf(*blocks(HALF)),
            buf(*blocks(OUT_COLS)),
            buf(L, WIDTH),
            buf(L, HALF),
            buf(L, Q_COLS),
            buf32(L, 8),
            buf32(L, 1),
            buf(L, LANES),
            buf(WIDTH, LANES),
            buf(*rows4),
            buf(2, ROWS, WIDTH),
            buf(ROWS, WIDTH),
            buf(ROWS, WIDTH),
            buf32(ROWS, WIDTH),
            buf(*rows4),
            buf(*rows4),
            buf(*blocks(FFN)),
            buf(*blocks(FFN)),
            buf(2, 2, ROWS, FFN),
            buf(2, ROWS, WIDTH + LANES),
            buf(ROWS, WIDTH + LANES),
            buf(2, ROWS, WIDTH),
            buf32(ROWS, LANES),
            buf32(ROWS, WIDTH),
            DMA((160,)),
            DMA((6,)),
            grid,
            grid,
            grid,
            grid,
            DMA((4,)),
            DMA((5,)),
            DMA((6,)),
            DMA((6,)),
            DMA((3,)),
            DMA((2,)),
            DMA((24,)),
        ],
    )

    far_out, grad_tokens, _, _, ffn_a_all, ffn_b_all, one_all, two_all = remote_call(
        finish_kernel,
        "finish",
        2,
        [
            ((ROWS, WIDTH), BF, False),
            ((ROWS, WIDTH), BF, True),
            ((WIDTH, FFN), BF, False),
            ((WIDTH, FFN), BF, False),
            ((SEQ, SHARD, FFN), BF, False),
            ((SEQ, SHARD, FFN), BF, False),
            ((SEQ, SHARD, KV), BF, False),
            ((SEQ, SHARD, HALF), BF, False),
        ],
        [
            (low_home, False),
            (normed_two.reshape(L, WIDTH), False),
            (all_cot, False),
            (pre_a, False),
            (pre_b, False),
            (normed_one, False),
            (qkv, False),
            (heads, False),
            (logs, False),
            (qkv_full.reshape(WIDTH, HALF), False),
            (out_full.reshape(WIDTH, OUT_COLS), False),
            (out_far, False),
            (seg_row, True),
            (gains, True),
            (grad_misc, True),
            (grad_hidden, True),
            (tokens, True),
        ],
        [
            buf(*rows4),
            buf(L, WIDTH),
            buf(*rows4),
            buf(L, FFN),
            buf(L, FFN),
            buf(2, CHUNK, FFN),
            buf(L, HALF),
            buf(L, Q_COLS),
            buf32(L, 8),
            buf(WIDTH, HALF),
            buf(WIDTH, OUT_COLS),
            buf(*blocks(KV)),
            buf(*blocks(HALF)),
            buf(L, Q_COLS),
            buf(L, HALF),
            buf32(L, 2 * HEAD),
            buf(2, ROWS, WIDTH),
            buf(ROWS, WIDTH),
            buf32(16, WIDTH),
            buf32(L, 1),
            buf(SHARD, FFN),
            buf(SHARD, FFN),
            buf(SHARD, KV),
            buf(SHARD, HALF),
            DMA((192,)),
            DMA((56,)),
            DMA((5,)),
            DMA((1,)),
            DMA((4, 6)),
            DMA((6,)),
            *scatter_buffers(FFN),
            *scatter_buffers(FFN),
            *scatter_buffers(KV),
            *scatter_buffers(HALF),
        ],
    )

    dims = [(ROWS, WIDTH), (SHARD, 4 * Q_COLS), (SHARD, 4 * HEAD), (SHARD, 4 * HEAD), (SHARD, 4 * Q_COLS), (1, SHARD), (1, SHARD), (E, SHARD)]
    dims += [(SHARD, 1024)] * 3 + [(SHARD, E, 512)] * 3
    output, wq, wk, wv, wo, gain_one, gain_two, router, *ffn = pl.pallas_call(
        outputs_kernel,
        out_shape=[jax.ShapeDtypeStruct(d, BF if d[0] == ROWS else F32) for d in dims],
        in_specs=[VMEM_ALL] * 6,
        out_specs=[VMEM_ALL] * len(dims),
        compiler_params=pltpu.CompilerParams(vmem_limit_bytes=LIMIT),
        name="outputs",
    )(ffn_a_all, ffn_b_all, one_all, two_all, out_own, far_out)
    return (output, grad_tokens, gain_one[0], wq, wk, wv, wo, gain_two[0], router.T, *ffn)


def solution(mesh):
    both = P(("fsdp", "seq"), None)
    one, two, three = P("fsdp"), P("fsdp", None), P("fsdp", None, None)
    return jax.shard_map(
        body,
        mesh=mesh,
        in_specs=(both, one, both, P(("fsdp", "seq")), one, two, two, two, two, one, two, two, two, two, three, three, three, both),
        out_specs=(both, both, one, two, two, two, two, one, two, two, two, two, three, three, three),
        check_vma=False,
    )
```
